32 devices in a mesh: groups: 2 (over x), bulk: 16 (over z, y, core).
Axes of the slice: x: 2, y: 2, z: 4, core: 2. Of those that a mesh axis runs over, the one named last changes fastest.
Arguments:
- electrons: float32 [1024, 128], P(('groups', 'bulk')), parts along dimension 0, may hold values from 0.05 to 0.95
- phonons: float32 [512, 128], P(('groups', 'bulk')), parts along dimension 0, may hold values from 0.05 to 2
- phonon_energy: float32 [256, 128], P('bulk'), may hold values from 0.5 to 3
- phonon_decay: float32 [256, 128], P('bulk'), may hold values from 0.5 to 5
- coupling: bfloat16 [4096, 128, 128], P('bulk'), may hold values from 0.00049972534 to 0.019897461
- tile_kblock: int32 [4096], P('bulk'), may hold values from 0 to 31
- tile_partner: int32 [4096], P('bulk'), may hold values from 0 to 31
- tile_qslot: int32 [4096], P('bulk'), may hold values from 0 to 31
- tile_count: int32 [16], P('bulk'), may hold values from 32 to 256, as said below
- partner_need: int32 [16, 32], P('bulk'), may hold values from 0 to 31
- phonon_need: int32 [16, 32], P('bulk'), may hold values from 0 to 15
Outputs:
- electrons_next: float32 [1024, 128], P(('groups', 'bulk')), parts along dimension 0
- phonons_next: float32 [512, 128], P(('groups', 'bulk')), parts along dimension 0
The draws below stay inside these ranges and needn't reach their ends.
There are 2 independent parts, one for each index of `groups`. The reference program is written for one: setup_inputs(seed, part) draws one part's arguments, and reference() takes and returns one part's arrays. A program takes and returns all parts, laid end to end along the dimension named above; an argument that names none is the same for every part. Nothing has to cross between parts.
Inputs may be any that keep to these rules, and one draw needn't show every extreme that they name: The first tile_count[e] of the 256 slots of bulk index e hold tiles, the others are unused. Each count is 256, 128, 64 or 32, and at least one device has 256. `tile_partner`: slot r of a device's partner list names local block partner_need[e, r] of bulk index r // 2; every device lists exactly 2 blocks of every device, itself included, repeats allowed. `tile_qslot`: slot s of a device's phonon list names local q block phonon_need[e, s] of bulk index s // 2; every device lists exactly 2 q blocks of every device, repeats allowed.
All inputs are finite; a program needn't handle non-finite values.
Results may differ from the reference program's by a relative error of at most 0.0003.
Values sent between devices are 32-bit elements; how exact they have to be, the bound alone decides.
No kernel may reach another device: no remote copies, remote signals or barrier semaphores. Data moves between devices by JAX's collectives and lax.ppermute only.
A program may use at most 64 MiB of HBM per device.

```python
import math
import jax
import jax.numpy as jnp
from jax import lax

BLK = 128
KB = 32
TPD = 256
CAP = 2
QCAP = 2
STEPS = 2
QB = 16
KBLK = 512
QBLK = 256
TILES = 4096
N_BULK = 16


def draw_tile_count(key, part):
    key = jax.random.fold_in(key, 11)
    shift_key, top_key = jax.random.split(key)
    shifts = jax.random.randint(shift_key, (N_BULK,), 0, 4)
    counts = TPD // jnp.left_shift(jnp.ones((N_BULK,), jnp.int32), shifts.astype(jnp.int32))
    chosen = jax.random.randint(top_key, (), 0, N_BULK)
    return jnp.where(jnp.arange(N_BULK) == chosen, TPD, counts).astype(jnp.int32)


def with_ends(array, stream_key, smallest, high):
    dims = array.shape
    spot = [jax.random.randint(jax.random.fold_in(stream_key, axis), (), 0, dims[axis]) for axis in range(len(dims))]
    array = array.at[tuple(spot)].set(smallest)
    longest = dims.index(max(dims))
    spot[longest] = (spot[longest] + 1) % dims[longest]
    return array.at[tuple(spot)].set(high)


def shard_levels(rng, dims, cuts, low, largest):
    level, own = 1.0, jax.random.fold_in(rng, 6)
    for position, blocks in cuts:
        heights = jnp.exp(jax.random.uniform(jax.random.fold_in(own, position), (blocks,), jnp.float32, low / len(cuts), largest / len(cuts)))
        level = level * jnp.repeat(heights, dims[position] // blocks).reshape([-1 if axis == position else 1 for axis in range(len(dims))])
    return level


def setup_inputs(seed: int = 0, part: int = 0) -> dict:
    keys = jax.random.split(jax.random.key(seed), 12)
    own_keys = jax.random.split(jax.random.fold_in(keys[11], part), 12)
    electrons = jnp.clip(0.05 + 0.9 * jax.random.uniform(own_keys[0], (KBLK, BLK), jnp.float32) ** shard_levels(own_keys[0], (KBLK, BLK), ((0, 16),), -0.2, 0.2), 0.05, 0.95)
    phonons = jnp.clip(jnp.exp(math.log(2.0) - 3.6888794 * jax.random.uniform(own_keys[1], (QBLK, BLK), jnp.float32) ** shard_levels(own_keys[1], (QBLK, BLK), ((0, 16),), -0.2, 0.2)), 0.05, 2.0)
    phonon_energy = jnp.clip(0.5 + 2.5 * jax.random.uniform(keys[2], (QBLK, BLK), jnp.float32) ** shard_levels(keys[2], (QBLK, BLK), ((0, 16),), -0.2, 0.2), 0.5, 3.0)
    phonon_decay = jnp.clip(jnp.exp(math.log(5.0) - 2.3025851 * jax.random.uniform(keys[3], (QBLK, BLK), jnp.float32) ** shard_levels(keys[3], (QBLK, BLK), ((0, 16),), -0.2, 0.2)), 0.5, 5.0)
    coupling = jnp.clip(jnp.exp(math.log(0.019897461) - 3.6842888 * jax.random.uniform(keys[4], (TILES, BLK, BLK), jnp.float32) ** shard_levels(keys[4], (TILES, BLK, BLK), ((0, 16),), -0.2, 0.2)), 0.00049972534, 0.019897461).astype(jnp.bfloat16)
    tile_kblock = with_ends(jax.random.randint(keys[5], (TILES,), 0, KB), jax.random.fold_in(keys[5], 1), 0, KB - 1).astype(jnp.int32)
    tile_partner = with_ends(jax.random.randint(keys[6], (TILES,), 0, N_BULK * CAP), jax.random.fold_in(keys[6], 1), 0, (N_BULK * CAP) - 1).astype(jnp.int32)
    tile_qslot = with_ends(jax.random.randint(keys[7], (TILES,), 0, N_BULK * QCAP), jax.random.fold_in(keys[7], 1), 0, (N_BULK * QCAP) - 1).astype(jnp.int32)
    tile_count = draw_tile_count(jax.random.fold_in(keys[11], 71), part)
    partner_need = with_ends(jax.random.randint(keys[9], (N_BULK, N_BULK * CAP), 0, KB), jax.random.fold_in(keys[9], 1), 0, KB - 1).astype(jnp.int32)
    phonon_need = with_ends(jax.random.randint(keys[10], (N_BULK, N_BULK * QCAP), 0, QB), jax.random.fold_in(keys[10], 1), 0, QB - 1).astype(jnp.int32)
    return {"electrons": electrons, "phonons": phonons, "phonon_energy": phonon_energy, "phonon_decay": phonon_decay, "coupling": coupling, "tile_kblock": tile_kblock, "tile_partner": tile_partner, "tile_qslot": tile_qslot, "tile_count": tile_count, "partner_need": partner_need, "phonon_need": phonon_need}


step_size = 0.05
highest = lax.Precision.HIGHEST


def collision_rates(occupied, bosons, thermal, phonon_decay, coupling, tile_kblock, tile_partner, tile_qslot, tile_count, partner_need, phonon_need):
    coupling_blocks = coupling.reshape(N_BULK, TPD, BLK, BLK)
    kblock_rows = tile_kblock.reshape(N_BULK, TPD)
    partner_rows = tile_partner.reshape(N_BULK, TPD)
    qslot_rows = tile_qslot.reshape(N_BULK, TPD)

    def one_device(phonon_total, device):
        local_k = kblock_rows[device]
        partner_slot = partner_rows[device]
        q_slot = qslot_rows[device]
        in_use = jnp.arange(TPD, dtype=jnp.int32) < tile_count[device]
        partner = (partner_slot // CAP) * KB + jnp.take(partner_need[device], partner_slot)
        qblock = (q_slot // QCAP) * QB + jnp.take(phonon_need[device], q_slot)
        own_fill = jnp.take(occupied, device * KB + local_k, axis=0)
        far_fill = jnp.take(occupied, partner, axis=0)
        far_bose = jnp.take(bosons, qblock, axis=0)
        pair_weights = jnp.stack([far_fill * (1.0 + far_bose), far_fill + far_bose], axis=1).astype(jnp.bfloat16)
        hole_weights = jnp.stack([1.0 - own_fill, own_fill], axis=1).astype(jnp.bfloat16)
        pair_weights, hole_weights = lax.optimization_barrier((pair_weights, hole_weights))
        matrix = coupling_blocks[device].astype(jnp.float32)
        forward = jnp.einsum("tsj,tij->tsi", pair_weights.astype(jnp.float32), matrix, precision=highest)
        backward = jnp.einsum("tsi,tij->tsj", hole_weights.astype(jnp.float32), matrix, precision=highest)
        electron_terms = jnp.where(in_use[:, None], forward[:, 0] - own_fill * forward[:, 1], 0.0)
        phonon_terms = jnp.where(in_use[:, None], far_fill * (1.0 + far_bose) * backward[:, 0] - far_bose * (1.0 - far_fill) * backward[:, 1], 0.0)
        electron_part = jax.ops.segment_sum(electron_terms, local_k, num_segments=KB)
        phonon_total = phonon_total + jax.ops.segment_sum(phonon_terms, qblock, num_segments=QBLK)
        return phonon_total, electron_part

    phonon_total, electron_parts = lax.scan(one_device, jnp.zeros((QBLK, BLK), jnp.float32), jnp.arange(N_BULK, dtype=jnp.int32))
    electron_rate = electron_parts.reshape(KBLK, BLK)
    phonon_rate = phonon_total - phonon_decay * (bosons - thermal)
    return electron_rate, phonon_rate


def reference(electrons, phonons, phonon_energy, phonon_decay, coupling, tile_kblock, tile_partner, tile_qslot, tile_count, partner_need, phonon_need):
    thermal = 1.0 / (jnp.exp(phonon_energy) - 1.0)
    occupied = electrons
    bosons = phonons
    for time_step in range(STEPS):
        electron_first, phonon_first = collision_rates(occupied, bosons, thermal, phonon_decay, coupling, tile_kblock, tile_partner, tile_qslot, tile_count, partner_need, phonon_need)
        occupied_mid = occupied + step_size * electron_first
        bosons_mid = bosons + step_size * phonon_first
        electron_second, phonon_second = collision_rates(occupied_mid, bosons_mid, thermal, phonon_decay, coupling, tile_kblock, tile_partner, tile_qslot, tile_count, partner_need, phonon_need)
        occupied = occupied + (step_size / 2.0) * (electron_first + electron_second)
        bosons = bosons + (step_size / 2.0) * (phonon_first + phonon_second)
    return occupied, bosons
```

```python
import functools

import jax
import jax.numpy as jnp
from jax import lax
from jax.experimental import pallas as pl
from jax.experimental.pallas import tpu as pltpu
from jax.sharding import PartitionSpec as P

STEPS = 2
DT = 0.05
f32 = jnp.float32
bf16 = jnp.bfloat16
VMEM_LIMIT = 24 * 1024 * 1024


def iota(shape, dim):
    return lax.broadcasted_iota(jnp.int32, shape, dim)


def dot(a, b):
    return lax.dot_general(a, b, (((1,), (0,)), ((), ())), preferred_element_type=f32)


def split(x):
    hi = x.astype(bf16)
    rest = x - hi.astype(f32)
    mid = rest.astype(bf16)
    lo = (rest - mid.astype(f32)).astype(bf16)
    return hi, mid, lo


def pick(onehot, x):
    hi, mid, lo = split(x)
    return dot(onehot, hi) + dot(onehot, mid) + dot(onehot, lo)


def stacked(first, second):
    tiles = first.shape[0]
    return jnp.concatenate(
        [first.reshape(tiles // 8, 8, 128), second.reshape(tiles // 8, 8, 128)], axis=1
    ).astype(bf16)


def row_is(r):
    return iota((16, 128), 0) % 8 == r


def backward_pass(own, c_ref, w_ref, out0, out1):
    groups = c_ref.shape[0] // 8
    w_ref[...] = stacked(1.0 - own, own)

    def body(g, _):
        w = w_ref[g].astype(f32)
        lhs = jnp.concatenate(
            [jnp.where(row_is(r), w, 0.0).astype(bf16) for r in range(8)], axis=1
        )
        rhs = c_ref[pl.ds(g * 8, 8)].reshape(1024, 128)
        res = dot(lhs, rhs)
        out0[g] = res[:8]
        out1[g] = res[8:]
        return 0

    lax.fori_loop(0, groups, body, 0, unroll=4)


def forward_pass(far, bose, c_ref, w_ref, out0, out1):
    groups = c_ref.shape[0] // 8
    w_ref[...] = stacked(far * (1.0 + bose), far + bose)

    def body(g, _):
        rhs = c_ref[pl.ds(g * 8, 8)].reshape(1024, 128)
        full = lax.dot_general(
            w_ref[g], rhs, (((1,), (1,)), ((), ())), preferred_element_type=f32
        )
        res = full[:, :128]
        for r in range(1, 8):
            res = jnp.where(row_is(r), full[:, r * 128 : (r + 1) * 128], res)
        out0[g] = res[:8]
        out1[g] = res[8:]
        return 0

    lax.fori_loop(0, groups, body, 0, unroll=4)


def flat(ref):
    return ref[...].reshape(-1, 128)


def electron_rate(sum_k, far, bose, f, c_ref, w_ref, o0, o1):
    forward_pass(far, bose, c_ref, w_ref, o0, o1)
    return pick(sum_k, flat(o0)) - f * pick(sum_k, flat(o1))


def need_kernel(kb, cap, pneed_ref, qneed_ref, out_ref):
    rows = out_ref.shape[0]
    slots = pneed_ref.shape[1]
    x = iota((rows, slots), 0)
    y = iota((rows, slots), 1)
    peer, r = x // (2 * cap), x % (2 * cap)
    e_here = (r < cap) & (y == peer * cap + r)
    p_here = (r >= cap) & (y == peer * cap + r - cap)
    pn = jnp.broadcast_to(pneed_ref[...].astype(f32), (rows, slots))
    qn = jnp.broadcast_to(qneed_ref[...].astype(f32), (rows, slots)) + float(kb)
    col = jnp.sum(jnp.where(e_here, pn, 0.0) + jnp.where(p_here, qn, 0.0), axis=1, keepdims=True)
    out_ref[...] = (iota((rows, 128), 1).astype(f32) == col).astype(f32)


def tables_kernel(
    cap,
    count_ref,
    kblock_ref,
    partner_ref,
    qslot_ref,
    f_ref,
    c_ref,
    ge4_ref,
    gp4_ref,
    gp8_ref,
    gk_ref,
    sk_ref,
    sp4_ref,
    sp8_ref,
    b0_ref,
    b1_ref,
    w_ref,
):
    tiles = kblock_ref.shape[1]
    kb = f_ref.shape[0]
    used = iota((1, tiles), 1) < count_ref[0]
    k = kblock_ref[...]
    e = partner_ref[...]
    q = qslot_ref[...]
    rows4 = sp4_ref.shape[0]
    rows8 = sp8_ref.shape[0]
    x = iota((kb, tiles), 0)
    ind = lambda m: jnp.where(m, 1.0, 0.0)
    k_hot = ind(x == k)
    sk_ref[...] = jnp.where(used, k_hot, 0.0).astype(bf16)
    gk_ref[...] = k_hot.T.astype(bf16)
    x = iota((rows4, tiles), 0)
    row_e = e // cap * (2 * cap) + e % cap
    row_p = q // cap * (2 * cap) + cap + q % cap
    ge4_ref[...] = ind(x == row_e).T.astype(bf16)
    p_hot = ind(x == row_p)
    gp4_ref[...] = p_hot.T.astype(bf16)
    sp4_ref[...] = jnp.where(used, p_hot, 0.0).astype(bf16)
    x = iota((rows8, tiles), 0)
    row_z = q // cap * (4 * cap) + q % cap
    gp8_ref[...] = ind(x == row_z).T.astype(bf16)
    sp8_ref[...] = jnp.concatenate(
        [
            jnp.where(used, ind(x == row_z + cap), 0.0),
            jnp.where(used, ind(x == row_z + 2 * cap), 0.0),
        ],
        axis=1,
    ).astype(bf16)
    own = pick(gk_ref[...], f_ref[...])
    backward_pass(own, c_ref, w_ref, b0_ref, b1_ref)


def serve_kernel(
    cap, s4_ref, f_ref, n_ref, send_ref, serve_ref, s8_ref, st4_ref, st8a_ref, st8b_ref
):
    kb, qb = f_ref.shape[0], n_ref.shape[0]
    s4 = s4_ref[...]
    rows4 = s4.shape[0]
    rows8 = s8_ref.shape[0]
    hot = s4.astype(bf16)
    serve_ref[...] = hot
    state = jnp.concatenate(
        [f_ref[...], n_ref[...], jnp.zeros((128 - kb - qb, 128), f32)], axis=0
    )
    send_ref[...] = pick(hot, state)
    x = iota((rows8, rows4), 0)
    y = iota((rows8, rows4), 1)
    peer, r = x // (4 * cap), x % (4 * cap)
    source = peer * (2 * cap) + cap + r % cap

    def rows_of(kind):
        here = (y == source) & (r // cap == kind)
        return dot(jnp.where(here, 1.0, 0.0).astype(bf16), hot)

    s8_ref[...] = rows_of(0).astype(bf16)
    st4_ref[...] = s4.T[kb : kb + qb].astype(bf16)
    st8a_ref[...] = rows_of(1).T[kb : kb + qb].astype(bf16)
    st8b_ref[...] = rows_of(2).T[kb : kb + qb].astype(bf16)


def first_kernel(
    recv_ref,
    f_ref,
    ge4_ref,
    gp4_ref,
    sk_ref,
    sp4_ref,
    serve_ref,
    b0_ref,
    b1_ref,
    c_ref,
    send_ref,
    e_ref,
    f1_ref,
    w_ref,
    o0,
    o1,
):
    kb = f_ref.shape[0]
    f = f_ref[...]
    recv = recv_ref[...]
    far = pick(ge4_ref[...], recv)
    bose = pick(gp4_ref[...], recv)
    gain = far * flat(b0_ref)
    terms = gain + bose * (gain - (1.0 - far) * flat(b1_ref))
    rate = electron_rate(sk_ref[...], far, bose, f, c_ref, w_ref, o0, o1)
    f1 = f + DT * rate
    e_ref[...] = rate
    f1_ref[...] = f1
    state = jnp.concatenate([f1, jnp.zeros((128 - kb, 128), f32)], axis=0)
    send_ref[...] = pick(serve_ref[...], state) + pick(sp4_ref[...], terms)


def backward_kernel(f_ref, gk_ref, c_ref, b0_ref, b1_ref, w_ref):
    own = pick(gk_ref[...], f_ref[...])
    backward_pass(own, c_ref, w_ref, b0_ref, b1_ref)


def phonon_kernel(
    recv_ref,
    n_ref,
    energy_ref,
    decay_ref,
    ge4_ref,
    st4_ref,
    sp8_ref,
    s8_ref,
    b0_ref,
    b1_ref,
    kb,
    send_ref,
    p_ref,
    n1_ref,
    far_ref,
):
    n = n_ref[...]
    qb = n.shape[0]
    recv = recv_ref[...]
    thermal = 1.0 / (jnp.exp(energy_ref[...]) - 1.0)
    rate = pick(st4_ref[...], recv) - decay_ref[...] * (n - thermal)
    n1 = n + DT * rate
    p_ref[...] = rate
    n1_ref[...] = n1
    far = pick(ge4_ref[...], recv)
    far_ref[...] = far
    gain = far * flat(b0_ref)
    both = jnp.concatenate([gain, gain - (1.0 - far) * flat(b1_ref)], axis=0)
    state = jnp.concatenate(
        [jnp.zeros((kb, 128), f32), n1, jnp.zeros((128 - kb - qb, 128), f32)], axis=0
    )
    send_ref[...] = pick(s8_ref[...], state) + pick(sp8_ref[...], both)


def second_kernel(
    with_send,
    recv_ref,
    far_ref,
    f_ref,
    f1_ref,
    e_ref,
    n_ref,
    n1_ref,
    p_ref,
    energy_ref,
    decay_ref,
    gp8_ref,
    sk_ref,
    st8a_ref,
    st8b_ref,
    serve_ref,
    c_ref,
    *rest,
):
    if with_send:
        f2_ref, n2_ref, send_ref, w_ref, o0, o1 = rest
    else:
        f2_ref, n2_ref, w_ref, o0, o1 = rest
    recv = recv_ref[...]
    n, n1 = n_ref[...], n1_ref[...]
    kb, qb = f_ref.shape[0], n.shape[0]
    thermal = 1.0 / (jnp.exp(energy_ref[...]) - 1.0)
    p1 = (
        pick(st8a_ref[...], recv)
        + n1 * pick(st8b_ref[...], recv)
        - decay_ref[...] * (n1 - thermal)
    )
    n2 = n + (DT / 2.0) * (p_ref[...] + p1)
    n2_ref[...] = n2
    bose = pick(gp8_ref[...], recv)
    rate = electron_rate(sk_ref[...], far_ref[...], bose, f1_ref[...], c_ref, w_ref, o0, o1)
    f2 = f_ref[...] + (DT / 2.0) * (e_ref[...] + rate)
    f2_ref[...] = f2
    if with_send:
        state = jnp.concatenate([f2, n2, jnp.zeros((128 - kb - qb, 128), f32)], axis=0)
        send_ref[...] = pick(serve_ref[...], state)


def call(kernel, name, outs, scratch=(), smem_first=False, flops=0, seen=0):
    vmem = pl.BlockSpec(memory_space=pltpu.VMEM)

    def run(*args):
        specs = [vmem] * len(args)
        if smem_first:
            specs[0] = pl.BlockSpec(memory_space=pltpu.SMEM)
        return pl.pallas_call(
            kernel,
            out_shape=[jax.ShapeDtypeStruct(s, d) for s, d in outs],
            in_specs=specs,
            out_specs=[vmem] * len(outs),
            scratch_shapes=list(scratch),
            compiler_params=pltpu.CompilerParams(vmem_limit_bytes=VMEM_LIMIT),
            cost_estimate=pl.CostEstimate(
                flops=flops, bytes_accessed=seen, transcendentals=0
            ),
            name=name,
        )(*args)

    return run


def on_device(
    electrons,
    phonons,
    phonon_energy,
    phonon_decay,
    coupling,
    tile_kblock,
    tile_partner,
    tile_qslot,
    tile_count,
    partner_need,
    phonon_need,
):
    devices = lax.axis_size("bulk")
    kb = electrons.shape[0]
    qb = phonons.shape[0]
    tiles = coupling.shape[0]
    cap = partner_need.shape[1] // devices
    assert cap == phonon_need.shape[1] // devices and kb + qb <= 128
    rows4 = devices * 2 * cap
    rows8 = devices * 4 * cap
    groups = tiles // 8
    weights = pltpu.VMEM((groups, 16, 128), bf16)
    partial_sums = pltpu.VMEM((groups, 8, 128), f32)
    pass_out = [((groups, 8, 128), f32)] * 2
    flops = 2 * tiles * 16 * 128 * 128
    c = pltpu.with_memory_space_constraint(coupling, pltpu.VMEM)

    def exchange(x):
        return lax.all_to_all(x, "bulk", split_axis=0, concat_axis=0, tiled=True)

    (need,) = call(functools.partial(need_kernel, kb, cap), "need", [((rows4, 128), f32)])(
        partner_need, phonon_need
    )
    served = exchange(need)
    ge4, gp4, gp8, gk, sk, sp4, sp8, b0, b1 = call(
        functools.partial(tables_kernel, cap),
        "tables",
        [
            ((tiles, rows4), bf16),
            ((tiles, rows4), bf16),
            ((tiles, rows8), bf16),
            ((tiles, kb), bf16),
            ((kb, tiles), bf16),
            ((rows4, tiles), bf16),
            ((rows8, 2 * tiles), bf16),
        ]
        + pass_out,
        [weights],
        smem_first=True,
        flops=flops,
    )(
        tile_count,
        tile_kblock.reshape(1, tiles),
        tile_partner.reshape(1, tiles),
        tile_qslot.reshape(1, tiles),
        electrons,
        c,
    )
    send, serve, s8, st4, st8a, st8b = call(
        functools.partial(serve_kernel, cap),
        "serve",
        [
            ((rows4, 128), f32),
            ((rows4, 128), bf16),
            ((rows8, 128), bf16),
            ((qb, rows4), bf16),
            ((qb, rows8), bf16),
            ((qb, rows8), bf16),
        ],
    )(served, electrons, phonons)

    back = call(backward_kernel, "backward", pass_out, [weights], flops=flops)
    f, n = electrons, phonons
    for step in range(STEPS):
        recv = exchange(send)
        if step:
            b0, b1 = back(f, gk, c)
        send, e0, f1 = call(
            first_kernel,
            "first",
            [((rows4, 128), f32), ((kb, 128), f32), ((kb, 128), f32)],
            [weights, partial_sums, partial_sums],
            flops=flops,
        )(recv, f, ge4, gp4, sk, sp4, serve, b0, b1, c)
        recv = exchange(send)
        b0, b1 = back(f1, gk, c)

        def phonon(*refs):
            phonon_kernel(*refs[:10], kb, *refs[10:])

        send, p0, n1, far = call(
            phonon,
            "phonon",
            [((rows8, 128), f32), ((qb, 128), f32), ((qb, 128), f32), ((tiles, 128), f32)],
        )(recv, n, phonon_energy, phonon_decay, ge4, st4, sp8, s8, b0, b1)
        recv = exchange(send)
        last = step == STEPS - 1
        outs = [((kb, 128), f32), ((qb, 128), f32)]
        if not last:
            outs.append(((rows4, 128), f32))
        f, n, *sent = call(
            functools.partial(second_kernel, not last),
            "second",
            outs,
            [weights, partial_sums, partial_sums],
            flops=flops,
        )(
            recv, far, f, f1, e0, n, n1, p0, phonon_energy, phonon_decay,
            gp8, sk, st8a, st8b, serve, c,
        )
        if not last:
            send = sent[0]
    return (f, n)


def solution(mesh):
    placed = (
        P(("groups", "bulk"), None),
        P(("groups", "bulk"), None),
        P("bulk", None),
        P("bulk", None),
        P("bulk", None, None),
        P("bulk"),
        P("bulk"),
        P("bulk"),
        P("bulk"),
        P("bulk", None),
        P("bulk", None),
    )
    return jax.shard_map(
        on_device,
        mesh=mesh,
        in_specs=placed,
        out_specs=(P(("groups", "bulk"), None), P(("groups", "bulk"), None)),
        check_vma=False,
    )
```

```python
import functools

import jax
import jax.numpy as jnp
from jax import lax
from jax.experimental import pallas as pl
from jax.experimental.pallas import tpu as pltpu
from jax.sharding import PartitionSpec as P

STEPS = 2
DT = 0.05
CHUNKS = 8
f32 = jnp.float32
bf16 = jnp.bfloat16
VMEM_LIMIT = 24 * 1024 * 1024


def iota(shape, dim):
    return lax.broadcasted_iota(jnp.int32, shape, dim)


def dot(a, b):
    return lax.dot_general(a, b, (((1,), (0,)), ((), ())), preferred_element_type=f32)


def split(x):
    hi = x.astype(bf16)
    rest = x - hi.astype(f32)
    mid = rest.astype(bf16)
    lo = (rest - mid.astype(f32)).astype(bf16)
    return hi, mid, lo


def pick(onehot, x):
    hi, mid, lo = split(x)
    return dot(onehot, hi) + dot(onehot, mid) + dot(onehot, lo)


def stacked(first, second):
    tiles = first.shape[0]
    return jnp.concatenate(
        [first.reshape(tiles // 8, 8, 128), second.reshape(tiles // 8, 8, 128)], axis=1
    ).astype(bf16)


def row_is(r):
    return iota((16, 128), 0) % 8 == r


def padded(*parts):
    rows = sum(p.shape[0] for p in parts)
    return jnp.concatenate([*parts, jnp.zeros((128 - rows, 128), f32)], axis=0)


def flat(ref):
    return ref[...].reshape(-1, 128)


def chunk_copies(c_hbm, c_ref, sems):
    size = c_ref.shape[0] // CHUNKS
    return [
        pltpu.make_async_copy(
            c_hbm.at[pl.ds(i * size, size)], c_ref.at[pl.ds(i * size, size)], sems.at[i]
        )
        for i in range(CHUNKS)
    ]


def start(copies):
    for copy in copies:
        copy.start()


def over_groups(copies, groups, body):
    size = groups // CHUNKS
    for i, copy in enumerate(copies):
        copy.wait()
        lax.fori_loop(i * size, (i + 1) * size, lambda g, _: body(g), 0, unroll=4)


def backward_pass(own, copies, c_ref, w_ref, out0, out1):
    groups = c_ref.shape[0] // 8
    w_ref[...] = stacked(1.0 - own, own)

    def body(g):
        w = w_ref[g].astype(f32)
        lhs = jnp.concatenate(
            [jnp.where(row_is(r), w, 0.0).astype(bf16) for r in range(8)], axis=1
        )
        rhs = c_ref[pl.ds(g * 8, 8)].reshape(1024, 128)
        res = dot(lhs, rhs)
        out0[g] = res[:8]
        out1[g] = res[8:]
        return 0

    over_groups(copies, groups, body)


def forward_pass(far, bose, copies, c_ref, w_ref, out0, out1):
    groups = c_ref.shape[0] // 8
    w_ref[...] = stacked(far * (1.0 + bose), far + bose)

    def body(g):
        rhs = c_ref[pl.ds(g * 8, 8)].reshape(1024, 128)
        full = lax.dot_general(
            w_ref[g], rhs, (((1,), (1,)), ((), ())), preferred_element_type=f32
        )
        res = full[:, :128]
        for r in range(1, 8):
            res = jnp.where(row_is(r), full[:, r * 128 : (r + 1) * 128], res)
        out0[g] = res[:8]
        out1[g] = res[8:]
        return 0

    over_groups(copies, groups, body)


def electron_rate(sum_k, far, bose, f, copies, c_ref, w_ref, o0, o1):
    forward_pass(far, bose, copies, c_ref, w_ref, o0, o1)
    return pick(sum_k, flat(o0)) - f * pick(sum_k, flat(o1))


def gather_blocks(blocks, into):
    rows = blocks[0].shape[0]
    for s, block in enumerate(blocks):
        into[s * rows : (s + 1) * rows, :] = block[...]
    return into[...]


def put_blocks(value, blocks):
    rows = blocks[0].shape[0]
    for s, block in enumerate(blocks):
        block[...] = value[s * rows : (s + 1) * rows]


def need_kernel(kb, cap, *refs):
    ins, outs = refs[:9], refs[9:]
    small, blocks = outs[:7], outs[7:-3]
    pneed_ref, qneed_ref, sems = outs[-3:]
    copies = [
        pltpu.make_async_copy(src, dst, sems.at[i])
        for i, (src, dst) in enumerate(zip(ins, [*small, pneed_ref, qneed_ref]))
    ]
    start(copies)
    me = lax.axis_index("bulk")
    rows = len(blocks) * 2 * cap
    slots = pneed_ref.shape[1]
    x = iota((rows, slots), 0)
    y = iota((rows, slots), 1)
    peer, r = (x // (2 * cap)) ^ me, x % (2 * cap)
    e_here = (r < cap) & (y == peer * cap + r)
    p_here = (r >= cap) & (y == peer * cap + r - cap)
    for copy in copies:
        copy.wait()
    pn = jnp.broadcast_to(pneed_ref[...].astype(f32), (rows, slots))
    qn = jnp.broadcast_to(qneed_ref[...].astype(f32), (rows, slots)) + float(kb)
    col = jnp.sum(jnp.where(e_here, pn, 0.0) + jnp.where(p_here, qn, 0.0), axis=1, keepdims=True)
    put_blocks((iota((rows, 128), 1).astype(f32) == col).astype(f32), blocks)


def tables_kernel(
    cap,
    count_ref,
    kblock_ref,
    partner_ref,
    qslot_ref,
    f_ref,
    c_hbm,
    ge4_ref,
    gp4_ref,
    gp6_ref,
    gk_ref,
    sk_ref,
    sp4_ref,
    sp6_ref,
    b0_ref,
    b1_ref,
    w_ref,
    c_ref,
    sems,
):
    copies = chunk_copies(c_hbm, c_ref, sems)
    start(copies)
    me = lax.axis_index("bulk")
    tiles = kblock_ref.shape[1]
    kb = f_ref.shape[0]
    used = iota((1, tiles), 1) < count_ref[0]
    k = kblock_ref[...]
    e = partner_ref[...]
    q = qslot_ref[...]
    rows4 = sp4_ref.shape[0]
    rows6 = sp6_ref.shape[0]
    ind = lambda m: jnp.where(m, 1.0, 0.0)
    k_hot = ind(iota((kb, tiles), 0) == k)
    sk_ref[...] = jnp.where(used, k_hot, 0.0).astype(bf16)
    gk_ref[...] = k_hot.T.astype(bf16)
    x = iota((rows4, tiles), 0)
    row_e = ((e // cap) ^ me) * (2 * cap) + e % cap
    row_p = ((q // cap) ^ me) * (2 * cap) + cap + q % cap
    ge4_ref[...] = ind(x == row_e).T.astype(bf16)
    p_hot = ind(x == row_p)
    gp4_ref[...] = p_hot.T.astype(bf16)
    sp4_ref[...] = jnp.where(used, p_hot, 0.0).astype(bf16)
    x = iota((rows6, tiles), 0)
    row_z = ((q // cap) ^ me) * (3 * cap) + q % cap
    gp6_ref[...] = ind(x == row_z).T.astype(bf16)
    sp6_ref[...] = jnp.concatenate(
        [
            jnp.where(used, ind(x == row_z + cap), 0.0),
            jnp.where(used, ind(x == row_z + 2 * cap), 0.0),
        ],
        axis=1,
    ).astype(bf16)
    own = pick(gk_ref[...], f_ref[...])
    backward_pass(own, copies, c_ref, w_ref, b0_ref, b1_ref)


def serve_kernel(devices, cap, *refs):
    recv, (f_ref, n_ref), outs = refs[:devices], refs[devices : devices + 2], refs[devices + 2 :]
    send, rest = outs[:devices], outs[devices:]
    serve_ref, s6_ref, st4_ref, st6a_ref, st6b_ref, into = rest
    kb, qb = f_ref.shape[0], n_ref.shape[0]
    s4 = gather_blocks(recv, into)
    rows4, rows6 = s4.shape[0], s6_ref.shape[0]
    hot = s4.astype(bf16)
    serve_ref[...] = hot
    put_blocks(pick(hot, padded(f_ref[...], n_ref[...])), send)
    x = iota((rows6, rows4), 0)
    y = iota((rows6, rows4), 1)
    peer, r = x // (3 * cap), x % (3 * cap)
    source = peer * (2 * cap) + cap + r % cap

    def rows_of(kind):
        here = (y == source) & (r // cap == kind)
        return dot(jnp.where(here, 1.0, 0.0).astype(bf16), hot)

    s6_ref[...] = rows_of(0).astype(bf16)
    st4_ref[...] = s4.T[kb : kb + qb].astype(bf16)
    st6a_ref[...] = rows_of(1).T[kb : kb + qb].astype(bf16)
    st6b_ref[...] = rows_of(2).T[kb : kb + qb].astype(bf16)


def first_kernel(devices, *refs):
    recv, refs = refs[:devices], refs[devices:]
    (f_ref, ge4_ref, gp4_ref, sk_ref, sp4_ref, serve_ref, b0_ref, b1_ref, c_hbm), refs = (
        refs[:9],
        refs[9:],
    )
    send, (e_ref, f1_ref, w_ref, c_ref, sems, o0, o1, into) = refs[:devices], refs[devices:]
    copies = chunk_copies(c_hbm, c_ref, sems)
    start(copies)
    f = f_ref[...]
    got = gather_blocks(recv, into)
    far = pick(ge4_ref[...], got)
    bose = pick(gp4_ref[...], got)
    rate = electron_rate(sk_ref[...], far, bose, f, copies, c_ref, w_ref, o0, o1)
    gain = far * flat(b0_ref)
    terms = gain + bose * (gain - (1.0 - far) * flat(b1_ref))
    f1 = f + DT * rate
    e_ref[...] = rate
    f1_ref[...] = f1
    put_blocks(pick(serve_ref[...], padded(f1)) + pick(sp4_ref[...], terms), send)


def backward_kernel(f_ref, gk_ref, c_hbm, b0_ref, b1_ref, w_ref, c_ref, sems):
    copies = chunk_copies(c_hbm, c_ref, sems)
    start(copies)
    own = pick(gk_ref[...], f_ref[...])
    backward_pass(own, copies, c_ref, w_ref, b0_ref, b1_ref)


def phonon_kernel(devices, kb, *refs):
    recv, refs = refs[:devices], refs[devices:]
    n_ref, energy_ref, decay_ref, ge4_ref, st4_ref, sp6_ref, s6_ref, b0_ref, b1_ref = refs[:9]
    refs = refs[9:]
    send, (p_ref, n1_ref, far_ref, into) = refs[:devices], refs[devices:]
    n = n_ref[...]
    got = gather_blocks(recv, into)
    thermal = 1.0 / (jnp.exp(energy_ref[...]) - 1.0)
    rate = pick(st4_ref[...], got) - decay_ref[...] * (n - thermal)
    n1 = n + DT * rate
    p_ref[...] = rate
    n1_ref[...] = n1
    far = pick(ge4_ref[...], got)
    far_ref[...] = far
    gain = far * flat(b0_ref)
    both = jnp.concatenate([gain, gain - (1.0 - far) * flat(b1_ref)], axis=0)
    state = padded(jnp.zeros((kb, 128), f32), n1)
    put_blocks(pick(s6_ref[...], state) + pick(sp6_ref[...], both), send)


def second_kernel(devices, with_send, *refs):
    recv, refs = refs[:devices], refs[devices:]
    far_ref, f_ref, f1_ref, e_ref, n_ref, n1_ref, p_ref, energy_ref, decay_ref = refs[:9]
    gp6_ref, sk_ref, st6a_ref, st6b_ref, serve_ref, c_hbm = refs[9:15]
    refs = refs[15:]
    send, refs = (refs[:devices], refs[devices:]) if with_send else ((), refs)
    f2_ref, n2_ref, w_ref, c_ref, sems, o0, o1, into = refs
    copies = chunk_copies(c_hbm, c_ref, sems)
    start(copies)
    got = gather_blocks(recv, into)
    n, n1 = n_ref[...], n1_ref[...]
    bose = pick(gp6_ref[...], got)
    rate = electron_rate(
        sk_ref[...], far_ref[...], bose, f1_ref[...], copies, c_ref, w_ref, o0, o1
    )
    thermal = 1.0 / (jnp.exp(energy_ref[...]) - 1.0)
    p1 = (
        pick(st6a_ref[...], got)
        + n1 * pick(st6b_ref[...], got)
        - decay_ref[...] * (n1 - thermal)
    )
    n2 = n + (DT / 2.0) * (p_ref[...] + p1)
    n2_ref[...] = n2
    f2 = f_ref[...] + (DT / 2.0) * (e_ref[...] + rate)
    f2_ref[...] = f2
    if with_send:
        put_blocks(pick(serve_ref[...], padded(f2, n2)), send)


def call(kernel, name, outs, scratch=(), spaces=None, flops=0, seen=0):
    def run(*args):
        places = dict(spaces or {})
        specs = [
            pl.BlockSpec(memory_space=places.get(i, pltpu.VMEM)) for i in range(len(args))
        ]
        return pl.pallas_call(
            kernel,
            out_shape=[jax.ShapeDtypeStruct(s, d) for s, d in outs],
            in_specs=specs,
            out_specs=[pl.BlockSpec(memory_space=pltpu.VMEM)] * len(outs),
            scratch_shapes=list(scratch),
            compiler_params=pltpu.CompilerParams(vmem_limit_bytes=VMEM_LIMIT),
            cost_estimate=pl.CostEstimate(
                flops=flops, bytes_accessed=seen, transcendentals=0
            ),
            name=name,
        )(*args)

    return run


def on_device(
    electrons,
    phonons,
    phonon_energy,
    phonon_decay,
    coupling,
    tile_kblock,
    tile_partner,
    tile_qslot,
    tile_count,
    partner_need,
    phonon_need,
):
    devices = lax.axis_size("bulk")
    kb = electrons.shape[0]
    qb = phonons.shape[0]
    tiles = coupling.shape[0]
    cap = partner_need.shape[1] // devices
    assert cap == phonon_need.shape[1] // devices and kb + qb <= 128
    assert devices & (devices - 1) == 0
    rows4 = devices * 2 * cap
    rows6 = devices * 3 * cap
    groups = tiles // 8
    streams = [
        pltpu.VMEM((groups, 16, 128), bf16),
        pltpu.VMEM(coupling.shape, bf16),
        pltpu.SemaphoreType.DMA((CHUNKS,)),
    ]
    sums = [pltpu.VMEM((groups, 8, 128), f32)] * 2
    pass_out = [((groups, 8, 128), f32)] * 2
    blocks4 = [((2 * cap, 128), f32)] * devices
    blocks6 = [((3 * cap, 128), f32)] * devices
    into4 = pltpu.VMEM((rows4, 128), f32)
    into6 = pltpu.VMEM((rows6, 128), f32)
    work = dict(flops=2 * tiles * 16 * 128 * 128, seen=tiles * 128 * 128 * 2)

    def exchange(blocks):
        return [blocks[0]] + [
            lax.ppermute(block, "bulk", [(i, i ^ s) for i in range(devices)])
            for s, block in enumerate(blocks)
            if s
        ]

    ints = ((1, tiles), jnp.int32)
    lists = ((1, partner_need.shape[1]), jnp.int32)
    small = [((kb, 128), f32)] + [((qb, 128), f32)] * 3 + [ints] * 3
    f, n, energy, decay, kblock, partner, qslot, *need = call(
        functools.partial(need_kernel, kb, cap),
        "need",
        small + blocks4,
        [pltpu.VMEM(*lists), pltpu.VMEM(*lists), pltpu.SemaphoreType.DMA((9,))],
        spaces={i: pltpu.HBM for i in range(9)},
    )(
        electrons,
        phonons,
        phonon_energy,
        phonon_decay,
        tile_kblock.reshape(1, tiles),
        tile_partner.reshape(1, tiles),
        tile_qslot.reshape(1, tiles),
        partner_need,
        phonon_need,
    )
    served = exchange(need)
    ge4, gp4, gp6, gk, sk, sp4, sp6, b0, b1 = call(
        functools.partial(tables_kernel, cap),
        "tables",
        [
            ((tiles, rows4), bf16),
            ((tiles, rows4), bf16),
            ((tiles, rows6), bf16),
            ((tiles, kb), bf16),
            ((kb, tiles), bf16),
            ((rows4, tiles), bf16),
            ((rows6, 2 * tiles), bf16),
        ]
        + pass_out,
        streams,
        spaces={0: pltpu.SMEM, 5: pltpu.HBM},
        **work,
    )(tile_count, kblock, partner, qslot, f, coupling)
    outs = call(
        functools.partial(serve_kernel, devices, cap),
        "serve",
        blocks4
        + [
            ((rows4, 128), bf16),
            ((rows6, 128), bf16),
            ((qb, rows4), bf16),
            ((qb, rows6), bf16),
            ((qb, rows6), bf16),
        ],
        [into4],
    )(*served, f, n)
    send, (serve, s6, st4, st6a, st6b) = outs[:devices], outs[devices:]

    back = call(backward_kernel, "backward", pass_out, streams, spaces={2: pltpu.HBM}, **work)
    for step in range(STEPS):
        recv = exchange(send)
        if step:
            b0, b1 = back(f, gk, coupling)
        outs = call(
            functools.partial(first_kernel, devices),
            "first",
            blocks4 + [((kb, 128), f32)] * 2,
            streams + sums + [into4],
            spaces={devices + 8: pltpu.HBM},
            **work,
        )(*recv, f, ge4, gp4, sk, sp4, serve, b0, b1, coupling)
        send, (e0, f1) = outs[:devices], outs[devices:]
        recv = exchange(send)
        b0, b1 = back(f1, gk, coupling)
        outs = call(
            functools.partial(phonon_kernel, devices, kb),
            "phonon",
            blocks6 + [((qb, 128), f32)] * 2 + [((tiles, 128), f32)],
            [into4],
        )(*recv, n, energy, decay, ge4, st4, sp6, s6, b0, b1)
        send, (p0, n1, far) = outs[:devices], outs[devices:]
        recv = exchange(send)
        last = step == STEPS - 1
        outs = call(
            functools.partial(second_kernel, devices, not last),
            "second",
            ([] if last else blocks4) + [((kb, 128), f32), ((qb, 128), f32)],
            streams + sums + [into6],
            spaces={devices + 14: pltpu.HBM},
            **work,
        )(
            *recv, far, f, f1, e0, n, n1, p0, energy, decay,
            gp6, sk, st6a, st6b, serve, coupling,
        )
        send, (f, n) = outs[:-2], outs[-2:]
    return (f, n)


def solution(mesh):
    placed = (
        P(("groups", "bulk"), None),
        P(("groups", "bulk"), None),
        P("bulk", None),
        P("bulk", None),
        P("bulk", None, None),
        P("bulk"),
        P("bulk"),
        P("bulk"),
        P("bulk"),
        P("bulk", None),
        P("bulk", None),
    )
    return jax.shard_map(
        on_device,
        mesh=mesh,
        in_specs=placed,
        out_specs=(P(("groups", "bulk"), None), P(("groups", "bulk"), None)),
        check_vma=False,
    )
```

```python
import functools

import jax
import jax.numpy as jnp
from jax import lax
from jax.experimental import pallas as pl
from jax.experimental.pallas import tpu as pltpu
from jax.sharding import PartitionSpec as P

STEPS = 2
DT = 0.05
CHUNKS = 8
f32 = jnp.float32
bf16 = jnp.bfloat16
VMEM_LIMIT = 24 * 1024 * 1024


def iota(shape, dim):
    return lax.broadcasted_iota(jnp.int32, shape, dim)


def dot(a, b):
    return lax.dot_general(a, b, (((1,), (0,)), ((), ())), preferred_element_type=f32)


def split(x):
    hi = x.astype(bf16)
    rest = x - hi.astype(f32)
    mid = rest.astype(bf16)
    lo = (rest - mid.astype(f32)).astype(bf16)
    return hi, mid, lo


def pick(onehot, x):
    hi, mid, lo = split(x)
    return dot(onehot, hi) + dot(onehot, mid) + dot(onehot, lo)


def stacked(first, second):
    tiles = first.shape[0]
    return jnp.concatenate(
        [first.reshape(tiles // 8, 8, 128), second.reshape(tiles // 8, 8, 128)], axis=1
    ).astype(bf16)


def row_is(r):
    return iota((16, 128), 0) % 8 == r


def padded(*parts):
    rows = sum(p.shape[0] for p in parts)
    return jnp.concatenate([*parts, jnp.zeros((128 - rows, 128), f32)], axis=0)


def flat(ref):
    return ref[...].reshape(-1, 128)


def chunk_copies(c_hbm, c_ref, sems):
    size = c_ref.shape[0] // CHUNKS
    return [
        pltpu.make_async_copy(
            c_hbm.at[pl.ds(i * size, size)], c_ref.at[pl.ds(i * size, size)], sems.at[i]
        )
        for i in range(CHUNKS)
    ]


def start(copies):
    for copy in copies:
        copy.start()


def over_groups(copies, groups, body):
    size = groups // CHUNKS
    for i, copy in enumerate(copies):
        copy.wait()
        lax.fori_loop(i * size, (i + 1) * size, lambda g, _: body(g), 0, unroll=4)


def backward_pass(own, copies, c_ref, w_ref, out0, out1):
    groups = c_ref.shape[0] // 8
    w_ref[...] = stacked(1.0 - own, own)

    def body(g):
        w = w_ref[g].astype(f32)
        lhs = jnp.concatenate(
            [jnp.where(row_is(r), w, 0.0).astype(bf16) for r in range(8)], axis=1
        )
        rhs = c_ref[pl.ds(g * 8, 8)].reshape(1024, 128)
        res = dot(lhs, rhs)
        out0[g] = res[:8]
        out1[g] = res[8:]
        return 0

    over_groups(copies, groups, body)


def forward_pass(far, bose, copies, c_ref, w_ref, out0, out1):
    groups = c_ref.shape[0] // 8
    w_ref[...] = stacked(far * (1.0 + bose), far + bose)

    def body(g):
        rhs = c_ref[pl.ds(g * 8, 8)].reshape(1024, 128)
        full = lax.dot_general(
            w_ref[g], rhs, (((1,), (1,)), ((), ())), preferred_element_type=f32
        )
        res = full[:, :128]
        for r in range(1, 8):
            res = jnp.where(row_is(r), full[:, r * 128 : (r + 1) * 128], res)
        out0[g] = res[:8]
        out1[g] = res[8:]
        return 0

    over_groups(copies, groups, body)


def electron_rate(sum_k, far, bose, f, copies, c_ref, w_ref, o0, o1):
    forward_pass(far, bose, copies, c_ref, w_ref, o0, o1)
    return pick(sum_k, flat(o0)) - f * pick(sum_k, flat(o1))


def need_kernel(kb, cap, *refs):
    ins, outs = refs[:9], refs[9:]
    small, out_ref = outs[:7], outs[7]
    pneed_ref, qneed_ref, sems = outs[-3:]
    copies = [
        pltpu.make_async_copy(src, dst, sems.at[i])
        for i, (src, dst) in enumerate(zip(ins, [*small, pneed_ref, qneed_ref]))
    ]
    start(copies)
    rows = out_ref.shape[0]
    slots = pneed_ref.shape[1]
    x = iota((rows, slots), 0)
    y = iota((rows, slots), 1)
    peer, r = x // (2 * cap), x % (2 * cap)
    e_here = (r < cap) & (y == peer * cap + r)
    p_here = (r >= cap) & (y == peer * cap + r - cap)
    for copy in copies:
        copy.wait()
    pn = jnp.broadcast_to(pneed_ref[...].astype(f32), (rows, slots))
    qn = jnp.broadcast_to(qneed_ref[...].astype(f32), (rows, slots)) + float(kb)
    col = jnp.sum(jnp.where(e_here, pn, 0.0) + jnp.where(p_here, qn, 0.0), axis=1, keepdims=True)
    out_ref[...] = (iota((rows, 128), 1).astype(f32) == col).astype(f32)


def tables_kernel(
    cap,
    count_ref,
    kblock_ref,
    partner_ref,
    qslot_ref,
    f_ref,
    c_hbm,
    ge4_ref,
    gp4_ref,
    gp8_ref,
    gk_ref,
    sk_ref,
    sp4_ref,
    sp8_ref,
    b0_ref,
    b1_ref,
    w_ref,
    c_ref,
    sems,
):
    copies = chunk_copies(c_hbm, c_ref, sems)
    start(copies)
    tiles = kblock_ref.shape[1]
    kb = f_ref.shape[0]
    used = iota((1, tiles), 1) < count_ref[0]
    k = kblock_ref[...]
    e = partner_ref[...]
    q = qslot_ref[...]
    rows4 = sp4_ref.shape[0]
    rows8 = sp8_ref.shape[0]
    ind = lambda m: jnp.where(m, 1.0, 0.0)
    k_hot = ind(iota((kb, tiles), 0) == k)
    sk_ref[...] = jnp.where(used, k_hot, 0.0).astype(bf16)
    gk_ref[...] = k_hot.T.astype(bf16)
    x = iota((rows4, tiles), 0)
    row_e = (e // cap) * (2 * cap) + e % cap
    row_p = (q // cap) * (2 * cap) + cap + q % cap
    ge4_ref[...] = ind(x == row_e).T.astype(bf16)
    p_hot = ind(x == row_p)
    gp4_ref[...] = p_hot.T.astype(bf16)
    sp4_ref[...] = jnp.where(used, p_hot, 0.0).astype(bf16)
    x = iota((rows8, tiles), 0)
    row_z = (q // cap) * (4 * cap) + q % cap
    gp8_ref[...] = ind(x == row_z).T.astype(bf16)
    sp8_ref[...] = jnp.concatenate(
        [
            jnp.where(used, ind(x == row_z + cap), 0.0),
            jnp.where(used, ind(x == row_z + 2 * cap), 0.0),
        ],
        axis=1,
    ).astype(bf16)
    own = pick(gk_ref[...], f_ref[...])
    backward_pass(own, copies, c_ref, w_ref, b0_ref, b1_ref)


def serve_kernel(
    cap, recv, f_ref, n_ref, send, serve_ref, s8_ref, st4_ref, st8a_ref, st8b_ref
):
    kb, qb = f_ref.shape[0], n_ref.shape[0]
    s4 = recv[...]
    rows4, rows8 = s4.shape[0], s8_ref.shape[0]
    hot = s4.astype(bf16)
    serve_ref[...] = hot
    send[...] = pick(hot, padded(f_ref[...], n_ref[...]))
    x = iota((rows8, rows4), 0)
    y = iota((rows8, rows4), 1)
    peer, r = x // (4 * cap), x % (4 * cap)
    source = peer * (2 * cap) + cap + r % cap

    def rows_of(kind):
        here = (y == source) & (r // cap == kind)
        return dot(jnp.where(here, 1.0, 0.0).astype(bf16), hot)

    s8_ref[...] = rows_of(0).astype(bf16)
    st4_ref[...] = s4.T[kb : kb + qb].astype(bf16)
    st8a_ref[...] = rows_of(1).T[kb : kb + qb].astype(bf16)
    st8b_ref[...] = rows_of(2).T[kb : kb + qb].astype(bf16)


def first_kernel(
    recv,
    f_ref,
    ge4_ref,
    gp4_ref,
    sk_ref,
    sp4_ref,
    serve_ref,
    b0_ref,
    b1_ref,
    c_hbm,
    send,
    e_ref,
    f1_ref,
    w_ref,
    c_ref,
    sems,
    o0,
    o1,
):
    copies = chunk_copies(c_hbm, c_ref, sems)
    start(copies)
    f = f_ref[...]
    got = recv[...]
    far = pick(ge4_ref[...], got)
    bose = pick(gp4_ref[...], got)
    rate = electron_rate(sk_ref[...], far, bose, f, copies, c_ref, w_ref, o0, o1)
    gain = far * flat(b0_ref)
    terms = gain + bose * (gain - (1.0 - far) * flat(b1_ref))
    f1 = f + DT * rate
    e_ref[...] = rate
    f1_ref[...] = f1
    send[...] = pick(serve_ref[...], padded(f1)) + pick(sp4_ref[...], terms)


def backward_kernel(f_ref, gk_ref, c_hbm, b0_ref, b1_ref, w_ref, c_ref, sems):
    copies = chunk_copies(c_hbm, c_ref, sems)
    start(copies)
    own = pick(gk_ref[...], f_ref[...])
    backward_pass(own, copies, c_ref, w_ref, b0_ref, b1_ref)


def phonon_kernel(
    kb,
    recv,
    n_ref,
    energy_ref,
    decay_ref,
    ge4_ref,
    st4_ref,
    sp8_ref,
    s8_ref,
    b0_ref,
    b1_ref,
    send,
    p_ref,
    n1_ref,
    far_ref,
):
    n = n_ref[...]
    got = recv[...]
    thermal = 1.0 / (jnp.exp(energy_ref[...]) - 1.0)
    rate = pick(st4_ref[...], got) - decay_ref[...] * (n - thermal)
    n1 = n + DT * rate
    p_ref[...] = rate
    n1_ref[...] = n1
    far = pick(ge4_ref[...], got)
    far_ref[...] = far
    gain = far * flat(b0_ref)
    both = jnp.concatenate([gain, gain - (1.0 - far) * flat(b1_ref)], axis=0)
    state = padded(jnp.zeros((kb, 128), f32), n1)
    send[...] = pick(s8_ref[...], state) + pick(sp8_ref[...], both)


def second_kernel(with_send, recv, *refs):
    far_ref, f_ref, f1_ref, e_ref, n_ref, n1_ref, p_ref, energy_ref, decay_ref = refs[:9]
    gp8_ref, sk_ref, st8a_ref, st8b_ref, serve_ref, c_hbm = refs[9:15]
    refs = refs[15:]
    f2_ref, n2_ref, *refs = refs
    send, refs = (refs[0], refs[1:]) if with_send else (None, refs)
    w_ref, c_ref, sems, o0, o1 = refs
    copies = chunk_copies(c_hbm, c_ref, sems)
    start(copies)
    got = recv[...]
    n, n1 = n_ref[...], n1_ref[...]
    bose = pick(gp8_ref[...], got)
    rate = electron_rate(
        sk_ref[...], far_ref[...], bose, f1_ref[...], copies, c_ref, w_ref, o0, o1
    )
    thermal = 1.0 / (jnp.exp(energy_ref[...]) - 1.0)
    p1 = (
        pick(st8a_ref[...], got)
        + n1 * pick(st8b_ref[...], got)
        - decay_ref[...] * (n1 - thermal)
    )
    n2 = n + (DT / 2.0) * (p_ref[...] + p1)
    n2_ref[...] = n2
    f2 = f_ref[...] + (DT / 2.0) * (e_ref[...] + rate)
    f2_ref[...] = f2
    if with_send:
        send[...] = pick(serve_ref[...], padded(f2, n2))


def call(kernel, name, outs, scratch=(), spaces=None, flops=0, seen=0):
    def run(*args):
        places = dict(spaces or {})
        args = [
            pltpu.with_memory_space_constraint(x, pltpu.HBM)
            if places.get(i) is pltpu.HBM
            else x
            for i, x in enumerate(args)
        ]
        specs = [
            pl.BlockSpec(memory_space=places.get(i, pltpu.VMEM)) for i in range(len(args))
        ]
        return pl.pallas_call(
            kernel,
            out_shape=[jax.ShapeDtypeStruct(s, d) for s, d in outs],
            in_specs=specs,
            out_specs=[pl.BlockSpec(memory_space=pltpu.VMEM)] * len(outs),
            scratch_shapes=list(scratch),
            compiler_params=pltpu.CompilerParams(vmem_limit_bytes=VMEM_LIMIT),
            cost_estimate=pl.CostEstimate(
                flops=flops, bytes_accessed=seen, transcendentals=0
            ),
            name=name,
        )(*args)

    return run


def on_device(
    electrons,
    phonons,
    phonon_energy,
    phonon_decay,
    coupling,
    tile_kblock,
    tile_partner,
    tile_qslot,
    tile_count,
    partner_need,
    phonon_need,
):
    devices = lax.axis_size("bulk")
    kb = electrons.shape[0]
    qb = phonons.shape[0]
    tiles = coupling.shape[0]
    cap = partner_need.shape[1] // devices
    assert cap == phonon_need.shape[1] // devices and kb + qb <= 128
    rows4 = devices * 2 * cap
    rows8 = devices * 4 * cap
    groups = tiles // 8
    streams = [
        pltpu.VMEM((groups, 16, 128), bf16),
        pltpu.VMEM(coupling.shape, bf16),
        pltpu.SemaphoreType.DMA((CHUNKS,)),
    ]
    sums = [pltpu.VMEM((groups, 8, 128), f32)] * 2
    pass_out = [((groups, 8, 128), f32)] * 2
    block4 = ((rows4, 128), f32)
    block8 = ((rows8, 128), f32)

    work = dict(flops=2 * tiles * 16 * 128 * 128, seen=tiles * 128 * 128 * 2)

    def exchange(x):
        return lax.all_to_all(x, "bulk", split_axis=0, concat_axis=0, tiled=True)

    ints = ((1, tiles), jnp.int32)
    lists = ((1, partner_need.shape[1]), jnp.int32)
    small = [((kb, 128), f32)] + [((qb, 128), f32)] * 3 + [ints] * 3
    f, n, energy, decay, kblock, partner, qslot, need = call(
        functools.partial(need_kernel, kb, cap),
        "need",
        small + [block4],
        [pltpu.VMEM(*lists), pltpu.VMEM(*lists), pltpu.SemaphoreType.DMA((9,))],
        spaces={i: pltpu.HBM for i in range(9)},
    )(
        electrons,
        phonons,
        phonon_energy,
        phonon_decay,
        tile_kblock.reshape(1, tiles),
        tile_partner.reshape(1, tiles),
        tile_qslot.reshape(1, tiles),
        partner_need,
        phonon_need,
    )
    served = exchange(need)
    ge4, gp4, gp8, gk, sk, sp4, sp8, b0, b1 = call(
        functools.partial(tables_kernel, cap),
        "tables",
        [
            ((tiles, rows4), bf16),
            ((tiles, rows4), bf16),
            ((tiles, rows8), bf16),
            ((tiles, kb), bf16),
            ((kb, tiles), bf16),
            ((rows4, tiles), bf16),
            ((rows8, 2 * tiles), bf16),
        ]
        + pass_out,
        streams,
        spaces={0: pltpu.SMEM, 5: pltpu.HBM},
        **work,
    )(tile_count, kblock, partner, qslot, f, coupling)
    send, serve, s8, st4, st8a, st8b = call(
        functools.partial(serve_kernel, cap),
        "serve",
        [
            block4,
            ((rows4, 128), bf16),
            ((rows8, 128), bf16),
            ((qb, rows4), bf16),
            ((qb, rows8), bf16),
            ((qb, rows8), bf16),
        ],
    )(served, f, n)

    back = call(backward_kernel, "backward", pass_out, streams, spaces={2: pltpu.HBM}, **work)
    for step in range(STEPS):
        recv = exchange(send)
        if step:
            b0, b1 = back(f, gk, coupling)
        send, e0, f1 = call(
            first_kernel,
            "first",
            [block4] + [((kb, 128), f32)] * 2,
            streams + sums,
            spaces={9: pltpu.HBM},
            **work,
        )(recv, f, ge4, gp4, sk, sp4, serve, b0, b1, coupling)
        recv = exchange(send)
        b0, b1 = back(f1, gk, coupling)
        send, p0, n1, far = call(
            functools.partial(phonon_kernel, kb),
            "phonon",
            [block8] + [((qb, 128), f32)] * 2 + [((tiles, 128), f32)],
        )(recv, n, energy, decay, ge4, st4, sp8, s8, b0, b1)
        recv = exchange(send)
        last = step == STEPS - 1
        f, n, *send = call(
            functools.partial(second_kernel, not last),
            "second",
            [((kb, 128), f32), ((qb, 128), f32)] + ([] if last else [block4]),
            streams + sums,
            spaces={15: pltpu.HBM},
            **work,
        )(
            recv, far, f, f1, e0, n, n1, p0, energy, decay,
            gp8, sk, st8a, st8b, serve, coupling,
        )
        send = send[0] if send else None
    return (f, n)


def solution(mesh):
    placed = (
        P(("groups", "bulk"), None),
        P(("groups", "bulk"), None),
        P("bulk", None),
        P("bulk", None),
        P("bulk", None, None),
        P("bulk"),
        P("bulk"),
        P("bulk"),
        P("bulk"),
        P("bulk", None),
        P("bulk", None),
    )
    return jax.shard_map(
        on_device,
        mesh=mesh,
        in_specs=placed,
        out_specs=(P(("groups", "bulk"), None), P(("groups", "bulk"), None)),
        check_vma=False,
    )
```

```python
import functools

import jax
import jax.numpy as jnp
from jax import lax
from jax.experimental import pallas as pl
from jax.experimental.pallas import tpu as pltpu
from jax.sharding import PartitionSpec as P

STEPS = 2
DT = 0.05
CHUNKS = 8
HELD_CHUNKS = 2
f32 = jnp.float32
bf16 = jnp.bfloat16
VMEM_LIMIT = 24 * 1024 * 1024


def iota(shape, dim):
    return lax.broadcasted_iota(jnp.int32, shape, dim)


def dot(a, b):
    return lax.dot_general(a, b, (((1,), (0,)), ((), ())), preferred_element_type=f32)


def split(x):
    hi = x.astype(bf16)
    rest = x - hi.astype(f32)
    mid = rest.astype(bf16)
    lo = (rest - mid.astype(f32)).astype(bf16)
    return hi, mid, lo


def pick(onehot, x):
    hi, mid, lo = split(x)
    return dot(onehot, hi) + dot(onehot, mid) + dot(onehot, lo)


def stacked(first, second):
    tiles = first.shape[0]
    return jnp.concatenate(
        [first.reshape(tiles // 8, 8, 128), second.reshape(tiles // 8, 8, 128)], axis=1
    ).astype(bf16)


def row_is(r):
    return iota((16, 128), 0) % 8 == r


def padded(*parts):
    rows = sum(p.shape[0] for p in parts)
    return jnp.concatenate([*parts, jnp.zeros((128 - rows, 128), f32)], axis=0)


def flat(ref):
    return ref[...].reshape(-1, 128)


def chunk_copies(src, dst, sems):
    count = sems.shape[0]
    size = src.shape[0] // count
    return [
        pltpu.make_async_copy(
            src.at[pl.ds(i * size, size)], dst.at[pl.ds(i * size, size)], sems.at[i]
        )
        for i in range(count)
    ]


def start(copies):
    for copy in copies:
        copy.start()


def block_diagonal(w):
    w = w.astype(f32)
    return jnp.concatenate(
        [jnp.where(row_is(r), w, 0.0).astype(bf16) for r in range(8)], axis=1
    )


def tile_products(w_ref, parts, out0, out1):
    base = 0
    for c_ref, copies in parts:
        groups = c_ref.shape[0] // 8
        chunks = len(copies) if copies else 1
        size = groups // chunks
        for i in range(chunks):
            if copies:
                copies[i].wait()
            for g in range(i * size, (i + 1) * size, 2):
                lhs = jnp.concatenate(
                    [block_diagonal(w_ref[base + g]), block_diagonal(w_ref[base + g + 1])],
                    axis=0,
                )
                rhs = jnp.concatenate(
                    [c_ref[(g + k) * 8 : (g + k + 1) * 8].reshape(1024, 128) for k in (0, 1)],
                    axis=1,
                )
                res = dot(lhs, rhs)
                for k in (0, 1):
                    own = res[16 * k : 16 * (k + 1), 128 * k : 128 * (k + 1)]
                    out0[base + g + k] = own[:8]
                    out1[base + g + k] = own[8:]
        base += groups


def backward_pass(own, copies, c_ref, w_ref, out0, out1):
    w_ref[...] = stacked(1.0 - own, own)
    tile_products(w_ref, [(c_ref, copies)], out0, out1)


def electron_rate(sum_k, far, bose, f, parts, w_ref, o0, o1):
    w_ref[...] = stacked(far * (1.0 + bose), far + bose)
    tile_products(w_ref, parts, o0, o1)
    return pick(sum_k, flat(o0)) - f * pick(sum_k, flat(o1))


def need_kernel(kb, cap, *refs):
    ins, outs = refs[:9], refs[9:]
    small, out_ref = outs[:7], outs[7]
    pneed_ref, qneed_ref, sems = outs[-3:]
    copies = [
        pltpu.make_async_copy(src, dst, sems.at[i])
        for i, (src, dst) in enumerate(zip(ins, [*small, pneed_ref, qneed_ref]))
    ]
    start(copies)
    rows = out_ref.shape[0]
    slots = pneed_ref.shape[1]
    x = iota((rows, slots), 0)
    y = iota((rows, slots), 1)
    peer, r = x // (2 * cap), x % (2 * cap)
    e_here = (r < cap) & (y == peer * cap + r)
    p_here = (r >= cap) & (y == peer * cap + r - cap)
    for copy in copies:
        copy.wait()
    pn = jnp.broadcast_to(pneed_ref[...].astype(f32), (rows, slots))
    qn = jnp.broadcast_to(qneed_ref[...].astype(f32), (rows, slots)) + float(kb)
    col = jnp.sum(jnp.where(e_here, pn, 0.0) + jnp.where(p_here, qn, 0.0), axis=1, keepdims=True)
    out_ref[...] = (iota((rows, 128), 1).astype(f32) == col).astype(f32)


def tables_kernel(
    cap,
    count_ref,
    kblock_ref,
    partner_ref,
    qslot_ref,
    f_ref,
    c_hbm,
    ge4_ref,
    gp4_ref,
    gp8_ref,
    gk_ref,
    sk_ref,
    sp4_ref,
    sp8_ref,
    b0_ref,
    b1_ref,
    w_ref,
    c_ref,
    sems,
):
    copies = chunk_copies(c_hbm, c_ref, sems)
    start(copies)
    tiles = kblock_ref.shape[1]
    kb = f_ref.shape[0]
    used = iota((1, tiles), 1) < count_ref[0]
    k = kblock_ref[...]
    e = partner_ref[...]
    q = qslot_ref[...]
    rows4 = sp4_ref.shape[0]
    rows8 = sp8_ref.shape[0]
    ind = lambda m: jnp.where(m, 1.0, 0.0)
    k_hot = ind(iota((kb, tiles), 0) == k)
    sk_ref[...] = jnp.where(used, k_hot, 0.0).astype(bf16)
    gk_ref[...] = k_hot.T.astype(bf16)
    x = iota((rows4, tiles), 0)
    row_e = (e // cap) * (2 * cap) + e % cap
    row_p = (q // cap) * (2 * cap) + cap + q % cap
    ge4_ref[...] = ind(x == row_e).T.astype(bf16)
    p_hot = ind(x == row_p)
    gp4_ref[...] = p_hot.T.astype(bf16)
    sp4_ref[...] = jnp.where(used, p_hot, 0.0).astype(bf16)
    x = iota((rows8, tiles), 0)
    row_z = (q // cap) * (4 * cap) + q % cap
    gp8_ref[...] = ind(x == row_z).T.astype(bf16)
    sp8_ref[...] = jnp.concatenate(
        [
            jnp.where(used, ind(x == row_z + cap), 0.0),
            jnp.where(used, ind(x == row_z + 2 * cap), 0.0),
        ],
        axis=1,
    ).astype(bf16)
    own = pick(gk_ref[...], f_ref[...])
    backward_pass(own, copies, c_ref, w_ref, b0_ref, b1_ref)


def transpose_kernel(after_ref, c_hbm, held_ref, t_hbm, c_ref, t_ref, in_sems, out_sems):
    copies_in = chunk_copies(c_hbm, c_ref, in_sems)
    copies_out = chunk_copies(t_ref, t_hbm, out_sems)
    start(copies_in)
    held = held_ref.shape[0]
    size = c_ref.shape[0] // len(copies_in)
    size_out = t_ref.shape[0] // len(copies_out)
    for i, copy in enumerate(copies_in):
        copy.wait()
        for t in range(i * size, (i + 1) * size):
            turned = c_ref[t].T
            if t < held:
                held_ref[t] = turned
            else:
                t_ref[t - held] = turned
                if (t - held + 1) % size_out == 0:
                    copies_out[(t - held) // size_out].start()
    for copy in copies_out:
        copy.wait()


def serve_kernel(
    cap, recv, f_ref, n_ref, held_ref, send, serve_ref, s8_ref, st4_ref, st8a_ref, st8b_ref
):
    kb, qb = f_ref.shape[0], n_ref.shape[0]
    s4 = recv[...]
    rows4, rows8 = s4.shape[0], s8_ref.shape[0]
    hot = s4.astype(bf16)
    serve_ref[...] = hot
    send[...] = pick(hot, padded(f_ref[...], n_ref[...]))
    x = iota((rows8, rows4), 0)
    y = iota((rows8, rows4), 1)
    peer, r = x // (4 * cap), x % (4 * cap)
    source = peer * (2 * cap) + cap + r % cap

    def rows_of(kind):
        here = (y == source) & (r // cap == kind)
        return dot(jnp.where(here, 1.0, 0.0).astype(bf16), hot)

    s8_ref[...] = rows_of(0).astype(bf16)
    st4_ref[...] = s4.T[kb : kb + qb].astype(bf16)
    st8a_ref[...] = rows_of(1).T[kb : kb + qb].astype(bf16)
    st8b_ref[...] = rows_of(2).T[kb : kb + qb].astype(bf16)


def first_kernel(
    recv,
    f_ref,
    ge4_ref,
    gp4_ref,
    sk_ref,
    sp4_ref,
    serve_ref,
    b0_ref,
    b1_ref,
    held_ref,
    c_hbm,
    send,
    e_ref,
    f1_ref,
    w_ref,
    c_ref,
    sems,
    o0,
    o1,
):
    copies = chunk_copies(c_hbm, c_ref, sems)
    start(copies)
    f = f_ref[...]
    got = recv[...]
    far = pick(ge4_ref[...], got)
    bose = pick(gp4_ref[...], got)
    parts = [(held_ref, None), (c_ref, copies)]
    rate = electron_rate(sk_ref[...], far, bose, f, parts, w_ref, o0, o1)
    gain = far * flat(b0_ref)
    terms = gain + bose * (gain - (1.0 - far) * flat(b1_ref))
    f1 = f + DT * rate
    e_ref[...] = rate
    f1_ref[...] = f1
    send[...] = pick(serve_ref[...], padded(f1)) + pick(sp4_ref[...], terms)


def backward_kernel(f_ref, gk_ref, c_hbm, b0_ref, b1_ref, w_ref, c_ref, sems):
    copies = chunk_copies(c_hbm, c_ref, sems)
    start(copies)
    own = pick(gk_ref[...], f_ref[...])
    backward_pass(own, copies, c_ref, w_ref, b0_ref, b1_ref)


def phonon_kernel(
    kb,
    recv,
    n_ref,
    energy_ref,
    decay_ref,
    ge4_ref,
    st4_ref,
    sp8_ref,
    s8_ref,
    b0_ref,
    b1_ref,
    send,
    p_ref,
    n1_ref,
    far_ref,
):
    n = n_ref[...]
    got = recv[...]
    thermal = 1.0 / (jnp.exp(energy_ref[...]) - 1.0)
    rate = pick(st4_ref[...], got) - decay_ref[...] * (n - thermal)
    n1 = n + DT * rate
    p_ref[...] = rate
    n1_ref[...] = n1
    far = pick(ge4_ref[...], got)
    far_ref[...] = far
    gain = far * flat(b0_ref)
    both = jnp.concatenate([gain, gain - (1.0 - far) * flat(b1_ref)], axis=0)
    state = padded(jnp.zeros((kb, 128), f32), n1)
    send[...] = pick(s8_ref[...], state) + pick(sp8_ref[...], both)


def second_kernel(with_send, recv, *refs):
    far_ref, f_ref, f1_ref, e_ref, n_ref, n1_ref, p_ref, energy_ref, decay_ref = refs[:9]
    gp8_ref, sk_ref, st8a_ref, st8b_ref, serve_ref, held_ref, c_hbm = refs[9:16]
    refs = refs[16:]
    f2_ref, n2_ref, *refs = refs
    send, refs = (refs[0], refs[1:]) if with_send else (None, refs)
    w_ref, c_ref, sems, o0, o1 = refs
    copies = chunk_copies(c_hbm, c_ref, sems)
    start(copies)
    got = recv[...]
    n, n1 = n_ref[...], n1_ref[...]
    bose = pick(gp8_ref[...], got)
    parts = [(held_ref, None), (c_ref, copies)]
    rate = electron_rate(sk_ref[...], far_ref[...], bose, f1_ref[...], parts, w_ref, o0, o1)
    thermal = 1.0 / (jnp.exp(energy_ref[...]) - 1.0)
    p1 = (
        pick(st8a_ref[...], got)
        + n1 * pick(st8b_ref[...], got)
        - decay_ref[...] * (n1 - thermal)
    )
    n2 = n + (DT / 2.0) * (p_ref[...] + p1)
    n2_ref[...] = n2
    f2 = f_ref[...] + (DT / 2.0) * (e_ref[...] + rate)
    f2_ref[...] = f2
    if with_send:
        send[...] = pick(serve_ref[...], padded(f2, n2))


def call(kernel, name, outs, scratch=(), spaces=None, out_spaces=None, flops=0, seen=0):
    def run(*args):
        places = dict(spaces or {})
        args = [
            pltpu.with_memory_space_constraint(x, pltpu.HBM)
            if places.get(i) is pltpu.HBM
            else x
            for i, x in enumerate(args)
        ]
        specs = [
            pl.BlockSpec(memory_space=places.get(i, pltpu.VMEM)) for i in range(len(args))
        ]
        return pl.pallas_call(
            kernel,
            out_shape=[
                pltpu.HBM(*o) if (out_spaces or {}).get(i) else jax.ShapeDtypeStruct(*o)
                for i, o in enumerate(outs)
            ],
            in_specs=specs,
            out_specs=[
                pl.BlockSpec(memory_space=(out_spaces or {}).get(i, pltpu.VMEM))
                for i in range(len(outs))
            ],
            scratch_shapes=list(scratch),
            compiler_params=pltpu.CompilerParams(vmem_limit_bytes=VMEM_LIMIT),
            cost_estimate=pl.CostEstimate(
                flops=flops, bytes_accessed=seen, transcendentals=0
            ),
            name=name,
        )(*args)

    return run


def on_device(
    electrons,
    phonons,
    phonon_energy,
    phonon_decay,
    coupling,
    tile_kblock,
    tile_partner,
    tile_qslot,
    tile_count,
    partner_need,
    phonon_need,
):
    devices = lax.axis_size("bulk")
    kb = electrons.shape[0]
    qb = phonons.shape[0]
    tiles = coupling.shape[0]
    cap = partner_need.shape[1] // devices
    assert cap == phonon_need.shape[1] // devices and kb + qb <= 128
    rows4 = devices * 2 * cap
    rows8 = devices * 4 * cap
    groups = tiles // 8
    held = HELD_CHUNKS * (tiles // CHUNKS)
    weights = pltpu.VMEM((groups, 16, 128), bf16)
    streams = [weights, pltpu.VMEM(coupling.shape, bf16), pltpu.SemaphoreType.DMA((CHUNKS,))]
    rest = (tiles - held, 128, 128)
    rest_sems = pltpu.SemaphoreType.DMA((CHUNKS - HELD_CHUNKS,))
    forward_streams = [weights, pltpu.VMEM(rest, bf16), rest_sems]
    sums = [pltpu.VMEM((groups, 8, 128), f32)] * 2
    pass_out = [((groups, 8, 128), f32)] * 2
    block4 = ((rows4, 128), f32)
    block8 = ((rows8, 128), f32)

    work = dict(flops=2 * tiles * 16 * 128 * 128, seen=tiles * 128 * 128 * 2)

    def exchange(x):
        return lax.all_to_all(x, "bulk", split_axis=0, concat_axis=0, tiled=True)

    ints = ((1, tiles), jnp.int32)
    lists = ((1, partner_need.shape[1]), jnp.int32)
    small = [((kb, 128), f32)] + [((qb, 128), f32)] * 3 + [ints] * 3
    f, n, energy, decay, kblock, partner, qslot, need = call(
        functools.partial(need_kernel, kb, cap),
        "need",
        small + [block4],
        [pltpu.VMEM(*lists), pltpu.VMEM(*lists), pltpu.SemaphoreType.DMA((9,))],
        spaces={i: pltpu.HBM for i in range(9)},
    )(
        electrons,
        phonons,
        phonon_energy,
        phonon_decay,
        tile_kblock.reshape(1, tiles),
        tile_partner.reshape(1, tiles),
        tile_qslot.reshape(1, tiles),
        partner_need,
        phonon_need,
    )
    served = exchange(need)
    c_held, c_rest = call(
        transpose_kernel,
        "transpose",
        [((held, 128, 128), bf16), (rest, bf16)],
        [pltpu.VMEM(coupling.shape, bf16), pltpu.VMEM(rest, bf16), streams[2], rest_sems],
        spaces={1: pltpu.HBM},
        out_spaces={1: pltpu.HBM},
        **work,
    )(f, coupling)
    ge4, gp4, gp8, gk, sk, sp4, sp8, b0, b1 = call(
        functools.partial(tables_kernel, cap),
        "tables",
        [
            ((tiles, rows4), bf16),
            ((tiles, rows4), bf16),
            ((tiles, rows8), bf16),
            ((tiles, kb), bf16),
            ((kb, tiles), bf16),
            ((rows4, tiles), bf16),
            ((rows8, 2 * tiles), bf16),
        ]
        + pass_out,
        streams,
        spaces={0: pltpu.SMEM, 5: pltpu.HBM},
        **work,
    )(tile_count, kblock, partner, qslot, f, coupling)
    send, serve, s8, st4, st8a, st8b = call(
        functools.partial(serve_kernel, cap),
        "serve",
        [
            block4,
            ((rows4, 128), bf16),
            ((rows8, 128), bf16),
            ((qb, rows4), bf16),
            ((qb, rows8), bf16),
            ((qb, rows8), bf16),
        ],
    )(served, f, n, c_held)

    back = call(backward_kernel, "backward", pass_out, streams, spaces={2: pltpu.HBM}, **work)
    for step in range(STEPS):
        recv = exchange(send)
        if step:
            b0, b1 = back(f, gk, coupling)
        send, e0, f1 = call(
            first_kernel,
            "first",
            [block4] + [((kb, 128), f32)] * 2,
            forward_streams + sums,
            spaces={10: pltpu.HBM},
            **work,
        )(recv, f, ge4, gp4, sk, sp4, serve, b0, b1, c_held, c_rest)
        recv = exchange(send)
        b0, b1 = back(f1, gk, coupling)
        send, p0, n1, far = call(
            functools.partial(phonon_kernel, kb),
            "phonon",
            [block8] + [((qb, 128), f32)] * 2 + [((tiles, 128), f32)],
        )(recv, n, energy, decay, ge4, st4, sp8, s8, b0, b1)
        recv = exchange(send)
        last = step == STEPS - 1
        f, n, *send = call(
            functools.partial(second_kernel, not last),
            "second",
            [((kb, 128), f32), ((qb, 128), f32)] + ([] if last else [block4]),
            forward_streams + sums,
            spaces={16: pltpu.HBM},
            **work,
        )(
            recv, far, f, f1, e0, n, n1, p0, energy, decay,
            gp8, sk, st8a, st8b, serve, c_held, c_rest,
        )
        send = send[0] if send else None
    return (f, n)


def solution(mesh):
    placed = (
        P(("groups", "bulk"), None),
        P(("groups", "bulk"), None),
        P("bulk", None),
        P("bulk", None),
        P("bulk", None, None),
        P("bulk"),
        P("bulk"),
        P("bulk"),
        P("bulk"),
        P("bulk", None),
        P("bulk", None),
    )
    return jax.shard_map(
        on_device,
        mesh=mesh,
        in_specs=placed,
        out_specs=(P(("groups", "bulk"), None), P(("groups", "bulk"), None)),
        check_vma=False,
    )
```

```python
import functools

import jax
import jax.numpy as jnp
from jax import lax
from jax.experimental import pallas as pl
from jax.experimental.pallas import tpu as pltpu
from jax.sharding import PartitionSpec as P

STEPS = 2
DT = 0.05
CHUNKS = 8
HELD_CHUNKS = 3
f32 = jnp.float32
bf16 = jnp.bfloat16
VMEM_LIMIT = 24 * 1024 * 1024


def iota(shape, dim):
    return lax.broadcasted_iota(jnp.int32, shape, dim)


def dot(a, b):
    return lax.dot_general(a, b, (((1,), (0,)), ((), ())), preferred_element_type=f32)


def split(x):
    hi = x.astype(bf16)
    rest = x - hi.astype(f32)
    mid = rest.astype(bf16)
    lo = (rest - mid.astype(f32)).astype(bf16)
    return hi, mid, lo


def pick(onehot, x):
    hi, mid, lo = split(x)
    return dot(onehot, hi) + dot(onehot, mid) + dot(onehot, lo)


def stacked(first, second):
    tiles = first.shape[0]
    return jnp.concatenate(
        [first.reshape(tiles // 8, 8, 128), second.reshape(tiles // 8, 8, 128)], axis=1
    ).astype(bf16)


def row_is(r):
    return iota((16, 128), 0) % 8 == r


def padded(*parts):
    rows = sum(p.shape[0] for p in parts)
    return jnp.concatenate([*parts, jnp.zeros((128 - rows, 128), f32)], axis=0)


def flat(ref):
    return ref[...].reshape(-1, 128)


def chunk_copies(src, dst, sems):
    count = sems.shape[0]
    size = src.shape[0] // count
    return [
        pltpu.make_async_copy(
            src.at[pl.ds(i * size, size)], dst.at[pl.ds(i * size, size)], sems.at[i]
        )
        for i in range(count)
    ]


def start(copies):
    for copy in copies:
        copy.start()


def block_diagonal(w):
    w = w.astype(f32)
    return jnp.concatenate(
        [jnp.where(row_is(r), w, 0.0).astype(bf16) for r in range(8)], axis=1
    )


def tile_products(w_ref, parts, out0, out1, after=None):
    size = w_ref.shape[0] // CHUNKS
    base = 0
    for c_ref, copies in parts:
        groups = c_ref.shape[0] // 8
        for i in range(groups // size):
            if copies:
                copies[i].wait()
            for g in range(i * size, (i + 1) * size, 2):
                lhs = jnp.concatenate(
                    [block_diagonal(w_ref[base + g]), block_diagonal(w_ref[base + g + 1])],
                    axis=0,
                )
                rhs = jnp.concatenate(
                    [c_ref[(g + k) * 8 : (g + k + 1) * 8].reshape(1024, 128) for k in (0, 1)],
                    axis=1,
                )
                res = dot(lhs, rhs)
                for k in (0, 1):
                    own = res[16 * k : 16 * (k + 1), 128 * k : 128 * (k + 1)]
                    out0[base + g + k] = own[:8]
                    out1[base + g + k] = own[8:]
            if after:
                after(base // size + i)
        base += groups


def backward_pass(own, copies, c_ref, w_ref, out0, out1):
    w_ref[...] = stacked(1.0 - own, own)
    tile_products(w_ref, [(c_ref, copies)], out0, out1)


def electron_rate(sum_k_ref, far, bose, f, parts, w_ref, o0, o1):
    w_ref[...] = stacked(far * (1.0 + bose), far + bose)
    totals = [jnp.zeros_like(f), jnp.zeros_like(f)]
    size = w_ref.shape[0] // CHUNKS

    def after(chunk):
        for k, out in enumerate((o0, o1)):
            rows = out[chunk * size : (chunk + 1) * size].reshape(-1, 128)
            totals[k] = totals[k] + pick(sum_k_ref[chunk], rows)

    tile_products(w_ref, parts, o0, o1, after)
    return totals[0] - f * totals[1]


def need_kernel(cap, *refs):
    ins, outs = refs[:9], refs[9:]
    small, send_ref, list_ref = outs[:7], outs[7], outs[8]
    pneed_ref, qneed_ref, sems = outs[-3:]
    copies = [
        pltpu.make_async_copy(src, dst, sems.at[i])
        for i, (src, dst) in enumerate(zip(ins, [*small, pneed_ref, qneed_ref]))
    ]
    start(copies)
    rows, sent = list_ref.shape
    slots = pneed_ref.shape[1]
    peers = slots // cap
    step = sent // peers
    x = iota((rows, slots), 0)
    y = iota((rows, slots), 1)
    peer, r = x // (2 * cap), x % (2 * cap)
    e_here = (r < cap) & (y == peer * cap + r)
    p_here = (r >= cap) & (y == peer * cap + r - cap)
    for copy in copies:
        copy.wait()
    f, n = small[0][...], small[1][...]
    kb, qb = f.shape[0], n.shape[0]
    pn = jnp.broadcast_to(pneed_ref[...].astype(f32), (rows, slots))
    qn = jnp.broadcast_to(qneed_ref[...].astype(f32), (rows, slots)) + float(kb)
    col = jnp.sum(jnp.where(e_here, pn, 0.0) + jnp.where(p_here, qn, 0.0), axis=1, keepdims=True)
    hot = (iota((rows, 128), 1).astype(f32) == col).astype(f32)
    start_of = (iota((rows, 1), 0) // (2 * cap) * step).astype(f32)
    list_ref[...] = jnp.where(iota((rows, sent), 1).astype(f32) == col + start_of, 1.0, 0.0).astype(
        bf16
    )
    blank = jnp.zeros((step - kb - qb - 2 * cap, 128), f32)
    for p in range(peers):
        lists = jnp.concatenate([hot[p * 2 * cap : (p + 1) * 2 * cap], blank], axis=0)
        send_ref[p * step : (p + 1) * step] = jnp.concatenate([f, n, lists], axis=0)


def tables_kernel(
    cap,
    count_ref,
    kblock_ref,
    partner_ref,
    qslot_ref,
    f_ref,
    c_hbm,
    ge4_ref,
    gp4_ref,
    gp8_ref,
    gk_ref,
    sk_ref,
    sp4_ref,
    sp8_ref,
    b0_ref,
    b1_ref,
    w_ref,
    c_ref,
    sems,
):
    copies = chunk_copies(c_hbm, c_ref, sems)
    start(copies)
    tiles = kblock_ref.shape[1]
    kb = f_ref.shape[0]
    used = iota((1, tiles), 1) < count_ref[0]
    k = kblock_ref[...]
    e = partner_ref[...]
    q = qslot_ref[...]
    rows4 = sp4_ref.shape[0]
    rows8 = sp8_ref.shape[0]
    ind = lambda m: jnp.where(m, 1.0, 0.0)
    k_hot = ind(iota((kb, tiles), 0) == k)
    sums = jnp.where(used, k_hot, 0.0)
    width = tiles // CHUNKS
    for i in range(CHUNKS):
        sk_ref[i] = sums[:, i * width : (i + 1) * width].astype(bf16)
    gk_ref[...] = k_hot.T.astype(bf16)
    x = iota((rows4, tiles), 0)
    row_e = (e // cap) * (2 * cap) + e % cap
    row_p = (q // cap) * (2 * cap) + cap + q % cap
    ge4_ref[...] = ind(x == row_e).T.astype(bf16)
    p_hot = ind(x == row_p)
    gp4_ref[...] = p_hot.T.astype(bf16)
    sp4_ref[...] = jnp.where(used, p_hot, 0.0).astype(bf16)
    x = iota((rows8, tiles), 0)
    row_z = (q // cap) * (4 * cap) + q % cap
    gp8_ref[...] = ind(x == row_z).T.astype(bf16)
    sp8_ref[...] = jnp.concatenate(
        [
            jnp.where(used, ind(x == row_z + cap), 0.0),
            jnp.where(used, ind(x == row_z + 2 * cap), 0.0),
        ],
        axis=1,
    ).astype(bf16)
    own = pick(gk_ref[...], f_ref[...])
    backward_pass(own, copies, c_ref, w_ref, b0_ref, b1_ref)


def transpose_kernel(after_ref, c_hbm, held_ref, t_hbm, c_ref, t_ref, in_sems, out_sems):
    copies_in = chunk_copies(c_hbm, c_ref, in_sems)
    copies_out = chunk_copies(t_ref, t_hbm, out_sems)
    start(copies_in)
    held = held_ref.shape[0]
    size = c_ref.shape[0] // len(copies_in)
    size_out = t_ref.shape[0] // len(copies_out)
    for i, copy in enumerate(copies_in):
        copy.wait()
        for t in range(i * size, (i + 1) * size):
            turned = c_ref[t].T
            if t < held:
                held_ref[t] = turned
            else:
                t_ref[t - held] = turned
                if (t - held + 1) % size_out == 0:
                    copies_out[(t - held) // size_out].start()
    for copy in copies_out:
        copy.wait()


def serve_kernel(cap, kb, qb, hot_ref, s8_ref, st4_ref, st8a_ref, st8b_ref):
    hot = hot_ref[...]
    rows4, rows8 = hot.shape[0], s8_ref.shape[0]
    x = iota((rows8, rows4), 0)
    y = iota((rows8, rows4), 1)
    peer, r = x // (4 * cap), x % (4 * cap)
    source = peer * (2 * cap) + cap + r % cap

    def rows_of(kind):
        here = (y == source) & (r // cap == kind)
        return dot(jnp.where(here, 1.0, 0.0).astype(bf16), hot)

    s8_ref[...] = rows_of(0).astype(bf16)
    st4_ref[...] = hot.astype(f32).T[kb : kb + qb].astype(bf16)
    st8a_ref[...] = rows_of(1).T[kb : kb + qb].astype(bf16)
    st8b_ref[...] = rows_of(2).T[kb : kb + qb].astype(bf16)


def first_kernel(
    cap,
    state_rows,
    recv,
    list_ref,
    f_ref,
    ge4_ref,
    gp4_ref,
    sk_ref,
    sp4_ref,
    b0_ref,
    b1_ref,
    held_ref,
    c_hbm,
    send,
    e_ref,
    f1_ref,
    *refs,
):
    starts = len(refs) == 6
    w_ref, c_ref, sems, o0, o1 = refs[-5:]
    copies = chunk_copies(c_hbm, c_ref, sems)
    start(copies)
    f = f_ref[...]
    got = recv[...]
    serve = list_ref[...]
    if starts:
        rows, sent = serve.shape
        got, every = pick(serve, got), got
        x = iota((rows, sent), 0)
        step = sent // (rows // (2 * cap))
        lists_at = x // (2 * cap) * step + state_rows + x % (2 * cap)
        at = jnp.where(iota((rows, sent), 1) == lists_at, 1.0, 0.0).astype(bf16)
        serve = dot(at, every.astype(bf16)).astype(bf16)
        refs[0][...] = serve
    far = pick(ge4_ref[...], got)
    bose = pick(gp4_ref[...], got)
    gain = far * flat(b0_ref)
    terms = gain + bose * (gain - (1.0 - far) * flat(b1_ref))
    phonon_rows = pick(sp4_ref[...], terms)
    parts = [(held_ref, None), (c_ref, copies)]
    rate = electron_rate(sk_ref, far, bose, f, parts, w_ref, o0, o1)
    f1 = f + DT * rate
    e_ref[...] = rate
    f1_ref[...] = f1
    send[...] = pick(serve, padded(f1)) + phonon_rows


def backward_kernel(f_ref, gk_ref, c_hbm, b0_ref, b1_ref, w_ref, c_ref, sems):
    copies = chunk_copies(c_hbm, c_ref, sems)
    start(copies)
    own = pick(gk_ref[...], f_ref[...])
    backward_pass(own, copies, c_ref, w_ref, b0_ref, b1_ref)


def phonon_kernel(
    kb,
    recv,
    n_ref,
    energy_ref,
    decay_ref,
    ge4_ref,
    st4_ref,
    sp8_ref,
    s8_ref,
    b0_ref,
    b1_ref,
    send,
    p_ref,
    n1_ref,
    far_ref,
):
    n = n_ref[...]
    got = recv[...]
    thermal = 1.0 / (jnp.exp(energy_ref[...]) - 1.0)
    rate = pick(st4_ref[...], got) - decay_ref[...] * (n - thermal)
    n1 = n + DT * rate
    p_ref[...] = rate
    n1_ref[...] = n1
    far = pick(ge4_ref[...], got)
    far_ref[...] = far
    gain = far * flat(b0_ref)
    both = jnp.concatenate([gain, gain - (1.0 - far) * flat(b1_ref)], axis=0)
    state = padded(jnp.zeros((kb, 128), f32), n1)
    send[...] = pick(s8_ref[...], state) + pick(sp8_ref[...], both)


def second_kernel(with_send, recv, *refs):
    far_ref, f_ref, f1_ref, e_ref, n_ref, n1_ref, p_ref, energy_ref, decay_ref = refs[:9]
    gp8_ref, sk_ref, st8a_ref, st8b_ref, serve_ref, held_ref, c_hbm = refs[9:16]
    refs = refs[16:]
    f2_ref, n2_ref, *refs = refs
    send, refs = (refs[0], refs[1:]) if with_send else (None, refs)
    w_ref, c_ref, sems, o0, o1 = refs
    copies = chunk_copies(c_hbm, c_ref, sems)
    start(copies)
    got = recv[...]
    n, n1 = n_ref[...], n1_ref[...]
    bose = pick(gp8_ref[...], got)
    thermal = 1.0 / (jnp.exp(energy_ref[...]) - 1.0)
    p1 = (
        pick(st8a_ref[...], got)
        + n1 * pick(st8b_ref[...], got)
        - decay_ref[...] * (n1 - thermal)
    )
    n2 = n + (DT / 2.0) * (p_ref[...] + p1)
    n2_ref[...] = n2
    parts = [(held_ref, None), (c_ref, copies)]
    rate = electron_rate(sk_ref, far_ref[...], bose, f1_ref[...], parts, w_ref, o0, o1)
    f2 = f_ref[...] + (DT / 2.0) * (e_ref[...] + rate)
    f2_ref[...] = f2
    if with_send:
        send[...] = pick(serve_ref[...], padded(f2, n2))


def call(kernel, name, outs, scratch=(), spaces=None, out_spaces=None, flops=0, seen=0):
    def run(*args):
        places = dict(spaces or {})
        args = [
            pltpu.with_memory_space_constraint(x, pltpu.HBM)
            if places.get(i) is pltpu.HBM
            else x
            for i, x in enumerate(args)
        ]
        specs = [
            pl.BlockSpec(memory_space=places.get(i, pltpu.VMEM)) for i in range(len(args))
        ]
        return pl.pallas_call(
            kernel,
            out_shape=[
                pltpu.HBM(*o) if (out_spaces or {}).get(i) else jax.ShapeDtypeStruct(*o)
                for i, o in enumerate(outs)
            ],
            in_specs=specs,
            out_specs=[
                pl.BlockSpec(memory_space=(out_spaces or {}).get(i, pltpu.VMEM))
                for i in range(len(outs))
            ],
            scratch_shapes=list(scratch),
            compiler_params=pltpu.CompilerParams(vmem_limit_bytes=VMEM_LIMIT),
            cost_estimate=pl.CostEstimate(
                flops=flops, bytes_accessed=seen, transcendentals=0
            ),
            name=name,
        )(*args)

    return run


def on_device(
    electrons,
    phonons,
    phonon_energy,
    phonon_decay,
    coupling,
    tile_kblock,
    tile_partner,
    tile_qslot,
    tile_count,
    partner_need,
    phonon_need,
):
    devices = lax.axis_size("bulk")
    kb = electrons.shape[0]
    qb = phonons.shape[0]
    tiles = coupling.shape[0]
    cap = partner_need.shape[1] // devices
    assert cap == phonon_need.shape[1] // devices and kb + qb <= 128
    rows4 = devices * 2 * cap
    rows8 = devices * 4 * cap
    groups = tiles // 8
    held = HELD_CHUNKS * (tiles // CHUNKS)
    weights = pltpu.VMEM((groups, 16, 128), bf16)
    streams = [weights, pltpu.VMEM(coupling.shape, bf16), pltpu.SemaphoreType.DMA((CHUNKS,))]
    rest = (tiles - held, 128, 128)
    rest_sems = pltpu.SemaphoreType.DMA((CHUNKS - HELD_CHUNKS,))
    forward_streams = [weights, pltpu.VMEM(rest, bf16), rest_sems]
    sums = [pltpu.VMEM((groups, 8, 128), f32)] * 2
    pass_out = [((groups, 8, 128), f32)] * 2
    block4 = ((rows4, 128), f32)
    block8 = ((rows8, 128), f32)

    work = dict(flops=2 * tiles * 16 * 128 * 128, seen=tiles * 128 * 128 * 2)

    def exchange(x):
        return lax.all_to_all(x, "bulk", split_axis=0, concat_axis=0, tiled=True)

    ints = ((1, tiles), jnp.int32)
    lists = ((1, partner_need.shape[1]), jnp.int32)
    small = [((kb, 128), f32)] + [((qb, 128), f32)] * 3 + [ints] * 3
    step_rows = -(-(kb + qb + 2 * cap) // 8) * 8
    f, n, energy, decay, kblock, partner, qslot, send, lists_in = call(
        functools.partial(need_kernel, cap),
        "need",
        small + [((devices * step_rows, 128), f32), ((rows4, devices * step_rows), bf16)],
        [pltpu.VMEM(*lists), pltpu.VMEM(*lists), pltpu.SemaphoreType.DMA((9,))],
        spaces={i: pltpu.HBM for i in range(9)},
    )(
        electrons,
        phonons,
        phonon_energy,
        phonon_decay,
        tile_kblock.reshape(1, tiles),
        tile_partner.reshape(1, tiles),
        tile_qslot.reshape(1, tiles),
        partner_need,
        phonon_need,
    )
    recv = exchange(send)
    c_held, c_rest = call(
        transpose_kernel,
        "transpose",
        [((held, 128, 128), bf16), (rest, bf16)],
        [pltpu.VMEM(coupling.shape, bf16), pltpu.VMEM(rest, bf16), streams[2], rest_sems],
        spaces={1: pltpu.HBM},
        out_spaces={1: pltpu.HBM},
        **work,
    )(f, coupling)
    ge4, gp4, gp8, gk, sk, sp4, sp8, b0, b1 = call(
        functools.partial(tables_kernel, cap),
        "tables",
        [
            ((tiles, rows4), bf16),
            ((tiles, rows4), bf16),
            ((tiles, rows8), bf16),
            ((tiles, kb), bf16),
            ((CHUNKS, kb, tiles // CHUNKS), bf16),
            ((rows4, tiles), bf16),
            ((rows8, 2 * tiles), bf16),
        ]
        + pass_out,
        streams,
        spaces={0: pltpu.SMEM, 5: pltpu.HBM},
        **work,
    )(tile_count, kblock, partner, qslot, f, coupling)
    back = call(backward_kernel, "backward", pass_out, streams, spaces={2: pltpu.HBM}, **work)
    for step in range(STEPS):
        if step:
            recv = exchange(send)
            b0, b1 = back(f, gk, coupling)
        send, e0, f1, *hot = call(
            functools.partial(first_kernel, cap, kb + qb),
            "first",
            [block4] + [((kb, 128), f32)] * 2 + ([] if step else [((rows4, 128), bf16)]),
            forward_streams + sums,
            spaces={10: pltpu.HBM},
            **work,
        )(recv, serve if step else lists_in, f, ge4, gp4, sk, sp4, b0, b1, c_held, c_rest)
        if not step:
            serve = hot[0]
            s8, st4, st8a, st8b = call(
                functools.partial(serve_kernel, cap, kb, qb),
                "serve",
                [
                    ((rows8, 128), bf16),
                    ((qb, rows4), bf16),
                    ((qb, rows8), bf16),
                    ((qb, rows8), bf16),
                ],
            )(serve)
        recv = exchange(send)
        b0, b1 = back(f1, gk, coupling)
        send, p0, n1, far = call(
            functools.partial(phonon_kernel, kb),
            "phonon",
            [block8] + [((qb, 128), f32)] * 2 + [((tiles, 128), f32)],
        )(recv, n, energy, decay, ge4, st4, sp8, s8, b0, b1)
        recv = exchange(send)
        last = step == STEPS - 1
        f, n, *send = call(
            functools.partial(second_kernel, not last),
            "second",
            [((kb, 128), f32), ((qb, 128), f32)] + ([] if last else [block4]),
            forward_streams + sums,
            spaces={16: pltpu.HBM},
            **work,
        )(
            recv, far, f, f1, e0, n, n1, p0, energy, decay,
            gp8, sk, st8a, st8b, serve, c_held, c_rest,
        )
        send = send[0] if send else None
    return (f, n)


def solution(mesh):
    placed = (
        P(("groups", "bulk"), None),
        P(("groups", "bulk"), None),
        P("bulk", None),
        P("bulk", None),
        P("bulk", None, None),
        P("bulk"),
        P("bulk"),
        P("bulk"),
        P("bulk"),
        P("bulk", None),
        P("bulk", None),
    )
    return jax.shard_map(
        on_device,
        mesh=mesh,
        in_specs=placed,
        out_specs=(P(("groups", "bulk"), None), P(("groups", "bulk"), None)),
        check_vma=False,
    )
```

```python
import functools

import jax
import jax.numpy as jnp
from jax import lax
from jax.experimental import pallas as pl
from jax.experimental.pallas import tpu as pltpu
from jax.sharding import PartitionSpec as P

STEPS = 2
DT = 0.05
CHUNKS = 8
HELD_CHUNKS = 2
f32 = jnp.float32
bf16 = jnp.bfloat16
VMEM_LIMIT = 24 * 1024 * 1024


def iota(shape, dim):
    return lax.broadcasted_iota(jnp.int32, shape, dim)


def dot(a, b):
    return lax.dot_general(a, b, (((1,), (0,)), ((), ())), preferred_element_type=f32)


def split(x):
    hi = x.astype(bf16)
    rest = x - hi.astype(f32)
    mid = rest.astype(bf16)
    lo = (rest - mid.astype(f32)).astype(bf16)
    return hi, mid, lo


def pick(onehot, x):
    hi, mid, lo = split(x)
    return dot(onehot, hi) + dot(onehot, mid) + dot(onehot, lo)


def stacked(first, second):
    tiles = first.shape[0]
    return jnp.concatenate(
        [first.reshape(tiles // 8, 8, 128), second.reshape(tiles // 8, 8, 128)], axis=1
    ).astype(bf16)


def row_is(r):
    return iota((16, 128), 0) % 8 == r


def padded(*parts):
    rows = sum(p.shape[0] for p in parts)
    return jnp.concatenate([*parts, jnp.zeros((128 - rows, 128), f32)], axis=0)


def flat(ref):
    return ref[...].reshape(-1, 128)


def chunk_copies(src, dst, sems):
    count = sems.shape[0]
    size = src.shape[0] // count
    return [
        pltpu.make_async_copy(
            src.at[pl.ds(i * size, size)], dst.at[pl.ds(i * size, size)], sems.at[i]
        )
        for i in range(count)
    ]


def start(copies):
    for copy in copies:
        copy.start()


def block_diagonal(w):
    w = w.astype(f32)
    return jnp.concatenate(
        [jnp.where(row_is(r), w, 0.0).astype(bf16) for r in range(8)], axis=1
    )


def tile_products(w_ref, parts, out0, out1, after=None):
    size = w_ref.shape[0] // CHUNKS
    base = 0
    for c_ref, copies in parts:
        groups = c_ref.shape[0] // 8
        for i in range(groups // size):
            if copies:
                copies[i].wait()
            for g in range(i * size, (i + 1) * size, 2):
                lhs = jnp.concatenate(
                    [block_diagonal(w_ref[base + g]), block_diagonal(w_ref[base + g + 1])],
                    axis=0,
                )
                rhs = jnp.concatenate(
                    [c_ref[(g + k) * 8 : (g + k + 1) * 8].reshape(1024, 128) for k in (0, 1)],
                    axis=1,
                )
                res = dot(lhs, rhs)
                for k in (0, 1):
                    own = res[16 * k : 16 * (k + 1), 128 * k : 128 * (k + 1)]
                    out0[base + g + k] = own[:8]
                    out1[base + g + k] = own[8:]
            if after:
                after(base // size + i)
        base += groups


def backward_pass(own, copies, c_ref, w_ref, out0, out1):
    w_ref[...] = stacked(1.0 - own, own)
    tile_products(w_ref, [(c_ref, copies)], out0, out1)


def electron_rate(sum_k_ref, far, bose, f, parts, w_ref, o0, o1):
    w_ref[...] = stacked(far * (1.0 + bose), far + bose)
    totals = [jnp.zeros_like(f), jnp.zeros_like(f)]
    size = w_ref.shape[0] // CHUNKS

    def after(chunk):
        for k, out in enumerate((o0, o1)):
            rows = out[chunk * size : (chunk + 1) * size].reshape(-1, 128)
            totals[k] = totals[k] + pick(sum_k_ref[chunk], rows)

    tile_products(w_ref, parts, o0, o1, after)
    return totals[0] - f * totals[1]


def need_kernel(cap, *refs):
    ins, outs = refs[:9], refs[9:]
    small, send_ref, list_ref = outs[:7], outs[7], outs[8]
    pneed_ref, qneed_ref, sems = outs[-3:]
    copies = [
        pltpu.make_async_copy(src, dst, sems.at[i])
        for i, (src, dst) in enumerate(zip(ins, [*small, pneed_ref, qneed_ref]))
    ]
    start(copies)
    rows, sent = list_ref.shape
    slots = pneed_ref.shape[1]
    peers = slots // cap
    step = sent // peers
    x = iota((rows, slots), 0)
    y = iota((rows, slots), 1)
    peer, r = x // (2 * cap), x % (2 * cap)
    e_here = (r < cap) & (y == peer * cap + r)
    p_here = (r >= cap) & (y == peer * cap + r - cap)
    for copy in copies:
        copy.wait()
    f, n = small[0][...], small[1][...]
    kb, qb = f.shape[0], n.shape[0]
    pn = jnp.broadcast_to(pneed_ref[...].astype(f32), (rows, slots))
    qn = jnp.broadcast_to(qneed_ref[...].astype(f32), (rows, slots)) + float(kb)
    col = jnp.sum(jnp.where(e_here, pn, 0.0) + jnp.where(p_here, qn, 0.0), axis=1, keepdims=True)
    hot = (iota((rows, 128), 1).astype(f32) == col).astype(f32)
    start_of = (iota((rows, 1), 0) // (2 * cap) * step).astype(f32)
    list_ref[...] = jnp.where(iota((rows, sent), 1).astype(f32) == col + start_of, 1.0, 0.0).astype(
        bf16
    )
    blank = jnp.zeros((step - kb - qb - 2 * cap, 128), f32)
    for p in range(peers):
        lists = jnp.concatenate([hot[p * 2 * cap : (p + 1) * 2 * cap], blank], axis=0)
        send_ref[p * step : (p + 1) * step] = jnp.concatenate([f, n, lists], axis=0)


def tables_kernel(
    cap,
    count_ref,
    kblock_ref,
    partner_ref,
    qslot_ref,
    f_ref,
    c_hbm,
    ge4_ref,
    gp4_ref,
    gp8_ref,
    gk_ref,
    sk_ref,
    sp4_ref,
    sp8_ref,
    b0_ref,
    b1_ref,
    w_ref,
    c_ref,
    sems,
):
    copies = chunk_copies(c_hbm, c_ref, sems)
    start(copies)
    tiles = kblock_ref.shape[1]
    kb = f_ref.shape[0]
    used = iota((1, tiles), 1) < count_ref[0]
    k = kblock_ref[...]
    e = partner_ref[...]
    q = qslot_ref[...]
    rows4 = sp4_ref.shape[0]
    rows8 = sp8_ref.shape[0]
    ind = lambda m: jnp.where(m, 1.0, 0.0)
    k_hot = ind(iota((kb, tiles), 0) == k)
    sums = jnp.where(used, k_hot, 0.0)
    width = tiles // CHUNKS
    for i in range(CHUNKS):
        sk_ref[i] = sums[:, i * width : (i + 1) * width].astype(bf16)
    gk_ref[...] = k_hot.T.astype(bf16)
    x = iota((rows4, tiles), 0)
    row_e = (e // cap) * (2 * cap) + e % cap
    row_p = (q // cap) * (2 * cap) + cap + q % cap
    ge4_ref[...] = ind(x == row_e).T.astype(bf16)
    p_hot = ind(x == row_p)
    gp4_ref[...] = p_hot.T.astype(bf16)
    sp4_ref[...] = jnp.where(used, p_hot, 0.0).astype(bf16)
    x = iota((rows8, tiles), 0)
    row_z = (q // cap) * (4 * cap) + q % cap
    gp8_ref[...] = ind(x == row_z).T.astype(bf16)
    sp8_ref[...] = jnp.concatenate(
        [
            jnp.where(used, ind(x == row_z + cap), 0.0),
            jnp.where(used, ind(x == row_z + 2 * cap), 0.0),
        ],
        axis=1,
    ).astype(bf16)
    own = pick(gk_ref[...], f_ref[...])
    backward_pass(own, copies, c_ref, w_ref, b0_ref, b1_ref)


def transpose_kernel(after_ref, c_hbm, held_ref, t_hbm, c_ref, t_ref, in_sems, out_sems):
    copies_in = chunk_copies(c_hbm, c_ref, in_sems)
    copies_out = chunk_copies(t_ref, t_hbm, out_sems)
    start(copies_in)
    held = held_ref.shape[0]
    size = c_ref.shape[0] // len(copies_in)
    size_out = t_ref.shape[0] // len(copies_out)
    for i, copy in enumerate(copies_in):
        copy.wait()
        for t in range(i * size, (i + 1) * size):
            turned = c_ref[t].T
            if t < held:
                held_ref[t] = turned
            else:
                t_ref[t - held] = turned
                if (t - held + 1) % size_out == 0:
                    copies_out[(t - held) // size_out].start()
    for copy in copies_out:
        copy.wait()


def serve_kernel(cap, kb, qb, hot_ref, s8_ref, st4_ref, st8a_ref, st8b_ref):
    hot = hot_ref[...]
    rows4, rows8 = hot.shape[0], s8_ref.shape[0]
    x = iota((rows8, rows4), 0)
    y = iota((rows8, rows4), 1)
    peer, r = x // (4 * cap), x % (4 * cap)
    source = peer * (2 * cap) + cap + r % cap

    def rows_of(kind):
        here = (y == source) & (r // cap == kind)
        return dot(jnp.where(here, 1.0, 0.0).astype(bf16), hot)

    s8_ref[...] = rows_of(0).astype(bf16)
    st4_ref[...] = hot.astype(f32).T[kb : kb + qb].astype(bf16)
    st8a_ref[...] = rows_of(1).T[kb : kb + qb].astype(bf16)
    st8b_ref[...] = rows_of(2).T[kb : kb + qb].astype(bf16)


def first_kernel(
    cap,
    state_rows,
    recv,
    list_ref,
    f_ref,
    ge4_ref,
    gp4_ref,
    sk_ref,
    sp4_ref,
    b0_ref,
    b1_ref,
    held_ref,
    c_hbm,
    send,
    e_ref,
    f1_ref,
    *refs,
):
    starts = len(refs) == 6
    w_ref, c_ref, sems, o0, o1 = refs[-5:]
    copies = chunk_copies(c_hbm, c_ref, sems)
    start(copies)
    f = f_ref[...]
    got = recv[...]
    serve = list_ref[...]
    if starts:
        rows, sent = serve.shape
        got, every = pick(serve, got), got
        x = iota((rows, sent), 0)
        step = sent // (rows // (2 * cap))
        lists_at = x // (2 * cap) * step + state_rows + x % (2 * cap)
        at = jnp.where(iota((rows, sent), 1) == lists_at, 1.0, 0.0).astype(bf16)
        serve = dot(at, every.astype(bf16)).astype(bf16)
        refs[0][...] = serve
    far = pick(ge4_ref[...], got)
    bose = pick(gp4_ref[...], got)
    gain = far * flat(b0_ref)
    terms = gain + bose * (gain - (1.0 - far) * flat(b1_ref))
    phonon_rows = pick(sp4_ref[...], terms)
    parts = [(held_ref, None), (c_ref, copies)]
    rate = electron_rate(sk_ref, far, bose, f, parts, w_ref, o0, o1)
    f1 = f + DT * rate
    e_ref[...] = rate
    f1_ref[...] = f1
    send[...] = pick(serve, padded(f1)) + phonon_rows


def backward_kernel(f_ref, gk_ref, c_hbm, b0_ref, b1_ref, w_ref, c_ref, sems):
    copies = chunk_copies(c_hbm, c_ref, sems)
    start(copies)
    own = pick(gk_ref[...], f_ref[...])
    backward_pass(own, copies, c_ref, w_ref, b0_ref, b1_ref)


def phonon_kernel(
    kb,
    recv,
    n_ref,
    energy_ref,
    decay_ref,
    ge4_ref,
    st4_ref,
    sp8_ref,
    s8_ref,
    b0_ref,
    b1_ref,
    send,
    p_ref,
    n1_ref,
    far_ref,
):
    n = n_ref[...]
    got = recv[...]
    thermal = 1.0 / (jnp.exp(energy_ref[...]) - 1.0)
    rate = pick(st4_ref[...], got) - decay_ref[...] * (n - thermal)
    n1 = n + DT * rate
    p_ref[...] = rate
    n1_ref[...] = n1
    far = pick(ge4_ref[...], got)
    far_ref[...] = far
    gain = far * flat(b0_ref)
    both = jnp.concatenate([gain, gain - (1.0 - far) * flat(b1_ref)], axis=0)
    state = padded(jnp.zeros((kb, 128), f32), n1)
    send[...] = pick(s8_ref[...], state) + pick(sp8_ref[...], both)


def second_kernel(with_send, recv, *refs):
    far_ref, f_ref, f1_ref, e_ref, n_ref, n1_ref, p_ref, energy_ref, decay_ref = refs[:9]
    gp8_ref, sk_ref, st8a_ref, st8b_ref, serve_ref, held_ref, c_hbm = refs[9:16]
    refs = refs[16:]
    f2_ref, n2_ref, *refs = refs
    send, refs = (refs[0], refs[1:]) if with_send else (None, refs)
    w_ref, c_ref, sems, o0, o1 = refs
    copies = chunk_copies(c_hbm, c_ref, sems)
    start(copies)
    got = recv[...]
    n, n1 = n_ref[...], n1_ref[...]
    bose = pick(gp8_ref[...], got)
    thermal = 1.0 / (jnp.exp(energy_ref[...]) - 1.0)
    p1 = (
        pick(st8a_ref[...], got)
        + n1 * pick(st8b_ref[...], got)
        - decay_ref[...] * (n1 - thermal)
    )
    n2 = n + (DT / 2.0) * (p_ref[...] + p1)
    n2_ref[...] = n2
    parts = [(held_ref, None), (c_ref, copies)]
    rate = electron_rate(sk_ref, far_ref[...], bose, f1_ref[...], parts, w_ref, o0, o1)
    f2 = f_ref[...] + (DT / 2.0) * (e_ref[...] + rate)
    f2_ref[...] = f2
    if with_send:
        send[...] = pick(serve_ref[...], padded(f2, n2))


def call(kernel, name, outs, scratch=(), spaces=None, out_spaces=None, flops=0, seen=0):
    def run(*args):
        places = dict(spaces or {})
        args = [
            pltpu.with_memory_space_constraint(x, pltpu.HBM)
            if places.get(i) is pltpu.HBM
            else x
            for i, x in enumerate(args)
        ]
        specs = [
            pl.BlockSpec(memory_space=places.get(i, pltpu.VMEM)) for i in range(len(args))
        ]
        return pl.pallas_call(
            kernel,
            out_shape=[
                pltpu.HBM(*o) if (out_spaces or {}).get(i) else jax.ShapeDtypeStruct(*o)
                for i, o in enumerate(outs)
            ],
            in_specs=specs,
            out_specs=[
                pl.BlockSpec(memory_space=(out_spaces or {}).get(i, pltpu.VMEM))
                for i in range(len(outs))
            ],
            scratch_shapes=list(scratch),
            compiler_params=pltpu.CompilerParams(vmem_limit_bytes=VMEM_LIMIT),
            cost_estimate=pl.CostEstimate(
                flops=flops, bytes_accessed=seen, transcendentals=0
            ),
            name=name,
        )(*args)

    return run


def on_device(
    electrons,
    phonons,
    phonon_energy,
    phonon_decay,
    coupling,
    tile_kblock,
    tile_partner,
    tile_qslot,
    tile_count,
    partner_need,
    phonon_need,
):
    devices = lax.axis_size("bulk")
    kb = electrons.shape[0]
    qb = phonons.shape[0]
    tiles = coupling.shape[0]
    cap = partner_need.shape[1] // devices
    assert cap == phonon_need.shape[1] // devices and kb + qb <= 128
    rows4 = devices * 2 * cap
    rows8 = devices * 4 * cap
    groups = tiles // 8
    held = HELD_CHUNKS * (tiles // CHUNKS)
    weights = pltpu.VMEM((groups, 16, 128), bf16)
    streams = [weights, pltpu.VMEM(coupling.shape, bf16), pltpu.SemaphoreType.DMA((CHUNKS,))]
    rest = (tiles - held, 128, 128)
    rest_sems = pltpu.SemaphoreType.DMA((CHUNKS - HELD_CHUNKS,))
    forward_streams = [weights, pltpu.VMEM(rest, bf16), rest_sems]
    sums = [pltpu.VMEM((groups, 8, 128), f32)] * 2
    pass_out = [((groups, 8, 128), f32)] * 2
    block4 = ((rows4, 128), f32)
    block8 = ((rows8, 128), f32)

    work = dict(flops=2 * tiles * 16 * 128 * 128, seen=tiles * 128 * 128 * 2)

    def exchange(x):
        return lax.all_to_all(x, "bulk", split_axis=0, concat_axis=0, tiled=True)

    ints = ((1, tiles), jnp.int32)
    lists = ((1, partner_need.shape[1]), jnp.int32)
    small = [((kb, 128), f32)] + [((qb, 128), f32)] * 3 + [ints] * 3
    step_rows = -(-(kb + qb + 2 * cap) // 8) * 8
    f, n, energy, decay, kblock, partner, qslot, send, lists_in = call(
        functools.partial(need_kernel, cap),
        "need",
        small + [((devices * step_rows, 128), f32), ((rows4, devices * step_rows), bf16)],
        [pltpu.VMEM(*lists), pltpu.VMEM(*lists), pltpu.SemaphoreType.DMA((9,))],
        spaces={i: pltpu.HBM for i in range(9)},
    )(
        electrons,
        phonons,
        phonon_energy,
        phonon_decay,
        tile_kblock.reshape(1, tiles),
        tile_partner.reshape(1, tiles),
        tile_qslot.reshape(1, tiles),
        partner_need,
        phonon_need,
    )
    recv = exchange(send)
    c_held, c_rest = call(
        transpose_kernel,
        "transpose",
        [((held, 128, 128), bf16), (rest, bf16)],
        [pltpu.VMEM(coupling.shape, bf16), pltpu.VMEM(rest, bf16), streams[2], rest_sems],
        spaces={1: pltpu.HBM},
        out_spaces={1: pltpu.HBM},
        **work,
    )(f, coupling)
    ge4, gp4, gp8, gk, sk, sp4, sp8, b0, b1 = call(
        functools.partial(tables_kernel, cap),
        "tables",
        [
            ((tiles, rows4), bf16),
            ((tiles, rows4), bf16),
            ((tiles, rows8), bf16),
            ((tiles, kb), bf16),
            ((CHUNKS, kb, tiles // CHUNKS), bf16),
            ((rows4, tiles), bf16),
            ((rows8, 2 * tiles), bf16),
        ]
        + pass_out,
        streams,
        spaces={0: pltpu.SMEM, 5: pltpu.HBM},
        **work,
    )(tile_count, kblock, partner, qslot, f, coupling)
    back = call(backward_kernel, "backward", pass_out, streams, spaces={2: pltpu.HBM}, **work)
    for step in range(STEPS):
        if step:
            recv = exchange(send)
            b0, b1 = back(f, gk, coupling)
        send, e0, f1, *hot = call(
            functools.partial(first_kernel, cap, kb + qb),
            "first",
            [block4] + [((kb, 128), f32)] * 2 + ([] if step else [((rows4, 128), bf16)]),
            forward_streams + sums,
            spaces={10: pltpu.HBM},
            **work,
        )(recv, serve if step else lists_in, f, ge4, gp4, sk, sp4, b0, b1, c_held, c_rest)
        if not step:
            serve = hot[0]
            s8, st4, st8a, st8b = call(
                functools.partial(serve_kernel, cap, kb, qb),
                "serve",
                [
                    ((rows8, 128), bf16),
                    ((qb, rows4), bf16),
                    ((qb, rows8), bf16),
                    ((qb, rows8), bf16),
                ],
            )(serve)
        recv = exchange(send)
        b0, b1 = back(f1, gk, coupling)
        send, p0, n1, far = call(
            functools.partial(phonon_kernel, kb),
            "phonon",
            [block8] + [((qb, 128), f32)] * 2 + [((tiles, 128), f32)],
        )(recv, n, energy, decay, ge4, st4, sp8, s8, b0, b1)
        recv = exchange(send)
        last = step == STEPS - 1
        f, n, *send = call(
            functools.partial(second_kernel, not last),
            "second",
            [((kb, 128), f32), ((qb, 128), f32)] + ([] if last else [block4]),
            forward_streams + sums,
            spaces={16: pltpu.HBM},
            **work,
        )(
            recv, far, f, f1, e0, n, n1, p0, energy, decay,
            gp8, sk, st8a, st8b, serve, c_held, c_rest,
        )
        send = send[0] if send else None
    return (f, n)


def solution(mesh):
    placed = (
        P(("groups", "bulk"), None),
        P(("groups", "bulk"), None),
        P("bulk", None),
        P("bulk", None),
        P("bulk", None, None),
        P("bulk"),
        P("bulk"),
        P("bulk"),
        P("bulk"),
        P("bulk", None),
        P("bulk", None),
    )
    return jax.shard_map(
        on_device,
        mesh=mesh,
        in_specs=placed,
        out_specs=(P(("groups", "bulk"), None), P(("groups", "bulk"), None)),
        check_vma=False,
    )
```

```python
import functools

import jax
import jax.numpy as jnp
from jax import lax
from jax.experimental import pallas as pl
from jax.experimental.pallas import tpu as pltpu
from jax.sharding import PartitionSpec as P

STEPS = 2
DT = 0.05
CHUNKS = 8
HELD_CHUNKS = 2
f32 = jnp.float32
bf16 = jnp.bfloat16
VMEM_LIMIT = 24 * 1024 * 1024


def iota(shape, dim):
    return lax.broadcasted_iota(jnp.int32, shape, dim)


def dot(a, b):
    return lax.dot_general(a, b, (((1,), (0,)), ((), ())), preferred_element_type=f32)


def split(x):
    hi = x.astype(bf16)
    rest = x - hi.astype(f32)
    mid = rest.astype(bf16)
    lo = (rest - mid.astype(f32)).astype(bf16)
    return hi, mid, lo


def pick(onehot, x):
    hi, mid, lo = split(x)
    return dot(onehot, hi) + dot(onehot, mid) + dot(onehot, lo)


def stacked(first, second):
    tiles = first.shape[0]
    return jnp.concatenate(
        [first.reshape(tiles // 8, 8, 128), second.reshape(tiles // 8, 8, 128)], axis=1
    ).astype(bf16)


def row_is(r):
    return iota((16, 128), 0) % 8 == r


def padded(*parts):
    rows = sum(p.shape[0] for p in parts)
    return jnp.concatenate([*parts, jnp.zeros((128 - rows, 128), f32)], axis=0)


def flat(ref):
    return ref[...].reshape(-1, 128)


def chunk_copy(src, dst, sems, i):
    size = src.shape[0] // sems.shape[0]
    here = pl.ds(i * size, size)
    return pltpu.make_async_copy(src.at[here], dst.at[here], sems.at[i])


def start_chunks(src, dst, sems):
    for i in range(sems.shape[0]):
        chunk_copy(src, dst, sems, i).start()


def start(copies):
    for copy in copies:
        copy.start()


def block_diagonal(w):
    w = w.astype(f32)
    return jnp.concatenate(
        [jnp.where(row_is(r), w, 0.0).astype(bf16) for r in range(8)], axis=1
    )


def tile_products(w_ref, parts, out0, out1):
    size = w_ref.shape[0] // CHUNKS
    base = 0
    for c_ref, c_hbm, sems in parts:
        groups = c_ref.shape[0] // 8

        def chunk(i, _):
            if c_hbm is not None:
                chunk_copy(c_hbm, c_ref, sems, i).wait()
            for k in range(0, size, 2):
                g = i * size + k
                at = base + g
                lhs = jnp.concatenate(
                    [block_diagonal(w_ref[at]), block_diagonal(w_ref[at + 1])], axis=0
                )
                rhs = jnp.concatenate(
                    [c_ref[pl.ds((g + j) * 8, 8)].reshape(1024, 128) for j in (0, 1)], axis=1
                )
                res = dot(lhs, rhs)
                for j in (0, 1):
                    own = res[16 * j : 16 * (j + 1), 128 * j : 128 * (j + 1)]
                    out0[at + j] = own[:8]
                    out1[at + j] = own[8:]
            return 0

        lax.fori_loop(0, groups // size, chunk, 0)
        base += groups


def backward_pass(own, c_hbm, c_ref, sems, w_ref, out0, out1):
    w_ref[...] = stacked(1.0 - own, own)
    tile_products(w_ref, [(c_ref, c_hbm, sems)], out0, out1)


def electron_rate(sum_k, far, bose, f, parts, w_ref, o0, o1):
    w_ref[...] = stacked(far * (1.0 + bose), far + bose)
    tile_products(w_ref, parts, o0, o1)
    return pick(sum_k, flat(o0)) - f * pick(sum_k, flat(o1))


def need_kernel(cap, *refs):
    ins, outs = refs[:9], refs[9:]
    small, send_ref, list_ref = outs[:7], outs[7], outs[8]
    pneed_ref, qneed_ref, sems = outs[-3:]
    copies = [
        pltpu.make_async_copy(src, dst, sems.at[i])
        for i, (src, dst) in enumerate(zip(ins, [*small, pneed_ref, qneed_ref]))
    ]
    start(copies)
    rows, sent = list_ref.shape
    slots = pneed_ref.shape[1]
    peers = slots // cap
    step = sent // peers
    x = iota((rows, slots), 0)
    y = iota((rows, slots), 1)
    peer, r = x // (2 * cap), x % (2 * cap)
    e_here = (r < cap) & (y == peer * cap + r)
    p_here = (r >= cap) & (y == peer * cap + r - cap)
    for copy in copies:
        copy.wait()
    f, n = small[0][...], small[1][...]
    kb, qb = f.shape[0], n.shape[0]
    pn = jnp.broadcast_to(pneed_ref[...].astype(f32), (rows, slots))
    qn = jnp.broadcast_to(qneed_ref[...].astype(f32), (rows, slots)) + float(kb)
    col = jnp.sum(jnp.where(e_here, pn, 0.0) + jnp.where(p_here, qn, 0.0), axis=1, keepdims=True)
    hot = (iota((rows, 128), 1).astype(f32) == col).astype(f32)
    core = lax.rem(lax.axis_index("bulk"), 2)
    peer1 = iota((rows, 1), 0) // (2 * cap)
    start_of = (peer1 // 2 + jnp.where(peer1 % 2 == core, 0, peers // 2)) * step
    list_ref[...] = jnp.where(
        iota((rows, sent), 1).astype(f32) == col + start_of.astype(f32), 1.0, 0.0
    ).astype(bf16)
    for chip in range(peers // 2):
        lists = hot[chip * 4 * cap : (chip + 1) * 4 * cap]
        send_ref[chip * step : (chip + 1) * step] = jnp.concatenate([f, n, lists], axis=0)


def tables_kernel(
    cap,
    count_ref,
    kblock_ref,
    partner_ref,
    qslot_ref,
    f_ref,
    c_hbm,
    ge4_ref,
    gp4_ref,
    gp8_ref,
    gk_ref,
    sk_ref,
    sp4_ref,
    sp8_ref,
    b0_ref,
    b1_ref,
    w_ref,
    c_ref,
    sems,
):
    start_chunks(c_hbm, c_ref, sems)
    tiles = kblock_ref.shape[1]
    kb = f_ref.shape[0]
    used = iota((1, tiles), 1) < count_ref[0]
    k = kblock_ref[...]
    e = partner_ref[...]
    q = qslot_ref[...]
    rows4 = sp4_ref.shape[0]
    rows8 = sp8_ref.shape[0]
    ind = lambda m: jnp.where(m, 1.0, 0.0)
    k_hot = ind(iota((kb, tiles), 0) == k)
    sk_ref[...] = jnp.where(used, k_hot, 0.0).astype(bf16)
    gk_ref[...] = k_hot.T.astype(bf16)
    x = iota((rows4, tiles), 0)
    row_e = (e // cap) * (2 * cap) + e % cap
    row_p = (q // cap) * (2 * cap) + cap + q % cap
    ge4_ref[...] = ind(x == row_e).T.astype(bf16)
    p_hot = ind(x == row_p)
    gp4_ref[...] = p_hot.T.astype(bf16)
    sp4_ref[...] = jnp.where(used, p_hot, 0.0).astype(bf16)
    x = iota((rows8, tiles), 0)
    row_z = (q // cap) * (4 * cap) + q % cap
    gp8_ref[...] = ind(x == row_z).T.astype(bf16)
    sp8_ref[...] = jnp.concatenate(
        [
            jnp.where(used, ind(x == row_z + cap), 0.0),
            jnp.where(used, ind(x == row_z + 2 * cap), 0.0),
        ],
        axis=1,
    ).astype(bf16)
    own = pick(gk_ref[...], f_ref[...])
    backward_pass(own, c_hbm, c_ref, sems, w_ref, b0_ref, b1_ref)


def transpose_kernel(after_ref, c_hbm, held_ref, t_hbm, c_ref, t_ref, in_sems, out_sems):
    start_chunks(c_hbm, c_ref, in_sems)
    size = c_ref.shape[0] // in_sems.shape[0]
    held = held_ref.shape[0] // size

    def to_held(i, _):
        chunk_copy(c_hbm, c_ref, in_sems, i).wait()
        for t in range(size):
            held_ref[i * size + t] = c_ref[i * size + t].T
        return 0

    def to_rest(i, _):
        chunk_copy(c_hbm, c_ref, in_sems, held + i).wait()
        for t in range(size):
            t_ref[i * size + t] = c_ref[(held + i) * size + t].T
        chunk_copy(t_ref, t_hbm, out_sems, i).start()
        return 0

    lax.fori_loop(0, held, to_held, 0)
    lax.fori_loop(0, out_sems.shape[0], to_rest, 0)
    for i in range(out_sems.shape[0]):
        chunk_copy(t_ref, t_hbm, out_sems, i).wait()


def serve_kernel(cap, kb, qb, hot_ref, s8_ref, st4_ref, st8a_ref, st8b_ref):
    hot = hot_ref[...]
    rows4, rows8 = hot.shape[0], s8_ref.shape[0]
    x = iota((rows8, rows4), 0)
    y = iota((rows8, rows4), 1)
    peer, r = x // (4 * cap), x % (4 * cap)
    source = peer * (2 * cap) + cap + r % cap

    def rows_of(kind):
        here = (y == source) & (r // cap == kind)
        return dot(jnp.where(here, 1.0, 0.0).astype(bf16), hot)

    s8_ref[...] = rows_of(0).astype(bf16)
    st4_ref[...] = hot.astype(f32).T[kb : kb + qb].astype(bf16)
    st8a_ref[...] = rows_of(1).T[kb : kb + qb].astype(bf16)
    st8b_ref[...] = rows_of(2).T[kb : kb + qb].astype(bf16)


def first_kernel(cap, state_rows, starts, recv, *refs):
    other, refs = (refs[0], refs[1:]) if starts else (None, refs)
    list_ref, f_ref, ge4_ref, gp4_ref, sk_ref, sp4_ref, b0_ref, b1_ref, held_ref, c_hbm = refs[:10]
    send, e_ref, f1_ref = refs[10:13]
    hot_ref = refs[13] if starts else None
    w_ref, c_ref, sems, o0, o1 = refs[-5:]
    start_chunks(c_hbm, c_ref, sems)
    f = f_ref[...]
    got = recv[...]
    serve = list_ref[...]
    if starts:
        rows, sent = serve.shape
        every = jnp.concatenate([got, other[...]], axis=0)
        got = pick(serve, every)
        x = iota((rows, sent), 0)
        peers = rows // (2 * cap)
        step = sent // peers
        core = lax.rem(lax.axis_index("bulk"), 2)
        peer = x // (2 * cap)
        chip_row = (peer // 2 + jnp.where(peer % 2 == core, 0, peers // 2)) * step
        lists_at = chip_row + state_rows + 2 * cap * core + x % (2 * cap)
        at = jnp.where(iota((rows, sent), 1) == lists_at, 1.0, 0.0).astype(bf16)
        serve = dot(at, every.astype(bf16)).astype(bf16)
        hot_ref[...] = serve
    far = pick(ge4_ref[...], got)
    bose = pick(gp4_ref[...], got)
    gain = far * flat(b0_ref)
    terms = gain + bose * (gain - (1.0 - far) * flat(b1_ref))
    phonon_rows = pick(sp4_ref[...], terms)
    parts = [(held_ref, None, None), (c_ref, c_hbm, sems)]
    rate = electron_rate(sk_ref[...], far, bose, f, parts, w_ref, o0, o1)
    f1 = f + DT * rate
    e_ref[...] = rate
    f1_ref[...] = f1
    send[...] = pick(serve, padded(f1)) + phonon_rows


def backward_kernel(f_ref, gk_ref, c_hbm, b0_ref, b1_ref, w_ref, c_ref, sems):
    start_chunks(c_hbm, c_ref, sems)
    own = pick(gk_ref[...], f_ref[...])
    backward_pass(own, c_hbm, c_ref, sems, w_ref, b0_ref, b1_ref)


def phonon_kernel(
    kb,
    recv,
    n_ref,
    energy_ref,
    decay_ref,
    ge4_ref,
    st4_ref,
    sp8_ref,
    s8_ref,
    b0_ref,
    b1_ref,
    send,
    p_ref,
    n1_ref,
    far_ref,
):
    n = n_ref[...]
    got = recv[...]
    thermal = 1.0 / (jnp.exp(energy_ref[...]) - 1.0)
    rate = pick(st4_ref[...], got) - decay_ref[...] * (n - thermal)
    n1 = n + DT * rate
    p_ref[...] = rate
    n1_ref[...] = n1
    far = pick(ge4_ref[...], got)
    far_ref[...] = far
    gain = far * flat(b0_ref)
    both = jnp.concatenate([gain, gain - (1.0 - far) * flat(b1_ref)], axis=0)
    state = padded(jnp.zeros((kb, 128), f32), n1)
    send[...] = pick(s8_ref[...], state) + pick(sp8_ref[...], both)


def second_kernel(with_send, recv, *refs):
    far_ref, f_ref, f1_ref, e_ref, n_ref, n1_ref, p_ref, energy_ref, decay_ref = refs[:9]
    gp8_ref, sk_ref, st8a_ref, st8b_ref, serve_ref, held_ref, c_hbm = refs[9:16]
    refs = refs[16:]
    f2_ref, n2_ref, *refs = refs
    send, refs = (refs[0], refs[1:]) if with_send else (None, refs)
    w_ref, c_ref, sems, o0, o1 = refs
    start_chunks(c_hbm, c_ref, sems)
    got = recv[...]
    n, n1 = n_ref[...], n1_ref[...]
    bose = pick(gp8_ref[...], got)
    thermal = 1.0 / (jnp.exp(energy_ref[...]) - 1.0)
    p1 = (
        pick(st8a_ref[...], got)
        + n1 * pick(st8b_ref[...], got)
        - decay_ref[...] * (n1 - thermal)
    )
    n2 = n + (DT / 2.0) * (p_ref[...] + p1)
    n2_ref[...] = n2
    parts = [(held_ref, None, None), (c_ref, c_hbm, sems)]
    rate = electron_rate(sk_ref[...], far_ref[...], bose, f1_ref[...], parts, w_ref, o0, o1)
    f2 = f_ref[...] + (DT / 2.0) * (e_ref[...] + rate)
    f2_ref[...] = f2
    if with_send:
        send[...] = pick(serve_ref[...], padded(f2, n2))


def call(kernel, name, outs, scratch=(), spaces=None, out_spaces=None, flops=0, seen=0):
    def run(*args):
        places = dict(spaces or {})
        args = [
            pltpu.with_memory_space_constraint(x, pltpu.HBM)
            if places.get(i) is pltpu.HBM
            else x
            for i, x in enumerate(args)
        ]
        specs = [
            pl.BlockSpec(memory_space=places.get(i, pltpu.VMEM)) for i in range(len(args))
        ]
        return pl.pallas_call(
            kernel,
            out_shape=[
                pltpu.HBM(*o) if (out_spaces or {}).get(i) else jax.ShapeDtypeStruct(*o)
                for i, o in enumerate(outs)
            ],
            in_specs=specs,
            out_specs=[
                pl.BlockSpec(memory_space=(out_spaces or {}).get(i, pltpu.VMEM))
                for i in range(len(outs))
            ],
            scratch_shapes=list(scratch),
            compiler_params=pltpu.CompilerParams(vmem_limit_bytes=VMEM_LIMIT),
            cost_estimate=pl.CostEstimate(
                flops=flops, bytes_accessed=seen, transcendentals=0
            ),
            name=name,
        )(*args)

    return run


def on_device(
    electrons,
    phonons,
    phonon_energy,
    phonon_decay,
    coupling,
    tile_kblock,
    tile_partner,
    tile_qslot,
    tile_count,
    partner_need,
    phonon_need,
):
    devices = lax.axis_size("bulk")
    kb = electrons.shape[0]
    qb = phonons.shape[0]
    tiles = coupling.shape[0]
    cap = partner_need.shape[1] // devices
    assert cap == phonon_need.shape[1] // devices and kb + qb <= 128
    rows4 = devices * 2 * cap
    rows8 = devices * 4 * cap
    groups = tiles // 8
    held = HELD_CHUNKS * (tiles // CHUNKS)
    weights = pltpu.VMEM((groups, 16, 128), bf16)
    streams = [weights, pltpu.VMEM(coupling.shape, bf16), pltpu.SemaphoreType.DMA((CHUNKS,))]
    rest = (tiles - held, 128, 128)
    rest_sems = pltpu.SemaphoreType.DMA((CHUNKS - HELD_CHUNKS,))
    forward_streams = [weights, pltpu.VMEM(rest, bf16), rest_sems]
    sums = [pltpu.VMEM((groups, 8, 128), f32)] * 2
    pass_out = [((groups, 8, 128), f32)] * 2
    block4 = ((rows4, 128), f32)
    block8 = ((rows8, 128), f32)

    work = dict(flops=2 * tiles * 16 * 128 * 128, seen=tiles * 128 * 128 * 2)

    def exchange(x):
        return lax.all_to_all(x, "bulk", split_axis=0, concat_axis=0, tiled=True)

    ints = ((1, tiles), jnp.int32)
    lists = ((1, partner_need.shape[1]), jnp.int32)
    small = [((kb, 128), f32)] + [((qb, 128), f32)] * 3 + [ints] * 3
    step_rows = kb + qb + 4 * cap
    assert step_rows % 8 == 0 and devices % 2 == 0
    f, n, energy, decay, kblock, partner, qslot, send, lists_in = call(
        functools.partial(need_kernel, cap),
        "need",
        small + [((devices // 2 * step_rows, 128), f32), ((rows4, devices * step_rows), bf16)],
        [pltpu.VMEM(*lists), pltpu.VMEM(*lists), pltpu.SemaphoreType.DMA((9,))],
        spaces={i: pltpu.HBM for i in range(9)},
    )(
        electrons,
        phonons,
        phonon_energy,
        phonon_decay,
        tile_kblock.reshape(1, tiles),
        tile_partner.reshape(1, tiles),
        tile_qslot.reshape(1, tiles),
        partner_need,
        phonon_need,
    )
    same_core = [list(range(core, devices, 2)) for core in (0, 1)]
    recv = lax.all_to_all(
        send, "bulk", split_axis=0, concat_axis=0, tiled=True, axis_index_groups=same_core
    )
    other = lax.ppermute(recv, "bulk", [(i, i ^ 1) for i in range(devices)])
    c_held, c_rest = call(
        transpose_kernel,
        "transpose",
        [((held, 128, 128), bf16), (rest, bf16)],
        [pltpu.VMEM(coupling.shape, bf16), pltpu.VMEM(rest, bf16), streams[2], rest_sems],
        spaces={1: pltpu.HBM},
        out_spaces={1: pltpu.HBM},
        **work,
    )(f, coupling)
    ge4, gp4, gp8, gk, sk, sp4, sp8, b0, b1 = call(
        functools.partial(tables_kernel, cap),
        "tables",
        [
            ((tiles, rows4), bf16),
            ((tiles, rows4), bf16),
            ((tiles, rows8), bf16),
            ((tiles, kb), bf16),
            ((kb, tiles), bf16),
            ((rows4, tiles), bf16),
            ((rows8, 2 * tiles), bf16),
        ]
        + pass_out,
        streams,
        spaces={0: pltpu.SMEM, 5: pltpu.HBM},
        **work,
    )(tile_count, kblock, partner, qslot, f, coupling)
    back = call(backward_kernel, "backward", pass_out, streams, spaces={2: pltpu.HBM}, **work)
    for step in range(STEPS):
        if step:
            recv = exchange(send)
            b0, b1 = back(f, gk, coupling)
        lists = (serve,) if step else (other, lists_in)
        send, e0, f1, *hot = call(
            functools.partial(first_kernel, cap, kb + qb, not step),
            "first",
            [block4] + [((kb, 128), f32)] * 2 + ([] if step else [((rows4, 128), bf16)]),
            forward_streams + sums,
            spaces={9 + len(lists): pltpu.HBM},
            **work,
        )(recv, *lists, f, ge4, gp4, sk, sp4, b0, b1, c_held, c_rest)
        if not step:
            serve = hot[0]
            s8, st4, st8a, st8b = call(
                functools.partial(serve_kernel, cap, kb, qb),
                "serve",
                [
                    ((rows8, 128), bf16),
                    ((qb, rows4), bf16),
                    ((qb, rows8), bf16),
                    ((qb, rows8), bf16),
                ],
            )(serve)
        recv = exchange(send)
        b0, b1 = back(f1, gk, coupling)
        send, p0, n1, far = call(
            functools.partial(phonon_kernel, kb),
            "phonon",
            [block8] + [((qb, 128), f32)] * 2 + [((tiles, 128), f32)],
        )(recv, n, energy, decay, ge4, st4, sp8, s8, b0, b1)
        recv = exchange(send)
        last = step == STEPS - 1
        f, n, *send = call(
            functools.partial(second_kernel, not last),
            "second",
            [((kb, 128), f32), ((qb, 128), f32)] + ([] if last else [block4]),
            forward_streams + sums,
            spaces={16: pltpu.HBM},
            **work,
        )(
            recv, far, f, f1, e0, n, n1, p0, energy, decay,
            gp8, sk, st8a, st8b, serve, c_held, c_rest,
        )
        send = send[0] if send else None
    return (f, n)


def solution(mesh):
    placed = (
        P(("groups", "bulk"), None),
        P(("groups", "bulk"), None),
        P("bulk", None),
        P("bulk", None),
        P("bulk", None, None),
        P("bulk"),
        P("bulk"),
        P("bulk"),
        P("bulk"),
        P("bulk", None),
        P("bulk", None),
    )
    return jax.shard_map(
        on_device,
        mesh=mesh,
        in_specs=placed,
        out_specs=(P(("groups", "bulk"), None), P(("groups", "bulk"), None)),
        check_vma=False,
    )
```

```python
import functools

import jax
import jax.numpy as jnp
from jax import lax
from jax.experimental import pallas as pl
from jax.experimental.pallas import tpu as pltpu
from jax.sharding import PartitionSpec as P

STEPS = 2
DT = 0.05
CHUNKS = 8
HELD_CHUNKS = 2
f32 = jnp.float32
bf16 = jnp.bfloat16
VMEM_LIMIT = 24 * 1024 * 1024


def iota(shape, dim):
    return lax.broadcasted_iota(jnp.int32, shape, dim)


def dot(a, b):
    return lax.dot_general(a, b, (((1,), (0,)), ((), ())), preferred_element_type=f32)


def split(x):
    hi = x.astype(bf16)
    rest = x - hi.astype(f32)
    mid = rest.astype(bf16)
    lo = (rest - mid.astype(f32)).astype(bf16)
    return hi, mid, lo


def pick(onehot, x):
    hi, mid, lo = split(x)
    return dot(onehot, hi) + dot(onehot, mid) + dot(onehot, lo)


def stacked(first, second):
    tiles = first.shape[0]
    return jnp.concatenate(
        [first.reshape(tiles // 8, 8, 128), second.reshape(tiles // 8, 8, 128)], axis=1
    ).astype(bf16)


def row_is(r):
    return iota((16, 128), 0) % 8 == r


def padded(*parts):
    rows = sum(p.shape[0] for p in parts)
    return jnp.concatenate([*parts, jnp.zeros((128 - rows, 128), f32)], axis=0)


def flat(ref):
    return ref[...].reshape(-1, 128)


def chunk_copy(src, dst, sems, i):
    size = src.shape[0] // sems.shape[0]
    here = pl.ds(i * size, size)
    return pltpu.make_async_copy(src.at[here], dst.at[here], sems.at[i])


def start_chunks(src, dst, sems):
    for i in range(sems.shape[0]):
        chunk_copy(src, dst, sems, i).start()


def start(copies):
    for copy in copies:
        copy.start()


def block_diagonal(w):
    w = w.astype(f32)
    return jnp.concatenate(
        [jnp.where(row_is(r), w, 0.0).astype(bf16) for r in range(8)], axis=1
    )


def left_sides(first, second, w_ref):
    tiles = first.shape[0]
    w = stacked(first, second)
    for p in range(tiles // 16):
        w_ref[p] = jnp.concatenate(
            [block_diagonal(w[2 * p]), block_diagonal(w[2 * p + 1])], axis=0
        )


def tile_products(w_ref, parts, out0, out1):
    size = 2 * w_ref.shape[0] // CHUNKS
    base = 0
    for c_ref, c_hbm, sems in parts:
        groups = c_ref.shape[0] // 8

        def chunk(i, _):
            if c_hbm is not None:
                chunk_copy(c_hbm, c_ref, sems, i).wait()
            for k in range(0, size, 2):
                g = i * size + k
                at = base + g
                rhs = jnp.concatenate(
                    [c_ref[pl.ds((g + j) * 8, 8)].reshape(1024, 128) for j in (0, 1)], axis=1
                )
                res = dot(w_ref[at // 2], rhs)
                for j in (0, 1):
                    own = res[16 * j : 16 * (j + 1), 128 * j : 128 * (j + 1)]
                    out0[at + j] = own[:8]
                    out1[at + j] = own[8:]
            return 0

        lax.fori_loop(0, groups // size, chunk, 0)
        base += groups


def backward_pass(own, c_hbm, c_ref, sems, w_ref, out0, out1):
    left_sides(1.0 - own, own, w_ref)
    tile_products(w_ref, [(c_ref, c_hbm, sems)], out0, out1)


def electron_rate(sum_k, far, bose, f, parts, w_ref, o0, o1):
    left_sides(far * (1.0 + bose), far + bose, w_ref)
    tile_products(w_ref, parts, o0, o1)
    return pick(sum_k, flat(o0)) - f * pick(sum_k, flat(o1))


def need_kernel(cap, *refs):
    ins, outs = refs[:9], refs[9:]
    small, send_ref, list_ref = outs[:7], outs[7], outs[8]
    pneed_ref, qneed_ref, sems = outs[-3:]
    copies = [
        pltpu.make_async_copy(src, dst, sems.at[i])
        for i, (src, dst) in enumerate(zip(ins, [*small, pneed_ref, qneed_ref]))
    ]
    start(copies)
    rows, sent = list_ref.shape
    slots = pneed_ref.shape[1]
    peers = slots // cap
    step = sent // peers
    x = iota((rows, slots), 0)
    y = iota((rows, slots), 1)
    peer, r = x // (2 * cap), x % (2 * cap)
    e_here = (r < cap) & (y == peer * cap + r)
    p_here = (r >= cap) & (y == peer * cap + r - cap)
    for copy in copies:
        copy.wait()
    f, n = small[0][...], small[1][...]
    kb, qb = f.shape[0], n.shape[0]
    pn = jnp.broadcast_to(pneed_ref[...].astype(f32), (rows, slots))
    qn = jnp.broadcast_to(qneed_ref[...].astype(f32), (rows, slots)) + float(kb)
    col = jnp.sum(jnp.where(e_here, pn, 0.0) + jnp.where(p_here, qn, 0.0), axis=1, keepdims=True)
    hot = (iota((rows, 128), 1).astype(f32) == col).astype(f32)
    core = lax.rem(lax.axis_index("bulk"), 2)
    peer1 = iota((rows, 1), 0) // (2 * cap)
    start_of = (peer1 // 2 + jnp.where(peer1 % 2 == core, 0, peers // 2)) * step
    list_ref[...] = jnp.where(
        iota((rows, sent), 1).astype(f32) == col + start_of.astype(f32), 1.0, 0.0
    ).astype(bf16)
    for chip in range(peers // 2):
        lists = hot[chip * 4 * cap : (chip + 1) * 4 * cap]
        send_ref[chip * step : (chip + 1) * step] = jnp.concatenate([f, n, lists], axis=0)


def tables_kernel(
    cap,
    count_ref,
    kblock_ref,
    partner_ref,
    qslot_ref,
    f_ref,
    c_hbm,
    ge4_ref,
    gp4_ref,
    gp8_ref,
    gk_ref,
    sk_ref,
    sp4_ref,
    sp8_ref,
    b0_ref,
    b1_ref,
    w_ref,
    c_ref,
    sems,
):
    start_chunks(c_hbm, c_ref, sems)
    tiles = kblock_ref.shape[1]
    kb = f_ref.shape[0]
    used = iota((1, tiles), 1) < count_ref[0]
    k = kblock_ref[...]
    e = partner_ref[...]
    q = qslot_ref[...]
    rows4 = sp4_ref.shape[0]
    rows8 = sp8_ref.shape[0]
    ind = lambda m: jnp.where(m, 1.0, 0.0)
    k_hot = ind(iota((kb, tiles), 0) == k)
    sk_ref[...] = jnp.where(used, k_hot, 0.0).astype(bf16)
    gk_ref[...] = k_hot.T.astype(bf16)
    x = iota((rows4, tiles), 0)
    row_e = (e // cap) * (2 * cap) + e % cap
    row_p = (q // cap) * (2 * cap) + cap + q % cap
    ge4_ref[...] = ind(x == row_e).T.astype(bf16)
    p_hot = ind(x == row_p)
    gp4_ref[...] = p_hot.T.astype(bf16)
    sp4_ref[...] = jnp.where(used, p_hot, 0.0).astype(bf16)
    x = iota((rows8, tiles), 0)
    row_z = (q // cap) * (4 * cap) + q % cap
    gp8_ref[...] = ind(x == row_z).T.astype(bf16)
    sp8_ref[...] = jnp.concatenate(
        [
            jnp.where(used, ind(x == row_z + cap), 0.0),
            jnp.where(used, ind(x == row_z + 2 * cap), 0.0),
        ],
        axis=1,
    ).astype(bf16)
    own = pick(gk_ref[...], f_ref[...])
    backward_pass(own, c_hbm, c_ref, sems, w_ref, b0_ref, b1_ref)


def transpose_kernel(after_ref, c_hbm, held_ref, t_hbm, c_ref, t_ref, in_sems, out_sems):
    start_chunks(c_hbm, c_ref, in_sems)
    size = c_ref.shape[0] // in_sems.shape[0]
    held = held_ref.shape[0] // size

    def to_held(i, _):
        chunk_copy(c_hbm, c_ref, in_sems, i).wait()
        for t in range(size):
            held_ref[i * size + t] = c_ref[i * size + t].T
        return 0

    def to_rest(i, _):
        chunk_copy(c_hbm, c_ref, in_sems, held + i).wait()
        for t in range(size):
            t_ref[i * size + t] = c_ref[(held + i) * size + t].T
        chunk_copy(t_ref, t_hbm, out_sems, i).start()
        return 0

    lax.fori_loop(0, held, to_held, 0)
    lax.fori_loop(0, out_sems.shape[0], to_rest, 0)
    for i in range(out_sems.shape[0]):
        chunk_copy(t_ref, t_hbm, out_sems, i).wait()


def serve_kernel(cap, kb, qb, hot_ref, s8_ref, st4_ref, st8a_ref, st8b_ref):
    hot = hot_ref[...]
    rows4, rows8 = hot.shape[0], s8_ref.shape[0]
    x = iota((rows8, rows4), 0)
    y = iota((rows8, rows4), 1)
    peer, r = x // (4 * cap), x % (4 * cap)
    source = peer * (2 * cap) + cap + r % cap

    def rows_of(kind):
        here = (y == source) & (r // cap == kind)
        return dot(jnp.where(here, 1.0, 0.0).astype(bf16), hot)

    s8_ref[...] = rows_of(0).astype(bf16)
    st4_ref[...] = hot.astype(f32).T[kb : kb + qb].astype(bf16)
    st8a_ref[...] = rows_of(1).T[kb : kb + qb].astype(bf16)
    st8b_ref[...] = rows_of(2).T[kb : kb + qb].astype(bf16)


def first_kernel(cap, state_rows, starts, recv, *refs):
    other, refs = (refs[0], refs[1:]) if starts else (None, refs)
    list_ref, f_ref, ge4_ref, gp4_ref, sk_ref, sp4_ref, b0_ref, b1_ref, held_ref, c_hbm = refs[:10]
    send, e_ref, f1_ref = refs[10:13]
    hot_ref = refs[13] if starts else None
    w_ref, c_ref, sems, o0, o1 = refs[-5:]
    start_chunks(c_hbm, c_ref, sems)
    f = f_ref[...]
    got = recv[...]
    serve = list_ref[...]
    if starts:
        rows, sent = serve.shape
        every = jnp.concatenate([got, other[...]], axis=0)
        got = pick(serve, every)
        x = iota((rows, sent), 0)
        peers = rows // (2 * cap)
        step = sent // peers
        core = lax.rem(lax.axis_index("bulk"), 2)
        peer = x // (2 * cap)
        chip_row = (peer // 2 + jnp.where(peer % 2 == core, 0, peers // 2)) * step
        lists_at = chip_row + state_rows + 2 * cap * core + x % (2 * cap)
        at = jnp.where(iota((rows, sent), 1) == lists_at, 1.0, 0.0).astype(bf16)
        serve = dot(at, every.astype(bf16)).astype(bf16)
        hot_ref[...] = serve
    far = pick(ge4_ref[...], got)
    bose = pick(gp4_ref[...], got)
    gain = far * flat(b0_ref)
    terms = gain + bose * (gain - (1.0 - far) * flat(b1_ref))
    phonon_rows = pick(sp4_ref[...], terms)
    parts = [(held_ref, None, None), (c_ref, c_hbm, sems)]
    rate = electron_rate(sk_ref[...], far, bose, f, parts, w_ref, o0, o1)
    f1 = f + DT * rate
    e_ref[...] = rate
    f1_ref[...] = f1
    send[...] = pick(serve, padded(f1)) + phonon_rows


def backward_kernel(f_ref, gk_ref, c_hbm, b0_ref, b1_ref, w_ref, c_ref, sems):
    start_chunks(c_hbm, c_ref, sems)
    own = pick(gk_ref[...], f_ref[...])
    backward_pass(own, c_hbm, c_ref, sems, w_ref, b0_ref, b1_ref)


def phonon_kernel(
    kb,
    recv,
    n_ref,
    energy_ref,
    decay_ref,
    ge4_ref,
    st4_ref,
    sp8_ref,
    s8_ref,
    b0_ref,
    b1_ref,
    send,
    p_ref,
    n1_ref,
    far_ref,
):
    n = n_ref[...]
    got = recv[...]
    thermal = 1.0 / (jnp.exp(energy_ref[...]) - 1.0)
    rate = pick(st4_ref[...], got) - decay_ref[...] * (n - thermal)
    n1 = n + DT * rate
    p_ref[...] = rate
    n1_ref[...] = n1
    far = pick(ge4_ref[...], got)
    far_ref[...] = far
    gain = far * flat(b0_ref)
    both = jnp.concatenate([gain, gain - (1.0 - far) * flat(b1_ref)], axis=0)
    state = padded(jnp.zeros((kb, 128), f32), n1)
    send[...] = pick(s8_ref[...], state) + pick(sp8_ref[...], both)


def second_kernel(with_send, recv, *refs):
    far_ref, f_ref, f1_ref, e_ref, n_ref, n1_ref, p_ref, energy_ref, decay_ref = refs[:9]
    gp8_ref, sk_ref, st8a_ref, st8b_ref, serve_ref, held_ref, c_hbm = refs[9:16]
    refs = refs[16:]
    f2_ref, n2_ref, *refs = refs
    send, refs = (refs[0], refs[1:]) if with_send else (None, refs)
    w_ref, c_ref, sems, o0, o1 = refs
    start_chunks(c_hbm, c_ref, sems)
    got = recv[...]
    n, n1 = n_ref[...], n1_ref[...]
    bose = pick(gp8_ref[...], got)
    thermal = 1.0 / (jnp.exp(energy_ref[...]) - 1.0)
    p1 = (
        pick(st8a_ref[...], got)
        + n1 * pick(st8b_ref[...], got)
        - decay_ref[...] * (n1 - thermal)
    )
    n2 = n + (DT / 2.0) * (p_ref[...] + p1)
    n2_ref[...] = n2
    parts = [(held_ref, None, None), (c_ref, c_hbm, sems)]
    rate = electron_rate(sk_ref[...], far_ref[...], bose, f1_ref[...], parts, w_ref, o0, o1)
    f2 = f_ref[...] + (DT / 2.0) * (e_ref[...] + rate)
    f2_ref[...] = f2
    if with_send:
        send[...] = pick(serve_ref[...], padded(f2, n2))


def call(kernel, name, outs, scratch=(), spaces=None, out_spaces=None, flops=0, seen=0):
    def run(*args):
        places = dict(spaces or {})
        args = [
            pltpu.with_memory_space_constraint(x, pltpu.HBM)
            if places.get(i) is pltpu.HBM
            else x
            for i, x in enumerate(args)
        ]
        specs = [
            pl.BlockSpec(memory_space=places.get(i, pltpu.VMEM)) for i in range(len(args))
        ]
        return pl.pallas_call(
            kernel,
            out_shape=[
                pltpu.HBM(*o) if (out_spaces or {}).get(i) else jax.ShapeDtypeStruct(*o)
                for i, o in enumerate(outs)
            ],
            in_specs=specs,
            out_specs=[
                pl.BlockSpec(memory_space=(out_spaces or {}).get(i, pltpu.VMEM))
                for i in range(len(outs))
            ],
            scratch_shapes=list(scratch),
            compiler_params=pltpu.CompilerParams(vmem_limit_bytes=VMEM_LIMIT),
            cost_estimate=pl.CostEstimate(
                flops=flops, bytes_accessed=seen, transcendentals=0
            ),
            name=name,
        )(*args)

    return run


def on_device(
    electrons,
    phonons,
    phonon_energy,
    phonon_decay,
    coupling,
    tile_kblock,
    tile_partner,
    tile_qslot,
    tile_count,
    partner_need,
    phonon_need,
):
    devices = lax.axis_size("bulk")
    kb = electrons.shape[0]
    qb = phonons.shape[0]
    tiles = coupling.shape[0]
    cap = partner_need.shape[1] // devices
    assert cap == phonon_need.shape[1] // devices and kb + qb <= 128
    rows4 = devices * 2 * cap
    rows8 = devices * 4 * cap
    groups = tiles // 8
    held = HELD_CHUNKS * (tiles // CHUNKS)
    weights = pltpu.VMEM((groups // 2, 32, 1024), bf16)
    streams = [weights, pltpu.VMEM(coupling.shape, bf16), pltpu.SemaphoreType.DMA((CHUNKS,))]
    rest = (tiles - held, 128, 128)
    rest_sems = pltpu.SemaphoreType.DMA((CHUNKS - HELD_CHUNKS,))
    forward_streams = [weights, pltpu.VMEM(rest, bf16), rest_sems]
    sums = [pltpu.VMEM((groups, 8, 128), f32)] * 2
    pass_out = [((groups, 8, 128), f32)] * 2
    block4 = ((rows4, 128), f32)
    block8 = ((rows8, 128), f32)

    work = dict(flops=2 * tiles * 16 * 128 * 128, seen=tiles * 128 * 128 * 2)

    def exchange(x):
        return lax.all_to_all(x, "bulk", split_axis=0, concat_axis=0, tiled=True)

    ints = ((1, tiles), jnp.int32)
    lists = ((1, partner_need.shape[1]), jnp.int32)
    small = [((kb, 128), f32)] + [((qb, 128), f32)] * 3 + [ints] * 3
    step_rows = kb + qb + 4 * cap
    assert step_rows % 8 == 0 and devices % 2 == 0
    f, n, energy, decay, kblock, partner, qslot, send, lists_in = call(
        functools.partial(need_kernel, cap),
        "need",
        small + [((devices // 2 * step_rows, 128), f32), ((rows4, devices * step_rows), bf16)],
        [pltpu.VMEM(*lists), pltpu.VMEM(*lists), pltpu.SemaphoreType.DMA((9,))],
        spaces={i: pltpu.HBM for i in range(9)},
    )(
        electrons,
        phonons,
        phonon_energy,
        phonon_decay,
        tile_kblock.reshape(1, tiles),
        tile_partner.reshape(1, tiles),
        tile_qslot.reshape(1, tiles),
        partner_need,
        phonon_need,
    )
    same_core = [list(range(core, devices, 2)) for core in (0, 1)]
    recv = lax.all_to_all(
        send, "bulk", split_axis=0, concat_axis=0, tiled=True, axis_index_groups=same_core
    )
    c_held, c_rest = call(
        transpose_kernel,
        "transpose",
        [((held, 128, 128), bf16), (rest, bf16)],
        [pltpu.VMEM(coupling.shape, bf16), pltpu.VMEM(rest, bf16), streams[2], rest_sems],
        spaces={1: pltpu.HBM},
        out_spaces={1: pltpu.HBM},
        **work,
    )(f, coupling)
    ge4, gp4, gp8, gk, sk, sp4, sp8, b0, b1 = call(
        functools.partial(tables_kernel, cap),
        "tables",
        [
            ((tiles, rows4), bf16),
            ((tiles, rows4), bf16),
            ((tiles, rows8), bf16),
            ((tiles, kb), bf16),
            ((kb, tiles), bf16),
            ((rows4, tiles), bf16),
            ((rows8, 2 * tiles), bf16),
        ]
        + pass_out,
        streams,
        spaces={0: pltpu.SMEM, 5: pltpu.HBM},
        **work,
    )(tile_count, kblock, partner, qslot, f, coupling)
    recv, c_held, b0 = lax.optimization_barrier((recv, c_held, b0))
    other = lax.ppermute(recv, "bulk", [(i, i ^ 1) for i in range(devices)])
    back = call(backward_kernel, "backward", pass_out, streams, spaces={2: pltpu.HBM}, **work)
    for step in range(STEPS):
        if step:
            recv = exchange(send)
            b0, b1 = back(f, gk, coupling)
        lists = (serve,) if step else (other, lists_in)
        send, e0, f1, *hot = call(
            functools.partial(first_kernel, cap, kb + qb, not step),
            "first",
            [block4] + [((kb, 128), f32)] * 2 + ([] if step else [((rows4, 128), bf16)]),
            forward_streams + sums,
            spaces={9 + len(lists): pltpu.HBM},
            **work,
        )(recv, *lists, f, ge4, gp4, sk, sp4, b0, b1, c_held, c_rest)
        if not step:
            serve = hot[0]
            s8, st4, st8a, st8b = call(
                functools.partial(serve_kernel, cap, kb, qb),
                "serve",
                [
                    ((rows8, 128), bf16),
                    ((qb, rows4), bf16),
                    ((qb, rows8), bf16),
                    ((qb, rows8), bf16),
                ],
            )(serve)
        recv = exchange(send)
        b0, b1 = back(f1, gk, coupling)
        send, p0, n1, far = call(
            functools.partial(phonon_kernel, kb),
            "phonon",
            [block8] + [((qb, 128), f32)] * 2 + [((tiles, 128), f32)],
        )(recv, n, energy, decay, ge4, st4, sp8, s8, b0, b1)
        recv = exchange(send)
        last = step == STEPS - 1
        f, n, *send = call(
            functools.partial(second_kernel, not last),
            "second",
            [((kb, 128), f32), ((qb, 128), f32)] + ([] if last else [block4]),
            forward_streams + sums,
            spaces={16: pltpu.HBM},
            **work,
        )(
            recv, far, f, f1, e0, n, n1, p0, energy, decay,
            gp8, sk, st8a, st8b, serve, c_held, c_rest,
        )
        send = send[0] if send else None
    return (f, n)


def solution(mesh):
    placed = (
        P(("groups", "bulk"), None),
        P(("groups", "bulk"), None),
        P("bulk", None),
        P("bulk", None),
        P("bulk", None, None),
        P("bulk"),
        P("bulk"),
        P("bulk"),
        P("bulk"),
        P("bulk", None),
        P("bulk", None),
    )
    return jax.shard_map(
        on_device,
        mesh=mesh,
        in_specs=placed,
        out_specs=(P(("groups", "bulk"), None), P(("groups", "bulk"), None)),
        check_vma=False,
    )
```

```python
import functools

import jax
import jax.numpy as jnp
from jax import lax
from jax.experimental import pallas as pl
from jax.experimental.pallas import tpu as pltpu
from jax.sharding import PartitionSpec as P

DT = 0.05
CHUNKS = 8
HELD_CHUNKS = 2
f32 = jnp.float32
bf16 = jnp.bfloat16
VMEM_LIMIT = 48 * 1024 * 1024


def iota(shape, dim):
    return lax.broadcasted_iota(jnp.int32, shape, dim)


def dot(a, b):
    return lax.dot_general(a, b, (((1,), (0,)), ((), ())), preferred_element_type=f32)


def split(x):
    hi = x.astype(bf16)
    rest = x - hi.astype(f32)
    mid = rest.astype(bf16)
    lo = (rest - mid.astype(f32)).astype(bf16)
    return hi, mid, lo


def pick(onehot, x):
    hi, mid, lo = split(x)
    return dot(onehot, hi) + dot(onehot, mid) + dot(onehot, lo)


def stacked(first, second):
    tiles = first.shape[0]
    return jnp.concatenate(
        [first.reshape(tiles // 8, 8, 128), second.reshape(tiles // 8, 8, 128)], axis=1
    ).astype(bf16)


def row_is(r):
    return iota((16, 128), 0) % 8 == r


def padded(*parts):
    rows = sum(p.shape[0] for p in parts)
    return jnp.concatenate([*parts, jnp.zeros((128 - rows, 128), f32)], axis=0)


def flat(ref):
    return ref[...].reshape(-1, 128)


def chunk_copy(src, dst, sems, i):
    size = src.shape[0] // sems.shape[0]
    here = pl.ds(i * size, size)
    return pltpu.make_async_copy(src.at[here], dst.at[here], sems.at[i])


def start_chunks(src, dst, sems):
    for i in range(sems.shape[0]):
        chunk_copy(src, dst, sems, i).start()


def start(copies):
    for copy in copies:
        copy.start()


def block_diagonal(w):
    w = w.astype(f32)
    return jnp.concatenate(
        [jnp.where(row_is(r), w, 0.0).astype(bf16) for r in range(8)], axis=1
    )


def left_sides(first, second, w_ref):
    tiles = first.shape[0]
    w = stacked(first, second)
    for p in range(tiles // 16):
        w_ref[p] = jnp.concatenate(
            [block_diagonal(w[2 * p]), block_diagonal(w[2 * p + 1])], axis=0
        )


def chunk_products(w_ref, c_ref, i, base, out0, out1):
    size = 2 * w_ref.shape[0] // CHUNKS
    for k in range(0, size, 2):
        g = i * size + k
        at = base + g
        rhs = jnp.concatenate(
            [c_ref[pl.ds((g + j) * 8, 8)].reshape(1024, 128) for j in (0, 1)], axis=1
        )
        res = dot(w_ref[at // 2], rhs)
        for j in (0, 1):
            own = res[16 * j : 16 * (j + 1), 128 * j : 128 * (j + 1)]
            out0[at + j] = own[:8]
            out1[at + j] = own[8:]


def tile_products(w_ref, parts, out0, out1):
    size = 2 * w_ref.shape[0] // CHUNKS
    base = 0
    for c_ref, c_hbm, sems in parts:
        groups = c_ref.shape[0] // 8

        def chunk(i, _):
            if c_hbm is not None:
                chunk_copy(c_hbm, c_ref, sems, i).wait()
            chunk_products(w_ref, c_ref, i, base, out0, out1)
            return 0

        lax.fori_loop(0, groups // size, chunk, 0)
        base += groups


def backward_pass(own, c_hbm, c_ref, sems, w_ref, out0, out1):
    left_sides(1.0 - own, own, w_ref)
    tile_products(w_ref, [(c_ref, c_hbm, sems)], out0, out1)


def electron_rate(sum_k, far, bose, f, parts, w_ref, o0, o1):
    left_sides(far * (1.0 + bose), far + bose, w_ref)
    tile_products(w_ref, parts, o0, o1)
    return pick(sum_k, flat(o0)) - f * pick(sum_k, flat(o1))


def my_core():
    return lax.rem(lax.axis_index("bulk"), 2)


def block_of(peer, peers):
    return peer // 2 + jnp.where(peer % 2 == my_core(), 0, peers // 2)


def need_kernel(cap, *refs):
    ins, outs = refs[:9], refs[9:]
    small, send_ref, list_ref, mine_ref = outs[:7], outs[7], outs[8], outs[9]
    pneed_ref, qneed_ref, sems = outs[-3:]
    copies = [
        pltpu.make_async_copy(src, dst, sems.at[i])
        for i, (src, dst) in enumerate(zip(ins, [*small, pneed_ref, qneed_ref]))
    ]
    start(copies)
    rows, sent = list_ref.shape
    slots = pneed_ref.shape[1]
    peers = slots // cap
    step = sent // peers
    x = iota((rows, slots), 0)
    y = iota((rows, slots), 1)
    peer, r = x // (2 * cap), x % (2 * cap)
    e_here = (r < cap) & (y == peer * cap + r)
    p_here = (r >= cap) & (y == peer * cap + r - cap)
    for copy in copies:
        copy.wait()
    f, n = small[0][...], small[1][...]
    kb, qb = f.shape[0], n.shape[0]
    own_p, own_q = pneed_ref[...].astype(f32), qneed_ref[...].astype(f32)
    pn = jnp.broadcast_to(own_p, (rows, slots))
    qn = jnp.broadcast_to(own_q, (rows, slots)) + float(kb)
    col = jnp.sum(jnp.where(e_here, pn, 0.0) + jnp.where(p_here, qn, 0.0), axis=1, keepdims=True)
    mine_ref[...] = jnp.broadcast_to(col, (rows, 128))
    start_of = block_of(iota((rows, 1), 0) // (2 * cap), peers) * step
    list_ref[...] = jnp.where(
        iota((rows, sent), 1).astype(f32) == col + start_of.astype(f32), 1.0, 0.0
    ).astype(bf16)
    row = iota((8, slots), 0)
    lists = jnp.where(row == 0, own_p, jnp.where(row == 1, own_q, 0.0))
    if slots < 128:
        lists = jnp.concatenate([lists, jnp.zeros((8, 128 - slots), f32)], axis=1)
    block = jnp.concatenate([f, n, lists], axis=0)
    for chip in range(peers // 2):
        send_ref[chip * step : (chip + 1) * step] = block


def prepare_kernel(
    cap,
    count_ref,
    kblock_ref,
    partner_ref,
    qslot_ref,
    f_ref,
    c_hbm,
    held_ref,
    t_hbm,
    ge4_ref,
    gp4_ref,
    gp8_ref,
    gk_ref,
    sk_ref,
    sp_ref,
    sp4_ref,
    sp8_ref,
    b0_ref,
    b1_ref,
    w_ref,
    c_ref,
    in_sems,
    t_ref,
    out_sems,
):
    start_chunks(c_hbm, c_ref, in_sems)
    tiles = kblock_ref.shape[1]
    kb = f_ref.shape[0]
    used = iota((1, tiles), 1) < count_ref[0]
    k = kblock_ref[...]
    e = partner_ref[...]
    q = qslot_ref[...]
    rows4 = sp4_ref.shape[0]
    rows8 = sp8_ref.shape[0]
    ind = lambda m: jnp.where(m, 1.0, 0.0)
    k_hot = ind(iota((kb, tiles), 0) == k)
    gk_ref[...] = k_hot.T.astype(bf16)
    own = pick(gk_ref[...], f_ref[...])
    left_sides(1.0 - own, own, w_ref)
    sk_ref[...] = jnp.where(used, k_hot, 0.0).astype(bf16)
    x = iota((rows4, tiles), 0)
    row_e = (e // cap) * (2 * cap) + e % cap
    row_p = (q // cap) * (2 * cap) + cap + q % cap
    ge4_ref[...] = ind(x == row_e).T.astype(bf16)
    p_hot = ind(x == row_p)
    gp4_ref[...] = p_hot.T.astype(bf16)
    sp4_ref[...] = jnp.where(used, p_hot, 0.0).astype(bf16)
    sp_ref[...] = jnp.where(used, ind(iota(sp_ref.shape, 0) == q), 0.0).astype(bf16)
    x = iota((rows8, tiles), 0)
    row_z = (q // cap) * (4 * cap) + q % cap
    gp8_ref[...] = ind(x == row_z).T.astype(bf16)
    sp8_ref[...] = jnp.concatenate(
        [
            jnp.where(used, ind(x == row_z + cap), 0.0),
            jnp.where(used, ind(x == row_z + 2 * cap), 0.0),
        ],
        axis=1,
    ).astype(bf16)

    size = c_ref.shape[0] // CHUNKS
    held = held_ref.shape[0] // size

    def to_held(i, _):
        chunk_copy(c_hbm, c_ref, in_sems, i).wait()
        chunk_products(w_ref, c_ref, i, 0, b0_ref, b1_ref)
        for t in range(size):
            held_ref[i * size + t] = c_ref[i * size + t].T
        return 0

    def to_rest(i, _):
        chunk_copy(c_hbm, c_ref, in_sems, held + i).wait()
        chunk_products(w_ref, c_ref, held + i, 0, b0_ref, b1_ref)
        for t in range(size):
            t_ref[i * size + t] = c_ref[(held + i) * size + t].T
        chunk_copy(t_ref, t_hbm, out_sems, i).start()
        return 0

    lax.fori_loop(0, held, to_held, 0)
    lax.fori_loop(0, out_sems.shape[0], to_rest, 0)
    for i in range(out_sems.shape[0]):
        chunk_copy(t_ref, t_hbm, out_sems, i).wait()


def blocks(same_ref, other_ref, peers, first, count):
    step = 2 * same_ref.shape[0] // peers
    parts = [
        ref[b * step + first : b * step + first + count]
        for ref in (same_ref, other_ref)
        for b in range(peers // 2)
    ]
    return jnp.concatenate(parts, axis=0)


def serve_kernel(
    cap,
    kb,
    qb,
    same_ref,
    other_ref,
    hot_ref,
    mine_ref,
    share_ref,
    owner_ref,
    s8_ref,
    st4_ref,
    st8a_ref,
    st8b_ref,
):
    hot = hot_ref[...]
    rows4, rows8 = hot.shape[0], s8_ref.shape[0]
    x = iota((rows8, rows4), 0)
    y = iota((rows8, rows4), 1)
    peer, r = x // (4 * cap), x % (4 * cap)
    source = peer * (2 * cap) + cap + r % cap

    def rows_of(kind):
        here = (y == source) & (r // cap == kind)
        return dot(jnp.where(here, 1.0, 0.0).astype(bf16), hot)

    s8_ref[...] = rows_of(0).astype(bf16)
    st4_ref[...] = hot.astype(f32).T[kb : kb + qb].astype(bf16)
    st8a_ref[...] = rows_of(1).T[kb : kb + qb].astype(bf16)
    st8b_ref[...] = rows_of(2).T[kb : kb + qb].astype(bf16)

    peers = rows4 // (2 * cap)
    slots = peers * cap
    wide = peers * slots
    lists = blocks(same_ref, other_ref, peers, kb + qb, 8).astype(bf16)
    pick_q = iota((peers, 8 * peers), 1) == 8 * iota((peers, 8 * peers), 0) + 1
    every_q = dot(jnp.where(pick_q, 1.0, 0.0).astype(bf16), lists).astype(bf16)
    tiled = iota((128, wide), 0) == iota((128, wide), 1) % slots
    spread = dot(every_q, jnp.where(tiled, 1.0, 0.0).astype(bf16))
    lane = iota((1, wide), 1)
    here = iota((peers, wide), 0) == lane // slots
    q = jnp.sum(jnp.where(here, spread, 0.0), axis=0, keepdims=True)
    ids = q + (lane % slots // cap * qb).astype(f32)
    row = iota((rows4, 1), 0)
    col = mine_ref[...][:, :1]
    my_ids = col - float(kb) + (row // (2 * cap) * qb).astype(f32)
    my_ids = jnp.where(row % (2 * cap) >= cap, my_ids, -1.0)
    share_ref[...] = jnp.where(ids == my_ids, 1.0, 0.0).astype(bf16)
    owned = (lax.axis_index("bulk") * qb + iota((qb, 1), 0)).astype(f32)
    owner_ref[...] = jnp.where(ids == owned, 1.0, 0.0).astype(bf16)


def thermal_of(energy_ref):
    return 1.0 / (jnp.exp(energy_ref[...]) - 1.0)


def put_broadcast(send, served, contributions):
    slots = contributions.shape[0]
    for chip in range(served.shape[0] // 8):
        at = chip * (8 + slots)
        send[at : at + 8] = served[chip * 8 : chip * 8 + 8]
        send[at + 8 : at + 8 + slots] = contributions


def phonon_terms(far, bose, b0_ref, b1_ref):
    gain = far * flat(b0_ref)
    return gain + bose * (gain - (1.0 - far) * flat(b1_ref))


def first_kernel(
    cap,
    same_ref,
    other_ref,
    list_ref,
    f_ref,
    n_ref,
    energy_ref,
    decay_ref,
    ge4_ref,
    gp4_ref,
    sk_ref,
    sp_ref,
    b0_ref,
    b1_ref,
    held_ref,
    c_hbm,
    send,
    e_ref,
    f1_ref,
    hot_ref,
    w_ref,
    c_ref,
    sems,
    o0,
    o1,
):
    start_chunks(c_hbm, c_ref, sems)
    f, n = f_ref[...], n_ref[...]
    kb, qb = f.shape[0], n.shape[0]
    rows4 = list_ref.shape[0]
    peers = rows4 // (2 * cap)
    got = pick(list_ref[...], jnp.concatenate([same_ref[...], other_ref[...]], axis=0))
    far = pick(ge4_ref[...], got)
    bose = pick(gp4_ref[...], got)
    contributions = pick(sp_ref[...], phonon_terms(far, bose, b0_ref, b1_ref))
    lists = blocks(same_ref, other_ref, peers, kb + qb, 8).astype(bf16)
    x = iota((rows4, 8 * peers), 0)
    r = x % (2 * cap)
    kind = jnp.where(r < cap, 0, 1)
    at = iota((rows4, 8 * peers), 1) == 8 * block_of(x // (2 * cap), peers) + kind
    asked = dot(jnp.where(at, 1.0, 0.0).astype(bf16), lists)
    r = iota((rows4, 128), 0) % (2 * cap)
    lane = iota((rows4, 128), 1)
    wanted = lane == lax.axis_index("bulk") * cap + r % cap
    col = jnp.sum(jnp.where(wanted, asked, 0.0), axis=1, keepdims=True)
    col = col + jnp.where(r[:, :1] < cap, 0.0, float(kb))
    hot = jnp.where(lane.astype(f32) == col, 1.0, 0.0).astype(bf16)
    hot_ref[...] = hot
    base = n - DT * decay_ref[...] * (n - thermal_of(energy_ref))
    parts = [(held_ref, None, None), (c_ref, c_hbm, sems)]
    rate = electron_rate(sk_ref[...], far, bose, f, parts, w_ref, o0, o1)
    f1 = f + DT * rate
    e_ref[...] = rate
    f1_ref[...] = f1
    put_broadcast(send, pick(hot, padded(f1, base)), contributions)


def middle_kernel(
    cap,
    ends,
    same_ref,
    other_ref,
    share_ref,
    owner_ref,
    serve_ref,
    f_ref,
    e_ref,
    own_ref,
    n_ref,
    energy_ref,
    decay_ref,
    ge4_ref,
    gp4_ref,
    sk_ref,
    sp_ref,
    b0_ref,
    b1_ref,
    held_ref,
    c_hbm,
    send,
    *refs,
):
    w_ref, c_ref, sems, o0, o1 = refs[-5:]
    start_chunks(c_hbm, c_ref, sems)
    rows4 = serve_ref.shape[0]
    peers = rows4 // (2 * cap)
    slots = peers * cap
    x = iota((rows4, 8 * peers), 0)
    source = 8 * block_of(x // (2 * cap), peers) + 2 * cap * my_core() + x % (2 * cap)
    at = jnp.where(iota((rows4, 8 * peers), 1) == source, 1.0, 0.0).astype(bf16)
    heads = blocks(same_ref, other_ref, peers, 0, 8)
    tails = split(blocks(same_ref, other_ref, peers, 8, slots))
    weight = DT / 2.0 if ends else DT
    shares = sum(dot(share_ref[...], part) for part in tails)
    got = pick(at, heads) + weight * shares
    far = pick(ge4_ref[...], got)
    bose = pick(gp4_ref[...], got)
    terms = phonon_terms(far, bose, b0_ref, b1_ref)
    contributions = pick(sp_ref[...], terms)
    total = sum(dot(owner_ref[...], part) for part in tails)
    n = n_ref[...]
    own = own_ref[...]
    parts = [(held_ref, None, None), (c_ref, c_hbm, sems)]
    if ends:
        n2_ref, e2_ref, f3_ref = refs[:3]
        n2_ref[...] = n + (DT / 2.0) * total
        rate = electron_rate(sk_ref[...], far, bose, own, parts, w_ref, o0, o1)
        f3 = own + DT * rate
        e2_ref[...] = rate
        f3_ref[...] = f3
        send[...] = pick(serve_ref[...], padded(f3)) + contributions
    else:
        base_ref, f2_ref = refs[:2]
        thermal = thermal_of(energy_ref)
        decay = decay_ref[...]
        p0 = total - decay * (n - thermal)
        n1 = n + DT * p0
        base = n + (DT / 2.0) * (p0 - decay * (n1 - thermal))
        base_ref[...] = base
        rate = electron_rate(sk_ref[...], far, bose, own, parts, w_ref, o0, o1)
        f2 = f_ref[...] + (DT / 2.0) * (e_ref[...] + rate)
        f2_ref[...] = f2
        put_broadcast(send, pick(serve_ref[...], padded(f2, base)), contributions)


def backward_kernel(f_ref, gk_ref, c_hbm, b0_ref, b1_ref, w_ref, c_ref, sems):
    start_chunks(c_hbm, c_ref, sems)
    own = pick(gk_ref[...], f_ref[...])
    backward_pass(own, c_hbm, c_ref, sems, w_ref, b0_ref, b1_ref)


def phonon_kernel(
    kb,
    recv,
    n_ref,
    energy_ref,
    decay_ref,
    ge4_ref,
    st4_ref,
    sp8_ref,
    s8_ref,
    b0_ref,
    b1_ref,
    send,
    p_ref,
    n1_ref,
    far_ref,
):
    n = n_ref[...]
    got = recv[...]
    thermal = thermal_of(energy_ref)
    rate = pick(st4_ref[...], got) - decay_ref[...] * (n - thermal)
    n1 = n + DT * rate
    p_ref[...] = rate
    n1_ref[...] = n1
    far = pick(ge4_ref[...], got)
    far_ref[...] = far
    gain = far * flat(b0_ref)
    both = jnp.concatenate([gain, gain - (1.0 - far) * flat(b1_ref)], axis=0)
    state = padded(jnp.zeros((kb, 128), f32), n1)
    send[...] = pick(s8_ref[...], state) + pick(sp8_ref[...], both)


def last_kernel(recv, *refs):
    far_ref, f_ref, f1_ref, e_ref, n_ref, n1_ref, p_ref, energy_ref, decay_ref = refs[:9]
    gp8_ref, sk_ref, st8a_ref, st8b_ref, held_ref, c_hbm = refs[9:15]
    refs = refs[15:]
    f2_ref, n2_ref, w_ref, c_ref, sems, o0, o1 = refs
    start_chunks(c_hbm, c_ref, sems)
    got = recv[...]
    n, n1 = n_ref[...], n1_ref[...]
    bose = pick(gp8_ref[...], got)
    thermal = thermal_of(energy_ref)
    p1 = (
        pick(st8a_ref[...], got)
        + n1 * pick(st8b_ref[...], got)
        - decay_ref[...] * (n1 - thermal)
    )
    n2 = n + (DT / 2.0) * (p_ref[...] + p1)
    n2_ref[...] = n2
    parts = [(held_ref, None, None), (c_ref, c_hbm, sems)]
    rate = electron_rate(sk_ref[...], far_ref[...], bose, f1_ref[...], parts, w_ref, o0, o1)
    f2 = f_ref[...] + (DT / 2.0) * (e_ref[...] + rate)
    f2_ref[...] = f2


def call(kernel, name, outs, scratch=(), spaces=None, out_spaces=None, flops=0, seen=0):
    def run(*args):
        places = dict(spaces or {})
        args = [
            pltpu.with_memory_space_constraint(x, pltpu.HBM)
            if places.get(i) is pltpu.HBM
            else x
            for i, x in enumerate(args)
        ]
        specs = [
            pl.BlockSpec(memory_space=places.get(i, pltpu.VMEM)) for i in range(len(args))
        ]
        return pl.pallas_call(
            kernel,
            out_shape=[
                pltpu.HBM(*o) if (out_spaces or {}).get(i) else jax.ShapeDtypeStruct(*o)
                for i, o in enumerate(outs)
            ],
            in_specs=specs,
            out_specs=[
                pl.BlockSpec(memory_space=(out_spaces or {}).get(i, pltpu.VMEM))
                for i in range(len(outs))
            ],
            scratch_shapes=list(scratch),
            compiler_params=pltpu.CompilerParams(vmem_limit_bytes=VMEM_LIMIT),
            cost_estimate=pl.CostEstimate(
                flops=flops, bytes_accessed=seen, transcendentals=0
            ),
            name=name,
        )(*args)

    return run


def on_device(
    electrons,
    phonons,
    phonon_energy,
    phonon_decay,
    coupling,
    tile_kblock,
    tile_partner,
    tile_qslot,
    tile_count,
    partner_need,
    phonon_need,
):
    devices = lax.axis_size("bulk")
    kb = electrons.shape[0]
    qb = phonons.shape[0]
    tiles = coupling.shape[0]
    cap = partner_need.shape[1] // devices
    assert cap == phonon_need.shape[1] // devices and kb + qb <= 128
    rows4 = devices * 2 * cap
    rows8 = devices * 4 * cap
    groups = tiles // 8
    held = HELD_CHUNKS * (tiles // CHUNKS)
    weights = pltpu.VMEM((groups // 2, 32, 1024), bf16)
    streams = [weights, pltpu.VMEM(coupling.shape, bf16), pltpu.SemaphoreType.DMA((CHUNKS,))]
    rest = (tiles - held, 128, 128)
    rest_sems = pltpu.SemaphoreType.DMA((CHUNKS - HELD_CHUNKS,))
    forward_streams = [weights, pltpu.VMEM(rest, bf16), rest_sems]
    sums = [pltpu.VMEM((groups, 8, 128), f32)] * 2
    pass_out = [((groups, 8, 128), f32)] * 2
    block4 = ((rows4, 128), f32)
    block8 = ((rows8, 128), f32)

    work = dict(flops=2 * tiles * 16 * 128 * 128, seen=tiles * 128 * 128 * 2)

    def exchange(x):
        return lax.all_to_all(x, "bulk", split_axis=0, concat_axis=0, tiled=True)

    ints = ((1, tiles), jnp.int32)
    lists = ((1, partner_need.shape[1]), jnp.int32)
    small = [((kb, 128), f32)] + [((qb, 128), f32)] * 3 + [ints] * 3
    step_rows = kb + qb + 8
    slots = devices * cap
    wide = 8 + slots
    assert step_rows % 8 == 0 and slots % 8 == 0 and slots <= 128
    assert devices % 2 == 0 and cap == 2
    chips = devices // 2
    same_core = [list(range(core, devices, 2)) for core in (0, 1)]

    def to_chips(x):
        return lax.all_to_all(
            x, "bulk", split_axis=0, concat_axis=0, tiled=True, axis_index_groups=same_core
        )

    def between_cores(x):
        return lax.ppermute(x, "bulk", [(i, i ^ 1) for i in range(devices)])

    f, n, energy, decay, kblock, partner, qslot, send, lists, mine = call(
        functools.partial(need_kernel, cap),
        "need",
        small
        + [
            ((chips * step_rows, 128), f32),
            ((rows4, devices * step_rows), bf16),
            ((rows4, 128), f32),
        ],
        [
            pltpu.VMEM(*lists),
            pltpu.VMEM((1, phonon_need.shape[1]), jnp.int32),
            pltpu.SemaphoreType.DMA((9,)),
        ],
        spaces={i: pltpu.HBM for i in range(9)},
    )(
        electrons,
        phonons,
        phonon_energy,
        phonon_decay,
        tile_kblock.reshape(1, tiles),
        tile_partner.reshape(1, tiles),
        tile_qslot.reshape(1, tiles),
        partner_need,
        phonon_need,
    )
    same = to_chips(send)
    c_held, c_rest, ge4, gp4, gp8, gk, sk, sp, sp4, sp8, b0, b1 = call(
        functools.partial(prepare_kernel, cap),
        "prepare",
        [
            ((held, 128, 128), bf16),
            (rest, bf16),
            ((tiles, rows4), bf16),
            ((tiles, rows4), bf16),
            ((tiles, rows8), bf16),
            ((tiles, kb), bf16),
            ((kb, tiles), bf16),
            ((slots, tiles), bf16),
            ((rows4, tiles), bf16),
            ((rows8, 2 * tiles), bf16),
        ]
        + pass_out,
        [*streams, pltpu.VMEM(rest, bf16), rest_sems],
        spaces={0: pltpu.SMEM, 5: pltpu.HBM},
        out_spaces={1: pltpu.HBM},
        **work,
    )(tile_count, kblock, partner, qslot, f, coupling)
    same, c_held, b0 = lax.optimization_barrier((same, c_held, b0))
    other = between_cores(same)
    wide_block = ((chips * wide, 128), f32)
    k_rows, q_rows = ((kb, 128), f32), ((qb, 128), f32)
    forward_scratch = forward_streams + sums
    send, e0, f1, serve = call(
        functools.partial(first_kernel, cap),
        "first",
        [wide_block, k_rows, k_rows, ((rows4, 128), bf16)],
        forward_scratch,
        spaces={14: pltpu.HBM},
        **work,
    )(same, other, lists, f, n, energy, decay, ge4, gp4, sk, sp, b0, b1, c_held, c_rest)
    share, owner, s8, st4, st8a, st8b = call(
        functools.partial(serve_kernel, cap, kb, qb),
        "serve",
        [
            ((rows4, devices * slots), bf16),
            ((qb, devices * slots), bf16),
            ((rows8, 128), bf16),
            ((qb, rows4), bf16),
            ((qb, rows8), bf16),
            ((qb, rows8), bf16),
        ],
    )(same, other, serve, mine)
    back = call(backward_kernel, "backward", pass_out, streams, spaces={2: pltpu.HBM}, **work)

    def middle(ends, send, outs, f, e, own, n, contributions):
        same = to_chips(send)
        b0, b1 = back(own, gk, coupling)
        same, b0 = lax.optimization_barrier((same, b0))
        other = between_cores(same)
        return call(
            functools.partial(middle_kernel, cap, ends),
            "middle",
            outs,
            forward_scratch,
            spaces={18: pltpu.HBM},
            **work,
        )(
            same, other, share, owner, serve, f, e, own, n, energy, decay,
            ge4, gp4, sk, contributions, b0, b1, c_held, c_rest,
        )

    send, base, f2 = middle(False, send, [wide_block, q_rows, k_rows], f, e0, f1, n, sp)
    send, n2, e2, f3 = middle(
        True, send, [block4, q_rows, k_rows, k_rows], f2, e0, f2, base, sp4
    )
    recv = exchange(send)
    b0, b1 = back(f3, gk, coupling)
    send, p2, n3, far = call(
        functools.partial(phonon_kernel, kb),
        "phonon",
        [block8, q_rows, q_rows, ((tiles, 128), f32)],
    )(recv, n2, energy, decay, ge4, st4, sp8, s8, b0, b1)
    recv = exchange(send)
    f, n = call(
        last_kernel,
        "last",
        [k_rows, q_rows],
        forward_scratch,
        spaces={15: pltpu.HBM},
        **work,
    )(
        recv, far, f2, f3, e2, n2, n3, p2, energy, decay,
        gp8, sk, st8a, st8b, c_held, c_rest,
    )
    return (f, n)


def solution(mesh):
    placed = (
        P(("groups", "bulk"), None),
        P(("groups", "bulk"), None),
        P("bulk", None),
        P("bulk", None),
        P("bulk", None, None),
        P("bulk"),
        P("bulk"),
        P("bulk"),
        P("bulk"),
        P("bulk", None),
        P("bulk", None),
    )
    return jax.shard_map(
        on_device,
        mesh=mesh,
        in_specs=placed,
        out_specs=(P(("groups", "bulk"), None), P(("groups", "bulk"), None)),
        check_vma=False,
    )
```

```python
import functools

import jax
import jax.numpy as jnp
from jax import lax
from jax.experimental import pallas as pl
from jax.experimental.pallas import tpu as pltpu
from jax.sharding import PartitionSpec as P

DT = 0.05
CHUNKS = 8
HELD_CHUNKS = 2
f32 = jnp.float32
bf16 = jnp.bfloat16
VMEM_LIMIT = 48 * 1024 * 1024


def iota(shape, dim):
    return lax.broadcasted_iota(jnp.int32, shape, dim)


def dot(a, b):
    return lax.dot_general(a, b, (((1,), (0,)), ((), ())), preferred_element_type=f32)


def split(x):
    hi = x.astype(bf16)
    rest = x - hi.astype(f32)
    mid = rest.astype(bf16)
    lo = (rest - mid.astype(f32)).astype(bf16)
    return hi, mid, lo


def pick(onehot, x):
    hi, mid, lo = split(x)
    both = dot(onehot, jnp.concatenate([hi, mid], axis=1))
    return both[:, :128] + both[:, 128:] + dot(onehot, lo)


def add_rows(onehot, x):
    hi = x.astype(bf16)
    mid = (x - hi.astype(f32)).astype(bf16)
    both = dot(onehot, jnp.concatenate([hi, mid], axis=1))
    return both[:, :128] + both[:, 128:]


def stacked(first, second):
    tiles = first.shape[0]
    return jnp.concatenate(
        [first.reshape(tiles // 8, 8, 128), second.reshape(tiles // 8, 8, 128)], axis=1
    ).astype(bf16)


def row_is(r):
    return iota((16, 128), 0) % 8 == r


def padded(*parts):
    rows = sum(p.shape[0] for p in parts)
    return jnp.concatenate([*parts, jnp.zeros((128 - rows, 128), f32)], axis=0)


def flat(ref):
    return ref[...].reshape(-1, 128)


def chunk_copy(src, dst, sems, i):
    size = src.shape[0] // sems.shape[0]
    here = pl.ds(i * size, size)
    return pltpu.make_async_copy(src.at[here], dst.at[here], sems.at[i])


def start_chunks(src, dst, sems):
    for i in range(sems.shape[0]):
        chunk_copy(src, dst, sems, i).start()


def start(copies):
    for copy in copies:
        copy.start()


def block_diagonal(w):
    w = w.astype(f32)
    return jnp.concatenate(
        [jnp.where(row_is(r), w, 0.0).astype(bf16) for r in range(8)], axis=1
    )


def left_sides(first, second, w_ref):
    w = stacked(first, second)
    for g in range(w.shape[0]):
        w_ref[g] = block_diagonal(w[g])


def chunk_products(w_ref, c_ref, i, base, out0, out1):
    size = w_ref.shape[0] // CHUNKS
    for k in range(size):
        g = i * size + k
        res = dot(w_ref[base + g], c_ref[pl.ds(g * 8, 8)].reshape(1024, 128))
        out0[base + g] = res[:8]
        out1[base + g] = res[8:]


def tile_products(w_ref, parts, out0, out1):
    size = w_ref.shape[0] // CHUNKS
    base = 0
    for c_ref, c_hbm, sems in parts:
        groups = c_ref.shape[0] // 8

        def chunk(i, _):
            if c_hbm is not None:
                chunk_copy(c_hbm, c_ref, sems, i).wait()
            chunk_products(w_ref, c_ref, i, base, out0, out1)
            return 0

        lax.fori_loop(0, groups // size, chunk, 0)
        base += groups


def backward_pass(own, c_hbm, c_ref, sems, w_ref, out0, out1):
    left_sides(1.0 - own, own, w_ref)
    tile_products(w_ref, [(c_ref, c_hbm, sems)], out0, out1)


def electron_rate(sum_k, far, bose, f, parts, w_ref, o0, o1):
    left_sides(far * (1.0 + bose), far + bose, w_ref)
    tile_products(w_ref, parts, o0, o1)
    return add_rows(sum_k, flat(o0)) - f * add_rows(sum_k, flat(o1))


def my_core():
    return lax.rem(lax.axis_index("bulk"), 2)


def block_of(peer, peers):
    return peer // 2 + jnp.where(peer % 2 == my_core(), 0, peers // 2)


def need_kernel(cap, *refs):
    ins, outs = refs[:9], refs[9:]
    *small, pneed_ref, qneed_ref, send_ref, sems = outs
    copies = [
        pltpu.make_async_copy(src, dst, sems.at[i])
        for i, (src, dst) in enumerate(zip(ins, [*small, pneed_ref, qneed_ref]))
    ]
    start(copies)
    slots = pneed_ref.shape[1]
    step = send_ref.shape[0] // (slots // cap // 2)
    for copy in copies:
        copy.wait()
    f, n = small[0][...], small[1][...]
    own_p, own_q = pneed_ref[...].astype(f32), qneed_ref[...].astype(f32)
    row = iota((8, slots), 0)
    lists = jnp.where(row == 0, own_p, jnp.where(row == 1, own_q, 0.0))
    if slots < 128:
        lists = jnp.concatenate([lists, jnp.zeros((8, 128 - slots), f32)], axis=1)
    block = jnp.concatenate([f, n, lists], axis=0)
    for chip in range(slots // cap // 2):
        send_ref[chip * step : (chip + 1) * step] = block


def prepare_kernel(
    cap,
    count_ref,
    kblock_ref,
    partner_ref,
    qslot_ref,
    f_ref,
    pneed_ref,
    qneed_ref,
    c_hbm,
    held_ref,
    t_hbm,
    ge4_ref,
    gp4_ref,
    gp8_ref,
    gk_ref,
    sk_ref,
    sp_ref,
    sp4_ref,
    sp8_ref,
    list_ref,
    mine_ref,
    b0_ref,
    b1_ref,
    w_ref,
    c_ref,
    in_sems,
    t_ref,
    out_sems,
):
    start_chunks(c_hbm, c_ref, in_sems)
    tiles = kblock_ref.shape[1]
    kb = f_ref.shape[0]
    used = iota((1, tiles), 1) < count_ref[0]
    k = kblock_ref[...]
    e = partner_ref[...]
    q = qslot_ref[...]
    rows4 = sp4_ref.shape[0]
    rows8 = sp8_ref.shape[0]
    ind = lambda m: jnp.where(m, 1.0, 0.0)
    k_hot = ind(iota((kb, tiles), 0) == k)
    gk_ref[...] = k_hot.T.astype(bf16)
    own = add_rows(gk_ref[...], f_ref[...])
    left_sides(1.0 - own, own, w_ref)
    sk_ref[...] = jnp.where(used, k_hot, 0.0).astype(bf16)
    x = iota((rows4, tiles), 0)
    row_e = (e // cap) * (2 * cap) + e % cap
    row_p = (q // cap) * (2 * cap) + cap + q % cap
    ge4_ref[...] = ind(x == row_e).T.astype(bf16)
    p_hot = ind(x == row_p)
    gp4_ref[...] = p_hot.T.astype(bf16)
    sp4_ref[...] = jnp.where(used, p_hot, 0.0).astype(bf16)
    sp_ref[...] = jnp.where(used, ind(iota(sp_ref.shape, 0) == q), 0.0).astype(bf16)
    x = iota((rows8, tiles), 0)
    row_z = (q // cap) * (4 * cap) + q % cap
    gp8_ref[...] = ind(x == row_z).T.astype(bf16)
    sp8_ref[...] = jnp.concatenate(
        [
            jnp.where(used, ind(x == row_z + cap), 0.0),
            jnp.where(used, ind(x == row_z + 2 * cap), 0.0),
        ],
        axis=1,
    ).astype(bf16)

    rows, sent = list_ref.shape
    slots = pneed_ref.shape[1]
    peers = slots // cap
    x = iota((rows, slots), 0)
    y = iota((rows, slots), 1)
    peer, r = x // (2 * cap), x % (2 * cap)
    e_here = (r < cap) & (y == peer * cap + r)
    p_here = (r >= cap) & (y == peer * cap + r - cap)
    pn = jnp.broadcast_to(pneed_ref[...].astype(f32), (rows, slots))
    qn = jnp.broadcast_to(qneed_ref[...].astype(f32), (rows, slots)) + float(kb)
    col = jnp.sum(jnp.where(e_here, pn, 0.0) + jnp.where(p_here, qn, 0.0), axis=1, keepdims=True)
    mine_ref[...] = jnp.broadcast_to(col, (rows, 128))
    start_of = block_of(iota((rows, 1), 0) // (2 * cap), peers) * (sent // peers)
    list_ref[...] = jnp.where(
        iota((rows, sent), 1).astype(f32) == col + start_of.astype(f32), 1.0, 0.0
    ).astype(bf16)

    size = c_ref.shape[0] // CHUNKS
    held = held_ref.shape[0] // size

    def to_held(i, _):
        chunk_copy(c_hbm, c_ref, in_sems, i).wait()
        chunk_products(w_ref, c_ref, i, 0, b0_ref, b1_ref)
        for t in range(size):
            held_ref[i * size + t] = c_ref[i * size + t].T
        return 0

    def to_rest(i, _):
        chunk_copy(c_hbm, c_ref, in_sems, held + i).wait()
        chunk_products(w_ref, c_ref, held + i, 0, b0_ref, b1_ref)
        for t in range(size):
            t_ref[i * size + t] = c_ref[(held + i) * size + t].T
        chunk_copy(t_ref, t_hbm, out_sems, i).start()
        return 0

    lax.fori_loop(0, held, to_held, 0)
    lax.fori_loop(0, out_sems.shape[0], to_rest, 0)
    for i in range(out_sems.shape[0]):
        chunk_copy(t_ref, t_hbm, out_sems, i).wait()


def blocks(same_ref, other_ref, peers, first, count):
    step = 2 * same_ref.shape[0] // peers
    parts = [
        ref[b * step + first : b * step + first + count]
        for ref in (same_ref, other_ref)
        for b in range(peers // 2)
    ]
    return jnp.concatenate(parts, axis=0)


def serve_kernel(
    cap,
    kb,
    qb,
    asked_ref,
    hot_ref,
    mine_ref,
    share_ref,
    s8_ref,
    st4_ref,
    st8a_ref,
    st8b_ref,
):
    hot = hot_ref[...]
    rows4, rows8 = hot.shape[0], s8_ref.shape[0]
    x = iota((rows8, rows4), 0)
    y = iota((rows8, rows4), 1)
    peer, r = x // (4 * cap), x % (4 * cap)
    source = peer * (2 * cap) + cap + r % cap

    def rows_of(kind):
        here = (y == source) & (r // cap == kind)
        return dot(jnp.where(here, 1.0, 0.0).astype(bf16), hot)

    s8_ref[...] = rows_of(0).astype(bf16)
    st4_ref[...] = hot.astype(f32).T[kb : kb + qb].astype(bf16)
    st8a_ref[...] = rows_of(1).T[kb : kb + qb].astype(bf16)
    st8b_ref[...] = rows_of(2).T[kb : kb + qb].astype(bf16)

    peers = rows4 // (2 * cap)
    slots = peers * cap
    wide = peers * slots
    lists = asked_ref[...]
    pick_q = iota((peers, 8 * peers), 1) == 8 * iota((peers, 8 * peers), 0) + 1
    every_q = dot(jnp.where(pick_q, 1.0, 0.0).astype(bf16), lists).astype(bf16)
    tiled = iota((128, wide), 0) == iota((128, wide), 1) % slots
    spread = dot(every_q, jnp.where(tiled, 1.0, 0.0).astype(bf16))
    lane = iota((1, wide), 1)
    here = iota((peers, wide), 0) == lane // slots
    q = jnp.sum(jnp.where(here, spread, 0.0), axis=0, keepdims=True)
    ids = q + (lane % slots // cap * qb).astype(f32)
    row = iota((rows4, 1), 0)
    col = mine_ref[...][:, :1]
    my_ids = col - float(kb) + (row // (2 * cap) * qb).astype(f32)
    my_ids = jnp.where(row % (2 * cap) >= cap, my_ids, -1.0)
    owned = (lax.axis_index("bulk") * qb + iota((qb, 1), 0)).astype(f32)
    wanted = jnp.concatenate([my_ids, owned], axis=0)
    share_ref[...] = jnp.where(ids == wanted, 1.0, 0.0).astype(bf16)


def thermal_of(energy_ref):
    return 1.0 / (jnp.exp(energy_ref[...]) - 1.0)


def put_broadcast(send, served, contributions):
    slots = contributions.shape[0]
    for chip in range(served.shape[0] // 8):
        at = chip * (8 + slots)
        send[at : at + 8] = served[chip * 8 : chip * 8 + 8]
        send[at + 8 : at + 8 + slots] = contributions


def phonon_terms(far, bose, b0_ref, b1_ref):
    gain = far * flat(b0_ref)
    return gain + bose * (gain - (1.0 - far) * flat(b1_ref))


def first_kernel(
    cap,
    same_ref,
    other_ref,
    list_ref,
    f_ref,
    n_ref,
    energy_ref,
    decay_ref,
    ge4_ref,
    gp4_ref,
    sk_ref,
    sp_ref,
    b0_ref,
    b1_ref,
    held_ref,
    c_hbm,
    send,
    e_ref,
    f1_ref,
    hot_ref,
    asked_ref,
    w_ref,
    c_ref,
    sems,
    o0,
    o1,
):
    start_chunks(c_hbm, c_ref, sems)
    f, n = f_ref[...], n_ref[...]
    kb, qb = f.shape[0], n.shape[0]
    rows4 = list_ref.shape[0]
    peers = rows4 // (2 * cap)
    got = pick(list_ref[...], jnp.concatenate([same_ref[...], other_ref[...]], axis=0))
    far = add_rows(ge4_ref[...], got)
    bose = add_rows(gp4_ref[...], got)
    contributions = add_rows(sp_ref[...], phonon_terms(far, bose, b0_ref, b1_ref))
    lists = blocks(same_ref, other_ref, peers, kb + qb, 8).astype(bf16)
    asked_ref[...] = lists
    x = iota((rows4, 8 * peers), 0)
    r = x % (2 * cap)
    kind = jnp.where(r < cap, 0, 1)
    at = iota((rows4, 8 * peers), 1) == 8 * block_of(x // (2 * cap), peers) + kind
    asked = dot(jnp.where(at, 1.0, 0.0).astype(bf16), lists)
    r = iota((rows4, 128), 0) % (2 * cap)
    lane = iota((rows4, 128), 1)
    wanted = lane == lax.axis_index("bulk") * cap + r % cap
    col = jnp.sum(jnp.where(wanted, asked, 0.0), axis=1, keepdims=True)
    col = col + jnp.where(r[:, :1] < cap, 0.0, float(kb))
    hot = jnp.where(lane.astype(f32) == col, 1.0, 0.0).astype(bf16)
    hot_ref[...] = hot
    base = n - DT * decay_ref[...] * (n - thermal_of(energy_ref))
    parts = [(held_ref, None, None), (c_ref, c_hbm, sems)]
    rate = electron_rate(sk_ref[...], far, bose, f, parts, w_ref, o0, o1)
    f1 = f + DT * rate
    e_ref[...] = rate
    f1_ref[...] = f1
    put_broadcast(send, pick(hot, padded(f1, base)), contributions)


def middle_kernel(
    cap,
    ends,
    same_ref,
    other_ref,
    share_ref,
    serve_ref,
    f_ref,
    e_ref,
    own_ref,
    n_ref,
    energy_ref,
    decay_ref,
    ge4_ref,
    gp4_ref,
    sk_ref,
    sp_ref,
    b0_ref,
    b1_ref,
    held_ref,
    c_hbm,
    send,
    *refs,
):
    w_ref, c_ref, sems, o0, o1 = refs[-5:]
    start_chunks(c_hbm, c_ref, sems)
    rows4 = serve_ref.shape[0]
    peers = rows4 // (2 * cap)
    slots = peers * cap
    x = iota((rows4, 8 * peers), 0)
    source = 8 * block_of(x // (2 * cap), peers) + 2 * cap * my_core() + x % (2 * cap)
    at = jnp.where(iota((rows4, 8 * peers), 1) == source, 1.0, 0.0).astype(bf16)
    heads = blocks(same_ref, other_ref, peers, 0, 8)
    tails = blocks(same_ref, other_ref, peers, 8, slots)
    weight = DT / 2.0 if ends else DT
    both = add_rows(share_ref[...], tails)
    shares, total = both[:rows4], both[rows4:]
    got = pick(at, heads) + weight * shares
    far = add_rows(ge4_ref[...], got)
    bose = add_rows(gp4_ref[...], got)
    terms = phonon_terms(far, bose, b0_ref, b1_ref)
    contributions = add_rows(sp_ref[...], terms)
    n = n_ref[...]
    own = own_ref[...]
    parts = [(held_ref, None, None), (c_ref, c_hbm, sems)]
    if ends:
        n2_ref, e2_ref, f3_ref = refs[:3]
        n2_ref[...] = n + (DT / 2.0) * total
        rate = electron_rate(sk_ref[...], far, bose, own, parts, w_ref, o0, o1)
        f3 = own + DT * rate
        e2_ref[...] = rate
        f3_ref[...] = f3
        send[...] = pick(serve_ref[...], padded(f3)) + contributions
    else:
        base_ref, f2_ref = refs[:2]
        thermal = thermal_of(energy_ref)
        decay = decay_ref[...]
        p0 = total - decay * (n - thermal)
        n1 = n + DT * p0
        base = n + (DT / 2.0) * (p0 - decay * (n1 - thermal))
        base_ref[...] = base
        rate = electron_rate(sk_ref[...], far, bose, own, parts, w_ref, o0, o1)
        f2 = f_ref[...] + (DT / 2.0) * (e_ref[...] + rate)
        f2_ref[...] = f2
        put_broadcast(send, pick(serve_ref[...], padded(f2, base)), contributions)


def backward_kernel(f_ref, gk_ref, c_hbm, b0_ref, b1_ref, w_ref, c_ref, sems):
    start_chunks(c_hbm, c_ref, sems)
    own = add_rows(gk_ref[...], f_ref[...])
    backward_pass(own, c_hbm, c_ref, sems, w_ref, b0_ref, b1_ref)


def phonon_kernel(
    kb,
    recv,
    n_ref,
    energy_ref,
    decay_ref,
    ge4_ref,
    st4_ref,
    sp8_ref,
    s8_ref,
    b0_ref,
    b1_ref,
    send,
    p_ref,
    n1_ref,
    far_ref,
):
    n = n_ref[...]
    got = recv[...]
    thermal = thermal_of(energy_ref)
    rate = add_rows(st4_ref[...], got) - decay_ref[...] * (n - thermal)
    n1 = n + DT * rate
    p_ref[...] = rate
    n1_ref[...] = n1
    far = add_rows(ge4_ref[...], got)
    far_ref[...] = far
    gain = far * flat(b0_ref)
    both = jnp.concatenate([gain, gain - (1.0 - far) * flat(b1_ref)], axis=0)
    state = padded(jnp.zeros((kb, 128), f32), n1)
    send[...] = pick(s8_ref[...], state) + add_rows(sp8_ref[...], both)


def last_kernel(recv, *refs):
    far_ref, f_ref, f1_ref, e_ref, n_ref, n1_ref, p_ref, energy_ref, decay_ref = refs[:9]
    gp8_ref, sk_ref, st8a_ref, st8b_ref, held_ref, c_hbm = refs[9:15]
    refs = refs[15:]
    f2_ref, n2_ref, w_ref, c_ref, sems, o0, o1 = refs
    start_chunks(c_hbm, c_ref, sems)
    got = recv[...]
    n, n1 = n_ref[...], n1_ref[...]
    bose = add_rows(gp8_ref[...], got)
    thermal = thermal_of(energy_ref)
    p1 = (
        add_rows(st8a_ref[...], got)
        + n1 * add_rows(st8b_ref[...], got)
        - decay_ref[...] * (n1 - thermal)
    )
    n2 = n + (DT / 2.0) * (p_ref[...] + p1)
    n2_ref[...] = n2
    parts = [(held_ref, None, None), (c_ref, c_hbm, sems)]
    rate = electron_rate(sk_ref[...], far_ref[...], bose, f1_ref[...], parts, w_ref, o0, o1)
    f2 = f_ref[...] + (DT / 2.0) * (e_ref[...] + rate)
    f2_ref[...] = f2


def call(kernel, name, outs, scratch=(), spaces=None, out_spaces=None, flops=0, seen=0):
    def run(*args):
        places = dict(spaces or {})
        args = [
            pltpu.with_memory_space_constraint(x, pltpu.HBM)
            if places.get(i) is pltpu.HBM
            else x
            for i, x in enumerate(args)
        ]
        specs = [
            pl.BlockSpec(memory_space=places.get(i, pltpu.VMEM)) for i in range(len(args))
        ]
        return pl.pallas_call(
            kernel,
            out_shape=[
                pltpu.HBM(*o) if (out_spaces or {}).get(i) else jax.ShapeDtypeStruct(*o)
                for i, o in enumerate(outs)
            ],
            in_specs=specs,
            out_specs=[
                pl.BlockSpec(memory_space=(out_spaces or {}).get(i, pltpu.VMEM))
                for i in range(len(outs))
            ],
            scratch_shapes=list(scratch),
            compiler_params=pltpu.CompilerParams(vmem_limit_bytes=VMEM_LIMIT),
            cost_estimate=pl.CostEstimate(
                flops=flops, bytes_accessed=seen, transcendentals=0
            ),
            name=name,
        )(*args)

    return run


def on_device(
    electrons,
    phonons,
    phonon_energy,
    phonon_decay,
    coupling,
    tile_kblock,
    tile_partner,
    tile_qslot,
    tile_count,
    partner_need,
    phonon_need,
):
    devices = lax.axis_size("bulk")
    kb = electrons.shape[0]
    qb = phonons.shape[0]
    tiles = coupling.shape[0]
    cap = partner_need.shape[1] // devices
    assert cap == phonon_need.shape[1] // devices and kb + qb <= 128
    rows4 = devices * 2 * cap
    rows8 = devices * 4 * cap
    groups = tiles // 8
    held = HELD_CHUNKS * (tiles // CHUNKS)
    weights = pltpu.VMEM((groups, 16, 1024), bf16)
    streams = [weights, pltpu.VMEM(coupling.shape, bf16), pltpu.SemaphoreType.DMA((CHUNKS,))]
    rest = (tiles - held, 128, 128)
    rest_sems = pltpu.SemaphoreType.DMA((CHUNKS - HELD_CHUNKS,))
    forward_streams = [weights, pltpu.VMEM(rest, bf16), rest_sems]
    sums = [pltpu.VMEM((groups, 8, 128), f32)] * 2
    pass_out = [((groups, 8, 128), f32)] * 2
    block4 = ((rows4, 128), f32)
    block8 = ((rows8, 128), f32)

    work = dict(flops=2 * tiles * 16 * 128 * 128, seen=tiles * 128 * 128 * 2)

    def exchange(x):
        return lax.all_to_all(x, "bulk", split_axis=0, concat_axis=0, tiled=True)

    ints = ((1, tiles), jnp.int32)
    lists = ((1, partner_need.shape[1]), jnp.int32)
    small = [((kb, 128), f32)] + [((qb, 128), f32)] * 3 + [ints] * 3
    step_rows = kb + qb + 8
    slots = devices * cap
    wide = 8 + slots
    assert step_rows % 8 == 0 and slots % 8 == 0 and slots <= 128
    assert devices % 2 == 0 and cap == 2
    chips = devices // 2
    same_core = [list(range(core, devices, 2)) for core in (0, 1)]

    def to_chips(x):
        return lax.all_to_all(
            x, "bulk", split_axis=0, concat_axis=0, tiled=True, axis_index_groups=same_core
        )

    def between_cores(x):
        return lax.ppermute(x, "bulk", [(i, i ^ 1) for i in range(devices)])

    f, n, energy, decay, kblock, partner, qslot, pneed, qneed, send = call(
        functools.partial(need_kernel, cap),
        "need",
        small + [lists, lists, ((chips * step_rows, 128), f32)],
        [pltpu.SemaphoreType.DMA((9,))],
        spaces={i: pltpu.HBM for i in range(9)},
    )(
        electrons,
        phonons,
        phonon_energy,
        phonon_decay,
        tile_kblock.reshape(1, tiles),
        tile_partner.reshape(1, tiles),
        tile_qslot.reshape(1, tiles),
        partner_need,
        phonon_need,
    )
    same = to_chips(send)
    c_held, c_rest, ge4, gp4, gp8, gk, sk, sp, sp4, sp8, picks, mine, b0, b1 = call(
        functools.partial(prepare_kernel, cap),
        "prepare",
        [
            ((held, 128, 128), bf16),
            (rest, bf16),
            ((tiles, rows4), bf16),
            ((tiles, rows4), bf16),
            ((tiles, rows8), bf16),
            ((tiles, kb), bf16),
            ((kb, tiles), bf16),
            ((slots, tiles), bf16),
            ((rows4, tiles), bf16),
            ((rows8, 2 * tiles), bf16),
            ((rows4, devices * step_rows), bf16),
            ((rows4, 128), f32),
        ]
        + pass_out,
        [*streams, pltpu.VMEM(rest, bf16), rest_sems],
        spaces={0: pltpu.SMEM, 7: pltpu.HBM},
        out_spaces={1: pltpu.HBM},
        **work,
    )(tile_count, kblock, partner, qslot, f, pneed, qneed, coupling)
    same, c_held, b0 = lax.optimization_barrier((same, c_held, b0))
    other = between_cores(same)
    wide_block = ((chips * wide, 128), f32)
    k_rows, q_rows = ((kb, 128), f32), ((qb, 128), f32)
    forward_scratch = forward_streams + sums
    send, e0, f1, serve, asked = call(
        functools.partial(first_kernel, cap),
        "first",
        [wide_block, k_rows, k_rows, ((rows4, 128), bf16), ((8 * devices, 128), bf16)],
        forward_scratch,
        spaces={14: pltpu.HBM},
        **work,
    )(same, other, picks, f, n, energy, decay, ge4, gp4, sk, sp, b0, b1, c_held, c_rest)
    share, s8, st4, st8a, st8b = call(
        functools.partial(serve_kernel, cap, kb, qb),
        "serve",
        [
            ((rows4 + qb, devices * slots), bf16),
            ((rows8, 128), bf16),
            ((qb, rows4), bf16),
            ((qb, rows8), bf16),
            ((qb, rows8), bf16),
        ],
    )(asked, serve, mine)
    back = call(backward_kernel, "backward", pass_out, streams, spaces={2: pltpu.HBM}, **work)

    def middle(ends, send, outs, f, e, own, n, contributions):
        same = to_chips(send)
        b0, b1 = back(own, gk, coupling)
        same, b0 = lax.optimization_barrier((same, b0))
        other = between_cores(same)
        return call(
            functools.partial(middle_kernel, cap, ends),
            "middle",
            outs,
            forward_scratch,
            spaces={17: pltpu.HBM},
            **work,
        )(
            same, other, share, serve, f, e, own, n, energy, decay,
            ge4, gp4, sk, contributions, b0, b1, c_held, c_rest,
        )

    send, base, f2 = middle(False, send, [wide_block, q_rows, k_rows], f, e0, f1, n, sp)
    send, n2, e2, f3 = middle(
        True, send, [block4, q_rows, k_rows, k_rows], f2, e0, f2, base, sp4
    )
    recv = exchange(send)
    b0, b1 = back(f3, gk, coupling)
    send, p2, n3, far = call(
        functools.partial(phonon_kernel, kb),
        "phonon",
        [block8, q_rows, q_rows, ((tiles, 128), f32)],
    )(recv, n2, energy, decay, ge4, st4, sp8, s8, b0, b1)
    recv = exchange(send)
    f, n = call(
        last_kernel,
        "last",
        [k_rows, q_rows],
        forward_scratch,
        spaces={15: pltpu.HBM},
        **work,
    )(
        recv, far, f2, f3, e2, n2, n3, p2, energy, decay,
        gp8, sk, st8a, st8b, c_held, c_rest,
    )
    return (f, n)


def solution(mesh):
    placed = (
        P(("groups", "bulk"), None),
        P(("groups", "bulk"), None),
        P("bulk", None),
        P("bulk", None),
        P("bulk", None, None),
        P("bulk"),
        P("bulk"),
        P("bulk"),
        P("bulk"),
        P("bulk", None),
        P("bulk", None),
    )
    return jax.shard_map(
        on_device,
        mesh=mesh,
        in_specs=placed,
        out_specs=(P(("groups", "bulk"), None), P(("groups", "bulk"), None)),
        check_vma=False,
    )
```

```python
import functools

import jax
import jax.numpy as jnp
from jax import lax
from jax.experimental import pallas as pl
from jax.experimental.pallas import tpu as pltpu
from jax.sharding import PartitionSpec as P

DT = 0.05
CHUNKS = 8
HELD_CHUNKS = 2
f32 = jnp.float32
bf16 = jnp.bfloat16
VMEM_LIMIT = 48 * 1024 * 1024


def iota(shape, dim):
    return lax.broadcasted_iota(jnp.int32, shape, dim)


def dot(a, b):
    return lax.dot_general(a, b, (((1,), (0,)), ((), ())), preferred_element_type=f32)


def split(x):
    hi = x.astype(bf16)
    rest = x - hi.astype(f32)
    mid = rest.astype(bf16)
    lo = (rest - mid.astype(f32)).astype(bf16)
    return hi, mid, lo


def pick(onehot, x):
    hi, mid, lo = split(x)
    both = dot(onehot, jnp.concatenate([hi, mid], axis=1))
    return both[:, :128] + both[:, 128:] + dot(onehot, lo)


def add_rows(onehot, x):
    hi = x.astype(bf16)
    mid = (x - hi.astype(f32)).astype(bf16)
    both = dot(onehot, jnp.concatenate([hi, mid], axis=1))
    return both[:, :128] + both[:, 128:]


def gather_pair(table, x):
    rows = x.shape[0]
    hi = x.astype(bf16)
    mid = (x - hi.astype(f32)).astype(bf16)
    blank = jnp.zeros((rows, 128), bf16)

    def both(part):
        upper = jnp.concatenate([part, blank], axis=1)
        lower = jnp.concatenate([blank, part], axis=1)
        return dot(table, jnp.concatenate([upper, lower], axis=0))

    res = both(hi) + both(mid)
    return res[:, :128], res[:, 128:]


def stacked(first, second):
    tiles = first.shape[0]
    return jnp.concatenate(
        [first.reshape(tiles // 8, 8, 128), second.reshape(tiles // 8, 8, 128)], axis=1
    ).astype(bf16)


def row_is(r):
    return iota((16, 128), 0) % 8 == r


def padded(*parts):
    rows = sum(p.shape[0] for p in parts)
    return jnp.concatenate([*parts, jnp.zeros((128 - rows, 128), f32)], axis=0)


def flat(ref):
    return ref[...].reshape(-1, 128)


def chunk_copy(src, dst, sems, i):
    size = src.shape[0] // sems.shape[0]
    here = pl.ds(i * size, size)
    return pltpu.make_async_copy(src.at[here], dst.at[here], sems.at[i])


def start_chunks(src, dst, sems):
    for i in range(sems.shape[0]):
        chunk_copy(src, dst, sems, i).start(priority=i % 2)


def start(copies):
    for copy in copies:
        copy.start()


def block_diagonal(w):
    w = w.astype(f32)
    return jnp.concatenate(
        [jnp.where(row_is(r), w, 0.0).astype(bf16) for r in range(8)], axis=1
    )


def left_sides(first, second, w_ref):
    w = stacked(first, second)
    for g in range(w.shape[0]):
        w_ref[g] = block_diagonal(w[g])


def chunk_products(w_ref, c_ref, i, base, out0, out1):
    size = w_ref.shape[0] // CHUNKS
    for k in range(size):
        g = i * size + k
        res = dot(w_ref[base + g], c_ref[pl.ds(g * 8, 8)].reshape(1024, 128))
        out0[base + g] = res[:8]
        out1[base + g] = res[8:]


def tile_products(w_ref, parts, out0, out1):
    size = w_ref.shape[0] // CHUNKS
    base = 0
    for c_ref, c_hbm, sems in parts:
        groups = c_ref.shape[0] // 8

        def chunk(i, _):
            if c_hbm is not None:
                chunk_copy(c_hbm, c_ref, sems, i).wait()
            chunk_products(w_ref, c_ref, i, base, out0, out1)
            return 0

        lax.fori_loop(0, groups // size, chunk, 0)
        base += groups


def backward_pass(own, c_hbm, c_ref, sems, w_ref, out0, out1):
    left_sides(1.0 - own, own, w_ref)
    tile_products(w_ref, [(c_ref, c_hbm, sems)], out0, out1)


def electron_rate(sum_k, far, bose, f, parts, w_ref, o0, o1):
    left_sides(far * (1.0 + bose), far + bose, w_ref)
    tile_products(w_ref, parts, o0, o1)
    return add_rows(sum_k, flat(o0)) - f * add_rows(sum_k, flat(o1))


def my_core():
    return lax.rem(lax.axis_index("bulk"), 2)


def block_of(peer, peers):
    return peer // 2 + jnp.where(peer % 2 == my_core(), 0, peers // 2)


def need_kernel(cap, *refs):
    ins, outs = refs[:9], refs[9:]
    *small, pneed_ref, qneed_ref, send_ref, sems = outs
    copies = [
        pltpu.make_async_copy(src, dst, sems.at[i])
        for i, (src, dst) in enumerate(zip(ins, [*small, pneed_ref, qneed_ref]))
    ]
    start(copies)
    slots = pneed_ref.shape[1]
    step = send_ref.shape[0] // (slots // cap // 2)
    for copy in copies:
        copy.wait()
    f, n = small[0][...], small[1][...]
    own_p, own_q = pneed_ref[...].astype(f32), qneed_ref[...].astype(f32)
    row = iota((8, slots), 0)
    lists = jnp.where(row == 0, own_p, jnp.where(row == 1, own_q, 0.0))
    if slots < 128:
        lists = jnp.concatenate([lists, jnp.zeros((8, 128 - slots), f32)], axis=1)
    block = jnp.concatenate([f, n, lists], axis=0)
    for chip in range(slots // cap // 2):
        send_ref[chip * step : (chip + 1) * step] = block


def prepare_kernel(
    cap,
    count_ref,
    kblock_ref,
    partner_ref,
    qslot_ref,
    f_ref,
    pneed_ref,
    qneed_ref,
    c_hbm,
    held_ref,
    t_hbm,
    pair_ref,
    gp8_ref,
    gk_ref,
    sk_ref,
    sp_ref,
    sp4_ref,
    sp8_ref,
    list_ref,
    mine_ref,
    b0_ref,
    b1_ref,
    w_ref,
    c_ref,
    in_sems,
    t_ref,
    out_sems,
):
    start_chunks(c_hbm, c_ref, in_sems)
    tiles = kblock_ref.shape[1]
    kb = f_ref.shape[0]
    used = iota((1, tiles), 1) < count_ref[0]
    k = kblock_ref[...]
    e = partner_ref[...]
    q = qslot_ref[...]
    rows4 = sp4_ref.shape[0]
    rows8 = sp8_ref.shape[0]
    ind = lambda m: jnp.where(m, 1.0, 0.0)
    k_hot = ind(iota((kb, tiles), 0) == k)
    gk_ref[...] = k_hot.T.astype(bf16)
    own = add_rows(gk_ref[...], f_ref[...])
    left_sides(1.0 - own, own, w_ref)
    sk_ref[...] = jnp.where(used, k_hot, 0.0).astype(bf16)
    x = iota((rows4, tiles), 0)
    row_e = (e // cap) * (2 * cap) + e % cap
    row_p = (q // cap) * (2 * cap) + cap + q % cap
    p_hot = ind(x == row_p)
    pair_ref[...] = jnp.concatenate([ind(x == row_e), p_hot], axis=0).T.astype(bf16)
    sp4_ref[...] = jnp.where(used, p_hot, 0.0).astype(bf16)
    sp_ref[...] = jnp.where(used, ind(iota(sp_ref.shape, 0) == q), 0.0).astype(bf16)
    x = iota((rows8, tiles), 0)
    row_z = (q // cap) * (4 * cap) + q % cap
    gp8_ref[...] = ind(x == row_z).T.astype(bf16)
    sp8_ref[...] = jnp.concatenate(
        [
            jnp.where(used, ind(x == row_z + cap), 0.0),
            jnp.where(used, ind(x == row_z + 2 * cap), 0.0),
        ],
        axis=1,
    ).astype(bf16)

    rows, sent = list_ref.shape
    slots = pneed_ref.shape[1]
    peers = slots // cap
    x = iota((rows, slots), 0)
    y = iota((rows, slots), 1)
    peer, r = x // (2 * cap), x % (2 * cap)
    e_here = (r < cap) & (y == peer * cap + r)
    p_here = (r >= cap) & (y == peer * cap + r - cap)
    pn = jnp.broadcast_to(pneed_ref[...].astype(f32), (rows, slots))
    qn = jnp.broadcast_to(qneed_ref[...].astype(f32), (rows, slots)) + float(kb)
    col = jnp.sum(jnp.where(e_here, pn, 0.0) + jnp.where(p_here, qn, 0.0), axis=1, keepdims=True)
    mine_ref[...] = jnp.broadcast_to(col, (rows, 128))
    start_of = block_of(iota((rows, 1), 0) // (2 * cap), peers) * (sent // peers)
    list_ref[...] = jnp.where(
        iota((rows, sent), 1).astype(f32) == col + start_of.astype(f32), 1.0, 0.0
    ).astype(bf16)

    size = c_ref.shape[0] // CHUNKS
    held = held_ref.shape[0] // size

    def to_held(i, _):
        chunk_copy(c_hbm, c_ref, in_sems, i).wait()
        chunk_products(w_ref, c_ref, i, 0, b0_ref, b1_ref)
        for t in range(size):
            held_ref[i * size + t] = c_ref[i * size + t].T
        return 0

    def to_rest(i, _):
        chunk_copy(c_hbm, c_ref, in_sems, held + i).wait()
        chunk_products(w_ref, c_ref, held + i, 0, b0_ref, b1_ref)
        for t in range(size):
            t_ref[i * size + t] = c_ref[(held + i) * size + t].T
        chunk_copy(t_ref, t_hbm, out_sems, i).start()
        return 0

    lax.fori_loop(0, held, to_held, 0)
    lax.fori_loop(0, out_sems.shape[0], to_rest, 0)
    for i in range(out_sems.shape[0]):
        chunk_copy(t_ref, t_hbm, out_sems, i).wait()


def blocks(same_ref, other_ref, peers, first, count):
    step = 2 * same_ref.shape[0] // peers
    parts = [
        ref[b * step + first : b * step + first + count]
        for ref in (same_ref, other_ref)
        for b in range(peers // 2)
    ]
    return jnp.concatenate(parts, axis=0)


def serve_kernel(
    cap,
    kb,
    qb,
    asked_ref,
    hot_ref,
    mine_ref,
    share_ref,
    s8_ref,
    st4_ref,
    st8a_ref,
    st8b_ref,
):
    hot = hot_ref[...]
    rows4, rows8 = hot.shape[0], s8_ref.shape[0]
    x = iota((rows8, rows4), 0)
    y = iota((rows8, rows4), 1)
    peer, r = x // (4 * cap), x % (4 * cap)
    source = peer * (2 * cap) + cap + r % cap

    def rows_of(kind):
        here = (y == source) & (r // cap == kind)
        return dot(jnp.where(here, 1.0, 0.0).astype(bf16), hot)

    s8_ref[...] = rows_of(0).astype(bf16)
    st4_ref[...] = hot.astype(f32).T[kb : kb + qb].astype(bf16)
    st8a_ref[...] = rows_of(1).T[kb : kb + qb].astype(bf16)
    st8b_ref[...] = rows_of(2).T[kb : kb + qb].astype(bf16)

    peers = rows4 // (2 * cap)
    slots = peers * cap
    wide = peers * slots
    lists = asked_ref[...]
    pick_q = iota((peers, 8 * peers), 1) == 8 * iota((peers, 8 * peers), 0) + 1
    every_q = dot(jnp.where(pick_q, 1.0, 0.0).astype(bf16), lists).astype(bf16)
    tiled = iota((128, wide), 0) == iota((128, wide), 1) % slots
    spread = dot(every_q, jnp.where(tiled, 1.0, 0.0).astype(bf16))
    lane = iota((1, wide), 1)
    here = iota((peers, wide), 0) == lane // slots
    q = jnp.sum(jnp.where(here, spread, 0.0), axis=0, keepdims=True)
    ids = q + (lane % slots // cap * qb).astype(f32)
    row = iota((rows4, 1), 0)
    col = mine_ref[...][:, :1]
    my_ids = col - float(kb) + (row // (2 * cap) * qb).astype(f32)
    my_ids = jnp.where(row % (2 * cap) >= cap, my_ids, -1.0)
    owned = (lax.axis_index("bulk") * qb + iota((qb, 1), 0)).astype(f32)
    wanted = jnp.concatenate([my_ids, owned], axis=0)
    share_ref[...] = jnp.where(ids == wanted, 1.0, 0.0).astype(bf16)


def thermal_of(energy_ref):
    return 1.0 / (jnp.exp(energy_ref[...]) - 1.0)


def put_broadcast(send, served, contributions):
    slots = contributions.shape[0]
    for chip in range(served.shape[0] // 8):
        at = chip * (8 + slots)
        send[at : at + 8] = served[chip * 8 : chip * 8 + 8]
        send[at + 8 : at + 8 + slots] = contributions


def phonon_terms(far, bose, b0_ref, b1_ref):
    gain = far * flat(b0_ref)
    return gain + bose * (gain - (1.0 - far) * flat(b1_ref))


def first_kernel(
    cap,
    same_ref,
    other_ref,
    list_ref,
    f_ref,
    n_ref,
    energy_ref,
    decay_ref,
    pair_ref,
    sk_ref,
    sp_ref,
    b0_ref,
    b1_ref,
    held_ref,
    c_hbm,
    send,
    e_ref,
    f1_ref,
    hot_ref,
    asked_ref,
    w_ref,
    c_ref,
    sems,
    o0,
    o1,
):
    start_chunks(c_hbm, c_ref, sems)
    f, n = f_ref[...], n_ref[...]
    kb, qb = f.shape[0], n.shape[0]
    rows4 = list_ref.shape[0]
    peers = rows4 // (2 * cap)
    got = pick(list_ref[...], jnp.concatenate([same_ref[...], other_ref[...]], axis=0))
    far, bose = gather_pair(pair_ref[...], got)
    contributions = add_rows(sp_ref[...], phonon_terms(far, bose, b0_ref, b1_ref))
    lists = blocks(same_ref, other_ref, peers, kb + qb, 8).astype(bf16)
    asked_ref[...] = lists
    x = iota((rows4, 8 * peers), 0)
    r = x % (2 * cap)
    kind = jnp.where(r < cap, 0, 1)
    at = iota((rows4, 8 * peers), 1) == 8 * block_of(x // (2 * cap), peers) + kind
    asked = dot(jnp.where(at, 1.0, 0.0).astype(bf16), lists)
    r = iota((rows4, 128), 0) % (2 * cap)
    lane = iota((rows4, 128), 1)
    wanted = lane == lax.axis_index("bulk") * cap + r % cap
    col = jnp.sum(jnp.where(wanted, asked, 0.0), axis=1, keepdims=True)
    col = col + jnp.where(r[:, :1] < cap, 0.0, float(kb))
    hot = jnp.where(lane.astype(f32) == col, 1.0, 0.0).astype(bf16)
    hot_ref[...] = hot
    base = n - DT * decay_ref[...] * (n - thermal_of(energy_ref))
    parts = [(held_ref, None, None), (c_ref, c_hbm, sems)]
    rate = electron_rate(sk_ref[...], far, bose, f, parts, w_ref, o0, o1)
    f1 = f + DT * rate
    e_ref[...] = rate
    f1_ref[...] = f1
    put_broadcast(send, pick(hot, padded(f1, base)), contributions)


def middle_kernel(
    cap,
    ends,
    same_ref,
    other_ref,
    share_ref,
    serve_ref,
    f_ref,
    e_ref,
    own_ref,
    n_ref,
    energy_ref,
    decay_ref,
    pair_ref,
    sk_ref,
    sp_ref,
    b0_ref,
    b1_ref,
    held_ref,
    c_hbm,
    send,
    *refs,
):
    w_ref, c_ref, sems, o0, o1 = refs[-5:]
    start_chunks(c_hbm, c_ref, sems)
    rows4 = serve_ref.shape[0]
    peers = rows4 // (2 * cap)
    slots = peers * cap
    x = iota((rows4, 8 * peers), 0)
    source = 8 * block_of(x // (2 * cap), peers) + 2 * cap * my_core() + x % (2 * cap)
    at = jnp.where(iota((rows4, 8 * peers), 1) == source, 1.0, 0.0).astype(bf16)
    heads = blocks(same_ref, other_ref, peers, 0, 8)
    tails = blocks(same_ref, other_ref, peers, 8, slots)
    weight = DT / 2.0 if ends else DT
    both = add_rows(share_ref[...], tails)
    shares, total = both[:rows4], both[rows4:]
    got = pick(at, heads) + weight * shares
    far, bose = gather_pair(pair_ref[...], got)
    terms = phonon_terms(far, bose, b0_ref, b1_ref)
    contributions = add_rows(sp_ref[...], terms)
    n = n_ref[...]
    own = own_ref[...]
    parts = [(held_ref, None, None), (c_ref, c_hbm, sems)]
    if ends:
        n2_ref, e2_ref, f3_ref = refs[:3]
        n2_ref[...] = n + (DT / 2.0) * total
        rate = electron_rate(sk_ref[...], far, bose, own, parts, w_ref, o0, o1)
        f3 = own + DT * rate
        e2_ref[...] = rate
        f3_ref[...] = f3
        send[...] = pick(serve_ref[...], padded(f3)) + contributions
    else:
        base_ref, f2_ref = refs[:2]
        thermal = thermal_of(energy_ref)
        decay = decay_ref[...]
        p0 = total - decay * (n - thermal)
        n1 = n + DT * p0
        base = n + (DT / 2.0) * (p0 - decay * (n1 - thermal))
        base_ref[...] = base
        rate = electron_rate(sk_ref[...], far, bose, own, parts, w_ref, o0, o1)
        f2 = f_ref[...] + (DT / 2.0) * (e_ref[...] + rate)
        f2_ref[...] = f2
        put_broadcast(send, pick(serve_ref[...], padded(f2, base)), contributions)


def backward_kernel(f_ref, gk_ref, c_hbm, b0_ref, b1_ref, w_ref, c_ref, sems):
    start_chunks(c_hbm, c_ref, sems)
    own = add_rows(gk_ref[...], f_ref[...])
    backward_pass(own, c_hbm, c_ref, sems, w_ref, b0_ref, b1_ref)


def phonon_kernel(
    kb,
    recv,
    n_ref,
    energy_ref,
    decay_ref,
    pair_ref,
    st4_ref,
    sp8_ref,
    s8_ref,
    b0_ref,
    b1_ref,
    send,
    p_ref,
    n1_ref,
    far_ref,
):
    n = n_ref[...]
    got = recv[...]
    thermal = thermal_of(energy_ref)
    rate = add_rows(st4_ref[...], got) - decay_ref[...] * (n - thermal)
    n1 = n + DT * rate
    p_ref[...] = rate
    n1_ref[...] = n1
    far = add_rows(pair_ref[:, : got.shape[0]], got)
    far_ref[...] = far
    gain = far * flat(b0_ref)
    both = jnp.concatenate([gain, gain - (1.0 - far) * flat(b1_ref)], axis=0)
    state = padded(jnp.zeros((kb, 128), f32), n1)
    send[...] = pick(s8_ref[...], state) + add_rows(sp8_ref[...], both)


def last_kernel(recv, *refs):
    far_ref, f_ref, f1_ref, e_ref, n_ref, n1_ref, p_ref, energy_ref, decay_ref = refs[:9]
    gp8_ref, sk_ref, st8a_ref, st8b_ref, held_ref, c_hbm = refs[9:15]
    refs = refs[15:]
    f2_ref, n2_ref, w_ref, c_ref, sems, o0, o1 = refs
    start_chunks(c_hbm, c_ref, sems)
    got = recv[...]
    n, n1 = n_ref[...], n1_ref[...]
    bose = add_rows(gp8_ref[...], got)
    thermal = thermal_of(energy_ref)
    p1 = (
        add_rows(st8a_ref[...], got)
        + n1 * add_rows(st8b_ref[...], got)
        - decay_ref[...] * (n1 - thermal)
    )
    n2 = n + (DT / 2.0) * (p_ref[...] + p1)
    n2_ref[...] = n2
    parts = [(held_ref, None, None), (c_ref, c_hbm, sems)]
    rate = electron_rate(sk_ref[...], far_ref[...], bose, f1_ref[...], parts, w_ref, o0, o1)
    f2 = f_ref[...] + (DT / 2.0) * (e_ref[...] + rate)
    f2_ref[...] = f2


def call(kernel, name, outs, scratch=(), spaces=None, out_spaces=None, flops=0, seen=0):
    def run(*args):
        places = dict(spaces or {})
        args = [
            pltpu.with_memory_space_constraint(x, pltpu.HBM)
            if places.get(i) is pltpu.HBM
            else x
            for i, x in enumerate(args)
        ]
        specs = [
            pl.BlockSpec(memory_space=places.get(i, pltpu.VMEM)) for i in range(len(args))
        ]
        return pl.pallas_call(
            kernel,
            out_shape=[
                pltpu.HBM(*o) if (out_spaces or {}).get(i) else jax.ShapeDtypeStruct(*o)
                for i, o in enumerate(outs)
            ],
            in_specs=specs,
            out_specs=[
                pl.BlockSpec(memory_space=(out_spaces or {}).get(i, pltpu.VMEM))
                for i in range(len(outs))
            ],
            scratch_shapes=list(scratch),
            compiler_params=pltpu.CompilerParams(vmem_limit_bytes=VMEM_LIMIT),
            cost_estimate=pl.CostEstimate(
                flops=flops, bytes_accessed=seen, transcendentals=0
            ),
            name=name,
        )(*args)

    return run


def on_device(
    electrons,
    phonons,
    phonon_energy,
    phonon_decay,
    coupling,
    tile_kblock,
    tile_partner,
    tile_qslot,
    tile_count,
    partner_need,
    phonon_need,
):
    devices = lax.axis_size("bulk")
    kb = electrons.shape[0]
    qb = phonons.shape[0]
    tiles = coupling.shape[0]
    cap = partner_need.shape[1] // devices
    assert cap == phonon_need.shape[1] // devices and kb + qb <= 128
    rows4 = devices * 2 * cap
    rows8 = devices * 4 * cap
    groups = tiles // 8
    held = HELD_CHUNKS * (tiles // CHUNKS)
    weights = pltpu.VMEM((groups, 16, 1024), bf16)
    streams = [weights, pltpu.VMEM(coupling.shape, bf16), pltpu.SemaphoreType.DMA((CHUNKS,))]
    rest = (tiles - held, 128, 128)
    rest_sems = pltpu.SemaphoreType.DMA((CHUNKS - HELD_CHUNKS,))
    forward_streams = [weights, pltpu.VMEM(rest, bf16), rest_sems]
    sums = [pltpu.VMEM((groups, 8, 128), f32)] * 2
    pass_out = [((groups, 8, 128), f32)] * 2
    block4 = ((rows4, 128), f32)
    block8 = ((rows8, 128), f32)

    work = dict(flops=2 * tiles * 16 * 128 * 128, seen=tiles * 128 * 128 * 2)

    def exchange(x):
        return lax.all_to_all(x, "bulk", split_axis=0, concat_axis=0, tiled=True)

    ints = ((1, tiles), jnp.int32)
    lists = ((1, partner_need.shape[1]), jnp.int32)
    small = [((kb, 128), f32)] + [((qb, 128), f32)] * 3 + [ints] * 3
    step_rows = kb + qb + 8
    slots = devices * cap
    wide = 8 + slots
    assert step_rows % 8 == 0 and slots % 8 == 0 and slots <= 128
    assert devices % 2 == 0 and cap == 2
    chips = devices // 2
    same_core = [list(range(core, devices, 2)) for core in (0, 1)]

    def to_chips(x):
        return lax.all_to_all(
            x, "bulk", split_axis=0, concat_axis=0, tiled=True, axis_index_groups=same_core
        )

    def between_cores(x):
        return lax.ppermute(x, "bulk", [(i, i ^ 1) for i in range(devices)])

    f, n, energy, decay, kblock, partner, qslot, pneed, qneed, send = call(
        functools.partial(need_kernel, cap),
        "need",
        small + [lists, lists, ((chips * step_rows, 128), f32)],
        [pltpu.SemaphoreType.DMA((9,))],
        spaces={i: pltpu.HBM for i in range(9)},
    )(
        electrons,
        phonons,
        phonon_energy,
        phonon_decay,
        tile_kblock.reshape(1, tiles),
        tile_partner.reshape(1, tiles),
        tile_qslot.reshape(1, tiles),
        partner_need,
        phonon_need,
    )
    same = to_chips(send)
    c_held, c_rest, pair, gp8, gk, sk, sp, sp4, sp8, picks, mine, b0, b1 = call(
        functools.partial(prepare_kernel, cap),
        "prepare",
        [
            ((held, 128, 128), bf16),
            (rest, bf16),
            ((tiles, 2 * rows4), bf16),
            ((tiles, rows8), bf16),
            ((tiles, kb), bf16),
            ((kb, tiles), bf16),
            ((slots, tiles), bf16),
            ((rows4, tiles), bf16),
            ((rows8, 2 * tiles), bf16),
            ((rows4, devices * step_rows), bf16),
            ((rows4, 128), f32),
        ]
        + pass_out,
        [*streams, pltpu.VMEM(rest, bf16), rest_sems],
        spaces={0: pltpu.SMEM, 7: pltpu.HBM},
        out_spaces={1: pltpu.HBM},
        **work,
    )(tile_count, kblock, partner, qslot, f, pneed, qneed, coupling)
    same, c_held, b0 = lax.optimization_barrier((same, c_held, b0))
    other = between_cores(same)
    wide_block = ((chips * wide, 128), f32)
    k_rows, q_rows = ((kb, 128), f32), ((qb, 128), f32)
    forward_scratch = forward_streams + sums
    send, e0, f1, serve, asked = call(
        functools.partial(first_kernel, cap),
        "first",
        [wide_block, k_rows, k_rows, ((rows4, 128), bf16), ((8 * devices, 128), bf16)],
        forward_scratch,
        spaces={13: pltpu.HBM},
        **work,
    )(same, other, picks, f, n, energy, decay, pair, sk, sp, b0, b1, c_held, c_rest)
    share, s8, st4, st8a, st8b = call(
        functools.partial(serve_kernel, cap, kb, qb),
        "serve",
        [
            ((rows4 + qb, devices * slots), bf16),
            ((rows8, 128), bf16),
            ((qb, rows4), bf16),
            ((qb, rows8), bf16),
            ((qb, rows8), bf16),
        ],
    )(asked, serve, mine)
    back = call(backward_kernel, "backward", pass_out, streams, spaces={2: pltpu.HBM}, **work)

    def middle(ends, send, outs, f, e, own, n, contributions):
        same = to_chips(send)
        b0, b1 = back(own, gk, coupling)
        same, b0 = lax.optimization_barrier((same, b0))
        other = between_cores(same)
        return call(
            functools.partial(middle_kernel, cap, ends),
            "middle",
            outs,
            forward_scratch,
            spaces={16: pltpu.HBM},
            **work,
        )(
            same, other, share, serve, f, e, own, n, energy, decay,
            pair, sk, contributions, b0, b1, c_held, c_rest,
        )

    send, base, f2 = middle(False, send, [wide_block, q_rows, k_rows], f, e0, f1, n, sp)
    send, n2, e2, f3 = middle(
        True, send, [block4, q_rows, k_rows, k_rows], f2, e0, f2, base, sp4
    )
    recv = exchange(send)
    b0, b1 = back(f3, gk, coupling)
    send, p2, n3, far = call(
        functools.partial(phonon_kernel, kb),
        "phonon",
        [block8, q_rows, q_rows, ((tiles, 128), f32)],
    )(recv, n2, energy, decay, pair, st4, sp8, s8, b0, b1)
    recv = exchange(send)
    f, n = call(
        last_kernel,
        "last",
        [k_rows, q_rows],
        forward_scratch,
        spaces={15: pltpu.HBM},
        **work,
    )(
        recv, far, f2, f3, e2, n2, n3, p2, energy, decay,
        gp8, sk, st8a, st8b, c_held, c_rest,
    )
    return (f, n)


def solution(mesh):
    placed = (
        P(("groups", "bulk"), None),
        P(("groups", "bulk"), None),
        P("bulk", None),
        P("bulk", None),
        P("bulk", None, None),
        P("bulk"),
        P("bulk"),
        P("bulk"),
        P("bulk"),
        P("bulk", None),
        P("bulk", None),
    )
    return jax.shard_map(
        on_device,
        mesh=mesh,
        in_specs=placed,
        out_specs=(P(("groups", "bulk"), None), P(("groups", "bulk"), None)),
        check_vma=False,
    )
```

```python
import functools

import jax
import jax.numpy as jnp
from jax import lax
from jax.experimental import pallas as pl
from jax.experimental.pallas import tpu as pltpu
from jax.sharding import PartitionSpec as P

DT = 0.05
CHUNKS = 8
HELD_CHUNKS = 2
FETCHED_CHUNKS = 2
f32 = jnp.float32
bf16 = jnp.bfloat16
VMEM_LIMIT = 48 * 1024 * 1024


def iota(shape, dim):
    return lax.broadcasted_iota(jnp.int32, shape, dim)


def dot(a, b):
    return lax.dot_general(a, b, (((1,), (0,)), ((), ())), preferred_element_type=f32)


def split(x):
    hi = x.astype(bf16)
    rest = x - hi.astype(f32)
    mid = rest.astype(bf16)
    lo = (rest - mid.astype(f32)).astype(bf16)
    return hi, mid, lo


def pick(onehot, x):
    hi, mid, lo = split(x)
    both = dot(onehot, jnp.concatenate([hi, mid], axis=1))
    return both[:, :128] + both[:, 128:] + dot(onehot, lo)


def add_rows(onehot, x):
    hi = x.astype(bf16)
    mid = (x - hi.astype(f32)).astype(bf16)
    both = dot(onehot, jnp.concatenate([hi, mid], axis=1))
    return both[:, :128] + both[:, 128:]


def gather_pair(table, x):
    rows = x.shape[0]
    hi = x.astype(bf16)
    mid = (x - hi.astype(f32)).astype(bf16)
    blank = jnp.zeros((rows, 128), bf16)

    def both(part):
        upper = jnp.concatenate([part, blank], axis=1)
        lower = jnp.concatenate([blank, part], axis=1)
        return dot(table, jnp.concatenate([upper, lower], axis=0))

    res = both(hi) + both(mid)
    return res[:, :128], res[:, 128:]


def stacked(first, second):
    tiles = first.shape[0]
    return jnp.concatenate(
        [first.reshape(tiles // 8, 8, 128), second.reshape(tiles // 8, 8, 128)], axis=1
    ).astype(bf16)


def row_is(r):
    return iota((16, 128), 0) % 8 == r


def padded(*parts):
    rows = sum(p.shape[0] for p in parts)
    return jnp.concatenate([*parts, jnp.zeros((128 - rows, 128), f32)], axis=0)


def flat(ref):
    return ref[...].reshape(-1, 128)


def chunk_copy(src, dst, sems, i, skip=0):
    size = dst.shape[0] // sems.shape[0]
    return pltpu.make_async_copy(
        src.at[pl.ds(skip + i * size, size)], dst.at[pl.ds(i * size, size)], sems.at[i]
    )


def start_chunks(src, dst, sems, skip=0):
    for i in range(sems.shape[0]):
        chunk_copy(src, dst, sems, i, skip).start()


def start(copies):
    for copy in copies:
        copy.start()


def block_diagonal(w):
    w = w.astype(f32)
    return jnp.concatenate(
        [jnp.where(row_is(r), w, 0.0).astype(bf16) for r in range(8)], axis=1
    )


def left_sides(first, second, w_ref):
    w = stacked(first, second)
    for g in range(w.shape[0]):
        w_ref[g] = block_diagonal(w[g])


def chunk_products(w_ref, c_ref, i, base, out0, out1):
    size = w_ref.shape[0] // CHUNKS
    for k in range(size):
        g = i * size + k
        res = dot(w_ref[base + g], c_ref[pl.ds(g * 8, 8)].reshape(1024, 128))
        out0[base + g] = res[:8]
        out1[base + g] = res[8:]


def tile_products(w_ref, parts, out0, out1, after=None, carry=0):
    size = w_ref.shape[0] // CHUNKS
    base = 0
    for c_ref, c_hbm, sems in parts:
        groups = c_ref.shape[0] // 8

        def chunk(i, carry):
            if c_hbm is not None:
                chunk_copy(c_hbm, c_ref, sems, i).wait()
            chunk_products(w_ref, c_ref, i, base, out0, out1)
            return after(base // size + i, carry) if after else carry

        carry = lax.fori_loop(0, groups // size, chunk, carry)
        base += groups
    return carry


def backward_pass(own, c_hbm, c_ref, sems, w_ref, out0, out1):
    left_sides(1.0 - own, own, w_ref)
    tile_products(w_ref, [(c_ref, c_hbm, sems)], out0, out1)


def electron_rate(sum_k_ref, far, bose, f, parts, w_ref, o0, o1):
    left_sides(far * (1.0 + bose), far + bose, w_ref)
    size = w_ref.shape[0] // CHUNKS

    def after(i, totals):
        sums = sum_k_ref[i]
        return tuple(
            total + add_rows(sums, out[pl.ds(i * size, size)].reshape(-1, 128))
            for total, out in zip(totals, (o0, o1))
        )

    nothing = jnp.zeros_like(f)
    gain, loss = tile_products(w_ref, parts, o0, o1, after, (nothing, nothing))
    return gain - f * loss


def my_core():
    return lax.rem(lax.axis_index("bulk"), 2)


def block_of(peer, peers):
    return peer // 2 + jnp.where(peer % 2 == my_core(), 0, peers // 2)


def need_kernel(cap, *refs):
    ins, outs = refs[:9], refs[9:]
    *small, pneed_ref, qneed_ref, send_ref, sems = outs
    copies = [
        pltpu.make_async_copy(src, dst, sems.at[i])
        for i, (src, dst) in enumerate(zip(ins, [*small, pneed_ref, qneed_ref]))
    ]
    start(copies)
    slots = pneed_ref.shape[1]
    step = send_ref.shape[0] // (slots // cap // 2)
    for copy in copies:
        copy.wait()
    f, n = small[0][...], small[1][...]
    own_p, own_q = pneed_ref[...].astype(f32), qneed_ref[...].astype(f32)
    row = iota((8, slots), 0)
    lists = jnp.where(row == 0, own_p, jnp.where(row == 1, own_q, 0.0))
    if slots < 128:
        lists = jnp.concatenate([lists, jnp.zeros((8, 128 - slots), f32)], axis=1)
    block = jnp.concatenate([f, n, lists], axis=0)
    for chip in range(slots // cap // 2):
        send_ref[chip * step : (chip + 1) * step] = block


def prepare_kernel(
    cap,
    count_ref,
    kblock_ref,
    partner_ref,
    qslot_ref,
    f_ref,
    pneed_ref,
    qneed_ref,
    c_hbm,
    held_ref,
    t_hbm,
    pair_ref,
    gp8_ref,
    gk_ref,
    sk_ref,
    sp_ref,
    sp4_ref,
    sp8_ref,
    list_ref,
    mine_ref,
    b0_ref,
    b1_ref,
    w_ref,
    c_ref,
    in_sems,
    t_ref,
    out_sems,
):
    start_chunks(c_hbm, c_ref, in_sems)
    tiles = kblock_ref.shape[1]
    kb = f_ref.shape[0]
    used = iota((1, tiles), 1) < count_ref[0]
    k = kblock_ref[...]
    e = partner_ref[...]
    q = qslot_ref[...]
    rows4 = sp4_ref.shape[0]
    rows8 = sp8_ref.shape[0]
    ind = lambda m: jnp.where(m, 1.0, 0.0)
    k_hot = ind(iota((kb, tiles), 0) == k)
    gk_ref[...] = k_hot.T.astype(bf16)
    own = add_rows(gk_ref[...], f_ref[...])
    left_sides(1.0 - own, own, w_ref)
    sums = jnp.where(used, k_hot, 0.0)
    width = tiles // CHUNKS
    for i in range(CHUNKS):
        sk_ref[i] = sums[:, i * width : (i + 1) * width].astype(bf16)
    x = iota((rows4, tiles), 0)
    row_e = (e // cap) * (2 * cap) + e % cap
    row_p = (q // cap) * (2 * cap) + cap + q % cap
    p_hot = ind(x == row_p)
    pair_ref[...] = jnp.concatenate([ind(x == row_e), p_hot], axis=0).T.astype(bf16)
    sp4_ref[...] = jnp.where(used, p_hot, 0.0).astype(bf16)
    sp_ref[...] = jnp.where(used, ind(iota(sp_ref.shape, 0) == q), 0.0).astype(bf16)
    x = iota((rows8, tiles), 0)
    row_z = (q // cap) * (4 * cap) + q % cap
    gp8_ref[...] = ind(x == row_z).T.astype(bf16)
    sp8_ref[...] = jnp.concatenate(
        [
            jnp.where(used, ind(x == row_z + cap), 0.0),
            jnp.where(used, ind(x == row_z + 2 * cap), 0.0),
        ],
        axis=1,
    ).astype(bf16)

    rows, sent = list_ref.shape
    slots = pneed_ref.shape[1]
    peers = slots // cap
    x = iota((rows, slots), 0)
    y = iota((rows, slots), 1)
    peer, r = x // (2 * cap), x % (2 * cap)
    e_here = (r < cap) & (y == peer * cap + r)
    p_here = (r >= cap) & (y == peer * cap + r - cap)
    pn = jnp.broadcast_to(pneed_ref[...].astype(f32), (rows, slots))
    qn = jnp.broadcast_to(qneed_ref[...].astype(f32), (rows, slots)) + float(kb)
    col = jnp.sum(jnp.where(e_here, pn, 0.0) + jnp.where(p_here, qn, 0.0), axis=1, keepdims=True)
    mine_ref[...] = jnp.broadcast_to(col, (rows, 128))
    start_of = block_of(iota((rows, 1), 0) // (2 * cap), peers) * (sent // peers)
    list_ref[...] = jnp.where(
        iota((rows, sent), 1).astype(f32) == col + start_of.astype(f32), 1.0, 0.0
    ).astype(bf16)

    size = c_ref.shape[0] // CHUNKS
    held = held_ref.shape[0] // size

    def to_held(i, _):
        chunk_copy(c_hbm, c_ref, in_sems, i).wait()
        chunk_products(w_ref, c_ref, i, 0, b0_ref, b1_ref)
        for t in range(size):
            held_ref[i * size + t] = c_ref[i * size + t].T
        return 0

    def to_rest(i, _):
        chunk_copy(c_hbm, c_ref, in_sems, held + i).wait()
        chunk_products(w_ref, c_ref, held + i, 0, b0_ref, b1_ref)
        for t in range(size):
            t_ref[i * size + t] = c_ref[(held + i) * size + t].T
        chunk_copy(t_ref, t_hbm, out_sems, i).start()
        return 0

    lax.fori_loop(0, held, to_held, 0)
    lax.fori_loop(0, out_sems.shape[0], to_rest, 0)
    for i in range(out_sems.shape[0]):
        chunk_copy(t_ref, t_hbm, out_sems, i).wait()


def blocks(same_ref, other_ref, peers, first, count):
    step = 2 * same_ref.shape[0] // peers
    parts = [
        ref[b * step + first : b * step + first + count]
        for ref in (same_ref, other_ref)
        for b in range(peers // 2)
    ]
    return jnp.concatenate(parts, axis=0)


def serve_kernel(
    cap,
    kb,
    qb,
    asked_ref,
    hot_ref,
    mine_ref,
    share_ref,
    s8_ref,
    st4_ref,
    st8a_ref,
    st8b_ref,
):
    hot = hot_ref[...]
    rows4, rows8 = hot.shape[0], s8_ref.shape[0]
    x = iota((rows8, rows4), 0)
    y = iota((rows8, rows4), 1)
    peer, r = x // (4 * cap), x % (4 * cap)
    source = peer * (2 * cap) + cap + r % cap

    def rows_of(kind):
        here = (y == source) & (r // cap == kind)
        return dot(jnp.where(here, 1.0, 0.0).astype(bf16), hot)

    s8_ref[...] = rows_of(0).astype(bf16)
    st4_ref[...] = hot.astype(f32).T[kb : kb + qb].astype(bf16)
    st8a_ref[...] = rows_of(1).T[kb : kb + qb].astype(bf16)
    st8b_ref[...] = rows_of(2).T[kb : kb + qb].astype(bf16)

    peers = rows4 // (2 * cap)
    slots = peers * cap
    wide = peers * slots
    lists = asked_ref[...]
    pick_q = iota((peers, 8 * peers), 1) == 8 * iota((peers, 8 * peers), 0) + 1
    every_q = dot(jnp.where(pick_q, 1.0, 0.0).astype(bf16), lists).astype(bf16)
    tiled = iota((128, wide), 0) == iota((128, wide), 1) % slots
    spread = dot(every_q, jnp.where(tiled, 1.0, 0.0).astype(bf16))
    lane = iota((1, wide), 1)
    here = iota((peers, wide), 0) == lane // slots
    q = jnp.sum(jnp.where(here, spread, 0.0), axis=0, keepdims=True)
    ids = q + (lane % slots // cap * qb).astype(f32)
    row = iota((rows4, 1), 0)
    col = mine_ref[...][:, :1]
    my_ids = col - float(kb) + (row // (2 * cap) * qb).astype(f32)
    my_ids = jnp.where(row % (2 * cap) >= cap, my_ids, -1.0)
    owned = (lax.axis_index("bulk") * qb + iota((qb, 1), 0)).astype(f32)
    wanted = jnp.concatenate([my_ids, owned], axis=0)
    share_ref[...] = jnp.where(ids == wanted, 1.0, 0.0).astype(bf16)


def thermal_of(energy_ref):
    return 1.0 / (jnp.exp(energy_ref[...]) - 1.0)


def put_broadcast(send, served, contributions):
    slots = contributions.shape[0]
    for chip in range(served.shape[0] // 8):
        at = chip * (8 + slots)
        send[at : at + 8] = served[chip * 8 : chip * 8 + 8]
        send[at + 8 : at + 8 + slots] = contributions


def phonon_terms(far, bose, b0_ref, b1_ref):
    gain = far * flat(b0_ref)
    return gain + bose * (gain - (1.0 - far) * flat(b1_ref))


def first_kernel(
    cap,
    same_ref,
    other_ref,
    list_ref,
    f_ref,
    n_ref,
    energy_ref,
    decay_ref,
    pair_ref,
    sk_ref,
    sp_ref,
    b0_ref,
    b1_ref,
    held_ref,
    fetched_ref,
    c_hbm,
    send,
    e_ref,
    f1_ref,
    hot_ref,
    asked_ref,
    w_ref,
    c_ref,
    sems,
    o0,
    o1,
):
    start_chunks(c_hbm, c_ref, sems, fetched_ref.shape[0])
    f, n = f_ref[...], n_ref[...]
    kb, qb = f.shape[0], n.shape[0]
    rows4 = list_ref.shape[0]
    peers = rows4 // (2 * cap)
    got = add_rows(list_ref[...], jnp.concatenate([same_ref[...], other_ref[...]], axis=0))
    far, bose = gather_pair(pair_ref[...], got)
    contributions = add_rows(sp_ref[...], phonon_terms(far, bose, b0_ref, b1_ref))
    lists = blocks(same_ref, other_ref, peers, kb + qb, 8).astype(bf16)
    asked_ref[...] = lists
    x = iota((rows4, 8 * peers), 0)
    r = x % (2 * cap)
    kind = jnp.where(r < cap, 0, 1)
    at = iota((rows4, 8 * peers), 1) == 8 * block_of(x // (2 * cap), peers) + kind
    asked = dot(jnp.where(at, 1.0, 0.0).astype(bf16), lists)
    r = iota((rows4, 128), 0) % (2 * cap)
    lane = iota((rows4, 128), 1)
    wanted = lane == lax.axis_index("bulk") * cap + r % cap
    col = jnp.sum(jnp.where(wanted, asked, 0.0), axis=1, keepdims=True)
    col = col + jnp.where(r[:, :1] < cap, 0.0, float(kb))
    hot = jnp.where(lane.astype(f32) == col, 1.0, 0.0).astype(bf16)
    hot_ref[...] = hot
    base = n - DT * decay_ref[...] * (n - thermal_of(energy_ref))
    parts = [(held_ref, None, None), (fetched_ref, None, None), (c_ref, c_hbm, sems)]
    rate = electron_rate(sk_ref, far, bose, f, parts, w_ref, o0, o1)
    f1 = f + DT * rate
    e_ref[...] = rate
    f1_ref[...] = f1
    put_broadcast(send, pick(hot, padded(f1, base)), contributions)


def middle_kernel(
    cap,
    ends,
    same_ref,
    other_ref,
    share_ref,
    serve_ref,
    f_ref,
    e_ref,
    own_ref,
    n_ref,
    energy_ref,
    decay_ref,
    pair_ref,
    sk_ref,
    sp_ref,
    b0_ref,
    b1_ref,
    held_ref,
    fetched_ref,
    c_hbm,
    send,
    *refs,
):
    w_ref, c_ref, sems, o0, o1 = refs[-5:]
    start_chunks(c_hbm, c_ref, sems, fetched_ref.shape[0])
    rows4 = serve_ref.shape[0]
    peers = rows4 // (2 * cap)
    slots = peers * cap
    x = iota((rows4, 8 * peers), 0)
    source = 8 * block_of(x // (2 * cap), peers) + 2 * cap * my_core() + x % (2 * cap)
    at = jnp.where(iota((rows4, 8 * peers), 1) == source, 1.0, 0.0).astype(bf16)
    heads = blocks(same_ref, other_ref, peers, 0, 8)
    tails = blocks(same_ref, other_ref, peers, 8, slots)
    weight = DT / 2.0 if ends else DT
    both = add_rows(share_ref[...], tails)
    shares, total = both[:rows4], both[rows4:]
    got = add_rows(at, heads) + weight * shares
    far, bose = gather_pair(pair_ref[...], got)
    terms = phonon_terms(far, bose, b0_ref, b1_ref)
    contributions = add_rows(sp_ref[...], terms)
    n = n_ref[...]
    own = own_ref[...]
    parts = [(held_ref, None, None), (fetched_ref, None, None), (c_ref, c_hbm, sems)]
    if ends:
        n2_ref, e2_ref, f3_ref = refs[:3]
        n2_ref[...] = n + (DT / 2.0) * total
        rate = electron_rate(sk_ref, far, bose, own, parts, w_ref, o0, o1)
        f3 = own + DT * rate
        e2_ref[...] = rate
        f3_ref[...] = f3
        send[...] = pick(serve_ref[...], padded(f3)) + contributions
    else:
        base_ref, f2_ref = refs[:2]
        thermal = thermal_of(energy_ref)
        decay = decay_ref[...]
        p0 = total - decay * (n - thermal)
        n1 = n + DT * p0
        base = n + (DT / 2.0) * (p0 - decay * (n1 - thermal))
        base_ref[...] = base
        rate = electron_rate(sk_ref, far, bose, own, parts, w_ref, o0, o1)
        f2 = f_ref[...] + (DT / 2.0) * (e_ref[...] + rate)
        f2_ref[...] = f2
        put_broadcast(send, pick(serve_ref[...], padded(f2, base)), contributions)


def backward_kernel(f_ref, gk_ref, c_hbm, b0_ref, b1_ref, w_ref, c_ref, sems):
    start_chunks(c_hbm, c_ref, sems)
    own = add_rows(gk_ref[...], f_ref[...])
    backward_pass(own, c_hbm, c_ref, sems, w_ref, b0_ref, b1_ref)


def fetch_kernel(after_ref, c_hbm, fetched_ref, sems):
    start_chunks(c_hbm, fetched_ref, sems)
    for i in range(sems.shape[0]):
        chunk_copy(c_hbm, fetched_ref, sems, i).wait()


def phonon_kernel(
    kb,
    recv,
    n_ref,
    energy_ref,
    decay_ref,
    pair_ref,
    st4_ref,
    sp8_ref,
    s8_ref,
    b0_ref,
    b1_ref,
    send,
    p_ref,
    n1_ref,
    far_ref,
):
    n = n_ref[...]
    got = recv[...]
    thermal = thermal_of(energy_ref)
    rate = add_rows(st4_ref[...], got) - decay_ref[...] * (n - thermal)
    n1 = n + DT * rate
    p_ref[...] = rate
    n1_ref[...] = n1
    far = add_rows(pair_ref[:, : got.shape[0]], got)
    far_ref[...] = far
    gain = far * flat(b0_ref)
    both = jnp.concatenate([gain, gain - (1.0 - far) * flat(b1_ref)], axis=0)
    state = padded(jnp.zeros((kb, 128), f32), n1)
    send[...] = pick(s8_ref[...], state) + add_rows(sp8_ref[...], both)


def last_kernel(recv, *refs):
    far_ref, f_ref, f1_ref, e_ref, n_ref, n1_ref, p_ref, energy_ref, decay_ref = refs[:9]
    gp8_ref, sk_ref, st8a_ref, st8b_ref, held_ref, c_hbm = refs[9:15]
    refs = refs[15:]
    f2_ref, n2_ref, w_ref, c_ref, sems, o0, o1 = refs
    start_chunks(c_hbm, c_ref, sems)
    got = recv[...]
    n, n1 = n_ref[...], n1_ref[...]
    bose = add_rows(gp8_ref[...], got)
    thermal = thermal_of(energy_ref)
    p1 = (
        add_rows(st8a_ref[...], got)
        + n1 * add_rows(st8b_ref[...], got)
        - decay_ref[...] * (n1 - thermal)
    )
    n2 = n + (DT / 2.0) * (p_ref[...] + p1)
    n2_ref[...] = n2
    parts = [(held_ref, None, None), (c_ref, c_hbm, sems)]
    rate = electron_rate(sk_ref, far_ref[...], bose, f1_ref[...], parts, w_ref, o0, o1)
    f2 = f_ref[...] + (DT / 2.0) * (e_ref[...] + rate)
    f2_ref[...] = f2


def call(kernel, name, outs, scratch=(), spaces=None, out_spaces=None, flops=0, seen=0):
    def run(*args):
        places = dict(spaces or {})
        args = [
            pltpu.with_memory_space_constraint(x, pltpu.HBM)
            if places.get(i) is pltpu.HBM
            else x
            for i, x in enumerate(args)
        ]
        specs = [
            pl.BlockSpec(memory_space=places.get(i, pltpu.VMEM)) for i in range(len(args))
        ]
        return pl.pallas_call(
            kernel,
            out_shape=[
                (out_spaces or {}).get(i, jax.ShapeDtypeStruct)(*o) for i, o in enumerate(outs)
            ],
            in_specs=specs,
            out_specs=[
                pl.BlockSpec(memory_space=(out_spaces or {}).get(i, pltpu.VMEM))
                for i in range(len(outs))
            ],
            scratch_shapes=list(scratch),
            compiler_params=pltpu.CompilerParams(vmem_limit_bytes=VMEM_LIMIT),
            cost_estimate=pl.CostEstimate(
                flops=flops, bytes_accessed=seen, transcendentals=0
            ),
            name=name,
        )(*args)

    return run


def on_device(
    electrons,
    phonons,
    phonon_energy,
    phonon_decay,
    coupling,
    tile_kblock,
    tile_partner,
    tile_qslot,
    tile_count,
    partner_need,
    phonon_need,
):
    devices = lax.axis_size("bulk")
    kb = electrons.shape[0]
    qb = phonons.shape[0]
    tiles = coupling.shape[0]
    cap = partner_need.shape[1] // devices
    assert cap == phonon_need.shape[1] // devices and kb + qb <= 128
    rows4 = devices * 2 * cap
    rows8 = devices * 4 * cap
    groups = tiles // 8
    held = HELD_CHUNKS * (tiles // CHUNKS)
    weights = pltpu.VMEM((groups, 16, 1024), bf16)
    streams = [weights, pltpu.VMEM(coupling.shape, bf16), pltpu.SemaphoreType.DMA((CHUNKS,))]
    rest = (tiles - held, 128, 128)
    rest_sems = pltpu.SemaphoreType.DMA((CHUNKS - HELD_CHUNKS,))
    forward_streams = [weights, pltpu.VMEM(rest, bf16), rest_sems]
    fetched = (FETCHED_CHUNKS * (tiles // CHUNKS), 128, 128)
    short = (rest[0] - fetched[0], 128, 128)
    short_sems = pltpu.SemaphoreType.DMA((CHUNKS - HELD_CHUNKS - FETCHED_CHUNKS,))
    sums = [pltpu.VMEM((groups, 8, 128), f32)] * 2
    pass_out = [((groups, 8, 128), f32)] * 2
    block4 = ((rows4, 128), f32)
    block8 = ((rows8, 128), f32)

    work = dict(flops=2 * tiles * 16 * 128 * 128, seen=tiles * 128 * 128 * 2)

    def exchange(x):
        return lax.all_to_all(x, "bulk", split_axis=0, concat_axis=0, tiled=True)

    ints = ((1, tiles), jnp.int32)
    lists = ((1, partner_need.shape[1]), jnp.int32)
    small = [((kb, 128), f32)] + [((qb, 128), f32)] * 3 + [ints] * 3
    step_rows = kb + qb + 8
    slots = devices * cap
    wide = 8 + slots
    assert step_rows % 8 == 0 and slots % 8 == 0 and slots <= 128
    assert devices % 2 == 0 and cap == 2
    chips = devices // 2
    same_core = [list(range(core, devices, 2)) for core in (0, 1)]

    def to_chips(x):
        return lax.all_to_all(
            x, "bulk", split_axis=0, concat_axis=0, tiled=True, axis_index_groups=same_core
        )

    def between_cores(x):
        return lax.ppermute(x, "bulk", [(i, i ^ 1) for i in range(devices)])

    f, n, energy, decay, kblock, partner, qslot, pneed, qneed, send = call(
        functools.partial(need_kernel, cap),
        "need",
        small + [lists, lists, ((chips * step_rows, 128), f32)],
        [pltpu.SemaphoreType.DMA((9,))],
        spaces={i: pltpu.HBM for i in range(9)},
    )(
        electrons,
        phonons,
        phonon_energy,
        phonon_decay,
        tile_kblock.reshape(1, tiles),
        tile_partner.reshape(1, tiles),
        tile_qslot.reshape(1, tiles),
        partner_need,
        phonon_need,
    )
    same = to_chips(send)
    c_held, c_rest, pair, gp8, gk, sk, sp, sp4, sp8, picks, mine, b0, b1 = call(
        functools.partial(prepare_kernel, cap),
        "prepare",
        [
            ((held, 128, 128), bf16),
            (rest, bf16),
            ((tiles, 2 * rows4), bf16),
            ((tiles, rows8), bf16),
            ((tiles, kb), bf16),
            ((CHUNKS, kb, tiles // CHUNKS), bf16),
            ((slots, tiles), bf16),
            ((rows4, tiles), bf16),
            ((rows8, 2 * tiles), bf16),
            ((rows4, devices * step_rows), bf16),
            ((rows4, 128), f32),
        ]
        + pass_out,
        [*streams, pltpu.VMEM(rest, bf16), rest_sems],
        spaces={0: pltpu.SMEM, 7: pltpu.HBM},
        out_spaces={1: pltpu.HBM},
        **work,
    )(tile_count, kblock, partner, qslot, f, pneed, qneed, coupling)
    same, c_held, b0 = lax.optimization_barrier((same, c_held, b0))
    wide_block = ((chips * wide, 128), f32)
    k_rows, q_rows = ((kb, 128), f32), ((qb, 128), f32)
    forward_scratch = [weights, pltpu.VMEM(short, bf16), short_sems] + sums

    def fetch(after):
        return call(
            fetch_kernel,
            "fetch",
            [(fetched, bf16)],
            [pltpu.SemaphoreType.DMA((FETCHED_CHUNKS,))],
            spaces={0: pl.ANY, 1: pltpu.HBM},
            out_spaces={0: pltpu.VMEM},
            seen=fetched[0] * 128 * 128 * 2,
        )(after, c_rest)[0]

    other = between_cores(same)
    c_fetched = fetch(same)
    send, e0, f1, serve, asked = call(
        functools.partial(first_kernel, cap),
        "first",
        [wide_block, k_rows, k_rows, ((rows4, 128), bf16), ((8 * devices, 128), bf16)],
        forward_scratch,
        spaces={14: pltpu.HBM},
        **work,
    )(same, other, picks, f, n, energy, decay, pair, sk, sp, b0, b1, c_held, c_fetched, c_rest)
    share, s8, st4, st8a, st8b = call(
        functools.partial(serve_kernel, cap, kb, qb),
        "serve",
        [
            ((rows4 + qb, devices * slots), bf16),
            ((rows8, 128), bf16),
            ((qb, rows4), bf16),
            ((qb, rows8), bf16),
            ((qb, rows8), bf16),
        ],
    )(asked, serve, mine)
    back = call(backward_kernel, "backward", pass_out, streams, spaces={2: pltpu.HBM}, **work)

    def middle(ends, send, outs, f, e, own, n, contributions):
        same = to_chips(send)
        b0, b1 = back(own, gk, coupling)
        same, b0 = lax.optimization_barrier((same, b0))
        other = between_cores(same)
        c_fetched = fetch(same)
        return call(
            functools.partial(middle_kernel, cap, ends),
            "middle",
            outs,
            forward_scratch,
            spaces={17: pltpu.HBM},
            **work,
        )(
            same, other, share, serve, f, e, own, n, energy, decay,
            pair, sk, contributions, b0, b1, c_held, c_fetched, c_rest,
        )

    send, base, f2 = middle(False, send, [wide_block, q_rows, k_rows], f, e0, f1, n, sp)
    send, n2, e2, f3 = middle(
        True, send, [block4, q_rows, k_rows, k_rows], f2, e0, f2, base, sp4
    )
    recv = exchange(send)
    b0, b1 = back(f3, gk, coupling)
    send, p2, n3, far = call(
        functools.partial(phonon_kernel, kb),
        "phonon",
        [block8, q_rows, q_rows, ((tiles, 128), f32)],
    )(recv, n2, energy, decay, pair, st4, sp8, s8, b0, b1)
    recv = exchange(send)
    f, n = call(
        last_kernel,
        "last",
        [k_rows, q_rows],
        forward_streams + sums,
        spaces={15: pltpu.HBM},
        **work,
    )(
        recv, far, f2, f3, e2, n2, n3, p2, energy, decay,
        gp8, sk, st8a, st8b, c_held, c_rest,
    )
    return (f, n)


def solution(mesh):
    placed = (
        P(("groups", "bulk"), None),
        P(("groups", "bulk"), None),
        P("bulk", None),
        P("bulk", None),
        P("bulk", None, None),
        P("bulk"),
        P("bulk"),
        P("bulk"),
        P("bulk"),
        P("bulk", None),
        P("bulk", None),
    )
    return jax.shard_map(
        on_device,
        mesh=mesh,
        in_specs=placed,
        out_specs=(P(("groups", "bulk"), None), P(("groups", "bulk"), None)),
        check_vma=False,
    )
```

```python
import functools

import jax
import jax.numpy as jnp
from jax import lax
from jax.experimental import pallas as pl
from jax.experimental.pallas import tpu as pltpu
from jax.sharding import PartitionSpec as P

DT = 0.05
CHUNKS = 8
HELD_CHUNKS = 2
FETCHED_CHUNKS = 2
f32 = jnp.float32
bf16 = jnp.bfloat16
VMEM_LIMIT = 48 * 1024 * 1024


def iota(shape, dim):
    return lax.broadcasted_iota(jnp.int32, shape, dim)


def dot(a, b):
    return lax.dot_general(a, b, (((1,), (0,)), ((), ())), preferred_element_type=f32)


def split(x):
    hi = x.astype(bf16)
    rest = x - hi.astype(f32)
    mid = rest.astype(bf16)
    lo = (rest - mid.astype(f32)).astype(bf16)
    return hi, mid, lo


def pick(onehot, x):
    hi, mid, lo = split(x)
    both = dot(onehot, jnp.concatenate([hi, mid], axis=1))
    return both[:, :128] + both[:, 128:] + dot(onehot, lo)


def add_rows(onehot, x):
    hi = x.astype(bf16)
    mid = (x - hi.astype(f32)).astype(bf16)
    both = dot(onehot, jnp.concatenate([hi, mid], axis=1))
    return both[:, :128] + both[:, 128:]


def gather_pair(table, x):
    rows = x.shape[0]
    hi = x.astype(bf16)
    mid = (x - hi.astype(f32)).astype(bf16)
    blank = jnp.zeros((rows, 128), bf16)

    def both(part):
        upper = jnp.concatenate([part, blank], axis=1)
        lower = jnp.concatenate([blank, part], axis=1)
        return dot(table, jnp.concatenate([upper, lower], axis=0))

    res = both(hi) + both(mid)
    return res[:, :128], res[:, 128:]


def stacked(first, second):
    tiles = first.shape[0]
    return jnp.concatenate(
        [first.reshape(tiles // 8, 8, 128), second.reshape(tiles // 8, 8, 128)], axis=1
    ).astype(bf16)


def row_is(r):
    return iota((16, 128), 0) % 8 == r


def padded(*parts):
    rows = sum(p.shape[0] for p in parts)
    return jnp.concatenate([*parts, jnp.zeros((128 - rows, 128), f32)], axis=0)


def flat(ref):
    return ref[...].reshape(-1, 128)


def chunk_copy(src, dst, sems, i, skip=0):
    size = dst.shape[0] // sems.shape[0]
    return pltpu.make_async_copy(
        src.at[pl.ds(skip + i * size, size)], dst.at[pl.ds(i * size, size)], sems.at[i]
    )


def start_chunks(src, dst, sems, skip=0):
    for i in range(sems.shape[0]):
        chunk_copy(src, dst, sems, i, skip).start()


def start(copies):
    for copy in copies:
        copy.start()


def block_diagonal(w):
    w = w.astype(f32)
    return jnp.concatenate(
        [jnp.where(row_is(r), w, 0.0).astype(bf16) for r in range(8)], axis=1
    )


def left_sides(first, second, w_ref):
    w = stacked(first, second)
    for g in range(w.shape[0]):
        w_ref[g] = block_diagonal(w[g])


def chunk_products(w_ref, c_ref, i, base, out0, out1):
    size = w_ref.shape[0] // CHUNKS
    for k in range(size):
        g = i * size + k
        res = dot(w_ref[base + g], c_ref[pl.ds(g * 8, 8)].reshape(1024, 128))
        out0[base + g] = res[:8]
        out1[base + g] = res[8:]


def tile_products(w_ref, parts, out0, out1):
    size = w_ref.shape[0] // CHUNKS
    base = 0
    for c_ref, c_hbm, sems in parts:
        chunks = c_ref.shape[0] // 8 // size

        def chunk(i, _):
            if c_hbm is not None:
                chunk_copy(c_hbm, c_ref, sems, i).wait()
            chunk_products(w_ref, c_ref, i, base, out0, out1)
            return 0

        lax.fori_loop(0, chunks, chunk, 0, unroll=1 if c_hbm is not None else 2)
        base += chunks * size


def backward_pass(own, c_hbm, c_ref, sems, w_ref, out0, out1):
    left_sides(1.0 - own, own, w_ref)
    tile_products(w_ref, [(c_ref, c_hbm, sems)], out0, out1)


def electron_rate(sum_k, far, bose, f, parts, w_ref, o0, o1):
    left_sides(far * (1.0 + bose), far + bose, w_ref)
    tile_products(w_ref, parts, o0, o1)
    return add_rows(sum_k, flat(o0)) - f * add_rows(sum_k, flat(o1))


def my_core():
    return lax.rem(lax.axis_index("bulk"), 2)


def block_of(peer, peers):
    return peer // 2 + jnp.where(peer % 2 == my_core(), 0, peers // 2)


def need_kernel(cap, *refs):
    ins, outs = refs[:9], refs[9:]
    *small, pneed_ref, qneed_ref, send_ref, sems = outs
    copies = [
        pltpu.make_async_copy(src, dst, sems.at[i])
        for i, (src, dst) in enumerate(zip(ins, [*small, pneed_ref, qneed_ref]))
    ]
    start(copies)
    slots = pneed_ref.shape[1]
    step = send_ref.shape[0] // (slots // cap // 2)
    for copy in copies:
        copy.wait()
    f, n = small[0][...], small[1][...]
    own_p, own_q = pneed_ref[...].astype(f32), qneed_ref[...].astype(f32)
    row = iota((8, slots), 0)
    lists = jnp.where(row == 0, own_p, jnp.where(row == 1, own_q, 0.0))
    if slots < 128:
        lists = jnp.concatenate([lists, jnp.zeros((8, 128 - slots), f32)], axis=1)
    block = jnp.concatenate([f, n, lists], axis=0)
    for chip in range(slots // cap // 2):
        send_ref[chip * step : (chip + 1) * step] = block


def prepare_kernel(
    cap,
    count_ref,
    kblock_ref,
    partner_ref,
    qslot_ref,
    f_ref,
    pneed_ref,
    qneed_ref,
    c_hbm,
    held_ref,
    t_hbm,
    pair_ref,
    gp8_ref,
    gk_ref,
    sk_ref,
    sp_ref,
    sp4_ref,
    sp8_ref,
    list_ref,
    mine_ref,
    b0_ref,
    b1_ref,
    w_ref,
    c_ref,
    in_sems,
    t_ref,
    out_sems,
):
    start_chunks(c_hbm, c_ref, in_sems)
    tiles = kblock_ref.shape[1]
    kb = f_ref.shape[0]
    used = iota((1, tiles), 1) < count_ref[0]
    k = kblock_ref[...]
    e = partner_ref[...]
    q = qslot_ref[...]
    rows4 = sp4_ref.shape[0]
    rows8 = sp8_ref.shape[0]
    ind = lambda m: jnp.where(m, 1.0, 0.0)
    k_hot = ind(iota((kb, tiles), 0) == k)
    gk_ref[...] = k_hot.T.astype(bf16)
    own = add_rows(gk_ref[...], f_ref[...])
    left_sides(1.0 - own, own, w_ref)
    sk_ref[...] = jnp.where(used, k_hot, 0.0).astype(bf16)
    x = iota((rows4, tiles), 0)
    row_e = (e // cap) * (2 * cap) + e % cap
    row_p = (q // cap) * (2 * cap) + cap + q % cap
    p_hot = ind(x == row_p)
    pair_ref[...] = jnp.concatenate([ind(x == row_e), p_hot], axis=0).T.astype(bf16)
    sp4_ref[...] = jnp.where(used, p_hot, 0.0).astype(bf16)
    sp_ref[...] = jnp.where(used, ind(iota(sp_ref.shape, 0) == q), 0.0).astype(bf16)
    x = iota((rows8, tiles), 0)
    row_z = (q // cap) * (4 * cap) + q % cap
    gp8_ref[...] = ind(x == row_z).T.astype(bf16)
    sp8_ref[...] = jnp.concatenate(
        [
            jnp.where(used, ind(x == row_z + cap), 0.0),
            jnp.where(used, ind(x == row_z + 2 * cap), 0.0),
        ],
        axis=1,
    ).astype(bf16)

    rows, sent = list_ref.shape
    slots = pneed_ref.shape[1]
    peers = slots // cap
    x = iota((rows, slots), 0)
    y = iota((rows, slots), 1)
    peer, r = x // (2 * cap), x % (2 * cap)
    e_here = (r < cap) & (y == peer * cap + r)
    p_here = (r >= cap) & (y == peer * cap + r - cap)
    pn = jnp.broadcast_to(pneed_ref[...].astype(f32), (rows, slots))
    qn = jnp.broadcast_to(qneed_ref[...].astype(f32), (rows, slots)) + float(kb)
    col = jnp.sum(jnp.where(e_here, pn, 0.0) + jnp.where(p_here, qn, 0.0), axis=1, keepdims=True)
    mine_ref[...] = jnp.broadcast_to(col, (rows, 128))
    start_of = block_of(iota((rows, 1), 0) // (2 * cap), peers) * (sent // peers)
    list_ref[...] = jnp.where(
        iota((rows, sent), 1).astype(f32) == col + start_of.astype(f32), 1.0, 0.0
    ).astype(bf16)

    size = c_ref.shape[0] // CHUNKS
    held = held_ref.shape[0] // size

    def to_held(i, _):
        chunk_copy(c_hbm, c_ref, in_sems, i).wait()
        chunk_products(w_ref, c_ref, i, 0, b0_ref, b1_ref)
        for t in range(size):
            held_ref[i * size + t] = c_ref[i * size + t].T
        return 0

    def to_rest(i, _):
        chunk_copy(c_hbm, c_ref, in_sems, held + i).wait()
        chunk_products(w_ref, c_ref, held + i, 0, b0_ref, b1_ref)
        for t in range(size):
            t_ref[i * size + t] = c_ref[(held + i) * size + t].T
        chunk_copy(t_ref, t_hbm, out_sems, i).start()
        return 0

    lax.fori_loop(0, held, to_held, 0)
    lax.fori_loop(0, out_sems.shape[0], to_rest, 0)
    for i in range(out_sems.shape[0]):
        chunk_copy(t_ref, t_hbm, out_sems, i).wait()


def blocks(same_ref, other_ref, peers, first, count):
    step = 2 * same_ref.shape[0] // peers
    parts = [
        ref[b * step + first : b * step + first + count]
        for ref in (same_ref, other_ref)
        for b in range(peers // 2)
    ]
    return jnp.concatenate(parts, axis=0)


def serve_kernel(
    cap,
    kb,
    qb,
    asked_ref,
    hot_ref,
    mine_ref,
    share_ref,
    s8_ref,
    st4_ref,
    st8a_ref,
    st8b_ref,
):
    hot = hot_ref[...]
    rows4, rows8 = hot.shape[0], s8_ref.shape[0]
    x = iota((rows8, rows4), 0)
    y = iota((rows8, rows4), 1)
    peer, r = x // (4 * cap), x % (4 * cap)
    source = peer * (2 * cap) + cap + r % cap

    def rows_of(kind):
        here = (y == source) & (r // cap == kind)
        return dot(jnp.where(here, 1.0, 0.0).astype(bf16), hot)

    s8_ref[...] = rows_of(0).astype(bf16)
    st4_ref[...] = hot.astype(f32).T[kb : kb + qb].astype(bf16)
    st8a_ref[...] = rows_of(1).T[kb : kb + qb].astype(bf16)
    st8b_ref[...] = rows_of(2).T[kb : kb + qb].astype(bf16)

    peers = rows4 // (2 * cap)
    slots = peers * cap
    wide = peers * slots
    lists = asked_ref[...]
    pick_q = iota((peers, 8 * peers), 1) == 8 * iota((peers, 8 * peers), 0) + 1
    every_q = dot(jnp.where(pick_q, 1.0, 0.0).astype(bf16), lists).astype(bf16)
    tiled = iota((128, wide), 0) == iota((128, wide), 1) % slots
    spread = dot(every_q, jnp.where(tiled, 1.0, 0.0).astype(bf16))
    lane = iota((1, wide), 1)
    here = iota((peers, wide), 0) == lane // slots
    q = jnp.sum(jnp.where(here, spread, 0.0), axis=0, keepdims=True)
    ids = q + (lane % slots // cap * qb).astype(f32)
    row = iota((rows4, 1), 0)
    col = mine_ref[...][:, :1]
    my_ids = col - float(kb) + (row // (2 * cap) * qb).astype(f32)
    my_ids = jnp.where(row % (2 * cap) >= cap, my_ids, -1.0)
    owned = (lax.axis_index("bulk") * qb + iota((qb, 1), 0)).astype(f32)
    wanted = jnp.concatenate([my_ids, owned], axis=0)
    share_ref[...] = jnp.where(ids == wanted, 1.0, 0.0).astype(bf16)


def thermal_of(energy_ref):
    return 1.0 / (jnp.exp(energy_ref[...]) - 1.0)


def put_broadcast(send, served, contributions):
    slots = contributions.shape[0]
    for chip in range(served.shape[0] // 8):
        at = chip * (8 + slots)
        send[at : at + 8] = served[chip * 8 : chip * 8 + 8]
        send[at + 8 : at + 8 + slots] = contributions


def phonon_terms(far, bose, b0_ref, b1_ref):
    gain = far * flat(b0_ref)
    return gain + bose * (gain - (1.0 - far) * flat(b1_ref))


def first_kernel(
    cap,
    same_ref,
    other_ref,
    list_ref,
    f_ref,
    n_ref,
    energy_ref,
    decay_ref,
    pair_ref,
    sk_ref,
    sp_ref,
    b0_ref,
    b1_ref,
    held_ref,
    fetched_ref,
    c_hbm,
    send,
    e_ref,
    f1_ref,
    hot_ref,
    asked_ref,
    w_ref,
    c_ref,
    sems,
    o0,
    o1,
):
    start_chunks(c_hbm, c_ref, sems, fetched_ref.shape[0])
    f, n = f_ref[...], n_ref[...]
    kb, qb = f.shape[0], n.shape[0]
    rows4 = list_ref.shape[0]
    peers = rows4 // (2 * cap)
    got = add_rows(list_ref[...], jnp.concatenate([same_ref[...], other_ref[...]], axis=0))
    far, bose = gather_pair(pair_ref[...], got)
    contributions = add_rows(sp_ref[...], phonon_terms(far, bose, b0_ref, b1_ref))
    lists = blocks(same_ref, other_ref, peers, kb + qb, 8).astype(bf16)
    asked_ref[...] = lists
    x = iota((rows4, 8 * peers), 0)
    r = x % (2 * cap)
    kind = jnp.where(r < cap, 0, 1)
    at = iota((rows4, 8 * peers), 1) == 8 * block_of(x // (2 * cap), peers) + kind
    asked = dot(jnp.where(at, 1.0, 0.0).astype(bf16), lists)
    r = iota((rows4, 128), 0) % (2 * cap)
    lane = iota((rows4, 128), 1)
    wanted = lane == lax.axis_index("bulk") * cap + r % cap
    col = jnp.sum(jnp.where(wanted, asked, 0.0), axis=1, keepdims=True)
    col = col + jnp.where(r[:, :1] < cap, 0.0, float(kb))
    hot = jnp.where(lane.astype(f32) == col, 1.0, 0.0).astype(bf16)
    hot_ref[...] = hot
    base = n - DT * decay_ref[...] * (n - thermal_of(energy_ref))
    parts = [(held_ref, None, None), (fetched_ref, None, None), (c_ref, c_hbm, sems)]
    rate = electron_rate(sk_ref[...], far, bose, f, parts, w_ref, o0, o1)
    f1 = f + DT * rate
    e_ref[...] = rate
    f1_ref[...] = f1
    put_broadcast(send, pick(hot, padded(f1, base)), contributions)


def middle_kernel(
    cap,
    ends,
    same_ref,
    other_ref,
    share_ref,
    serve_ref,
    f_ref,
    e_ref,
    own_ref,
    n_ref,
    energy_ref,
    decay_ref,
    pair_ref,
    sk_ref,
    sp_ref,
    b0_ref,
    b1_ref,
    held_ref,
    fetched_ref,
    c_hbm,
    send,
    *refs,
):
    w_ref, c_ref, sems, o0, o1 = refs[-5:]
    start_chunks(c_hbm, c_ref, sems, fetched_ref.shape[0])
    rows4 = serve_ref.shape[0]
    peers = rows4 // (2 * cap)
    slots = peers * cap
    x = iota((rows4, 8 * peers), 0)
    source = 8 * block_of(x // (2 * cap), peers) + 2 * cap * my_core() + x % (2 * cap)
    at = jnp.where(iota((rows4, 8 * peers), 1) == source, 1.0, 0.0).astype(bf16)
    heads = blocks(same_ref, other_ref, peers, 0, 8)
    tails = blocks(same_ref, other_ref, peers, 8, slots)
    weight = DT / 2.0 if ends else DT
    both = add_rows(share_ref[...], tails)
    shares, total = both[:rows4], both[rows4:]
    got = add_rows(at, heads) + weight * shares
    far, bose = gather_pair(pair_ref[...], got)
    terms = phonon_terms(far, bose, b0_ref, b1_ref)
    contributions = add_rows(sp_ref[...], terms)
    n = n_ref[...]
    own = own_ref[...]
    parts = [(held_ref, None, None), (fetched_ref, None, None), (c_ref, c_hbm, sems)]
    if ends:
        n2_ref, e2_ref, f3_ref = refs[:3]
        n2_ref[...] = n + (DT / 2.0) * total
        rate = electron_rate(sk_ref[...], far, bose, own, parts, w_ref, o0, o1)
        f3 = own + DT * rate
        e2_ref[...] = rate
        f3_ref[...] = f3
        send[...] = pick(serve_ref[...], padded(f3)) + contributions
    else:
        base_ref, f2_ref = refs[:2]
        thermal = thermal_of(energy_ref)
        decay = decay_ref[...]
        p0 = total - decay * (n - thermal)
        n1 = n + DT * p0
        base = n + (DT / 2.0) * (p0 - decay * (n1 - thermal))
        base_ref[...] = base
        rate = electron_rate(sk_ref[...], far, bose, own, parts, w_ref, o0, o1)
        f2 = f_ref[...] + (DT / 2.0) * (e_ref[...] + rate)
        f2_ref[...] = f2
        put_broadcast(send, pick(serve_ref[...], padded(f2, base)), contributions)


def backward_kernel(f_ref, gk_ref, c_hbm, b0_ref, b1_ref, w_ref, c_ref, sems):
    start_chunks(c_hbm, c_ref, sems)
    own = add_rows(gk_ref[...], f_ref[...])
    backward_pass(own, c_hbm, c_ref, sems, w_ref, b0_ref, b1_ref)


def fetch_kernel(after_ref, c_hbm, fetched_ref, sems):
    start_chunks(c_hbm, fetched_ref, sems)
    for i in range(sems.shape[0]):
        chunk_copy(c_hbm, fetched_ref, sems, i).wait()


def phonon_kernel(
    kb,
    recv,
    n_ref,
    energy_ref,
    decay_ref,
    pair_ref,
    st4_ref,
    sp8_ref,
    s8_ref,
    b0_ref,
    b1_ref,
    send,
    p_ref,
    n1_ref,
    far_ref,
):
    n = n_ref[...]
    got = recv[...]
    thermal = thermal_of(energy_ref)
    rate = add_rows(st4_ref[...], got) - decay_ref[...] * (n - thermal)
    n1 = n + DT * rate
    p_ref[...] = rate
    n1_ref[...] = n1
    far = add_rows(pair_ref[:, : got.shape[0]], got)
    far_ref[...] = far
    gain = far * flat(b0_ref)
    both = jnp.concatenate([gain, gain - (1.0 - far) * flat(b1_ref)], axis=0)
    state = padded(jnp.zeros((kb, 128), f32), n1)
    send[...] = pick(s8_ref[...], state) + add_rows(sp8_ref[...], both)


def last_kernel(recv, *refs):
    far_ref, f_ref, f1_ref, e_ref, n_ref, n1_ref, p_ref, energy_ref, decay_ref = refs[:9]
    gp8_ref, sk_ref, st8a_ref, st8b_ref, held_ref, c_hbm = refs[9:15]
    refs = refs[15:]
    f2_ref, n2_ref, w_ref, c_ref, sems, o0, o1 = refs
    start_chunks(c_hbm, c_ref, sems)
    got = recv[...]
    n, n1 = n_ref[...], n1_ref[...]
    bose = add_rows(gp8_ref[...], got)
    thermal = thermal_of(energy_ref)
    p1 = (
        add_rows(st8a_ref[...], got)
        + n1 * add_rows(st8b_ref[...], got)
        - decay_ref[...] * (n1 - thermal)
    )
    n2 = n + (DT / 2.0) * (p_ref[...] + p1)
    n2_ref[...] = n2
    parts = [(held_ref, None, None), (c_ref, c_hbm, sems)]
    rate = electron_rate(sk_ref[...], far_ref[...], bose, f1_ref[...], parts, w_ref, o0, o1)
    f2 = f_ref[...] + (DT / 2.0) * (e_ref[...] + rate)
    f2_ref[...] = f2


def call(kernel, name, outs, scratch=(), spaces=None, out_spaces=None, flops=0, seen=0):
    def run(*args):
        places = dict(spaces or {})
        args = [
            pltpu.with_memory_space_constraint(x, pltpu.HBM)
            if places.get(i) is pltpu.HBM
            else x
            for i, x in enumerate(args)
        ]
        specs = [
            pl.BlockSpec(memory_space=places.get(i, pltpu.VMEM)) for i in range(len(args))
        ]
        return pl.pallas_call(
            kernel,
            out_shape=[
                (out_spaces or {}).get(i, jax.ShapeDtypeStruct)(*o) for i, o in enumerate(outs)
            ],
            in_specs=specs,
            out_specs=[
                pl.BlockSpec(memory_space=(out_spaces or {}).get(i, pltpu.VMEM))
                for i in range(len(outs))
            ],
            scratch_shapes=list(scratch),
            compiler_params=pltpu.CompilerParams(vmem_limit_bytes=VMEM_LIMIT),
            cost_estimate=pl.CostEstimate(
                flops=flops, bytes_accessed=seen, transcendentals=0
            ),
            name=name,
        )(*args)

    return run


def on_device(
    electrons,
    phonons,
    phonon_energy,
    phonon_decay,
    coupling,
    tile_kblock,
    tile_partner,
    tile_qslot,
    tile_count,
    partner_need,
    phonon_need,
):
    devices = lax.axis_size("bulk")
    kb = electrons.shape[0]
    qb = phonons.shape[0]
    tiles = coupling.shape[0]
    cap = partner_need.shape[1] // devices
    assert cap == phonon_need.shape[1] // devices and kb + qb <= 128
    rows4 = devices * 2 * cap
    rows8 = devices * 4 * cap
    groups = tiles // 8
    held = HELD_CHUNKS * (tiles // CHUNKS)
    weights = pltpu.VMEM((groups, 16, 1024), bf16)
    streams = [weights, pltpu.VMEM(coupling.shape, bf16), pltpu.SemaphoreType.DMA((CHUNKS,))]
    rest = (tiles - held, 128, 128)
    rest_sems = pltpu.SemaphoreType.DMA((CHUNKS - HELD_CHUNKS,))
    forward_streams = [weights, pltpu.VMEM(rest, bf16), rest_sems]
    fetched = (FETCHED_CHUNKS * (tiles // CHUNKS), 128, 128)
    short = (rest[0] - fetched[0], 128, 128)
    short_sems = pltpu.SemaphoreType.DMA((CHUNKS - HELD_CHUNKS - FETCHED_CHUNKS,))
    sums = [pltpu.VMEM((groups, 8, 128), f32)] * 2
    pass_out = [((groups, 8, 128), f32)] * 2
    block4 = ((rows4, 128), f32)
    block8 = ((rows8, 128), f32)

    work = dict(flops=2 * tiles * 16 * 128 * 128, seen=tiles * 128 * 128 * 2)

    def exchange(x):
        return lax.all_to_all(x, "bulk", split_axis=0, concat_axis=0, tiled=True)

    ints = ((1, tiles), jnp.int32)
    lists = ((1, partner_need.shape[1]), jnp.int32)
    small = [((kb, 128), f32)] + [((qb, 128), f32)] * 3 + [ints] * 3
    step_rows = kb + qb + 8
    slots = devices * cap
    wide = 8 + slots
    assert step_rows % 8 == 0 and slots % 8 == 0 and slots <= 128
    assert devices % 2 == 0 and cap == 2
    chips = devices // 2
    same_core = [list(range(core, devices, 2)) for core in (0, 1)]

    def to_chips(x):
        return lax.all_to_all(
            x, "bulk", split_axis=0, concat_axis=0, tiled=True, axis_index_groups=same_core
        )

    def between_cores(x):
        return lax.ppermute(x, "bulk", [(i, i ^ 1) for i in range(devices)])

    f, n, energy, decay, kblock, partner, qslot, pneed, qneed, send = call(
        functools.partial(need_kernel, cap),
        "need",
        small + [lists, lists, ((chips * step_rows, 128), f32)],
        [pltpu.SemaphoreType.DMA((9,))],
        spaces={i: pltpu.HBM for i in range(9)},
        out_spaces={9: pltpu.VMEM},
    )(
        electrons,
        phonons,
        phonon_energy,
        phonon_decay,
        tile_kblock.reshape(1, tiles),
        tile_partner.reshape(1, tiles),
        tile_qslot.reshape(1, tiles),
        partner_need,
        phonon_need,
    )
    same = to_chips(send)
    c_held, c_rest, pair, gp8, gk, sk, sp, sp4, sp8, picks, mine, b0, b1 = call(
        functools.partial(prepare_kernel, cap),
        "prepare",
        [
            ((held, 128, 128), bf16),
            (rest, bf16),
            ((tiles, 2 * rows4), bf16),
            ((tiles, rows8), bf16),
            ((tiles, kb), bf16),
            ((kb, tiles), bf16),
            ((slots, tiles), bf16),
            ((rows4, tiles), bf16),
            ((rows8, 2 * tiles), bf16),
            ((rows4, devices * step_rows), bf16),
            ((rows4, 128), f32),
        ]
        + pass_out,
        [*streams, pltpu.VMEM(rest, bf16), rest_sems],
        spaces={0: pltpu.SMEM, 7: pltpu.HBM},
        out_spaces={1: pltpu.HBM},
        **work,
    )(tile_count, kblock, partner, qslot, f, pneed, qneed, coupling)
    same, c_held, b0 = lax.optimization_barrier((same, c_held, b0))
    wide_block = ((chips * wide, 128), f32)
    k_rows, q_rows = ((kb, 128), f32), ((qb, 128), f32)
    forward_scratch = [weights, pltpu.VMEM(short, bf16), short_sems] + sums

    def fetch(after):
        return call(
            fetch_kernel,
            "fetch",
            [(fetched, bf16)],
            [pltpu.SemaphoreType.DMA((FETCHED_CHUNKS,))],
            spaces={0: pl.ANY, 1: pltpu.HBM},
            out_spaces={0: pltpu.VMEM},
            seen=fetched[0] * 128 * 128 * 2,
        )(after, c_rest)[0]

    other = between_cores(same)
    c_fetched = fetch(same)
    send, e0, f1, serve, asked = call(
        functools.partial(first_kernel, cap),
        "first",
        [wide_block, k_rows, k_rows, ((rows4, 128), bf16), ((8 * devices, 128), bf16)],
        forward_scratch,
        spaces={14: pltpu.HBM},
        out_spaces={0: pltpu.VMEM},
        **work,
    )(same, other, picks, f, n, energy, decay, pair, sk, sp, b0, b1, c_held, c_fetched, c_rest)
    share, s8, st4, st8a, st8b = call(
        functools.partial(serve_kernel, cap, kb, qb),
        "serve",
        [
            ((rows4 + qb, devices * slots), bf16),
            ((rows8, 128), bf16),
            ((qb, rows4), bf16),
            ((qb, rows8), bf16),
            ((qb, rows8), bf16),
        ],
    )(asked, serve, mine)
    back = call(backward_kernel, "backward", pass_out, streams, spaces={2: pltpu.HBM}, **work)

    def middle(ends, send, outs, f, e, own, n, contributions):
        same = to_chips(send)
        b0, b1 = back(own, gk, coupling)
        same, b0 = lax.optimization_barrier((same, b0))
        other = between_cores(same)
        c_fetched = fetch(same)
        return call(
            functools.partial(middle_kernel, cap, ends),
            "middle",
            outs,
            forward_scratch,
            spaces={17: pltpu.HBM},
            out_spaces={0: pltpu.VMEM},
            **work,
        )(
            same, other, share, serve, f, e, own, n, energy, decay,
            pair, sk, contributions, b0, b1, c_held, c_fetched, c_rest,
        )

    send, base, f2 = middle(False, send, [wide_block, q_rows, k_rows], f, e0, f1, n, sp)
    send, n2, e2, f3 = middle(
        True, send, [block4, q_rows, k_rows, k_rows], f2, e0, f2, base, sp4
    )
    recv = exchange(send)
    b0, b1 = back(f3, gk, coupling)
    send, p2, n3, far = call(
        functools.partial(phonon_kernel, kb),
        "phonon",
        [block8, q_rows, q_rows, ((tiles, 128), f32)],
    )(recv, n2, energy, decay, pair, st4, sp8, s8, b0, b1)
    recv = exchange(send)
    f, n = call(
        last_kernel,
        "last",
        [k_rows, q_rows],
        forward_streams + sums,
        spaces={15: pltpu.HBM},
        **work,
    )(
        recv, far, f2, f3, e2, n2, n3, p2, energy, decay,
        gp8, sk, st8a, st8b, c_held, c_rest,
    )
    return (f, n)


def solution(mesh):
    placed = (
        P(("groups", "bulk"), None),
        P(("groups", "bulk"), None),
        P("bulk", None),
        P("bulk", None),
        P("bulk", None, None),
        P("bulk"),
        P("bulk"),
        P("bulk"),
        P("bulk"),
        P("bulk", None),
        P("bulk", None),
    )
    return jax.shard_map(
        on_device,
        mesh=mesh,
        in_specs=placed,
        out_specs=(P(("groups", "bulk"), None), P(("groups", "bulk"), None)),
        check_vma=False,
    )
```

```python
import functools

import jax
import jax.numpy as jnp
from jax import lax
from jax.experimental import pallas as pl
from jax.experimental.pallas import tpu as pltpu
from jax.sharding import PartitionSpec as P

DT = 0.05
CHUNKS = 8
HELD_CHUNKS = 2
f32 = jnp.float32
bf16 = jnp.bfloat16
VMEM_LIMIT = 48 * 1024 * 1024


def iota(shape, dim):
    return lax.broadcasted_iota(jnp.int32, shape, dim)


def dot(a, b):
    return lax.dot_general(a, b, (((1,), (0,)), ((), ())), preferred_element_type=f32)


def split(x):
    hi = x.astype(bf16)
    rest = x - hi.astype(f32)
    mid = rest.astype(bf16)
    lo = (rest - mid.astype(f32)).astype(bf16)
    return hi, mid, lo


def pick(onehot, x):
    hi, mid, lo = split(x)
    both = dot(onehot, jnp.concatenate([hi, mid], axis=1))
    return both[:, :128] + both[:, 128:] + dot(onehot, lo)


def add_rows(onehot, x):
    hi = x.astype(bf16)
    mid = (x - hi.astype(f32)).astype(bf16)
    both = dot(onehot, jnp.concatenate([hi, mid], axis=1))
    return both[:, :128] + both[:, 128:]


def gather_pair(table, x):
    rows = x.shape[0]
    hi = x.astype(bf16)
    mid = (x - hi.astype(f32)).astype(bf16)
    blank = jnp.zeros((rows, 128), bf16)

    def both(part):
        upper = jnp.concatenate([part, blank], axis=1)
        lower = jnp.concatenate([blank, part], axis=1)
        return dot(table, jnp.concatenate([upper, lower], axis=0))

    res = both(hi) + both(mid)
    return res[:, :128], res[:, 128:]


def stacked(first, second):
    tiles = first.shape[0]
    return jnp.concatenate(
        [first.reshape(tiles // 8, 8, 128), second.reshape(tiles // 8, 8, 128)], axis=1
    ).astype(bf16)


def row_is(r):
    return iota((16, 128), 0) % 8 == r


def padded(*parts):
    rows = sum(p.shape[0] for p in parts)
    return jnp.concatenate([*parts, jnp.zeros((128 - rows, 128), f32)], axis=0)


def flat(ref):
    return ref[...].reshape(-1, 128)


def chunk_copy(src, dst, sems, i):
    size = src.shape[0] // sems.shape[0]
    here = pl.ds(i * size, size)
    return pltpu.make_async_copy(src.at[here], dst.at[here], sems.at[i])


def start_chunks(src, dst, sems):
    for i in range(sems.shape[0]):
        chunk_copy(src, dst, sems, i).start()


def start(copies):
    for copy in copies:
        copy.start()


def block_diagonal(w):
    w = w.astype(f32)
    return jnp.concatenate(
        [jnp.where(row_is(r), w, 0.0).astype(bf16) for r in range(8)], axis=1
    )


def left_sides(first, second, w_ref):
    w = stacked(first, second)
    for g in range(w.shape[0]):
        w_ref[g] = block_diagonal(w[g])


def chunk_products(w_ref, c_ref, i, base, out0, out1):
    size = w_ref.shape[0] // CHUNKS
    for k in range(size):
        g = i * size + k
        res = dot(w_ref[base + g], c_ref[pl.ds(g * 8, 8)].reshape(1024, 128))
        out0[base + g] = res[:8]
        out1[base + g] = res[8:]


def tile_products(w_ref, parts, out0, out1):
    size = w_ref.shape[0] // CHUNKS
    base = 0
    for c_ref, c_hbm, sems in parts:
        chunks = c_ref.shape[0] // 8 // size

        def chunk(i, _):
            if c_hbm is not None:
                chunk_copy(c_hbm, c_ref, sems, i).wait()
            chunk_products(w_ref, c_ref, i, base, out0, out1)
            return 0

        lax.fori_loop(0, chunks, chunk, 0)
        base += chunks * size


def backward_pass(own, c_hbm, c_ref, sems, w_ref, out0, out1):
    left_sides(1.0 - own, own, w_ref)
    tile_products(w_ref, [(c_ref, c_hbm, sems)], out0, out1)


def electron_rate(sum_k, far, bose, f, parts, w_ref, o0, o1):
    left_sides(far * (1.0 + bose), far + bose, w_ref)
    tile_products(w_ref, parts, o0, o1)
    return add_rows(sum_k, flat(o0)) - f * add_rows(sum_k, flat(o1))


def my_core():
    return lax.rem(lax.axis_index("bulk"), 2)


def block_of(peer, peers):
    return peer // 2 + jnp.where(peer % 2 == my_core(), 0, peers // 2)


def need_kernel(cap, *refs):
    ins, outs = refs[:9], refs[9:]
    *small, pneed_ref, qneed_ref, send_ref, sems = outs
    copies = [
        pltpu.make_async_copy(src, dst, sems.at[i])
        for i, (src, dst) in enumerate(zip(ins, [*small, pneed_ref, qneed_ref]))
    ]
    start(copies)
    slots = pneed_ref.shape[1]
    step = send_ref.shape[0] // (slots // cap // 2)
    for copy in copies:
        copy.wait()
    f, n = small[0][...], small[1][...]
    own_p, own_q = pneed_ref[...].astype(f32), qneed_ref[...].astype(f32)
    row = iota((8, slots), 0)
    lists = jnp.where(row == 0, own_p, jnp.where(row == 1, own_q, 0.0))
    if slots < 128:
        lists = jnp.concatenate([lists, jnp.zeros((8, 128 - slots), f32)], axis=1)
    block = jnp.concatenate([f, n, lists], axis=0)
    for chip in range(slots // cap // 2):
        send_ref[chip * step : (chip + 1) * step] = block


def prepare_kernel(
    cap,
    count_ref,
    kblock_ref,
    partner_ref,
    qslot_ref,
    f_ref,
    pneed_ref,
    qneed_ref,
    c_hbm,
    held_ref,
    t_hbm,
    pair_ref,
    gp8_ref,
    gk_ref,
    sk_ref,
    sp_ref,
    sp4_ref,
    sp8_ref,
    near_ref,
    list_ref,
    mine_ref,
    b0_ref,
    b1_ref,
    w_ref,
    c_ref,
    in_sems,
    t_ref,
    out_sems,
):
    start_chunks(c_hbm, c_ref, in_sems)
    tiles = kblock_ref.shape[1]
    kb = f_ref.shape[0]
    used = iota((1, tiles), 1) < count_ref[0]
    k = kblock_ref[...]
    e = partner_ref[...]
    q = qslot_ref[...]
    rows4 = sp4_ref.shape[0]
    rows8 = sp8_ref.shape[0]
    ind = lambda m: jnp.where(m, 1.0, 0.0)
    k_hot = ind(iota((kb, tiles), 0) == k)
    gk_ref[...] = k_hot.T.astype(bf16)
    own = add_rows(gk_ref[...], f_ref[...])
    left_sides(1.0 - own, own, w_ref)
    sk_ref[...] = jnp.where(used, k_hot, 0.0).astype(bf16)
    x = iota((rows4, tiles), 0)
    row_e = (e // cap) * (2 * cap) + e % cap
    row_p = (q // cap) * (2 * cap) + cap + q % cap
    p_hot = ind(x == row_p)
    pair_ref[...] = jnp.concatenate([ind(x == row_e), p_hot], axis=0).T.astype(bf16)
    sp4_ref[...] = jnp.where(used, p_hot, 0.0).astype(bf16)
    sp_ref[...] = jnp.where(used, ind(iota(sp_ref.shape, 0) == q), 0.0).astype(bf16)
    x = iota((rows8, tiles), 0)
    row_z = (q // cap) * (4 * cap) + q % cap
    gp8_ref[...] = ind(x == row_z).T.astype(bf16)
    sp8_ref[...] = jnp.concatenate(
        [
            jnp.where(used, ind(x == row_z + cap), 0.0),
            jnp.where(used, ind(x == row_z + 2 * cap), 0.0),
        ],
        axis=1,
    ).astype(bf16)

    rows, half = list_ref.shape
    slots = pneed_ref.shape[1]
    peers = slots // cap
    x = iota((rows, slots), 0)
    y = iota((rows, slots), 1)
    peer, r = x // (2 * cap), x % (2 * cap)
    e_here = (r < cap) & (y == peer * cap + r)
    p_here = (r >= cap) & (y == peer * cap + r - cap)
    pn = jnp.broadcast_to(pneed_ref[...].astype(f32), (rows, slots))
    qn = jnp.broadcast_to(qneed_ref[...].astype(f32), (rows, slots)) + float(kb)
    col = jnp.sum(jnp.where(e_here, pn, 0.0) + jnp.where(p_here, qn, 0.0), axis=1, keepdims=True)
    mine_ref[...] = jnp.broadcast_to(col, (rows, 128))
    start_of = block_of(iota((rows, 1), 0) // (2 * cap), peers) * (2 * half // peers)
    place = col + start_of.astype(f32)
    lane = iota((rows, half), 1).astype(f32)
    near_ref[...] = ind(lane == place).astype(bf16)
    list_ref[...] = ind(lane + float(half) == place).astype(bf16)

    size = c_ref.shape[0] // CHUNKS
    held = held_ref.shape[0] // size

    def to_held(i, _):
        chunk_copy(c_hbm, c_ref, in_sems, i).wait()
        chunk_products(w_ref, c_ref, i, 0, b0_ref, b1_ref)
        for t in range(size):
            held_ref[i * size + t] = c_ref[i * size + t].T
        return 0

    def to_rest(i, _):
        chunk_copy(c_hbm, c_ref, in_sems, held + i).wait()
        chunk_products(w_ref, c_ref, held + i, 0, b0_ref, b1_ref)
        for t in range(size):
            t_ref[i * size + t] = c_ref[(held + i) * size + t].T
        chunk_copy(t_ref, t_hbm, out_sems, i).start()
        return 0

    lax.fori_loop(0, held, to_held, 0)
    lax.fori_loop(0, out_sems.shape[0], to_rest, 0)
    for i in range(out_sems.shape[0]):
        chunk_copy(t_ref, t_hbm, out_sems, i).wait()


def blocks(ref, count_of_blocks, first, count):
    step = ref.shape[0] // count_of_blocks
    parts = [ref[b * step + first : b * step + first + count] for b in range(count_of_blocks)]
    return jnp.concatenate(parts, axis=0)


def serve_kernel(
    cap,
    kb,
    qb,
    asked_ref,
    hot_ref,
    mine_ref,
    share_ref,
    s8_ref,
    st4_ref,
    st8a_ref,
    st8b_ref,
):
    hot = hot_ref[...]
    rows4, rows8 = hot.shape[0], s8_ref.shape[0]
    x = iota((rows8, rows4), 0)
    y = iota((rows8, rows4), 1)
    peer, r = x // (4 * cap), x % (4 * cap)
    source = peer * (2 * cap) + cap + r % cap

    def rows_of(kind):
        here = (y == source) & (r // cap == kind)
        return dot(jnp.where(here, 1.0, 0.0).astype(bf16), hot)

    s8_ref[...] = rows_of(0).astype(bf16)
    st4_ref[...] = hot.astype(f32).T[kb : kb + qb].astype(bf16)
    st8a_ref[...] = rows_of(1).T[kb : kb + qb].astype(bf16)
    st8b_ref[...] = rows_of(2).T[kb : kb + qb].astype(bf16)

    peers = rows4 // (2 * cap)
    slots = peers * cap
    wide = peers * slots
    lists = asked_ref[...]
    pick_q = iota((peers, 8 * peers), 1) == 8 * iota((peers, 8 * peers), 0) + 1
    every_q = dot(jnp.where(pick_q, 1.0, 0.0).astype(bf16), lists).astype(bf16)
    tiled = iota((128, wide), 0) == iota((128, wide), 1) % slots
    spread = dot(every_q, jnp.where(tiled, 1.0, 0.0).astype(bf16))
    lane = iota((1, wide), 1)
    here = iota((peers, wide), 0) == lane // slots
    q = jnp.sum(jnp.where(here, spread, 0.0), axis=0, keepdims=True)
    ids = q + (lane % slots // cap * qb).astype(f32)
    row = iota((rows4, 1), 0)
    col = mine_ref[...][:, :1]
    my_ids = col - float(kb) + (row // (2 * cap) * qb).astype(f32)
    my_ids = jnp.where(row % (2 * cap) >= cap, my_ids, -1.0)
    owned = (lax.axis_index("bulk") * qb + iota((qb, 1), 0)).astype(f32)
    wanted = jnp.concatenate([my_ids, owned], axis=0)
    share_ref[...] = jnp.where(ids == wanted, 1.0, 0.0).astype(bf16)


def thermal_of(energy_ref):
    return 1.0 / (jnp.exp(energy_ref[...]) - 1.0)


def put_broadcast(send, served, contributions):
    slots = contributions.shape[0]
    for chip in range(served.shape[0] // 8):
        at = chip * (8 + slots)
        send[at : at + 8] = served[chip * 8 : chip * 8 + 8]
        send[at + 8 : at + 8 + slots] = contributions


def phonon_terms(far, bose, b0_ref, b1_ref):
    gain = far * flat(b0_ref)
    return gain + bose * (gain - (1.0 - far) * flat(b1_ref))


def near_rows_kernel(same_ref, list_ref, part_ref):
    part_ref[...] = add_rows(list_ref[...], same_ref[...])


def half_of_devices(cap, chips, weight, others, ref, share_ref):
    rows4 = 4 * cap * chips
    wide = share_ref.shape[1] // 2
    x = iota((rows4, 8 * chips), 0)
    peer = x // (2 * cap)
    source = 8 * (peer // 2) + 2 * cap * my_core() + x % (2 * cap)
    wanted_core = (my_core() + others) % 2
    at = (iota((rows4, 8 * chips), 1) == source) & (peer % 2 == wanted_core)
    heads = add_rows(jnp.where(at, 1.0, 0.0).astype(bf16), blocks(ref, chips, 0, 8))
    tails = blocks(ref, chips, 8, wide // chips)
    sums = add_rows(share_ref[:, others * wide : (others + 1) * wide], tails)
    return heads + weight * sums[:rows4], sums[rows4:]


def near_half_kernel(cap, chips, weight, same_ref, share_ref, part_ref, total_ref):
    part, total = half_of_devices(cap, chips, weight, 0, same_ref, share_ref)
    part_ref[...] = part
    total_ref[...] = total


def first_kernel(
    cap,
    same_ref,
    other_ref,
    part_ref,
    list_ref,
    f_ref,
    n_ref,
    energy_ref,
    decay_ref,
    pair_ref,
    sk_ref,
    sp_ref,
    b0_ref,
    b1_ref,
    held_ref,
    c_hbm,
    send,
    e_ref,
    f1_ref,
    hot_ref,
    asked_ref,
    w_ref,
    c_ref,
    sems,
    o0,
    o1,
):
    start_chunks(c_hbm, c_ref, sems)
    f, n = f_ref[...], n_ref[...]
    kb, qb = f.shape[0], n.shape[0]
    rows4 = list_ref.shape[0]
    peers = rows4 // (2 * cap)
    got = part_ref[...] + add_rows(list_ref[...], other_ref[...])
    far, bose = gather_pair(pair_ref[...], got)
    contributions = add_rows(sp_ref[...], phonon_terms(far, bose, b0_ref, b1_ref))
    lists = jnp.concatenate(
        [blocks(ref, peers // 2, kb + qb, 8) for ref in (same_ref, other_ref)], axis=0
    ).astype(bf16)
    asked_ref[...] = lists
    x = iota((rows4, 8 * peers), 0)
    r = x % (2 * cap)
    kind = jnp.where(r < cap, 0, 1)
    at = iota((rows4, 8 * peers), 1) == 8 * block_of(x // (2 * cap), peers) + kind
    asked = dot(jnp.where(at, 1.0, 0.0).astype(bf16), lists)
    r = iota((rows4, 128), 0) % (2 * cap)
    lane = iota((rows4, 128), 1)
    wanted = lane == lax.axis_index("bulk") * cap + r % cap
    col = jnp.sum(jnp.where(wanted, asked, 0.0), axis=1, keepdims=True)
    col = col + jnp.where(r[:, :1] < cap, 0.0, float(kb))
    hot = jnp.where(lane.astype(f32) == col, 1.0, 0.0).astype(bf16)
    hot_ref[...] = hot
    base = n - DT * decay_ref[...] * (n - thermal_of(energy_ref))
    parts = [(held_ref, None, None), (c_ref, c_hbm, sems)]
    rate = electron_rate(sk_ref[...], far, bose, f, parts, w_ref, o0, o1)
    f1 = f + DT * rate
    e_ref[...] = rate
    f1_ref[...] = f1
    put_broadcast(send, pick(hot, padded(f1, base)), contributions)


def middle_kernel(
    cap,
    ends,
    part_ref,
    total_ref,
    other_ref,
    share_ref,
    serve_ref,
    f_ref,
    e_ref,
    own_ref,
    n_ref,
    energy_ref,
    decay_ref,
    pair_ref,
    sk_ref,
    sp_ref,
    b0_ref,
    b1_ref,
    held_ref,
    c_hbm,
    send,
    *refs,
):
    w_ref, c_ref, sems, o0, o1 = refs[-5:]
    start_chunks(c_hbm, c_ref, sems)
    chips = serve_ref.shape[0] // (4 * cap)
    weight = DT / 2.0 if ends else DT
    part, total = half_of_devices(cap, chips, weight, 1, other_ref, share_ref)
    got = part_ref[...] + part
    total = total_ref[...] + total
    far, bose = gather_pair(pair_ref[...], got)
    terms = phonon_terms(far, bose, b0_ref, b1_ref)
    contributions = add_rows(sp_ref[...], terms)
    n = n_ref[...]
    own = own_ref[...]
    parts = [(held_ref, None, None), (c_ref, c_hbm, sems)]
    if ends:
        n2_ref, e2_ref, f3_ref = refs[:3]
        n2_ref[...] = n + (DT / 2.0) * total
        rate = electron_rate(sk_ref[...], far, bose, own, parts, w_ref, o0, o1)
        f3 = own + DT * rate
        e2_ref[...] = rate
        f3_ref[...] = f3
        send[...] = pick(serve_ref[...], padded(f3)) + contributions
    else:
        base_ref, f2_ref = refs[:2]
        thermal = thermal_of(energy_ref)
        decay = decay_ref[...]
        p0 = total - decay * (n - thermal)
        n1 = n + DT * p0
        base = n + (DT / 2.0) * (p0 - decay * (n1 - thermal))
        base_ref[...] = base
        rate = electron_rate(sk_ref[...], far, bose, own, parts, w_ref, o0, o1)
        f2 = f_ref[...] + (DT / 2.0) * (e_ref[...] + rate)
        f2_ref[...] = f2
        put_broadcast(send, pick(serve_ref[...], padded(f2, base)), contributions)


def backward_kernel(f_ref, gk_ref, c_hbm, b0_ref, b1_ref, w_ref, c_ref, sems):
    start_chunks(c_hbm, c_ref, sems)
    own = add_rows(gk_ref[...], f_ref[...])
    backward_pass(own, c_hbm, c_ref, sems, w_ref, b0_ref, b1_ref)


def phonon_kernel(
    kb,
    recv,
    n_ref,
    energy_ref,
    decay_ref,
    pair_ref,
    st4_ref,
    sp8_ref,
    s8_ref,
    b0_ref,
    b1_ref,
    send,
    p_ref,
    n1_ref,
    far_ref,
):
    n = n_ref[...]
    got = recv[...]
    thermal = thermal_of(energy_ref)
    rate = add_rows(st4_ref[...], got) - decay_ref[...] * (n - thermal)
    n1 = n + DT * rate
    p_ref[...] = rate
    n1_ref[...] = n1
    far = add_rows(pair_ref[:, : got.shape[0]], got)
    far_ref[...] = far
    gain = far * flat(b0_ref)
    both = jnp.concatenate([gain, gain - (1.0 - far) * flat(b1_ref)], axis=0)
    state = padded(jnp.zeros((kb, 128), f32), n1)
    send[...] = pick(s8_ref[...], state) + add_rows(sp8_ref[...], both)


def last_kernel(recv, *refs):
    far_ref, f_ref, f1_ref, e_ref, n_ref, n1_ref, p_ref, energy_ref, decay_ref = refs[:9]
    gp8_ref, sk_ref, st8a_ref, st8b_ref, held_ref, c_hbm = refs[9:15]
    refs = refs[15:]
    f2_ref, n2_ref, w_ref, c_ref, sems, o0, o1 = refs
    start_chunks(c_hbm, c_ref, sems)
    got = recv[...]
    n, n1 = n_ref[...], n1_ref[...]
    bose = add_rows(gp8_ref[...], got)
    thermal = thermal_of(energy_ref)
    p1 = (
        add_rows(st8a_ref[...], got)
        + n1 * add_rows(st8b_ref[...], got)
        - decay_ref[...] * (n1 - thermal)
    )
    n2 = n + (DT / 2.0) * (p_ref[...] + p1)
    n2_ref[...] = n2
    parts = [(held_ref, None, None), (c_ref, c_hbm, sems)]
    rate = electron_rate(sk_ref[...], far_ref[...], bose, f1_ref[...], parts, w_ref, o0, o1)
    f2 = f_ref[...] + (DT / 2.0) * (e_ref[...] + rate)
    f2_ref[...] = f2


def call(kernel, name, outs, scratch=(), spaces=None, out_spaces=None, flops=0, seen=0):
    def run(*args):
        places = dict(spaces or {})
        args = [
            pltpu.with_memory_space_constraint(x, pltpu.HBM)
            if places.get(i) is pltpu.HBM
            else x
            for i, x in enumerate(args)
        ]
        specs = [
            pl.BlockSpec(memory_space=places.get(i, pltpu.VMEM)) for i in range(len(args))
        ]
        return pl.pallas_call(
            kernel,
            out_shape=[
                (out_spaces or {}).get(i, jax.ShapeDtypeStruct)(*o) for i, o in enumerate(outs)
            ],
            in_specs=specs,
            out_specs=[
                pl.BlockSpec(memory_space=(out_spaces or {}).get(i, pltpu.VMEM))
                for i in range(len(outs))
            ],
            scratch_shapes=list(scratch),
            compiler_params=pltpu.CompilerParams(vmem_limit_bytes=VMEM_LIMIT),
            cost_estimate=pl.CostEstimate(
                flops=flops, bytes_accessed=seen, transcendentals=0
            ),
            name=name,
        )(*args)

    return run


def on_device(
    electrons,
    phonons,
    phonon_energy,
    phonon_decay,
    coupling,
    tile_kblock,
    tile_partner,
    tile_qslot,
    tile_count,
    partner_need,
    phonon_need,
):
    devices = lax.axis_size("bulk")
    kb = electrons.shape[0]
    qb = phonons.shape[0]
    tiles = coupling.shape[0]
    cap = partner_need.shape[1] // devices
    assert cap == phonon_need.shape[1] // devices and kb + qb <= 128
    rows4 = devices * 2 * cap
    rows8 = devices * 4 * cap
    groups = tiles // 8
    held = HELD_CHUNKS * (tiles // CHUNKS)
    weights = pltpu.VMEM((groups, 16, 1024), bf16)
    streams = [weights, pltpu.VMEM(coupling.shape, bf16), pltpu.SemaphoreType.DMA((CHUNKS,))]
    rest = (tiles - held, 128, 128)
    rest_sems = pltpu.SemaphoreType.DMA((CHUNKS - HELD_CHUNKS,))
    forward_streams = [weights, pltpu.VMEM(rest, bf16), rest_sems]
    sums = [pltpu.VMEM((groups, 8, 128), f32)] * 2
    pass_out = [((groups, 8, 128), f32)] * 2
    block4 = ((rows4, 128), f32)
    block8 = ((rows8, 128), f32)

    work = dict(flops=2 * tiles * 16 * 128 * 128, seen=tiles * 128 * 128 * 2)

    def exchange(x):
        return lax.all_to_all(x, "bulk", split_axis=0, concat_axis=0, tiled=True)

    ints = ((1, tiles), jnp.int32)
    lists = ((1, partner_need.shape[1]), jnp.int32)
    small = [((kb, 128), f32)] + [((qb, 128), f32)] * 3 + [ints] * 3
    step_rows = kb + qb + 8
    slots = devices * cap
    wide = 8 + slots
    assert step_rows % 8 == 0 and slots % 8 == 0 and slots <= 128
    assert devices % 2 == 0 and cap == 2
    chips = devices // 2
    same_core = [list(range(core, devices, 2)) for core in (0, 1)]

    def to_chips(x):
        return lax.all_to_all(
            x, "bulk", split_axis=0, concat_axis=0, tiled=True, axis_index_groups=same_core
        )

    def between_cores(x):
        return lax.ppermute(x, "bulk", [(i, i ^ 1) for i in range(devices)])

    f, n, energy, decay, kblock, partner, qslot, pneed, qneed, send = call(
        functools.partial(need_kernel, cap),
        "need",
        small + [lists, lists, ((chips * step_rows, 128), f32)],
        [pltpu.SemaphoreType.DMA((9,))],
        spaces={i: pltpu.HBM for i in range(9)},
    )(
        electrons,
        phonons,
        phonon_energy,
        phonon_decay,
        tile_kblock.reshape(1, tiles),
        tile_partner.reshape(1, tiles),
        tile_qslot.reshape(1, tiles),
        partner_need,
        phonon_need,
    )
    same = to_chips(send)
    c_held, c_rest, pair, gp8, gk, sk, sp, sp4, sp8, near, far_picks, mine, b0, b1 = call(
        functools.partial(prepare_kernel, cap),
        "prepare",
        [
            ((held, 128, 128), bf16),
            (rest, bf16),
            ((tiles, 2 * rows4), bf16),
            ((tiles, rows8), bf16),
            ((tiles, kb), bf16),
            ((kb, tiles), bf16),
            ((slots, tiles), bf16),
            ((rows4, tiles), bf16),
            ((rows8, 2 * tiles), bf16),
            ((rows4, chips * step_rows), bf16),
            ((rows4, chips * step_rows), bf16),
            ((rows4, 128), f32),
        ]
        + pass_out,
        [*streams, pltpu.VMEM(rest, bf16), rest_sems],
        spaces={0: pltpu.SMEM, 7: pltpu.HBM},
        out_spaces={1: pltpu.HBM},
        **work,
    )(tile_count, kblock, partner, qslot, f, pneed, qneed, coupling)
    same, c_held, b0 = lax.optimization_barrier((same, c_held, b0))
    wide_block = ((chips * wide, 128), f32)
    k_rows, q_rows = ((kb, 128), f32), ((qb, 128), f32)
    forward_scratch = forward_streams + sums
    other = between_cores(same)
    (part,) = call(near_rows_kernel, "near_rows", [block4])(same, near)
    send, e0, f1, serve, asked = call(
        functools.partial(first_kernel, cap),
        "first",
        [wide_block, k_rows, k_rows, ((rows4, 128), bf16), ((8 * devices, 128), bf16)],
        forward_scratch,
        spaces={14: pltpu.HBM},
        **work,
    )(same, other, part, far_picks, f, n, energy, decay, pair, sk, sp, b0, b1, c_held, c_rest)
    share, s8, st4, st8a, st8b = call(
        functools.partial(serve_kernel, cap, kb, qb),
        "serve",
        [
            ((rows4 + qb, devices * slots), bf16),
            ((rows8, 128), bf16),
            ((qb, rows4), bf16),
            ((qb, rows8), bf16),
            ((qb, rows8), bf16),
        ],
    )(asked, serve, mine)
    back = call(backward_kernel, "backward", pass_out, streams, spaces={2: pltpu.HBM}, **work)

    def middle(ends, send, outs, f, e, own, n, contributions):
        same = to_chips(send)
        b0, b1 = back(own, gk, coupling)
        same, b0 = lax.optimization_barrier((same, b0))
        other = between_cores(same)
        weight = DT / 2.0 if ends else DT
        part, total = call(
            functools.partial(near_half_kernel, cap, chips, weight), "near_half", [block4, q_rows]
        )(same, share)
        return call(
            functools.partial(middle_kernel, cap, ends),
            "middle",
            outs,
            forward_scratch,
            spaces={17: pltpu.HBM},
            **work,
        )(
            part, total, other, share, serve, f, e, own, n, energy, decay,
            pair, sk, contributions, b0, b1, c_held, c_rest,
        )

    send, base, f2 = middle(False, send, [wide_block, q_rows, k_rows], f, e0, f1, n, sp)
    send, n2, e2, f3 = middle(
        True, send, [block4, q_rows, k_rows, k_rows], f2, e0, f2, base, sp4
    )
    recv = exchange(send)
    b0, b1 = back(f3, gk, coupling)
    send, p2, n3, far = call(
        functools.partial(phonon_kernel, kb),
        "phonon",
        [block8, q_rows, q_rows, ((tiles, 128), f32)],
    )(recv, n2, energy, decay, pair, st4, sp8, s8, b0, b1)
    recv = exchange(send)
    f, n = call(
        last_kernel,
        "last",
        [k_rows, q_rows],
        forward_streams + sums,
        spaces={15: pltpu.HBM},
        **work,
    )(
        recv, far, f2, f3, e2, n2, n3, p2, energy, decay,
        gp8, sk, st8a, st8b, c_held, c_rest,
    )
    return (f, n)


def solution(mesh):
    placed = (
        P(("groups", "bulk"), None),
        P(("groups", "bulk"), None),
        P("bulk", None),
        P("bulk", None),
        P("bulk", None, None),
        P("bulk"),
        P("bulk"),
        P("bulk"),
        P("bulk"),
        P("bulk", None),
        P("bulk", None),
    )
    return jax.shard_map(
        on_device,
        mesh=mesh,
        in_specs=placed,
        out_specs=(P(("groups", "bulk"), None), P(("groups", "bulk"), None)),
        check_vma=False,
    )
```

```python
import functools

import jax
import jax.numpy as jnp
from jax import lax
from jax.experimental import pallas as pl
from jax.experimental.pallas import tpu as pltpu
from jax.sharding import PartitionSpec as P

DT = 0.05
CHUNKS = 8
HELD_CHUNKS = 2
f32 = jnp.float32
bf16 = jnp.bfloat16
VMEM_LIMIT = 48 * 1024 * 1024


def iota(shape, dim):
    return lax.broadcasted_iota(jnp.int32, shape, dim)


def dot(a, b):
    return lax.dot_general(a, b, (((1,), (0,)), ((), ())), preferred_element_type=f32)


def split(x):
    hi = x.astype(bf16)
    rest = x - hi.astype(f32)
    mid = rest.astype(bf16)
    lo = (rest - mid.astype(f32)).astype(bf16)
    return hi, mid, lo


def pick(onehot, x):
    hi, mid, lo = split(x)
    both = dot(onehot, jnp.concatenate([hi, mid], axis=1))
    return both[:, :128] + both[:, 128:] + dot(onehot, lo)


def add_rows(onehot, x):
    hi = x.astype(bf16)
    mid = (x - hi.astype(f32)).astype(bf16)
    both = dot(onehot, jnp.concatenate([hi, mid], axis=1))
    return both[:, :128] + both[:, 128:]


def gather_pair(table, x):
    rows = x.shape[0]
    hi = x.astype(bf16)
    mid = (x - hi.astype(f32)).astype(bf16)
    blank = jnp.zeros((rows, 128), bf16)

    def both(part):
        upper = jnp.concatenate([part, blank], axis=1)
        lower = jnp.concatenate([blank, part], axis=1)
        return dot(table, jnp.concatenate([upper, lower], axis=0))

    res = both(hi) + both(mid)
    return res[:, :128], res[:, 128:]


def stacked(first, second):
    tiles = first.shape[0]
    return jnp.concatenate(
        [first.reshape(tiles // 8, 8, 128), second.reshape(tiles // 8, 8, 128)], axis=1
    ).astype(bf16)


def row_is(r):
    return iota((16, 128), 0) % 8 == r


def padded(*parts):
    rows = sum(p.shape[0] for p in parts)
    return jnp.concatenate([*parts, jnp.zeros((128 - rows, 128), f32)], axis=0)


def flat(ref):
    return ref[...].reshape(-1, 128)


def chunk_copy(src, dst, sems, i):
    size = src.shape[0] // sems.shape[0]
    here = pl.ds(i * size, size)
    return pltpu.make_async_copy(src.at[here], dst.at[here], sems.at[i])


def start_chunks(src, dst, sems):
    for i in range(sems.shape[0]):
        chunk_copy(src, dst, sems, i).start()


def start(copies):
    for copy in copies:
        copy.start()


def block_diagonal(w):
    w = w.astype(f32)
    return jnp.concatenate(
        [jnp.where(row_is(r), w, 0.0).astype(bf16) for r in range(8)], axis=1
    )


def left_sides(first, second, w_ref):
    w = stacked(first, second)
    for g in range(w.shape[0]):
        w_ref[g] = block_diagonal(w[g])


def chunk_products(w_ref, c_ref, i, base, out0, out1):
    size = w_ref.shape[0] // CHUNKS
    for k in range(size):
        g = i * size + k
        res = dot(w_ref[base + g], c_ref[pl.ds(g * 8, 8)].reshape(1024, 128))
        out0[base + g] = res[:8]
        out1[base + g] = res[8:]


def tile_products(w_ref, parts, out0, out1):
    size = w_ref.shape[0] // CHUNKS
    base = 0
    for c_ref, c_hbm, sems in parts:
        chunks = c_ref.shape[0] // 8 // size

        def chunk(i, _):
            if c_hbm is not None:
                chunk_copy(c_hbm, c_ref, sems, i).wait()
            chunk_products(w_ref, c_ref, i, base, out0, out1)
            return 0

        lax.fori_loop(0, chunks, chunk, 0)
        base += chunks * size


def backward_pass(own, c_hbm, c_ref, sems, w_ref, out0, out1):
    left_sides(1.0 - own, own, w_ref)
    tile_products(w_ref, [(c_ref, c_hbm, sems)], out0, out1)


def electron_rate(sum_k, far, bose, f, parts, w_ref, o0, o1):
    left_sides(far * (1.0 + bose), far + bose, w_ref)
    tile_products(w_ref, parts, o0, o1)
    return add_rows(sum_k, flat(o0)) - f * add_rows(sum_k, flat(o1))


def my_core():
    return lax.rem(lax.axis_index("bulk"), 2)


def place_of(chip, chips):
    return (chip + chips - chips // 2) % chips


def block_of(peer, peers):
    chips = peers // 2
    return place_of(peer // 2, chips) + jnp.where(peer % 2 == my_core(), 0, chips)


def to_wire(rows, send):
    half = rows.shape[0] // 4 * 2
    send[: rows.shape[0] - half] = rows[half:]
    send[rows.shape[0] - half :] = rows[:half]


def from_wire(recv):
    half = recv.shape[0] // 4 * 2
    return jnp.concatenate([recv[recv.shape[0] - half :], recv[: recv.shape[0] - half]], axis=0)


def need_kernel(cap, *refs):
    ins, outs = refs[:9], refs[9:]
    *small, pneed_ref, qneed_ref, send_ref, sems = outs
    copies = [
        pltpu.make_async_copy(src, dst, sems.at[i])
        for i, (src, dst) in enumerate(zip(ins, [*small, pneed_ref, qneed_ref]))
    ]
    start(copies)
    slots = pneed_ref.shape[1]
    step = send_ref.shape[0] // (slots // cap // 2)
    for copy in copies:
        copy.wait()
    f, n = small[0][...], small[1][...]
    own_p, own_q = pneed_ref[...].astype(f32), qneed_ref[...].astype(f32)
    row = iota((8, slots), 0)
    lists = jnp.where(row == 0, own_p, jnp.where(row == 1, own_q, 0.0))
    if slots < 128:
        lists = jnp.concatenate([lists, jnp.zeros((8, 128 - slots), f32)], axis=1)
    block = jnp.concatenate([f, n, lists], axis=0)
    for chip in range(slots // cap // 2):
        send_ref[chip * step : (chip + 1) * step] = block


def prepare_kernel(
    cap,
    count_ref,
    kblock_ref,
    partner_ref,
    qslot_ref,
    f_ref,
    pneed_ref,
    qneed_ref,
    c_hbm,
    held_ref,
    t_hbm,
    pair_ref,
    gp8_ref,
    gk_ref,
    sk_ref,
    sp_ref,
    sp4_ref,
    sp8_ref,
    near_ref,
    list_ref,
    mine_ref,
    b0_ref,
    b1_ref,
    w_ref,
    c_ref,
    in_sems,
    t_ref,
    out_sems,
):
    start_chunks(c_hbm, c_ref, in_sems)
    tiles = kblock_ref.shape[1]
    kb = f_ref.shape[0]
    used = iota((1, tiles), 1) < count_ref[0]
    k = kblock_ref[...]
    e = partner_ref[...]
    q = qslot_ref[...]
    rows4 = sp4_ref.shape[0]
    rows8 = sp8_ref.shape[0]
    ind = lambda m: jnp.where(m, 1.0, 0.0)
    k_hot = ind(iota((kb, tiles), 0) == k)
    gk_ref[...] = k_hot.T.astype(bf16)
    own = add_rows(gk_ref[...], f_ref[...])
    left_sides(1.0 - own, own, w_ref)
    sk_ref[...] = jnp.where(used, k_hot, 0.0).astype(bf16)
    x = iota((rows4, tiles), 0)
    row_e = (e // cap) * (2 * cap) + e % cap
    row_p = (q // cap) * (2 * cap) + cap + q % cap
    p_hot = ind(x == row_p)
    pair_ref[...] = jnp.concatenate([ind(x == row_e), p_hot], axis=0).T.astype(bf16)
    sp4_ref[...] = jnp.where(used, p_hot, 0.0).astype(bf16)
    sp_ref[...] = jnp.where(used, ind(iota(sp_ref.shape, 0) == q), 0.0).astype(bf16)
    x = iota((rows8, tiles), 0)
    row_z = (q // cap) * (4 * cap) + q % cap
    gp8_ref[...] = ind(x == row_z).T.astype(bf16)
    sp8_ref[...] = jnp.concatenate(
        [
            jnp.where(used, ind(x == row_z + cap), 0.0),
            jnp.where(used, ind(x == row_z + 2 * cap), 0.0),
        ],
        axis=1,
    ).astype(bf16)

    rows, half = list_ref.shape
    slots = pneed_ref.shape[1]
    peers = slots // cap
    x = iota((rows, slots), 0)
    y = iota((rows, slots), 1)
    peer, r = x // (2 * cap), x % (2 * cap)
    e_here = (r < cap) & (y == peer * cap + r)
    p_here = (r >= cap) & (y == peer * cap + r - cap)
    pn = jnp.broadcast_to(pneed_ref[...].astype(f32), (rows, slots))
    qn = jnp.broadcast_to(qneed_ref[...].astype(f32), (rows, slots)) + float(kb)
    col = jnp.sum(jnp.where(e_here, pn, 0.0) + jnp.where(p_here, qn, 0.0), axis=1, keepdims=True)
    mine_ref[...] = jnp.broadcast_to(col, (rows, 128))
    start_of = block_of(iota((rows, 1), 0) // (2 * cap), peers) * (2 * half // peers)
    place = col + start_of.astype(f32)
    lane = iota((rows, half), 1).astype(f32)
    near_ref[...] = ind(lane == place).astype(bf16)
    list_ref[...] = ind(lane + float(half) == place).astype(bf16)

    size = c_ref.shape[0] // CHUNKS
    held = held_ref.shape[0] // size

    def to_held(i, _):
        chunk_copy(c_hbm, c_ref, in_sems, i).wait()
        chunk_products(w_ref, c_ref, i, 0, b0_ref, b1_ref)
        for t in range(size):
            held_ref[i * size + t] = c_ref[i * size + t].T
        return 0

    def to_rest(i, _):
        chunk_copy(c_hbm, c_ref, in_sems, held + i).wait()
        chunk_products(w_ref, c_ref, held + i, 0, b0_ref, b1_ref)
        for t in range(size):
            t_ref[i * size + t] = c_ref[(held + i) * size + t].T
        chunk_copy(t_ref, t_hbm, out_sems, i).start()
        return 0

    lax.fori_loop(0, held, to_held, 0)
    lax.fori_loop(0, out_sems.shape[0], to_rest, 0)
    for i in range(out_sems.shape[0]):
        chunk_copy(t_ref, t_hbm, out_sems, i).wait()


def blocks(ref, count_of_blocks, first, count):
    step = ref.shape[0] // count_of_blocks
    parts = [ref[b * step + first : b * step + first + count] for b in range(count_of_blocks)]
    return jnp.concatenate(parts, axis=0)


def serve_kernel(
    cap,
    kb,
    qb,
    asked_ref,
    hot_ref,
    mine_ref,
    share_ref,
    s8_ref,
    st4_ref,
    st8a_ref,
    st8b_ref,
):
    hot = hot_ref[...]
    rows4, rows8 = hot.shape[0], s8_ref.shape[0]
    x = iota((rows8, rows4), 0)
    y = iota((rows8, rows4), 1)
    peer, r = x // (4 * cap), x % (4 * cap)
    source = peer * (2 * cap) + cap + r % cap

    def rows_of(kind):
        here = (y == source) & (r // cap == kind)
        return dot(jnp.where(here, 1.0, 0.0).astype(bf16), hot)

    s8_ref[...] = rows_of(0).astype(bf16)
    st4_ref[...] = hot.astype(f32).T[kb : kb + qb].astype(bf16)
    st8a_ref[...] = rows_of(1).T[kb : kb + qb].astype(bf16)
    st8b_ref[...] = rows_of(2).T[kb : kb + qb].astype(bf16)

    peers = rows4 // (2 * cap)
    slots = peers * cap
    wide = peers * slots
    lists = asked_ref[...]
    pick_q = iota((peers, 8 * peers), 1) == 8 * iota((peers, 8 * peers), 0) + 1
    every_q = dot(jnp.where(pick_q, 1.0, 0.0).astype(bf16), lists).astype(bf16)
    tiled = iota((128, wide), 0) == iota((128, wide), 1) % slots
    spread = dot(every_q, jnp.where(tiled, 1.0, 0.0).astype(bf16))
    lane = iota((1, wide), 1)
    here = iota((peers, wide), 0) == lane // slots
    q = jnp.sum(jnp.where(here, spread, 0.0), axis=0, keepdims=True)
    ids = q + (lane % slots // cap * qb).astype(f32)
    row = iota((rows4, 1), 0)
    col = mine_ref[...][:, :1]
    my_ids = col - float(kb) + (row // (2 * cap) * qb).astype(f32)
    my_ids = jnp.where(row % (2 * cap) >= cap, my_ids, -1.0)
    owned = (lax.axis_index("bulk") * qb + iota((qb, 1), 0)).astype(f32)
    wanted = jnp.concatenate([my_ids, owned], axis=0)
    share_ref[...] = jnp.where(ids == wanted, 1.0, 0.0).astype(bf16)


def thermal_of(energy_ref):
    return 1.0 / (jnp.exp(energy_ref[...]) - 1.0)


def put_broadcast(send, served, contributions):
    slots = contributions.shape[0]
    chips = served.shape[0] // 8
    for chip in range(chips):
        at = place_of(chip, chips) * (8 + slots)
        send[at : at + 8] = served[chip * 8 : chip * 8 + 8]
        send[at + 8 : at + 8 + slots] = contributions


def phonon_terms(far, bose, b0_ref, b1_ref):
    gain = far * flat(b0_ref)
    return gain + bose * (gain - (1.0 - far) * flat(b1_ref))


def near_rows_kernel(same_ref, list_ref, part_ref):
    part_ref[...] = add_rows(list_ref[...], same_ref[...])


def half_of_devices(cap, chips, weight, others, ref, share_ref):
    rows4 = 4 * cap * chips
    wide = share_ref.shape[1] // 2
    x = iota((rows4, 8 * chips), 0)
    peer = x // (2 * cap)
    source = 8 * place_of(peer // 2, chips) + 2 * cap * my_core() + x % (2 * cap)
    wanted_core = (my_core() + others) % 2
    at = (iota((rows4, 8 * chips), 1) == source) & (peer % 2 == wanted_core)
    heads = add_rows(jnp.where(at, 1.0, 0.0).astype(bf16), blocks(ref, chips, 0, 8))
    tails = blocks(ref, chips, 8, wide // chips)
    sums = add_rows(share_ref[:, others * wide : (others + 1) * wide], tails)
    return heads + weight * sums[:rows4], sums[rows4:]


def near_half_kernel(cap, chips, weight, same_ref, share_ref, part_ref, total_ref):
    part, total = half_of_devices(cap, chips, weight, 0, same_ref, share_ref)
    part_ref[...] = part
    total_ref[...] = total


def first_kernel(
    cap,
    same_ref,
    other_ref,
    part_ref,
    list_ref,
    f_ref,
    n_ref,
    energy_ref,
    decay_ref,
    pair_ref,
    sk_ref,
    sp_ref,
    b0_ref,
    b1_ref,
    held_ref,
    c_hbm,
    send,
    e_ref,
    f1_ref,
    hot_ref,
    asked_ref,
    w_ref,
    c_ref,
    sems,
    o0,
    o1,
):
    start_chunks(c_hbm, c_ref, sems)
    f, n = f_ref[...], n_ref[...]
    kb, qb = f.shape[0], n.shape[0]
    rows4 = list_ref.shape[0]
    peers = rows4 // (2 * cap)
    got = part_ref[...] + add_rows(list_ref[...], other_ref[...])
    far, bose = gather_pair(pair_ref[...], got)
    contributions = add_rows(sp_ref[...], phonon_terms(far, bose, b0_ref, b1_ref))
    lists = jnp.concatenate(
        [blocks(ref, peers // 2, kb + qb, 8) for ref in (same_ref, other_ref)], axis=0
    ).astype(bf16)
    asked_ref[...] = lists
    x = iota((rows4, 8 * peers), 0)
    r = x % (2 * cap)
    kind = jnp.where(r < cap, 0, 1)
    at = iota((rows4, 8 * peers), 1) == 8 * block_of(x // (2 * cap), peers) + kind
    asked = dot(jnp.where(at, 1.0, 0.0).astype(bf16), lists)
    r = iota((rows4, 128), 0) % (2 * cap)
    lane = iota((rows4, 128), 1)
    wanted = lane == lax.axis_index("bulk") * cap + r % cap
    col = jnp.sum(jnp.where(wanted, asked, 0.0), axis=1, keepdims=True)
    col = col + jnp.where(r[:, :1] < cap, 0.0, float(kb))
    hot = jnp.where(lane.astype(f32) == col, 1.0, 0.0).astype(bf16)
    hot_ref[...] = hot
    base = n - DT * decay_ref[...] * (n - thermal_of(energy_ref))
    parts = [(held_ref, None, None), (c_ref, c_hbm, sems)]
    rate = electron_rate(sk_ref[...], far, bose, f, parts, w_ref, o0, o1)
    f1 = f + DT * rate
    e_ref[...] = rate
    f1_ref[...] = f1
    put_broadcast(send, pick(hot, padded(f1, base)), contributions)


def middle_kernel(
    cap,
    ends,
    part_ref,
    total_ref,
    other_ref,
    share_ref,
    serve_ref,
    f_ref,
    e_ref,
    own_ref,
    n_ref,
    energy_ref,
    decay_ref,
    pair_ref,
    sk_ref,
    sp_ref,
    b0_ref,
    b1_ref,
    held_ref,
    c_hbm,
    send,
    *refs,
):
    w_ref, c_ref, sems, o0, o1 = refs[-5:]
    start_chunks(c_hbm, c_ref, sems)
    chips = serve_ref.shape[0] // (4 * cap)
    weight = DT / 2.0 if ends else DT
    part, total = half_of_devices(cap, chips, weight, 1, other_ref, share_ref)
    got = part_ref[...] + part
    total = total_ref[...] + total
    far, bose = gather_pair(pair_ref[...], got)
    terms = phonon_terms(far, bose, b0_ref, b1_ref)
    contributions = add_rows(sp_ref[...], terms)
    n = n_ref[...]
    own = own_ref[...]
    parts = [(held_ref, None, None), (c_ref, c_hbm, sems)]
    if ends:
        n2_ref, e2_ref, f3_ref = refs[:3]
        n2_ref[...] = n + (DT / 2.0) * total
        rate = electron_rate(sk_ref[...], far, bose, own, parts, w_ref, o0, o1)
        f3 = own + DT * rate
        e2_ref[...] = rate
        f3_ref[...] = f3
        to_wire(pick(serve_ref[...], padded(f3)) + contributions, send)
    else:
        base_ref, f2_ref = refs[:2]
        thermal = thermal_of(energy_ref)
        decay = decay_ref[...]
        p0 = total - decay * (n - thermal)
        n1 = n + DT * p0
        base = n + (DT / 2.0) * (p0 - decay * (n1 - thermal))
        base_ref[...] = base
        rate = electron_rate(sk_ref[...], far, bose, own, parts, w_ref, o0, o1)
        f2 = f_ref[...] + (DT / 2.0) * (e_ref[...] + rate)
        f2_ref[...] = f2
        put_broadcast(send, pick(serve_ref[...], padded(f2, base)), contributions)


def backward_kernel(f_ref, gk_ref, c_hbm, b0_ref, b1_ref, w_ref, c_ref, sems):
    start_chunks(c_hbm, c_ref, sems)
    own = add_rows(gk_ref[...], f_ref[...])
    backward_pass(own, c_hbm, c_ref, sems, w_ref, b0_ref, b1_ref)


def phonon_kernel(
    kb,
    recv,
    n_ref,
    energy_ref,
    decay_ref,
    pair_ref,
    st4_ref,
    sp8_ref,
    s8_ref,
    b0_ref,
    b1_ref,
    send,
    p_ref,
    n1_ref,
    far_ref,
):
    n = n_ref[...]
    got = from_wire(recv)
    thermal = thermal_of(energy_ref)
    rate = add_rows(st4_ref[...], got) - decay_ref[...] * (n - thermal)
    n1 = n + DT * rate
    p_ref[...] = rate
    n1_ref[...] = n1
    far = add_rows(pair_ref[:, : got.shape[0]], got)
    far_ref[...] = far
    gain = far * flat(b0_ref)
    both = jnp.concatenate([gain, gain - (1.0 - far) * flat(b1_ref)], axis=0)
    state = padded(jnp.zeros((kb, 128), f32), n1)
    to_wire(pick(s8_ref[...], state) + add_rows(sp8_ref[...], both), send)


def last_kernel(recv, *refs):
    far_ref, f_ref, f1_ref, e_ref, n_ref, n1_ref, p_ref, energy_ref, decay_ref = refs[:9]
    gp8_ref, sk_ref, st8a_ref, st8b_ref, held_ref, c_hbm = refs[9:15]
    refs = refs[15:]
    f2_ref, n2_ref, w_ref, c_ref, sems, o0, o1 = refs
    start_chunks(c_hbm, c_ref, sems)
    got = from_wire(recv)
    n, n1 = n_ref[...], n1_ref[...]
    bose = add_rows(gp8_ref[...], got)
    thermal = thermal_of(energy_ref)
    p1 = (
        add_rows(st8a_ref[...], got)
        + n1 * add_rows(st8b_ref[...], got)
        - decay_ref[...] * (n1 - thermal)
    )
    n2 = n + (DT / 2.0) * (p_ref[...] + p1)
    n2_ref[...] = n2
    parts = [(held_ref, None, None), (c_ref, c_hbm, sems)]
    rate = electron_rate(sk_ref[...], far_ref[...], bose, f1_ref[...], parts, w_ref, o0, o1)
    f2 = f_ref[...] + (DT / 2.0) * (e_ref[...] + rate)
    f2_ref[...] = f2


def call(kernel, name, outs, scratch=(), spaces=None, out_spaces=None, flops=0, seen=0):
    def run(*args):
        places = dict(spaces or {})
        args = [
            pltpu.with_memory_space_constraint(x, pltpu.HBM)
            if places.get(i) is pltpu.HBM
            else x
            for i, x in enumerate(args)
        ]
        specs = [
            pl.BlockSpec(memory_space=places.get(i, pltpu.VMEM)) for i in range(len(args))
        ]
        return pl.pallas_call(
            kernel,
            out_shape=[
                (out_spaces or {}).get(i, jax.ShapeDtypeStruct)(*o) for i, o in enumerate(outs)
            ],
            in_specs=specs,
            out_specs=[
                pl.BlockSpec(memory_space=(out_spaces or {}).get(i, pltpu.VMEM))
                for i in range(len(outs))
            ],
            scratch_shapes=list(scratch),
            compiler_params=pltpu.CompilerParams(vmem_limit_bytes=VMEM_LIMIT),
            cost_estimate=pl.CostEstimate(
                flops=flops, bytes_accessed=seen, transcendentals=0
            ),
            name=name,
        )(*args)

    return run


def on_device(
    electrons,
    phonons,
    phonon_energy,
    phonon_decay,
    coupling,
    tile_kblock,
    tile_partner,
    tile_qslot,
    tile_count,
    partner_need,
    phonon_need,
):
    devices = lax.axis_size("bulk")
    kb = electrons.shape[0]
    qb = phonons.shape[0]
    tiles = coupling.shape[0]
    cap = partner_need.shape[1] // devices
    assert cap == phonon_need.shape[1] // devices and kb + qb <= 128
    rows4 = devices * 2 * cap
    rows8 = devices * 4 * cap
    groups = tiles // 8
    held = HELD_CHUNKS * (tiles // CHUNKS)
    weights = pltpu.VMEM((groups, 16, 1024), bf16)
    streams = [weights, pltpu.VMEM(coupling.shape, bf16), pltpu.SemaphoreType.DMA((CHUNKS,))]
    rest = (tiles - held, 128, 128)
    rest_sems = pltpu.SemaphoreType.DMA((CHUNKS - HELD_CHUNKS,))
    forward_streams = [weights, pltpu.VMEM(rest, bf16), rest_sems]
    sums = [pltpu.VMEM((groups, 8, 128), f32)] * 2
    pass_out = [((groups, 8, 128), f32)] * 2
    block4 = ((rows4, 128), f32)
    block8 = ((rows8, 128), f32)

    work = dict(flops=2 * tiles * 16 * 128 * 128, seen=tiles * 128 * 128 * 2)

    def exchange(x):
        order = [[(i + devices // 4 * 2) % devices for i in range(devices)]]
        return lax.all_to_all(
            x, "bulk", split_axis=0, concat_axis=0, tiled=True, axis_index_groups=order
        )

    ints = ((1, tiles), jnp.int32)
    lists = ((1, partner_need.shape[1]), jnp.int32)
    small = [((kb, 128), f32)] + [((qb, 128), f32)] * 3 + [ints] * 3
    step_rows = kb + qb + 8
    slots = devices * cap
    wide = 8 + slots
    assert step_rows % 8 == 0 and slots % 8 == 0 and slots <= 128
    assert devices % 2 == 0 and cap == 2
    chips = devices // 2
    same_core = [
        [(i + chips // 2) % chips * 2 + core for i in range(chips)] for core in (0, 1)
    ]

    def to_chips(x):
        return lax.all_to_all(
            x, "bulk", split_axis=0, concat_axis=0, tiled=True, axis_index_groups=same_core
        )

    def between_cores(x):
        return lax.ppermute(x, "bulk", [(i, i ^ 1) for i in range(devices)])

    f, n, energy, decay, kblock, partner, qslot, pneed, qneed, send = call(
        functools.partial(need_kernel, cap),
        "need",
        small + [lists, lists, ((chips * step_rows, 128), f32)],
        [pltpu.SemaphoreType.DMA((9,))],
        spaces={i: pltpu.HBM for i in range(9)},
    )(
        electrons,
        phonons,
        phonon_energy,
        phonon_decay,
        tile_kblock.reshape(1, tiles),
        tile_partner.reshape(1, tiles),
        tile_qslot.reshape(1, tiles),
        partner_need,
        phonon_need,
    )
    same = to_chips(send)
    c_held, c_rest, pair, gp8, gk, sk, sp, sp4, sp8, near, far_picks, mine, b0, b1 = call(
        functools.partial(prepare_kernel, cap),
        "prepare",
        [
            ((held, 128, 128), bf16),
            (rest, bf16),
            ((tiles, 2 * rows4), bf16),
            ((tiles, rows8), bf16),
            ((tiles, kb), bf16),
            ((kb, tiles), bf16),
            ((slots, tiles), bf16),
            ((rows4, tiles), bf16),
            ((rows8, 2 * tiles), bf16),
            ((rows4, chips * step_rows), bf16),
            ((rows4, chips * step_rows), bf16),
            ((rows4, 128), f32),
        ]
        + pass_out,
        [*streams, pltpu.VMEM(rest, bf16), rest_sems],
        spaces={0: pltpu.SMEM, 7: pltpu.HBM},
        out_spaces={1: pltpu.HBM},
        **work,
    )(tile_count, kblock, partner, qslot, f, pneed, qneed, coupling)
    same, c_held, b0 = lax.optimization_barrier((same, c_held, b0))
    wide_block = ((chips * wide, 128), f32)
    k_rows, q_rows = ((kb, 128), f32), ((qb, 128), f32)
    forward_scratch = forward_streams + sums
    other = between_cores(same)
    (part,) = call(near_rows_kernel, "near_rows", [block4])(same, near)
    send, e0, f1, serve, asked = call(
        functools.partial(first_kernel, cap),
        "first",
        [wide_block, k_rows, k_rows, ((rows4, 128), bf16), ((8 * devices, 128), bf16)],
        forward_scratch,
        spaces={14: pltpu.HBM},
        **work,
    )(same, other, part, far_picks, f, n, energy, decay, pair, sk, sp, b0, b1, c_held, c_rest)
    share, s8, st4, st8a, st8b = call(
        functools.partial(serve_kernel, cap, kb, qb),
        "serve",
        [
            ((rows4 + qb, devices * slots), bf16),
            ((rows8, 128), bf16),
            ((qb, rows4), bf16),
            ((qb, rows8), bf16),
            ((qb, rows8), bf16),
        ],
    )(asked, serve, mine)
    back = call(backward_kernel, "backward", pass_out, streams, spaces={2: pltpu.HBM}, **work)

    def middle(ends, send, outs, f, e, own, n, contributions):
        same = to_chips(send)
        b0, b1 = back(own, gk, coupling)
        same, b0 = lax.optimization_barrier((same, b0))
        other = between_cores(same)
        weight = DT / 2.0 if ends else DT
        part, total = call(
            functools.partial(near_half_kernel, cap, chips, weight), "near_half", [block4, q_rows]
        )(same, share)
        return call(
            functools.partial(middle_kernel, cap, ends),
            "middle",
            outs,
            forward_scratch,
            spaces={17: pltpu.HBM},
            **work,
        )(
            part, total, other, share, serve, f, e, own, n, energy, decay,
            pair, sk, contributions, b0, b1, c_held, c_rest,
        )

    send, base, f2 = middle(False, send, [wide_block, q_rows, k_rows], f, e0, f1, n, sp)
    send, n2, e2, f3 = middle(
        True, send, [block4, q_rows, k_rows, k_rows], f2, e0, f2, base, sp4
    )
    recv = exchange(send)
    b0, b1 = back(f3, gk, coupling)
    send, p2, n3, far = call(
        functools.partial(phonon_kernel, kb),
        "phonon",
        [block8, q_rows, q_rows, ((tiles, 128), f32)],
    )(recv, n2, energy, decay, pair, st4, sp8, s8, b0, b1)
    recv = exchange(send)
    f, n = call(
        last_kernel,
        "last",
        [k_rows, q_rows],
        forward_streams + sums,
        spaces={15: pltpu.HBM},
        **work,
    )(
        recv, far, f2, f3, e2, n2, n3, p2, energy, decay,
        gp8, sk, st8a, st8b, c_held, c_rest,
    )
    return (f, n)


def solution(mesh):
    placed = (
        P(("groups", "bulk"), None),
        P(("groups", "bulk"), None),
        P("bulk", None),
        P("bulk", None),
        P("bulk", None, None),
        P("bulk"),
        P("bulk"),
        P("bulk"),
        P("bulk"),
        P("bulk", None),
        P("bulk", None),
    )
    return jax.shard_map(
        on_device,
        mesh=mesh,
        in_specs=placed,
        out_specs=(P(("groups", "bulk"), None), P(("groups", "bulk"), None)),
        check_vma=False,
    )
```

```python
import functools

import jax
import jax.numpy as jnp
from jax import lax
from jax.experimental import pallas as pl
from jax.experimental.pallas import tpu as pltpu
from jax.sharding import PartitionSpec as P

DT = 0.05
CHUNKS = 8
HELD_CHUNKS = 2
f32 = jnp.float32
bf16 = jnp.bfloat16
VMEM_LIMIT = 48 * 1024 * 1024


def iota(shape, dim):
    return lax.broadcasted_iota(jnp.int32, shape, dim)


def dot(a, b):
    return lax.dot_general(a, b, (((1,), (0,)), ((), ())), preferred_element_type=f32)


def add_rows(onehot, x):
    hi = x.astype(bf16)
    mid = (x - hi.astype(f32)).astype(bf16)
    both = dot(onehot, jnp.concatenate([hi, mid], axis=1))
    return both[:, :128] + both[:, 128:]


def gather_pair(table, x):
    rows = x.shape[0]
    hi = x.astype(bf16)
    mid = (x - hi.astype(f32)).astype(bf16)
    blank = jnp.zeros((rows, 128), bf16)

    def both(part):
        upper = jnp.concatenate([part, blank], axis=1)
        lower = jnp.concatenate([blank, part], axis=1)
        return dot(table, jnp.concatenate([upper, lower], axis=0))

    res = both(hi) + both(mid)
    return res[:, :128], res[:, 128:]


def stacked(first, second):
    tiles = first.shape[0]
    return jnp.concatenate(
        [first.reshape(tiles // 8, 8, 128), second.reshape(tiles // 8, 8, 128)], axis=1
    ).astype(bf16)


def row_is(r):
    return iota((16, 128), 0) % 8 == r


def padded(*parts):
    rows = sum(p.shape[0] for p in parts)
    return jnp.concatenate([*parts, jnp.zeros((128 - rows, 128), f32)], axis=0)


def flat(ref):
    return ref[...].reshape(-1, 128)


def chunk_copy(src, dst, sems, i):
    size = src.shape[0] // sems.shape[0]
    here = pl.ds(i * size, size)
    return pltpu.make_async_copy(src.at[here], dst.at[here], sems.at[i])


def start_chunks(src, dst, sems):
    for i in range(sems.shape[0]):
        chunk_copy(src, dst, sems, i).start()


def start(copies):
    for copy in copies:
        copy.start()


def block_diagonal(w):
    w = w.astype(f32)
    return jnp.concatenate(
        [jnp.where(row_is(r), w, 0.0).astype(bf16) for r in range(8)], axis=1
    )


def left_sides(first, second, w_ref):
    groups = w_ref.shape[0]
    w_ref[:, :, :128] = stacked(first, second)

    def spread(g, _):
        w_ref[g] = block_diagonal(w_ref[g, :, :128])
        return 0

    lax.fori_loop(0, groups, spread, 0, unroll=4)


def chunk_products(w_ref, c_ref, i, base, out0, out1):
    size = w_ref.shape[0] // CHUNKS
    for k in range(size):
        g = i * size + k
        res = dot(w_ref[base + g], c_ref[pl.ds(g * 8, 8)].reshape(1024, 128))
        out0[base + g] = res[:8]
        out1[base + g] = res[8:]


def tile_products(w_ref, parts, out0, out1):
    size = w_ref.shape[0] // CHUNKS
    base = 0
    for c_ref, c_hbm, sems in parts:
        chunks = c_ref.shape[0] // 8 // size

        def chunk(i, _):
            if c_hbm is not None:
                chunk_copy(c_hbm, c_ref, sems, i).wait()
            chunk_products(w_ref, c_ref, i, base, out0, out1)
            return 0

        lax.fori_loop(0, chunks, chunk, 0)
        base += chunks * size


def backward_pass(own, c_hbm, c_ref, sems, w_ref, out0, out1):
    left_sides(1.0 - own, own, w_ref)
    tile_products(w_ref, [(c_ref, c_hbm, sems)], out0, out1)


def electron_rate(sum_k, far, bose, f, parts, w_ref, o0, o1):
    left_sides(far * (1.0 + bose), far + bose, w_ref)
    tile_products(w_ref, parts, o0, o1)
    gain, loss = flat(o0), flat(o1)
    gain_hi, loss_hi = gain.astype(bf16), loss.astype(bf16)
    gain_lo = (gain - gain_hi.astype(f32)).astype(bf16)
    loss_lo = (loss - loss_hi.astype(f32)).astype(bf16)
    sums = dot(sum_k, jnp.concatenate([gain_hi, gain_lo, loss_hi, loss_lo], axis=1))
    return sums[:, :128] + sums[:, 128:256] - f * (sums[:, 256:384] + sums[:, 384:])


def my_core():
    return lax.rem(lax.axis_index("bulk"), 2)


def place_of(chip, chips):
    return (chip + chips - chips // 2) % chips


def block_of(peer, peers):
    chips = peers // 2
    return place_of(peer // 2, chips) + jnp.where(peer % 2 == my_core(), 0, chips)


def to_wire(rows, send):
    half = rows.shape[0] // 4 * 2
    send[: rows.shape[0] - half] = rows[half:]
    send[rows.shape[0] - half :] = rows[:half]


def from_wire(recv):
    half = recv.shape[0] // 4 * 2
    return jnp.concatenate([recv[recv.shape[0] - half :], recv[: recv.shape[0] - half]], axis=0)


def need_kernel(cap, *refs):
    ins, outs = refs[:9], refs[9:]
    *small, pneed_ref, qneed_ref, send_ref, sems = outs
    copies = [
        pltpu.make_async_copy(src, dst, sems.at[i])
        for i, (src, dst) in enumerate(zip(ins, [*small, pneed_ref, qneed_ref]))
    ]
    start(copies)
    slots = pneed_ref.shape[1]
    step = send_ref.shape[0] // (slots // cap // 2)
    for copy in copies:
        copy.wait()
    f, n = small[0][...], small[1][...]
    own_p, own_q = pneed_ref[...].astype(f32), qneed_ref[...].astype(f32)
    row = iota((8, slots), 0)
    lists = jnp.where(row == 0, own_p, jnp.where(row == 1, own_q, 0.0))
    if slots < 128:
        lists = jnp.concatenate([lists, jnp.zeros((8, 128 - slots), f32)], axis=1)
    block = jnp.concatenate([f, n, lists], axis=0)
    for chip in range(slots // cap // 2):
        send_ref[chip * step : (chip + 1) * step] = block


def prepare_kernel(
    cap,
    count_ref,
    kblock_ref,
    partner_ref,
    qslot_ref,
    f_ref,
    pneed_ref,
    qneed_ref,
    c_hbm,
    held_ref,
    t_hbm,
    pair_ref,
    gp8_ref,
    gk_ref,
    sk_ref,
    sp_ref,
    sp4_ref,
    sp8_ref,
    near_ref,
    list_ref,
    mine_ref,
    b0_ref,
    b1_ref,
    w_ref,
    c_ref,
    in_sems,
    t_ref,
    out_sems,
):
    start_chunks(c_hbm, c_ref, in_sems)
    tiles = kblock_ref.shape[1]
    kb = f_ref.shape[0]
    used = iota((1, tiles), 1) < count_ref[0]
    k = kblock_ref[...]
    e = partner_ref[...]
    q = qslot_ref[...]
    rows4 = sp4_ref.shape[0]
    rows8 = sp8_ref.shape[0]
    ind = lambda m: jnp.where(m, 1.0, 0.0)
    k_hot = ind(iota((kb, tiles), 0) == k)
    gk_ref[...] = k_hot.T.astype(bf16)
    own = add_rows(gk_ref[...], f_ref[...])
    left_sides(1.0 - own, own, w_ref)
    sk_ref[...] = jnp.where(used, k_hot, 0.0).astype(bf16)
    x = iota((rows4, tiles), 0)
    row_e = (e // cap) * (2 * cap) + e % cap
    row_p = (q // cap) * (2 * cap) + cap + q % cap
    p_hot = ind(x == row_p)
    pair_ref[...] = jnp.concatenate([ind(x == row_e), p_hot], axis=0).T.astype(bf16)
    sp4_ref[...] = jnp.where(used, p_hot, 0.0).astype(bf16)
    sp_ref[...] = jnp.where(used, ind(iota(sp_ref.shape, 0) == q), 0.0).astype(bf16)
    x = iota((rows8, tiles), 0)
    row_z = (q // cap) * (4 * cap) + q % cap
    gp8_ref[...] = ind(x == row_z).T.astype(bf16)
    sp8_ref[...] = jnp.concatenate(
        [
            jnp.where(used, ind(x == row_z + cap), 0.0),
            jnp.where(used, ind(x == row_z + 2 * cap), 0.0),
        ],
        axis=1,
    ).astype(bf16)

    rows, half = list_ref.shape
    slots = pneed_ref.shape[1]
    peers = slots // cap
    x = iota((rows, slots), 0)
    y = iota((rows, slots), 1)
    peer, r = x // (2 * cap), x % (2 * cap)
    e_here = (r < cap) & (y == peer * cap + r)
    p_here = (r >= cap) & (y == peer * cap + r - cap)
    pn = jnp.broadcast_to(pneed_ref[...].astype(f32), (rows, slots))
    qn = jnp.broadcast_to(qneed_ref[...].astype(f32), (rows, slots)) + float(kb)
    col = jnp.sum(jnp.where(e_here, pn, 0.0) + jnp.where(p_here, qn, 0.0), axis=1, keepdims=True)
    mine_ref[...] = jnp.broadcast_to(col, (rows, 128))
    start_of = block_of(iota((rows, 1), 0) // (2 * cap), peers) * (2 * half // peers)
    place = col + start_of.astype(f32)
    lane = iota((rows, half), 1).astype(f32)
    near_ref[...] = ind(lane == place).astype(bf16)
    list_ref[...] = ind(lane + float(half) == place).astype(bf16)

    size = c_ref.shape[0] // CHUNKS
    held = held_ref.shape[0] // size

    def to_held(i, _):
        chunk_copy(c_hbm, c_ref, in_sems, i).wait()
        chunk_products(w_ref, c_ref, i, 0, b0_ref, b1_ref)
        for t in range(size):
            held_ref[i * size + t] = c_ref[i * size + t].T
        return 0

    def to_rest(i, _):
        chunk_copy(c_hbm, c_ref, in_sems, held + i).wait()
        chunk_products(w_ref, c_ref, held + i, 0, b0_ref, b1_ref)
        for t in range(size):
            t_ref[i * size + t] = c_ref[(held + i) * size + t].T
        chunk_copy(t_ref, t_hbm, out_sems, i).start()
        return 0

    lax.fori_loop(0, held, to_held, 0)
    lax.fori_loop(0, out_sems.shape[0], to_rest, 0)
    for i in range(out_sems.shape[0]):
        chunk_copy(t_ref, t_hbm, out_sems, i).wait()


def blocks(ref, count_of_blocks, first, count):
    step = ref.shape[0] // count_of_blocks
    parts = [ref[b * step + first : b * step + first + count] for b in range(count_of_blocks)]
    return jnp.concatenate(parts, axis=0)


def serve_kernel(
    cap,
    kb,
    qb,
    asked_ref,
    hot_ref,
    mine_ref,
    share_ref,
    s8_ref,
    st4_ref,
    st8a_ref,
    st8b_ref,
):
    hot = hot_ref[...]
    rows4, rows8 = hot.shape[0], s8_ref.shape[0]
    x = iota((rows8, rows4), 0)
    y = iota((rows8, rows4), 1)
    peer, r = x // (4 * cap), x % (4 * cap)
    source = peer * (2 * cap) + cap + r % cap

    def rows_of(kind):
        here = (y == source) & (r // cap == kind)
        return dot(jnp.where(here, 1.0, 0.0).astype(bf16), hot)

    s8_ref[...] = rows_of(0).astype(bf16)
    st4_ref[...] = hot.astype(f32).T[kb : kb + qb].astype(bf16)
    st8a_ref[...] = rows_of(1).T[kb : kb + qb].astype(bf16)
    st8b_ref[...] = rows_of(2).T[kb : kb + qb].astype(bf16)

    peers = rows4 // (2 * cap)
    slots = peers * cap
    wide = peers * slots
    lists = asked_ref[...]
    pick_q = iota((peers, 8 * peers), 1) == 8 * iota((peers, 8 * peers), 0) + 1
    every_q = dot(jnp.where(pick_q, 1.0, 0.0).astype(bf16), lists).astype(bf16)
    tiled = iota((128, wide), 0) == iota((128, wide), 1) % slots
    spread = dot(every_q, jnp.where(tiled, 1.0, 0.0).astype(bf16))
    lane = iota((1, wide), 1)
    here = iota((peers, wide), 0) == lane // slots
    q = jnp.sum(jnp.where(here, spread, 0.0), axis=0, keepdims=True)
    ids = q + (lane % slots // cap * qb).astype(f32)
    row = iota((rows4, 1), 0)
    col = mine_ref[...][:, :1]
    my_ids = col - float(kb) + (row // (2 * cap) * qb).astype(f32)
    my_ids = jnp.where(row % (2 * cap) >= cap, my_ids, -1.0)
    owned = (lax.axis_index("bulk") * qb + iota((qb, 1), 0)).astype(f32)
    wanted = jnp.concatenate([my_ids, owned], axis=0)
    share_ref[...] = jnp.where(ids == wanted, 1.0, 0.0).astype(bf16)


def thermal_of(energy_ref):
    return 1.0 / (jnp.exp(energy_ref[...]) - 1.0)


def put_broadcast(send, served, contributions):
    slots = contributions.shape[0]
    chips = served.shape[0] // 8
    for chip in range(chips):
        at = place_of(chip, chips) * (8 + slots)
        send[at : at + 8] = served[chip * 8 : chip * 8 + 8]
        send[at + 8 : at + 8 + slots] = contributions


def phonon_terms(far, bose, b0_ref, b1_ref):
    gain = far * flat(b0_ref)
    return gain + bose * (gain - (1.0 - far) * flat(b1_ref))


def near_rows_kernel(same_ref, list_ref, part_ref):
    part_ref[...] = add_rows(list_ref[...], same_ref[...])


def half_of_devices(cap, chips, weight, others, ref, share_ref):
    rows4 = 4 * cap * chips
    wide = share_ref.shape[1] // 2
    x = iota((rows4, 8 * chips), 0)
    peer = x // (2 * cap)
    source = 8 * place_of(peer // 2, chips) + 2 * cap * my_core() + x % (2 * cap)
    wanted_core = (my_core() + others) % 2
    at = (iota((rows4, 8 * chips), 1) == source) & (peer % 2 == wanted_core)
    heads = add_rows(jnp.where(at, 1.0, 0.0).astype(bf16), blocks(ref, chips, 0, 8))
    tails = blocks(ref, chips, 8, wide // chips)
    sums = add_rows(share_ref[:, others * wide : (others + 1) * wide], tails)
    return heads + weight * sums[:rows4], sums[rows4:]


def near_half_kernel(cap, chips, weight, same_ref, share_ref, part_ref, total_ref):
    part, total = half_of_devices(cap, chips, weight, 0, same_ref, share_ref)
    part_ref[...] = part
    total_ref[...] = total


def first_kernel(
    cap,
    same_ref,
    other_ref,
    part_ref,
    list_ref,
    f_ref,
    n_ref,
    energy_ref,
    decay_ref,
    pair_ref,
    sk_ref,
    sp_ref,
    b0_ref,
    b1_ref,
    held_ref,
    c_hbm,
    send,
    e_ref,
    f1_ref,
    hot_ref,
    asked_ref,
    w_ref,
    c_ref,
    sems,
    o0,
    o1,
):
    start_chunks(c_hbm, c_ref, sems)
    f, n = f_ref[...], n_ref[...]
    kb, qb = f.shape[0], n.shape[0]
    rows4 = list_ref.shape[0]
    peers = rows4 // (2 * cap)
    got = part_ref[...] + add_rows(list_ref[...], other_ref[...])
    far, bose = gather_pair(pair_ref[...], got)
    contributions = add_rows(sp_ref[...], phonon_terms(far, bose, b0_ref, b1_ref))
    lists = jnp.concatenate(
        [blocks(ref, peers // 2, kb + qb, 8) for ref in (same_ref, other_ref)], axis=0
    ).astype(bf16)
    asked_ref[...] = lists
    x = iota((rows4, 8 * peers), 0)
    r = x % (2 * cap)
    kind = jnp.where(r < cap, 0, 1)
    at = iota((rows4, 8 * peers), 1) == 8 * block_of(x // (2 * cap), peers) + kind
    asked = dot(jnp.where(at, 1.0, 0.0).astype(bf16), lists)
    r = iota((rows4, 128), 0) % (2 * cap)
    lane = iota((rows4, 128), 1)
    wanted = lane == lax.axis_index("bulk") * cap + r % cap
    col = jnp.sum(jnp.where(wanted, asked, 0.0), axis=1, keepdims=True)
    col = col + jnp.where(r[:, :1] < cap, 0.0, float(kb))
    hot = jnp.where(lane.astype(f32) == col, 1.0, 0.0).astype(bf16)
    hot_ref[...] = hot
    base = n - DT * decay_ref[...] * (n - thermal_of(energy_ref))
    parts = [(held_ref, None, None), (c_ref, c_hbm, sems)]
    rate = electron_rate(sk_ref[...], far, bose, f, parts, w_ref, o0, o1)
    f1 = f + DT * rate
    e_ref[...] = rate
    f1_ref[...] = f1
    put_broadcast(send, add_rows(hot, padded(f1, base)), contributions)


def middle_kernel(
    cap,
    ends,
    part_ref,
    total_ref,
    other_ref,
    share_ref,
    serve_ref,
    f_ref,
    e_ref,
    own_ref,
    n_ref,
    energy_ref,
    decay_ref,
    pair_ref,
    sk_ref,
    sp_ref,
    b0_ref,
    b1_ref,
    held_ref,
    c_hbm,
    send,
    *refs,
):
    w_ref, c_ref, sems, o0, o1 = refs[-5:]
    start_chunks(c_hbm, c_ref, sems)
    chips = serve_ref.shape[0] // (4 * cap)
    weight = DT / 2.0 if ends else DT
    part, total = half_of_devices(cap, chips, weight, 1, other_ref, share_ref)
    got = part_ref[...] + part
    total = total_ref[...] + total
    far, bose = gather_pair(pair_ref[...], got)
    terms = phonon_terms(far, bose, b0_ref, b1_ref)
    contributions = add_rows(sp_ref[...], terms)
    n = n_ref[...]
    own = own_ref[...]
    parts = [(held_ref, None, None), (c_ref, c_hbm, sems)]
    if ends:
        n2_ref, e2_ref, f3_ref = refs[:3]
        n2_ref[...] = n + (DT / 2.0) * total
        rate = electron_rate(sk_ref[...], far, bose, own, parts, w_ref, o0, o1)
        f3 = own + DT * rate
        e2_ref[...] = rate
        f3_ref[...] = f3
        to_wire(add_rows(serve_ref[...], padded(f3)) + contributions, send)
    else:
        base_ref, f2_ref = refs[:2]
        thermal = thermal_of(energy_ref)
        decay = decay_ref[...]
        p0 = total - decay * (n - thermal)
        n1 = n + DT * p0
        base = n + (DT / 2.0) * (p0 - decay * (n1 - thermal))
        base_ref[...] = base
        rate = electron_rate(sk_ref[...], far, bose, own, parts, w_ref, o0, o1)
        f2 = f_ref[...] + (DT / 2.0) * (e_ref[...] + rate)
        f2_ref[...] = f2
        put_broadcast(send, add_rows(serve_ref[...], padded(f2, base)), contributions)


def backward_kernel(f_ref, gk_ref, c_hbm, b0_ref, b1_ref, w_ref, c_ref, sems):
    start_chunks(c_hbm, c_ref, sems)
    own = add_rows(gk_ref[...], f_ref[...])
    backward_pass(own, c_hbm, c_ref, sems, w_ref, b0_ref, b1_ref)


def phonon_kernel(
    kb,
    recv,
    n_ref,
    energy_ref,
    decay_ref,
    pair_ref,
    st4_ref,
    sp8_ref,
    s8_ref,
    b0_ref,
    b1_ref,
    send,
    p_ref,
    n1_ref,
    far_ref,
):
    n = n_ref[...]
    got = from_wire(recv)
    thermal = thermal_of(energy_ref)
    rate = add_rows(st4_ref[...], got) - decay_ref[...] * (n - thermal)
    n1 = n + DT * rate
    p_ref[...] = rate
    n1_ref[...] = n1
    far = add_rows(pair_ref[:, : got.shape[0]], got)
    far_ref[...] = far
    gain = far * flat(b0_ref)
    both = jnp.concatenate([gain, gain - (1.0 - far) * flat(b1_ref)], axis=0)
    state = padded(jnp.zeros((kb, 128), f32), n1)
    to_wire(add_rows(s8_ref[...], state) + add_rows(sp8_ref[...], both), send)


def last_kernel(recv, *refs):
    far_ref, f_ref, f1_ref, e_ref, n_ref, n1_ref, p_ref, energy_ref, decay_ref = refs[:9]
    gp8_ref, sk_ref, st8a_ref, st8b_ref, held_ref, c_hbm = refs[9:15]
    refs = refs[15:]
    f2_ref, n2_ref, w_ref, c_ref, sems, o0, o1 = refs
    start_chunks(c_hbm, c_ref, sems)
    got = from_wire(recv)
    n, n1 = n_ref[...], n1_ref[...]
    bose = add_rows(gp8_ref[...], got)
    thermal = thermal_of(energy_ref)
    p1 = (
        add_rows(st8a_ref[...], got)
        + n1 * add_rows(st8b_ref[...], got)
        - decay_ref[...] * (n1 - thermal)
    )
    n2 = n + (DT / 2.0) * (p_ref[...] + p1)
    n2_ref[...] = n2
    parts = [(held_ref, None, None), (c_ref, c_hbm, sems)]
    rate = electron_rate(sk_ref[...], far_ref[...], bose, f1_ref[...], parts, w_ref, o0, o1)
    f2 = f_ref[...] + (DT / 2.0) * (e_ref[...] + rate)
    f2_ref[...] = f2


def call(kernel, name, outs, scratch=(), spaces=None, out_spaces=None, flops=0, seen=0):
    def run(*args):
        places = dict(spaces or {})
        args = [
            pltpu.with_memory_space_constraint(x, pltpu.HBM)
            if places.get(i) is pltpu.HBM
            else x
            for i, x in enumerate(args)
        ]
        specs = [
            pl.BlockSpec(memory_space=places.get(i, pltpu.VMEM)) for i in range(len(args))
        ]
        return pl.pallas_call(
            kernel,
            out_shape=[
                (out_spaces or {}).get(i, jax.ShapeDtypeStruct)(*o) for i, o in enumerate(outs)
            ],
            in_specs=specs,
            out_specs=[
                pl.BlockSpec(memory_space=(out_spaces or {}).get(i, pltpu.VMEM))
                for i in range(len(outs))
            ],
            scratch_shapes=list(scratch),
            compiler_params=pltpu.CompilerParams(vmem_limit_bytes=VMEM_LIMIT),
            cost_estimate=pl.CostEstimate(
                flops=flops, bytes_accessed=seen, transcendentals=0
            ),
            name=name,
        )(*args)

    return run


def on_device(
    electrons,
    phonons,
    phonon_energy,
    phonon_decay,
    coupling,
    tile_kblock,
    tile_partner,
    tile_qslot,
    tile_count,
    partner_need,
    phonon_need,
):
    devices = lax.axis_size("bulk")
    kb = electrons.shape[0]
    qb = phonons.shape[0]
    tiles = coupling.shape[0]
    cap = partner_need.shape[1] // devices
    assert cap == phonon_need.shape[1] // devices and kb + qb <= 128
    rows4 = devices * 2 * cap
    rows8 = devices * 4 * cap
    groups = tiles // 8
    held = HELD_CHUNKS * (tiles // CHUNKS)
    weights = pltpu.VMEM((groups, 16, 1024), bf16)
    streams = [weights, pltpu.VMEM(coupling.shape, bf16), pltpu.SemaphoreType.DMA((CHUNKS,))]
    rest = (tiles - held, 128, 128)
    rest_sems = pltpu.SemaphoreType.DMA((CHUNKS - HELD_CHUNKS,))
    forward_streams = [weights, pltpu.VMEM(rest, bf16), rest_sems]
    sums = [pltpu.VMEM((groups, 8, 128), f32)] * 2
    pass_out = [((groups, 8, 128), f32)] * 2
    block4 = ((rows4, 128), f32)
    block8 = ((rows8, 128), f32)

    work = dict(flops=2 * tiles * 16 * 128 * 128, seen=tiles * 128 * 128 * 2)

    def exchange(x):
        order = [[(i + devices // 4 * 2) % devices for i in range(devices)]]
        return lax.all_to_all(
            x, "bulk", split_axis=0, concat_axis=0, tiled=True, axis_index_groups=order
        )

    ints = ((1, tiles), jnp.int32)
    lists = ((1, partner_need.shape[1]), jnp.int32)
    small = [((kb, 128), f32)] + [((qb, 128), f32)] * 3 + [ints] * 3
    step_rows = kb + qb + 8
    slots = devices * cap
    wide = 8 + slots
    assert step_rows % 8 == 0 and slots % 8 == 0 and slots <= 128
    assert devices % 2 == 0 and cap == 2
    chips = devices // 2
    same_core = [
        [(i + chips // 2) % chips * 2 + core for i in range(chips)] for core in (0, 1)
    ]

    def to_chips(x):
        return lax.all_to_all(
            x, "bulk", split_axis=0, concat_axis=0, tiled=True, axis_index_groups=same_core
        )

    def between_cores(x):
        return lax.ppermute(x, "bulk", [(i, i ^ 1) for i in range(devices)])

    f, n, energy, decay, kblock, partner, qslot, pneed, qneed, send = call(
        functools.partial(need_kernel, cap),
        "need",
        small + [lists, lists, ((chips * step_rows, 128), f32)],
        [pltpu.SemaphoreType.DMA((9,))],
        spaces={i: pltpu.HBM for i in range(9)},
    )(
        electrons,
        phonons,
        phonon_energy,
        phonon_decay,
        tile_kblock.reshape(1, tiles),
        tile_partner.reshape(1, tiles),
        tile_qslot.reshape(1, tiles),
        partner_need,
        phonon_need,
    )
    same = to_chips(send)
    c_held, c_rest, pair, gp8, gk, sk, sp, sp4, sp8, near, far_picks, mine, b0, b1 = call(
        functools.partial(prepare_kernel, cap),
        "prepare",
        [
            ((held, 128, 128), bf16),
            (rest, bf16),
            ((tiles, 2 * rows4), bf16),
            ((tiles, rows8), bf16),
            ((tiles, kb), bf16),
            ((kb, tiles), bf16),
            ((slots, tiles), bf16),
            ((rows4, tiles), bf16),
            ((rows8, 2 * tiles), bf16),
            ((rows4, chips * step_rows), bf16),
            ((rows4, chips * step_rows), bf16),
            ((rows4, 128), f32),
        ]
        + pass_out,
        [*streams, pltpu.VMEM(rest, bf16), rest_sems],
        spaces={0: pltpu.SMEM, 7: pltpu.HBM},
        out_spaces={1: pltpu.HBM},
        **work,
    )(tile_count, kblock, partner, qslot, f, pneed, qneed, coupling)
    same, c_held, b0 = lax.optimization_barrier((same, c_held, b0))
    wide_block = ((chips * wide, 128), f32)
    k_rows, q_rows = ((kb, 128), f32), ((qb, 128), f32)
    forward_scratch = forward_streams + sums
    other = between_cores(same)
    (part,) = call(near_rows_kernel, "near_rows", [block4])(same, near)
    send, e0, f1, serve, asked = call(
        functools.partial(first_kernel, cap),
        "first",
        [wide_block, k_rows, k_rows, ((rows4, 128), bf16), ((8 * devices, 128), bf16)],
        forward_scratch,
        spaces={14: pltpu.HBM},
        **work,
    )(same, other, part, far_picks, f, n, energy, decay, pair, sk, sp, b0, b1, c_held, c_rest)
    share, s8, st4, st8a, st8b = call(
        functools.partial(serve_kernel, cap, kb, qb),
        "serve",
        [
            ((rows4 + qb, devices * slots), bf16),
            ((rows8, 128), bf16),
            ((qb, rows4), bf16),
            ((qb, rows8), bf16),
            ((qb, rows8), bf16),
        ],
    )(asked, serve, mine)
    back = call(backward_kernel, "backward", pass_out, streams, spaces={2: pltpu.HBM}, **work)

    def middle(ends, send, outs, f, e, own, n, contributions):
        same = to_chips(send)
        b0, b1 = back(own, gk, coupling)
        same, b0 = lax.optimization_barrier((same, b0))
        other = between_cores(same)
        weight = DT / 2.0 if ends else DT
        part, total = call(
            functools.partial(near_half_kernel, cap, chips, weight), "near_half", [block4, q_rows]
        )(same, share)
        return call(
            functools.partial(middle_kernel, cap, ends),
            "middle",
            outs,
            forward_scratch,
            spaces={17: pltpu.HBM},
            **work,
        )(
            part, total, other, share, serve, f, e, own, n, energy, decay,
            pair, sk, contributions, b0, b1, c_held, c_rest,
        )

    send, base, f2 = middle(False, send, [wide_block, q_rows, k_rows], f, e0, f1, n, sp)
    send, n2, e2, f3 = middle(
        True, send, [block4, q_rows, k_rows, k_rows], f2, e0, f2, base, sp4
    )
    recv = exchange(send)
    b0, b1 = back(f3, gk, coupling)
    send, p2, n3, far = call(
        functools.partial(phonon_kernel, kb),
        "phonon",
        [block8, q_rows, q_rows, ((tiles, 128), f32)],
    )(recv, n2, energy, decay, pair, st4, sp8, s8, b0, b1)
    recv = exchange(send)
    f, n = call(
        last_kernel,
        "last",
        [k_rows, q_rows],
        forward_streams + sums,
        spaces={15: pltpu.HBM},
        **work,
    )(
        recv, far, f2, f3, e2, n2, n3, p2, energy, decay,
        gp8, sk, st8a, st8b, c_held, c_rest,
    )
    return (f, n)


def solution(mesh):
    placed = (
        P(("groups", "bulk"), None),
        P(("groups", "bulk"), None),
        P("bulk", None),
        P("bulk", None),
        P("bulk", None, None),
        P("bulk"),
        P("bulk"),
        P("bulk"),
        P("bulk"),
        P("bulk", None),
        P("bulk", None),
    )
    return jax.shard_map(
        on_device,
        mesh=mesh,
        in_specs=placed,
        out_specs=(P(("groups", "bulk"), None), P(("groups", "bulk"), None)),
        check_vma=False,
    )
```

```python
import functools

import jax
import jax.numpy as jnp
from jax import lax
from jax.experimental import pallas as pl
from jax.experimental.pallas import tpu as pltpu
from jax.sharding import PartitionSpec as P

DT = 0.05
CHUNKS = 8
HELD_CHUNKS = 2
f32 = jnp.float32
bf16 = jnp.bfloat16
VMEM_LIMIT = 48 * 1024 * 1024


def iota(shape, dim):
    return lax.broadcasted_iota(jnp.int32, shape, dim)


def dot(a, b):
    return lax.dot_general(a, b, (((1,), (0,)), ((), ())), preferred_element_type=f32)


def add_rows(onehot, x):
    hi = x.astype(bf16)
    mid = (x - hi.astype(f32)).astype(bf16)
    both = dot(onehot, jnp.concatenate([hi, mid], axis=1))
    return both[:, :128] + both[:, 128:]


def gather_pair(table, x):
    rows = x.shape[0]
    hi = x.astype(bf16)
    mid = (x - hi.astype(f32)).astype(bf16)
    blank = jnp.zeros((rows, 128), bf16)

    def both(part):
        upper = jnp.concatenate([part, blank], axis=1)
        lower = jnp.concatenate([blank, part], axis=1)
        return dot(table, jnp.concatenate([upper, lower], axis=0))

    res = both(hi) + both(mid)
    return res[:, :128], res[:, 128:]


def stacked(first, second):
    tiles = first.shape[0]
    return jnp.concatenate(
        [first.reshape(tiles // 8, 8, 128), second.reshape(tiles // 8, 8, 128)], axis=1
    ).astype(bf16)


def row_is(r):
    return iota((16, 128), 0) % 8 == r


def padded(*parts):
    rows = sum(p.shape[0] for p in parts)
    return jnp.concatenate([*parts, jnp.zeros((128 - rows, 128), f32)], axis=0)


def flat(ref):
    return ref[...].reshape(-1, 128)


def chunk_copy(src, dst, sems, i):
    size = min(src.shape[0], dst.shape[0]) // sems.shape[0]
    here = pl.ds(i * size, size)
    return pltpu.make_async_copy(src.at[here], dst.at[here], sems.at[i])


def start_chunks(src, dst, sems):
    for i in range(sems.shape[0]):
        chunk_copy(src, dst, sems, i).start()


def start(copies):
    for copy in copies:
        copy.start()


def block_diagonal(w):
    w = w.astype(f32)
    return jnp.concatenate(
        [jnp.where(row_is(r), w, 0.0).astype(bf16) for r in range(8)], axis=1
    )


def left_sides(first, second, w_ref):
    groups = w_ref.shape[0]
    w_ref[:, :, :128] = stacked(first, second)

    def spread(g, _):
        w_ref[g] = block_diagonal(w_ref[g, :, :128])
        return 0

    lax.fori_loop(0, groups, spread, 0, unroll=4)


def chunk_products(w_ref, c_ref, i, base, out0, out1):
    size = w_ref.shape[0] // CHUNKS
    for k in range(size):
        g = i * size + k
        res = dot(w_ref[base + g], c_ref[pl.ds(g * 8, 8)].reshape(1024, 128))
        out0[base + g] = res[:8]
        out1[base + g] = res[8:]


def tile_products(w_ref, parts, out0, out1):
    size = w_ref.shape[0] // CHUNKS
    for c_ref, c_hbm, sems, base in parts:
        chunks = c_ref.shape[0] // 8 // size

        def chunk(i, _):
            if c_hbm is not None:
                chunk_copy(c_hbm, c_ref, sems, i).wait()
            chunk_products(w_ref, c_ref, i, base, out0, out1)
            return 0

        lax.fori_loop(0, chunks, chunk, 0)


def backward_pass(own, c_hbm, c_ref, sems, w_ref, out0, out1):
    left_sides(1.0 - own, own, w_ref)
    tile_products(w_ref, [(c_ref, c_hbm, sems, 0)], out0, out1)


def forward_parts(w_ref, held_ref, fetched_ref, c_ref, c_hbm, sems):
    first = w_ref.shape[0] - held_ref.shape[0] // 8
    parts = [(held_ref, None, None, first)]
    if fetched_ref is not None:
        parts.append((fetched_ref, None, None, first - fetched_ref.shape[0] // 8))
    return parts + [(c_ref, c_hbm, sems, 0)]


def electron_rate(sum_k, far, bose, f, parts, w_ref, o0, o1):
    left_sides(far * (1.0 + bose), far + bose, w_ref)
    tile_products(w_ref, parts, o0, o1)
    gain, loss = flat(o0), flat(o1)
    gain_hi, loss_hi = gain.astype(bf16), loss.astype(bf16)
    gain_lo = (gain - gain_hi.astype(f32)).astype(bf16)
    loss_lo = (loss - loss_hi.astype(f32)).astype(bf16)
    sums = dot(sum_k, jnp.concatenate([gain_hi, gain_lo, loss_hi, loss_lo], axis=1))
    return sums[:, :128] + sums[:, 128:256] - f * (sums[:, 256:384] + sums[:, 384:])


def my_core():
    return lax.rem(lax.axis_index("bulk"), 2)


def place_of(chip, chips):
    return (chip + chips - chips // 2) % chips


def block_of(peer, peers):
    chips = peers // 2
    return place_of(peer // 2, chips) + jnp.where(peer % 2 == my_core(), 0, chips)


def to_wire(rows, send):
    half = rows.shape[0] // 4 * 2
    send[: rows.shape[0] - half] = rows[half:]
    send[rows.shape[0] - half :] = rows[:half]


def from_wire(recv):
    half = recv.shape[0] // 4 * 2
    return jnp.concatenate([recv[recv.shape[0] - half :], recv[: recv.shape[0] - half]], axis=0)


def need_kernel(cap, *refs):
    ins, outs = refs[:9], refs[9:]
    *small, pneed_ref, qneed_ref, send_ref, sems = outs
    copies = [
        pltpu.make_async_copy(src, dst, sems.at[i])
        for i, (src, dst) in enumerate(zip(ins, [*small, pneed_ref, qneed_ref]))
    ]
    start(copies)
    slots = pneed_ref.shape[1]
    step = send_ref.shape[0] // (slots // cap // 2)
    for copy in copies:
        copy.wait()
    f, n = small[0][...], small[1][...]
    own_p, own_q = pneed_ref[...].astype(f32), qneed_ref[...].astype(f32)
    row = iota((8, slots), 0)
    lists = jnp.where(row == 0, own_p, jnp.where(row == 1, own_q, 0.0))
    if slots < 128:
        lists = jnp.concatenate([lists, jnp.zeros((8, 128 - slots), f32)], axis=1)
    block = jnp.concatenate([f, n, lists], axis=0)
    for chip in range(slots // cap // 2):
        send_ref[chip * step : (chip + 1) * step] = block


def prepare_kernel(
    cap,
    count_ref,
    kblock_ref,
    partner_ref,
    qslot_ref,
    f_ref,
    pneed_ref,
    qneed_ref,
    c_hbm,
    held_ref,
    t_hbm,
    pair_ref,
    gk_ref,
    sk_ref,
    sp_ref,
    sp4_ref,
    near_ref,
    list_ref,
    mine_ref,
    b0_ref,
    b1_ref,
    w_ref,
    c_ref,
    in_sems,
    t_ref,
    out_sems,
):
    start_chunks(c_hbm, c_ref, in_sems)
    tiles = kblock_ref.shape[1]
    kb = f_ref.shape[0]
    used = iota((1, tiles), 1) < count_ref[0]
    k = kblock_ref[...]
    e = partner_ref[...]
    q = qslot_ref[...]
    rows4 = sp4_ref.shape[0]
    ind = lambda m: jnp.where(m, 1.0, 0.0)
    k_hot = ind(iota((kb, tiles), 0) == k)
    gk_ref[...] = k_hot.T.astype(bf16)
    own = add_rows(gk_ref[...], f_ref[...])
    left_sides(1.0 - own, own, w_ref)
    sk_ref[...] = jnp.where(used, k_hot, 0.0).astype(bf16)
    x = iota((rows4, tiles), 0)
    row_e = (e // cap) * (2 * cap) + e % cap
    row_p = (q // cap) * (2 * cap) + cap + q % cap
    p_hot = ind(x == row_p)
    pair_ref[...] = jnp.concatenate([ind(x == row_e), p_hot], axis=0).T.astype(bf16)
    sp4_ref[...] = jnp.where(used, p_hot, 0.0).astype(bf16)
    sp_ref[...] = jnp.where(used, ind(iota(sp_ref.shape, 0) == q), 0.0).astype(bf16)
    rows, half = list_ref.shape
    slots = pneed_ref.shape[1]
    peers = slots // cap
    x = iota((rows, slots), 0)
    y = iota((rows, slots), 1)
    peer, r = x // (2 * cap), x % (2 * cap)
    e_here = (r < cap) & (y == peer * cap + r)
    p_here = (r >= cap) & (y == peer * cap + r - cap)
    pn = jnp.broadcast_to(pneed_ref[...].astype(f32), (rows, slots))
    qn = jnp.broadcast_to(qneed_ref[...].astype(f32), (rows, slots)) + float(kb)
    col = jnp.sum(jnp.where(e_here, pn, 0.0) + jnp.where(p_here, qn, 0.0), axis=1, keepdims=True)
    mine_ref[...] = jnp.broadcast_to(col, (rows, 128))
    start_of = block_of(iota((rows, 1), 0) // (2 * cap), peers) * (2 * half // peers)
    place = col + start_of.astype(f32)
    lane = iota((rows, half), 1).astype(f32)
    near_ref[...] = ind(lane == place).astype(bf16)
    list_ref[...] = ind(lane + float(half) == place).astype(bf16)

    size = c_ref.shape[0] // CHUNKS
    held = held_ref.shape[0] // size

    rest = CHUNKS - held

    def to_rest(i, _):
        chunk_copy(c_hbm, c_ref, in_sems, i).wait()
        chunk_products(w_ref, c_ref, i, 0, b0_ref, b1_ref)
        for t in range(size):
            t_ref[i * size + t] = c_ref[i * size + t].T
        chunk_copy(t_ref, t_hbm, out_sems, i).start()
        return 0

    def to_held(i, _):
        chunk_copy(c_hbm, c_ref, in_sems, rest + i).wait()
        chunk_products(w_ref, c_ref, rest + i, 0, b0_ref, b1_ref)
        for t in range(size):
            held_ref[i * size + t] = c_ref[(rest + i) * size + t].T
        return 0

    lax.fori_loop(0, rest, to_rest, 0)
    lax.fori_loop(0, held, to_held, 0)
    for i in range(rest):
        chunk_copy(t_ref, t_hbm, out_sems, i).wait()


def blocks(ref, count_of_blocks, first, count):
    step = ref.shape[0] // count_of_blocks
    parts = [ref[b * step + first : b * step + first + count] for b in range(count_of_blocks)]
    return jnp.concatenate(parts, axis=0)


def serve_kernel(
    cap,
    kb,
    qb,
    count_ref,
    qslot_ref,
    asked_ref,
    hot_ref,
    mine_ref,
    share_ref,
    gp8_ref,
    sp8_ref,
    s8_ref,
    st4_ref,
    st8a_ref,
    st8b_ref,
):
    hot = hot_ref[...]
    rows4, rows8 = hot.shape[0], s8_ref.shape[0]
    q = qslot_ref[...]
    tiles = q.shape[1]
    used = iota((1, tiles), 1) < count_ref[0]
    ind = lambda m: jnp.where(m, 1.0, 0.0)
    x = iota((rows8, tiles), 0)
    row_z = (q // cap) * (4 * cap) + q % cap
    gp8_ref[...] = ind(x == row_z).T.astype(bf16)
    sp8_ref[...] = jnp.concatenate(
        [
            jnp.where(used, ind(x == row_z + cap), 0.0),
            jnp.where(used, ind(x == row_z + 2 * cap), 0.0),
        ],
        axis=1,
    ).astype(bf16)
    x = iota((rows8, rows4), 0)
    y = iota((rows8, rows4), 1)
    peer, r = x // (4 * cap), x % (4 * cap)
    source = peer * (2 * cap) + cap + r % cap

    def rows_of(kind):
        here = (y == source) & (r // cap == kind)
        return dot(jnp.where(here, 1.0, 0.0).astype(bf16), hot)

    s8_ref[...] = rows_of(0).astype(bf16)
    st4_ref[...] = hot.astype(f32).T[kb : kb + qb].astype(bf16)
    st8a_ref[...] = rows_of(1).T[kb : kb + qb].astype(bf16)
    st8b_ref[...] = rows_of(2).T[kb : kb + qb].astype(bf16)

    peers = rows4 // (2 * cap)
    slots = peers * cap
    wide = peers * slots
    lists = asked_ref[...]
    pick_q = iota((peers, 8 * peers), 1) == 8 * iota((peers, 8 * peers), 0) + 1
    every_q = dot(jnp.where(pick_q, 1.0, 0.0).astype(bf16), lists).astype(bf16)
    tiled = iota((128, wide), 0) == iota((128, wide), 1) % slots
    spread = dot(every_q, jnp.where(tiled, 1.0, 0.0).astype(bf16))
    lane = iota((1, wide), 1)
    here = iota((peers, wide), 0) == lane // slots
    q = jnp.sum(jnp.where(here, spread, 0.0), axis=0, keepdims=True)
    ids = q + (lane % slots // cap * qb).astype(f32)
    row = iota((rows4, 1), 0)
    col = mine_ref[...][:, :1]
    my_ids = col - float(kb) + (row // (2 * cap) * qb).astype(f32)
    my_ids = jnp.where(row % (2 * cap) >= cap, my_ids, -1.0)
    owned = (lax.axis_index("bulk") * qb + iota((qb, 1), 0)).astype(f32)
    wanted = jnp.concatenate([my_ids, owned], axis=0)
    share_ref[...] = jnp.where(ids == wanted, 1.0, 0.0).astype(bf16)


def thermal_of(energy_ref):
    return 1.0 / (jnp.exp(energy_ref[...]) - 1.0)


def put_broadcast(send, served, contributions):
    slots = contributions.shape[0]
    chips = served.shape[0] // 8
    for chip in range(chips):
        at = place_of(chip, chips) * (8 + slots)
        send[at : at + 8] = served[chip * 8 : chip * 8 + 8]
        send[at + 8 : at + 8 + slots] = contributions


def phonon_terms(far, bose, b0_ref, b1_ref):
    gain = far * flat(b0_ref)
    return gain + bose * (gain - (1.0 - far) * flat(b1_ref))


def fetch_copy(c_hbm, fetched_ref, sem):
    count = fetched_ref.shape[0]
    return pltpu.make_async_copy(
        c_hbm.at[pl.ds(c_hbm.shape[0] - count, count)], fetched_ref, sem.at[0]
    )


def near_rows_kernel(same_ref, list_ref, c_hbm, part_ref, fetched_ref, sem):
    copy = fetch_copy(c_hbm, fetched_ref, sem)
    copy.start()
    part_ref[...] = add_rows(list_ref[...], same_ref[...])
    copy.wait()


def half_of_devices(cap, chips, weight, others, ref, share_ref):
    rows4 = 4 * cap * chips
    wide = share_ref.shape[1] // 2
    x = iota((rows4, 8 * chips), 0)
    peer = x // (2 * cap)
    source = 8 * place_of(peer // 2, chips) + 2 * cap * my_core() + x % (2 * cap)
    wanted_core = (my_core() + others) % 2
    at = (iota((rows4, 8 * chips), 1) == source) & (peer % 2 == wanted_core)
    heads = add_rows(jnp.where(at, 1.0, 0.0).astype(bf16), blocks(ref, chips, 0, 8))
    tails = blocks(ref, chips, 8, wide // chips)
    sums = add_rows(share_ref[:, others * wide : (others + 1) * wide], tails)
    return heads + weight * sums[:rows4], sums[rows4:]


def near_half_kernel(
    cap, chips, weight, same_ref, share_ref, c_hbm, part_ref, total_ref, fetched_ref, sem
):
    copy = fetch_copy(c_hbm, fetched_ref, sem)
    copy.start()
    part, total = half_of_devices(cap, chips, weight, 0, same_ref, share_ref)
    part_ref[...] = part
    total_ref[...] = total
    copy.wait()


def first_kernel(
    cap,
    same_ref,
    other_ref,
    part_ref,
    list_ref,
    f_ref,
    n_ref,
    energy_ref,
    decay_ref,
    pair_ref,
    sk_ref,
    sp_ref,
    b0_ref,
    b1_ref,
    held_ref,
    fetched_ref,
    c_hbm,
    send,
    e_ref,
    f1_ref,
    hot_ref,
    asked_ref,
    w_ref,
    c_ref,
    sems,
    o0,
    o1,
):
    start_chunks(c_hbm, c_ref, sems)
    f, n = f_ref[...], n_ref[...]
    kb, qb = f.shape[0], n.shape[0]
    rows4 = list_ref.shape[0]
    peers = rows4 // (2 * cap)
    got = part_ref[...] + add_rows(list_ref[...], other_ref[...])
    far, bose = gather_pair(pair_ref[...], got)
    contributions = add_rows(sp_ref[...], phonon_terms(far, bose, b0_ref, b1_ref))
    lists = jnp.concatenate(
        [blocks(ref, peers // 2, kb + qb, 8) for ref in (same_ref, other_ref)], axis=0
    ).astype(bf16)
    asked_ref[...] = lists
    x = iota((rows4, 8 * peers), 0)
    r = x % (2 * cap)
    kind = jnp.where(r < cap, 0, 1)
    at = iota((rows4, 8 * peers), 1) == 8 * block_of(x // (2 * cap), peers) + kind
    asked = dot(jnp.where(at, 1.0, 0.0).astype(bf16), lists)
    r = iota((rows4, 128), 0) % (2 * cap)
    lane = iota((rows4, 128), 1)
    wanted = lane == lax.axis_index("bulk") * cap + r % cap
    col = jnp.sum(jnp.where(wanted, asked, 0.0), axis=1, keepdims=True)
    col = col + jnp.where(r[:, :1] < cap, 0.0, float(kb))
    hot = jnp.where(lane.astype(f32) == col, 1.0, 0.0).astype(bf16)
    hot_ref[...] = hot
    base = n - DT * decay_ref[...] * (n - thermal_of(energy_ref))
    parts = forward_parts(w_ref, held_ref, fetched_ref, c_ref, c_hbm, sems)
    rate = electron_rate(sk_ref[...], far, bose, f, parts, w_ref, o0, o1)
    f1 = f + DT * rate
    e_ref[...] = rate
    f1_ref[...] = f1
    put_broadcast(send, add_rows(hot, padded(f1, base)), contributions)


def middle_kernel(
    cap,
    ends,
    part_ref,
    total_ref,
    other_ref,
    share_ref,
    serve_ref,
    f_ref,
    e_ref,
    own_ref,
    n_ref,
    energy_ref,
    decay_ref,
    pair_ref,
    sk_ref,
    sp_ref,
    b0_ref,
    b1_ref,
    held_ref,
    fetched_ref,
    c_hbm,
    send,
    *refs,
):
    w_ref, c_ref, sems, o0, o1 = refs[-5:]
    start_chunks(c_hbm, c_ref, sems)
    chips = serve_ref.shape[0] // (4 * cap)
    weight = DT / 2.0 if ends else DT
    part, total = half_of_devices(cap, chips, weight, 1, other_ref, share_ref)
    got = part_ref[...] + part
    total = total_ref[...] + total
    far, bose = gather_pair(pair_ref[...], got)
    terms = phonon_terms(far, bose, b0_ref, b1_ref)
    contributions = add_rows(sp_ref[...], terms)
    n = n_ref[...]
    own = own_ref[...]
    parts = forward_parts(w_ref, held_ref, fetched_ref, c_ref, c_hbm, sems)
    if ends:
        n2_ref, e2_ref, f3_ref = refs[:3]
        n2_ref[...] = n + (DT / 2.0) * total
        rate = electron_rate(sk_ref[...], far, bose, own, parts, w_ref, o0, o1)
        f3 = own + DT * rate
        e2_ref[...] = rate
        f3_ref[...] = f3
        to_wire(add_rows(serve_ref[...], padded(f3)) + contributions, send)
    else:
        base_ref, f2_ref = refs[:2]
        thermal = thermal_of(energy_ref)
        decay = decay_ref[...]
        p0 = total - decay * (n - thermal)
        n1 = n + DT * p0
        base = n + (DT / 2.0) * (p0 - decay * (n1 - thermal))
        base_ref[...] = base
        rate = electron_rate(sk_ref[...], far, bose, own, parts, w_ref, o0, o1)
        f2 = f_ref[...] + (DT / 2.0) * (e_ref[...] + rate)
        f2_ref[...] = f2
        put_broadcast(send, add_rows(serve_ref[...], padded(f2, base)), contributions)


def backward_kernel(f_ref, gk_ref, c_hbm, b0_ref, b1_ref, w_ref, c_ref, sems):
    start_chunks(c_hbm, c_ref, sems)
    own = add_rows(gk_ref[...], f_ref[...])
    backward_pass(own, c_hbm, c_ref, sems, w_ref, b0_ref, b1_ref)


def phonon_kernel(
    kb,
    recv,
    n_ref,
    energy_ref,
    decay_ref,
    pair_ref,
    st4_ref,
    sp8_ref,
    s8_ref,
    b0_ref,
    b1_ref,
    send,
    p_ref,
    n1_ref,
    far_ref,
):
    n = n_ref[...]
    got = from_wire(recv)
    thermal = thermal_of(energy_ref)
    rate = add_rows(st4_ref[...], got) - decay_ref[...] * (n - thermal)
    n1 = n + DT * rate
    p_ref[...] = rate
    n1_ref[...] = n1
    far = add_rows(pair_ref[:, : got.shape[0]], got)
    far_ref[...] = far
    gain = far * flat(b0_ref)
    both = jnp.concatenate([gain, gain - (1.0 - far) * flat(b1_ref)], axis=0)
    state = padded(jnp.zeros((kb, 128), f32), n1)
    to_wire(add_rows(s8_ref[...], state) + add_rows(sp8_ref[...], both), send)


def last_kernel(recv, *refs):
    far_ref, f_ref, f1_ref, e_ref, n_ref, n1_ref, p_ref, energy_ref, decay_ref = refs[:9]
    gp8_ref, sk_ref, st8a_ref, st8b_ref, held_ref, c_hbm = refs[9:15]
    refs = refs[15:]
    f2_ref, n2_ref, w_ref, c_ref, sems, o0, o1 = refs
    start_chunks(c_hbm, c_ref, sems)
    got = from_wire(recv)
    n, n1 = n_ref[...], n1_ref[...]
    bose = add_rows(gp8_ref[...], got)
    thermal = thermal_of(energy_ref)
    p1 = (
        add_rows(st8a_ref[...], got)
        + n1 * add_rows(st8b_ref[...], got)
        - decay_ref[...] * (n1 - thermal)
    )
    n2 = n + (DT / 2.0) * (p_ref[...] + p1)
    n2_ref[...] = n2
    parts = forward_parts(w_ref, held_ref, None, c_ref, c_hbm, sems)
    rate = electron_rate(sk_ref[...], far_ref[...], bose, f1_ref[...], parts, w_ref, o0, o1)
    f2 = f_ref[...] + (DT / 2.0) * (e_ref[...] + rate)
    f2_ref[...] = f2


def call(kernel, name, outs, scratch=(), spaces=None, out_spaces=None, flops=0, seen=0):
    def run(*args):
        places = dict(spaces or {})
        args = [
            pltpu.with_memory_space_constraint(x, pltpu.HBM)
            if places.get(i) is pltpu.HBM
            else x
            for i, x in enumerate(args)
        ]
        specs = [
            pl.BlockSpec(memory_space=places.get(i, pltpu.VMEM)) for i in range(len(args))
        ]
        return pl.pallas_call(
            kernel,
            out_shape=[
                (out_spaces or {}).get(i, jax.ShapeDtypeStruct)(*o) for i, o in enumerate(outs)
            ],
            in_specs=specs,
            out_specs=[
                pl.BlockSpec(memory_space=(out_spaces or {}).get(i, pltpu.VMEM))
                for i in range(len(outs))
            ],
            scratch_shapes=list(scratch),
            compiler_params=pltpu.CompilerParams(vmem_limit_bytes=VMEM_LIMIT),
            cost_estimate=pl.CostEstimate(
                flops=flops, bytes_accessed=seen, transcendentals=0
            ),
            name=name,
        )(*args)

    return run


def on_device(
    electrons,
    phonons,
    phonon_energy,
    phonon_decay,
    coupling,
    tile_kblock,
    tile_partner,
    tile_qslot,
    tile_count,
    partner_need,
    phonon_need,
):
    devices = lax.axis_size("bulk")
    kb = electrons.shape[0]
    qb = phonons.shape[0]
    tiles = coupling.shape[0]
    cap = partner_need.shape[1] // devices
    assert cap == phonon_need.shape[1] // devices and kb + qb <= 128
    rows4 = devices * 2 * cap
    rows8 = devices * 4 * cap
    groups = tiles // 8
    held = HELD_CHUNKS * (tiles // CHUNKS)
    weights = pltpu.VMEM((groups, 16, 1024), bf16)
    streams = [weights, pltpu.VMEM(coupling.shape, bf16), pltpu.SemaphoreType.DMA((CHUNKS,))]
    rest = (tiles - held, 128, 128)
    rest_sems = pltpu.SemaphoreType.DMA((CHUNKS - HELD_CHUNKS,))
    forward_streams = [weights, pltpu.VMEM(rest, bf16), rest_sems]
    sums = [pltpu.VMEM((groups, 8, 128), f32)] * 2
    pass_out = [((groups, 8, 128), f32)] * 2
    block4 = ((rows4, 128), f32)
    block8 = ((rows8, 128), f32)

    work = dict(flops=2 * tiles * 16 * 128 * 128, seen=tiles * 128 * 128 * 2)

    def exchange(x):
        order = [[(i + devices // 4 * 2) % devices for i in range(devices)]]
        return lax.all_to_all(
            x, "bulk", split_axis=0, concat_axis=0, tiled=True, axis_index_groups=order
        )

    ints = ((1, tiles), jnp.int32)
    lists = ((1, partner_need.shape[1]), jnp.int32)
    small = [((kb, 128), f32)] + [((qb, 128), f32)] * 3 + [ints] * 3
    step_rows = kb + qb + 8
    slots = devices * cap
    wide = 8 + slots
    assert step_rows % 8 == 0 and slots % 8 == 0 and slots <= 128
    assert devices % 2 == 0 and cap == 2
    chips = devices // 2
    same_core = [
        [(i + chips // 2) % chips * 2 + core for i in range(chips)] for core in (0, 1)
    ]

    def to_chips(x):
        return lax.all_to_all(
            x, "bulk", split_axis=0, concat_axis=0, tiled=True, axis_index_groups=same_core
        )

    def between_cores(x):
        return lax.ppermute(x, "bulk", [(i, i ^ 1) for i in range(devices)])

    f, n, energy, decay, kblock, partner, qslot, pneed, qneed, send = call(
        functools.partial(need_kernel, cap),
        "need",
        small + [lists, lists, ((chips * step_rows, 128), f32)],
        [pltpu.SemaphoreType.DMA((9,))],
        spaces={i: pltpu.HBM for i in range(9)},
    )(
        electrons,
        phonons,
        phonon_energy,
        phonon_decay,
        tile_kblock.reshape(1, tiles),
        tile_partner.reshape(1, tiles),
        tile_qslot.reshape(1, tiles),
        partner_need,
        phonon_need,
    )
    same = to_chips(send)
    c_held, c_rest, pair, gk, sk, sp, sp4, near, far_picks, mine, b0, b1 = call(
        functools.partial(prepare_kernel, cap),
        "prepare",
        [
            ((held, 128, 128), bf16),
            (rest, bf16),
            ((tiles, 2 * rows4), bf16),
            ((tiles, kb), bf16),
            ((kb, tiles), bf16),
            ((slots, tiles), bf16),
            ((rows4, tiles), bf16),
            ((rows4, chips * step_rows), bf16),
            ((rows4, chips * step_rows), bf16),
            ((rows4, 128), f32),
        ]
        + pass_out,
        [*streams, pltpu.VMEM(rest, bf16), rest_sems],
        spaces={0: pltpu.SMEM, 7: pltpu.HBM},
        out_spaces={1: pltpu.HBM},
        **work,
    )(tile_count, kblock, partner, qslot, f, pneed, qneed, coupling)
    same, c_held, b0 = lax.optimization_barrier((same, c_held, b0))
    wide_block = ((chips * wide, 128), f32)
    k_rows, q_rows = ((kb, 128), f32), ((qb, 128), f32)
    width = tiles // CHUNKS
    fetched = ((width, 128, 128), bf16)
    fetch_sem = pltpu.SemaphoreType.DMA((1,))
    short = (rest[0] - width, 128, 128)
    short_sems = pltpu.SemaphoreType.DMA((CHUNKS - HELD_CHUNKS - 1,))
    forward_scratch = [weights, pltpu.VMEM(short, bf16), short_sems] + sums
    other = between_cores(same)
    part, c_fetched = call(
        near_rows_kernel,
        "near_rows",
        [block4, fetched],
        [fetch_sem],
        spaces={2: pltpu.HBM},
        out_spaces={1: pltpu.VMEM},
    )(same, near, c_rest)
    send, e0, f1, serve, asked = call(
        functools.partial(first_kernel, cap),
        "first",
        [wide_block, k_rows, k_rows, ((rows4, 128), bf16), ((8 * devices, 128), bf16)],
        forward_scratch,
        spaces={15: pltpu.HBM},
        **work,
    )(same, other, part, far_picks, f, n, energy, decay, pair, sk, sp, b0, b1, c_held, c_fetched, c_rest)
    share, gp8, sp8, s8, st4, st8a, st8b = call(
        functools.partial(serve_kernel, cap, kb, qb),
        "serve",
        [
            ((rows4 + qb, devices * slots), bf16),
            ((tiles, rows8), bf16),
            ((rows8, 2 * tiles), bf16),
            ((rows8, 128), bf16),
            ((qb, rows4), bf16),
            ((qb, rows8), bf16),
            ((qb, rows8), bf16),
        ],
        spaces={0: pltpu.SMEM},
    )(tile_count, qslot, asked, serve, mine)
    back = call(backward_kernel, "backward", pass_out, streams, spaces={2: pltpu.HBM}, **work)

    def middle(ends, send, outs, f, e, own, n, contributions, share):
        same = to_chips(send)
        b0, b1 = back(own, gk, coupling)
        same, b0, share = lax.optimization_barrier((same, b0, share))
        other = between_cores(same)
        weight = DT / 2.0 if ends else DT
        part, total, c_fetched = call(
            functools.partial(near_half_kernel, cap, chips, weight),
            "near_half",
            [block4, q_rows, fetched],
            [fetch_sem],
            spaces={2: pltpu.HBM},
            out_spaces={2: pltpu.VMEM},
        )(same, share, c_rest)
        return call(
            functools.partial(middle_kernel, cap, ends),
            "middle",
            outs,
            forward_scratch,
            spaces={18: pltpu.HBM},
            **work,
        )(
            part, total, other, share, serve, f, e, own, n, energy, decay,
            pair, sk, contributions, b0, b1, c_held, c_fetched, c_rest,
        )

    send, base, f2 = middle(False, send, [wide_block, q_rows, k_rows], f, e0, f1, n, sp, share)
    send, n2, e2, f3 = middle(
        True, send, [block4, q_rows, k_rows, k_rows], f2, e0, f2, base, sp4, share
    )
    recv = exchange(send)
    b0, b1 = back(f3, gk, coupling)
    send, p2, n3, far = call(
        functools.partial(phonon_kernel, kb),
        "phonon",
        [block8, q_rows, q_rows, ((tiles, 128), f32)],
    )(recv, n2, energy, decay, pair, st4, sp8, s8, b0, b1)
    recv = exchange(send)
    f, n = call(
        last_kernel,
        "last",
        [k_rows, q_rows],
        forward_streams + sums,
        spaces={15: pltpu.HBM},
        **work,
    )(
        recv, far, f2, f3, e2, n2, n3, p2, energy, decay,
        gp8, sk, st8a, st8b, c_held, c_rest,
    )
    return (f, n)


def solution(mesh):
    placed = (
        P(("groups", "bulk"), None),
        P(("groups", "bulk"), None),
        P("bulk", None),
        P("bulk", None),
        P("bulk", None, None),
        P("bulk"),
        P("bulk"),
        P("bulk"),
        P("bulk"),
        P("bulk", None),
        P("bulk", None),
    )
    return jax.shard_map(
        on_device,
        mesh=mesh,
        in_specs=placed,
        out_specs=(P(("groups", "bulk"), None), P(("groups", "bulk"), None)),
        check_vma=False,
    )
```

```python
import functools

import jax
import jax.numpy as jnp
from jax import lax
from jax.experimental import pallas as pl
from jax.experimental.pallas import tpu as pltpu
from jax.sharding import PartitionSpec as P

DT = 0.05
CHUNKS = 8
HELD_CHUNKS = 2
f32 = jnp.float32
bf16 = jnp.bfloat16
VMEM_LIMIT = 48 * 1024 * 1024


def iota(shape, dim):
    return lax.broadcasted_iota(jnp.int32, shape, dim)


def dot(a, b):
    return lax.dot_general(a, b, (((1,), (0,)), ((), ())), preferred_element_type=f32)


def add_rows(onehot, x):
    hi = x.astype(bf16)
    mid = (x - hi.astype(f32)).astype(bf16)
    both = dot(onehot, jnp.concatenate([hi, mid], axis=1))
    return both[:, :128] + both[:, 128:]


def gather_pair(table, x):
    rows = x.shape[0]
    hi = x.astype(bf16)
    mid = (x - hi.astype(f32)).astype(bf16)
    blank = jnp.zeros((rows, 128), bf16)

    def both(part):
        upper = jnp.concatenate([part, blank], axis=1)
        lower = jnp.concatenate([blank, part], axis=1)
        return dot(table, jnp.concatenate([upper, lower], axis=0))

    res = both(hi) + both(mid)
    return res[:, :128], res[:, 128:]


def stacked(first, second):
    tiles = first.shape[0]
    return jnp.concatenate(
        [first.reshape(tiles // 8, 8, 128), second.reshape(tiles // 8, 8, 128)], axis=1
    ).astype(bf16)


def row_is(r):
    return iota((16, 128), 0) % 8 == r


def padded(*parts):
    rows = sum(p.shape[0] for p in parts)
    return jnp.concatenate([*parts, jnp.zeros((128 - rows, 128), f32)], axis=0)


def flat(ref):
    return ref[...].reshape(-1, 128)


def chunk_copy(src, dst, sems, i):
    size = min(src.shape[0], dst.shape[0]) // sems.shape[0]
    here = pl.ds(i * size, size)
    return pltpu.make_async_copy(src.at[here], dst.at[here], sems.at[i])


def start_chunks(src, dst, sems):
    for i in range(sems.shape[0]):
        chunk_copy(src, dst, sems, i).start()


def start(copies):
    for copy in copies:
        copy.start()


def block_diagonal(w):
    w = w.astype(f32)
    return jnp.concatenate(
        [jnp.where(row_is(r), w, 0.0).astype(bf16) for r in range(8)], axis=1
    )


def left_sides(first, second, w_ref):
    groups = w_ref.shape[0]
    w_ref[:, :, :128] = stacked(first, second)

    def spread(g, _):
        w_ref[g] = block_diagonal(w_ref[g, :, :128])
        return 0

    lax.fori_loop(0, groups, spread, 0, unroll=4)


def chunk_products(w_ref, c_ref, i, base, out0, out1):
    size = w_ref.shape[0] // CHUNKS
    for k in range(size):
        g = i * size + k
        res = dot(w_ref[base + g], c_ref[pl.ds(g * 8, 8)].reshape(1024, 128))
        out0[base + g] = res[:8]
        out1[base + g] = res[8:]


def tile_products(w_ref, parts, out0, out1):
    size = w_ref.shape[0] // CHUNKS
    for c_ref, c_hbm, sems, base in parts:
        chunks = c_ref.shape[0] // 8 // size

        def chunk(i, _):
            if c_hbm is not None:
                chunk_copy(c_hbm, c_ref, sems, i).wait()
            chunk_products(w_ref, c_ref, i, base, out0, out1)
            return 0

        lax.fori_loop(0, chunks, chunk, 0)


def backward_pass(own, c_hbm, c_ref, sems, w_ref, out0, out1):
    left_sides(1.0 - own, own, w_ref)
    tile_products(w_ref, [(c_ref, c_hbm, sems, 0)], out0, out1)


def forward_parts(w_ref, held_ref, fetched_ref, c_ref, c_hbm, sems):
    parts = [(held_ref, None, None, 0)]
    if fetched_ref is not None:
        parts.append((fetched_ref, None, None, w_ref.shape[0] - fetched_ref.shape[0] // 8))
    return parts + [(c_ref, c_hbm, sems, held_ref.shape[0] // 8)]


def electron_rate(sum_k, far, bose, f, parts, w_ref, o0, o1):
    left_sides(far * (1.0 + bose), far + bose, w_ref)
    tile_products(w_ref, parts, o0, o1)
    gain, loss = flat(o0), flat(o1)
    gain_hi, loss_hi = gain.astype(bf16), loss.astype(bf16)
    gain_lo = (gain - gain_hi.astype(f32)).astype(bf16)
    loss_lo = (loss - loss_hi.astype(f32)).astype(bf16)
    sums = dot(sum_k, jnp.concatenate([gain_hi, gain_lo, loss_hi, loss_lo], axis=1))
    return sums[:, :128] + sums[:, 128:256] - f * (sums[:, 256:384] + sums[:, 384:])


def my_core():
    return lax.rem(lax.axis_index("bulk"), 2)


def place_of(chip, chips):
    return (chip + chips - chips // 2) % chips


def block_of(peer, peers):
    chips = peers // 2
    return place_of(peer // 2, chips) + jnp.where(peer % 2 == my_core(), 0, chips)


def to_wire(rows, send):
    half = rows.shape[0] // 4 * 2
    send[: rows.shape[0] - half] = rows[half:]
    send[rows.shape[0] - half :] = rows[:half]


def from_wire(recv):
    half = recv.shape[0] // 4 * 2
    return jnp.concatenate([recv[recv.shape[0] - half :], recv[: recv.shape[0] - half]], axis=0)


def need_kernel(cap, *refs):
    ins, outs = refs[:9], refs[9:]
    *small, pneed_ref, qneed_ref, send_ref, sems = outs
    copies = [
        pltpu.make_async_copy(src, dst, sems.at[i])
        for i, (src, dst) in enumerate(zip(ins, [*small, pneed_ref, qneed_ref]))
    ]
    start(copies)
    slots = pneed_ref.shape[1]
    step = send_ref.shape[0] // (slots // cap // 2)
    for copy in copies:
        copy.wait()
    f, n = small[0][...], small[1][...]
    own_p, own_q = pneed_ref[...].astype(f32), qneed_ref[...].astype(f32)
    row = iota((8, slots), 0)
    lists = jnp.where(row == 0, own_p, jnp.where(row == 1, own_q, 0.0))
    if slots < 128:
        lists = jnp.concatenate([lists, jnp.zeros((8, 128 - slots), f32)], axis=1)
    block = jnp.concatenate([f, n, lists], axis=0)
    for chip in range(slots // cap // 2):
        send_ref[chip * step : (chip + 1) * step] = block


def prepare_kernel(
    cap,
    count_ref,
    kblock_ref,
    partner_ref,
    qslot_ref,
    f_ref,
    pneed_ref,
    qneed_ref,
    c_hbm,
    held_ref,
    t_hbm,
    pair_ref,
    gk_ref,
    sk_ref,
    sp_ref,
    sp4_ref,
    near_ref,
    list_ref,
    mine_ref,
    b0_ref,
    b1_ref,
    w_ref,
    c_ref,
    in_sems,
    t_ref,
    out_sems,
):
    start_chunks(c_hbm, c_ref, in_sems)
    tiles = kblock_ref.shape[1]
    kb = f_ref.shape[0]
    used = iota((1, tiles), 1) < count_ref[0]
    k = kblock_ref[...]
    e = partner_ref[...]
    q = qslot_ref[...]
    rows4 = sp4_ref.shape[0]
    ind = lambda m: jnp.where(m, 1.0, 0.0)
    k_hot = ind(iota((kb, tiles), 0) == k)
    gk_ref[...] = k_hot.T.astype(bf16)
    own = add_rows(gk_ref[...], f_ref[...])
    left_sides(1.0 - own, own, w_ref)
    sk_ref[...] = jnp.where(used, k_hot, 0.0).astype(bf16)
    x = iota((rows4, tiles), 0)
    row_e = (e // cap) * (2 * cap) + e % cap
    row_p = (q // cap) * (2 * cap) + cap + q % cap
    p_hot = ind(x == row_p)
    pair_ref[...] = jnp.concatenate([ind(x == row_e), p_hot], axis=0).T.astype(bf16)
    sp4_ref[...] = jnp.where(used, p_hot, 0.0).astype(bf16)
    sp_ref[...] = jnp.where(used, ind(iota(sp_ref.shape, 0) == q), 0.0).astype(bf16)
    rows, half = list_ref.shape
    slots = pneed_ref.shape[1]
    peers = slots // cap
    x = iota((rows, slots), 0)
    y = iota((rows, slots), 1)
    peer, r = x // (2 * cap), x % (2 * cap)
    e_here = (r < cap) & (y == peer * cap + r)
    p_here = (r >= cap) & (y == peer * cap + r - cap)
    pn = jnp.broadcast_to(pneed_ref[...].astype(f32), (rows, slots))
    qn = jnp.broadcast_to(qneed_ref[...].astype(f32), (rows, slots)) + float(kb)
    col = jnp.sum(jnp.where(e_here, pn, 0.0) + jnp.where(p_here, qn, 0.0), axis=1, keepdims=True)
    mine_ref[...] = jnp.broadcast_to(col, (rows, 128))
    start_of = block_of(iota((rows, 1), 0) // (2 * cap), peers) * (2 * half // peers)
    place = col + start_of.astype(f32)
    lane = iota((rows, half), 1).astype(f32)
    near_ref[...] = ind(lane == place).astype(bf16)
    list_ref[...] = ind(lane + float(half) == place).astype(bf16)

    size = c_ref.shape[0] // CHUNKS
    held = held_ref.shape[0] // size

    rest = CHUNKS - held

    def to_held(i, _):
        chunk_copy(c_hbm, c_ref, in_sems, i).wait()
        chunk_products(w_ref, c_ref, i, 0, b0_ref, b1_ref)
        for t in range(size):
            held_ref[i * size + t] = c_ref[i * size + t].T
        return 0

    def to_rest(i, _):
        chunk_copy(c_hbm, c_ref, in_sems, held + i).wait()
        chunk_products(w_ref, c_ref, held + i, 0, b0_ref, b1_ref)
        for t in range(size):
            t_ref[i * size + t] = c_ref[(held + i) * size + t].T
        chunk_copy(t_ref, t_hbm, out_sems, i).start()
        return 0

    lax.fori_loop(0, held, to_held, 0)
    lax.fori_loop(0, rest, to_rest, 0)
    for i in range(rest):
        chunk_copy(t_ref, t_hbm, out_sems, i).wait()


def blocks(ref, count_of_blocks, first, count):
    step = ref.shape[0] // count_of_blocks
    parts = [ref[b * step + first : b * step + first + count] for b in range(count_of_blocks)]
    return jnp.concatenate(parts, axis=0)


def serve_kernel(
    cap,
    kb,
    qb,
    count_ref,
    qslot_ref,
    asked_ref,
    hot_ref,
    mine_ref,
    share_ref,
    gp8_ref,
    sp8_ref,
    s8_ref,
    st4_ref,
    st8a_ref,
    st8b_ref,
):
    hot = hot_ref[...]
    rows4, rows8 = hot.shape[0], s8_ref.shape[0]
    q = qslot_ref[...]
    tiles = q.shape[1]
    used = iota((1, tiles), 1) < count_ref[0]
    ind = lambda m: jnp.where(m, 1.0, 0.0)
    x = iota((rows8, tiles), 0)
    row_z = (q // cap) * (4 * cap) + q % cap
    gp8_ref[...] = ind(x == row_z).T.astype(bf16)
    sp8_ref[...] = jnp.concatenate(
        [
            jnp.where(used, ind(x == row_z + cap), 0.0),
            jnp.where(used, ind(x == row_z + 2 * cap), 0.0),
        ],
        axis=1,
    ).astype(bf16)
    x = iota((rows8, rows4), 0)
    y = iota((rows8, rows4), 1)
    peer, r = x // (4 * cap), x % (4 * cap)
    source = peer * (2 * cap) + cap + r % cap

    def rows_of(kind):
        here = (y == source) & (r // cap == kind)
        return dot(jnp.where(here, 1.0, 0.0).astype(bf16), hot)

    s8_ref[...] = rows_of(0).astype(bf16)
    st4_ref[...] = hot.astype(f32).T[kb : kb + qb].astype(bf16)
    st8a_ref[...] = rows_of(1).T[kb : kb + qb].astype(bf16)
    st8b_ref[...] = rows_of(2).T[kb : kb + qb].astype(bf16)

    peers = rows4 // (2 * cap)
    slots = peers * cap
    wide = peers * slots
    lists = asked_ref[...]
    pick_q = iota((peers, 8 * peers), 1) == 8 * iota((peers, 8 * peers), 0) + 1
    every_q = dot(jnp.where(pick_q, 1.0, 0.0).astype(bf16), lists).astype(bf16)
    tiled = iota((128, wide), 0) == iota((128, wide), 1) % slots
    spread = dot(every_q, jnp.where(tiled, 1.0, 0.0).astype(bf16))
    lane = iota((1, wide), 1)
    here = iota((peers, wide), 0) == lane // slots
    q = jnp.sum(jnp.where(here, spread, 0.0), axis=0, keepdims=True)
    ids = q + (lane % slots // cap * qb).astype(f32)
    row = iota((rows4, 1), 0)
    col = mine_ref[...][:, :1]
    my_ids = col - float(kb) + (row // (2 * cap) * qb).astype(f32)
    my_ids = jnp.where(row % (2 * cap) >= cap, my_ids, -1.0)
    owned = (lax.axis_index("bulk") * qb + iota((qb, 1), 0)).astype(f32)
    wanted = jnp.concatenate([my_ids, owned], axis=0)
    share_ref[...] = jnp.where(ids == wanted, 1.0, 0.0).astype(bf16)


def thermal_of(energy_ref):
    return 1.0 / (jnp.exp(energy_ref[...]) - 1.0)


def put_broadcast(send, served, contributions):
    slots = contributions.shape[0]
    chips = served.shape[0] // 8
    for chip in range(chips):
        at = place_of(chip, chips) * (8 + slots)
        send[at : at + 8] = served[chip * 8 : chip * 8 + 8]
        send[at + 8 : at + 8 + slots] = contributions


def phonon_terms(far, bose, b0_ref, b1_ref):
    gain = far * flat(b0_ref)
    return gain + bose * (gain - (1.0 - far) * flat(b1_ref))


def fetch_copy(c_hbm, fetched_ref, sem):
    count = fetched_ref.shape[0]
    return pltpu.make_async_copy(
        c_hbm.at[pl.ds(c_hbm.shape[0] - count, count)], fetched_ref, sem.at[0]
    )


def near_rows_kernel(same_ref, list_ref, c_hbm, part_ref, fetched_ref, sem):
    copy = fetch_copy(c_hbm, fetched_ref, sem)
    copy.start()
    part_ref[...] = add_rows(list_ref[...], same_ref[...])
    copy.wait()


def half_of_devices(cap, chips, weight, others, ref, share_ref):
    rows4 = 4 * cap * chips
    wide = share_ref.shape[1] // 2
    x = iota((rows4, 8 * chips), 0)
    peer = x // (2 * cap)
    source = 8 * place_of(peer // 2, chips) + 2 * cap * my_core() + x % (2 * cap)
    wanted_core = (my_core() + others) % 2
    at = (iota((rows4, 8 * chips), 1) == source) & (peer % 2 == wanted_core)
    heads = add_rows(jnp.where(at, 1.0, 0.0).astype(bf16), blocks(ref, chips, 0, 8))
    tails = blocks(ref, chips, 8, wide // chips)
    sums = add_rows(share_ref[:, others * wide : (others + 1) * wide], tails)
    return heads + weight * sums[:rows4], sums[rows4:]


def near_half_kernel(
    cap, chips, weight, same_ref, share_ref, c_hbm, part_ref, total_ref, fetched_ref, sem
):
    copy = fetch_copy(c_hbm, fetched_ref, sem)
    copy.start()
    part, total = half_of_devices(cap, chips, weight, 0, same_ref, share_ref)
    part_ref[...] = part
    total_ref[...] = total
    copy.wait()


def first_kernel(
    cap,
    same_ref,
    other_ref,
    part_ref,
    list_ref,
    f_ref,
    n_ref,
    energy_ref,
    decay_ref,
    pair_ref,
    sk_ref,
    sp_ref,
    b0_ref,
    b1_ref,
    held_ref,
    fetched_ref,
    c_hbm,
    send,
    e_ref,
    f1_ref,
    hot_ref,
    asked_ref,
    w_ref,
    c_ref,
    sems,
    o0,
    o1,
):
    start_chunks(c_hbm, c_ref, sems)
    f, n = f_ref[...], n_ref[...]
    kb, qb = f.shape[0], n.shape[0]
    rows4 = list_ref.shape[0]
    peers = rows4 // (2 * cap)
    got = part_ref[...] + add_rows(list_ref[...], other_ref[...])
    far, bose = gather_pair(pair_ref[...], got)
    contributions = add_rows(sp_ref[...], phonon_terms(far, bose, b0_ref, b1_ref))
    lists = jnp.concatenate(
        [blocks(ref, peers // 2, kb + qb, 8) for ref in (same_ref, other_ref)], axis=0
    ).astype(bf16)
    asked_ref[...] = lists
    x = iota((rows4, 8 * peers), 0)
    r = x % (2 * cap)
    kind = jnp.where(r < cap, 0, 1)
    at = iota((rows4, 8 * peers), 1) == 8 * block_of(x // (2 * cap), peers) + kind
    asked = dot(jnp.where(at, 1.0, 0.0).astype(bf16), lists)
    r = iota((rows4, 128), 0) % (2 * cap)
    lane = iota((rows4, 128), 1)
    wanted = lane == lax.axis_index("bulk") * cap + r % cap
    col = jnp.sum(jnp.where(wanted, asked, 0.0), axis=1, keepdims=True)
    col = col + jnp.where(r[:, :1] < cap, 0.0, float(kb))
    hot = jnp.where(lane.astype(f32) == col, 1.0, 0.0).astype(bf16)
    hot_ref[...] = hot
    base = n - DT * decay_ref[...] * (n - thermal_of(energy_ref))
    parts = forward_parts(w_ref, held_ref, fetched_ref, c_ref, c_hbm, sems)
    rate = electron_rate(sk_ref[...], far, bose, f, parts, w_ref, o0, o1)
    f1 = f + DT * rate
    e_ref[...] = rate
    f1_ref[...] = f1
    put_broadcast(send, add_rows(hot, padded(f1, base)), contributions)


def middle_kernel(
    cap,
    ends,
    part_ref,
    total_ref,
    other_ref,
    share_ref,
    serve_ref,
    f_ref,
    e_ref,
    own_ref,
    n_ref,
    energy_ref,
    decay_ref,
    pair_ref,
    sk_ref,
    sp_ref,
    b0_ref,
    b1_ref,
    held_ref,
    fetched_ref,
    c_hbm,
    send,
    *refs,
):
    w_ref, c_ref, sems, o0, o1 = refs[-5:]
    start_chunks(c_hbm, c_ref, sems)
    chips = serve_ref.shape[0] // (4 * cap)
    weight = DT / 2.0 if ends else DT
    part, total = half_of_devices(cap, chips, weight, 1, other_ref, share_ref)
    got = part_ref[...] + part
    total = total_ref[...] + total
    far, bose = gather_pair(pair_ref[...], got)
    terms = phonon_terms(far, bose, b0_ref, b1_ref)
    contributions = add_rows(sp_ref[...], terms)
    n = n_ref[...]
    own = own_ref[...]
    parts = forward_parts(w_ref, held_ref, fetched_ref, c_ref, c_hbm, sems)
    if ends:
        n2_ref, e2_ref, f3_ref = refs[:3]
        n2_ref[...] = n + (DT / 2.0) * total
        rate = electron_rate(sk_ref[...], far, bose, own, parts, w_ref, o0, o1)
        f3 = own + DT * rate
        e2_ref[...] = rate
        f3_ref[...] = f3
        to_wire(add_rows(serve_ref[...], padded(f3)) + contributions, send)
    else:
        base_ref, f2_ref = refs[:2]
        thermal = thermal_of(energy_ref)
        decay = decay_ref[...]
        p0 = total - decay * (n - thermal)
        n1 = n + DT * p0
        base = n + (DT / 2.0) * (p0 - decay * (n1 - thermal))
        base_ref[...] = base
        rate = electron_rate(sk_ref[...], far, bose, own, parts, w_ref, o0, o1)
        f2 = f_ref[...] + (DT / 2.0) * (e_ref[...] + rate)
        f2_ref[...] = f2
        put_broadcast(send, add_rows(serve_ref[...], padded(f2, base)), contributions)


def backward_kernel(f_ref, gk_ref, c_hbm, b0_ref, b1_ref, w_ref, c_ref, sems):
    start_chunks(c_hbm, c_ref, sems)
    own = add_rows(gk_ref[...], f_ref[...])
    backward_pass(own, c_hbm, c_ref, sems, w_ref, b0_ref, b1_ref)


def phonon_kernel(
    kb,
    recv,
    n_ref,
    energy_ref,
    decay_ref,
    pair_ref,
    st4_ref,
    sp8_ref,
    s8_ref,
    b0_ref,
    b1_ref,
    send,
    p_ref,
    n1_ref,
    far_ref,
):
    n = n_ref[...]
    got = from_wire(recv)
    thermal = thermal_of(energy_ref)
    rate = add_rows(st4_ref[...], got) - decay_ref[...] * (n - thermal)
    n1 = n + DT * rate
    p_ref[...] = rate
    n1_ref[...] = n1
    far = add_rows(pair_ref[:, : got.shape[0]], got)
    far_ref[...] = far
    gain = far * flat(b0_ref)
    both = jnp.concatenate([gain, gain - (1.0 - far) * flat(b1_ref)], axis=0)
    state = padded(jnp.zeros((kb, 128), f32), n1)
    to_wire(add_rows(s8_ref[...], state) + add_rows(sp8_ref[...], both), send)


def last_kernel(recv, *refs):
    far_ref, f_ref, f1_ref, e_ref, n_ref, n1_ref, p_ref, energy_ref, decay_ref = refs[:9]
    gp8_ref, sk_ref, st8a_ref, st8b_ref, held_ref, c_hbm = refs[9:15]
    refs = refs[15:]
    f2_ref, n2_ref, w_ref, c_ref, sems, o0, o1 = refs
    start_chunks(c_hbm, c_ref, sems)
    got = from_wire(recv)
    n, n1 = n_ref[...], n1_ref[...]
    bose = add_rows(gp8_ref[...], got)
    thermal = thermal_of(energy_ref)
    p1 = (
        add_rows(st8a_ref[...], got)
        + n1 * add_rows(st8b_ref[...], got)
        - decay_ref[...] * (n1 - thermal)
    )
    n2 = n + (DT / 2.0) * (p_ref[...] + p1)
    n2_ref[...] = n2
    parts = forward_parts(w_ref, held_ref, None, c_ref, c_hbm, sems)
    rate = electron_rate(sk_ref[...], far_ref[...], bose, f1_ref[...], parts, w_ref, o0, o1)
    f2 = f_ref[...] + (DT / 2.0) * (e_ref[...] + rate)
    f2_ref[...] = f2


def call(kernel, name, outs, scratch=(), spaces=None, out_spaces=None, flops=0, seen=0):
    def run(*args):
        places = dict(spaces or {})
        args = [
            pltpu.with_memory_space_constraint(x, pltpu.HBM)
            if places.get(i) is pltpu.HBM
            else x
            for i, x in enumerate(args)
        ]
        specs = [
            pl.BlockSpec(memory_space=places.get(i, pltpu.VMEM)) for i in range(len(args))
        ]
        return pl.pallas_call(
            kernel,
            out_shape=[
                (out_spaces or {}).get(i, jax.ShapeDtypeStruct)(*o) for i, o in enumerate(outs)
            ],
            in_specs=specs,
            out_specs=[
                pl.BlockSpec(memory_space=(out_spaces or {}).get(i, pltpu.VMEM))
                for i in range(len(outs))
            ],
            scratch_shapes=list(scratch),
            compiler_params=pltpu.CompilerParams(vmem_limit_bytes=VMEM_LIMIT),
            cost_estimate=pl.CostEstimate(
                flops=flops, bytes_accessed=seen, transcendentals=0
            ),
            name=name,
        )(*args)

    return run


def on_device(
    electrons,
    phonons,
    phonon_energy,
    phonon_decay,
    coupling,
    tile_kblock,
    tile_partner,
    tile_qslot,
    tile_count,
    partner_need,
    phonon_need,
):
    devices = lax.axis_size("bulk")
    kb = electrons.shape[0]
    qb = phonons.shape[0]
    tiles = coupling.shape[0]
    cap = partner_need.shape[1] // devices
    assert cap == phonon_need.shape[1] // devices and kb + qb <= 128
    rows4 = devices * 2 * cap
    rows8 = devices * 4 * cap
    groups = tiles // 8
    held = HELD_CHUNKS * (tiles // CHUNKS)
    weights = pltpu.VMEM((groups, 16, 1024), bf16)
    streams = [weights, pltpu.VMEM(coupling.shape, bf16), pltpu.SemaphoreType.DMA((CHUNKS,))]
    rest = (tiles - held, 128, 128)
    rest_sems = pltpu.SemaphoreType.DMA((CHUNKS - HELD_CHUNKS,))
    forward_streams = [weights, pltpu.VMEM(rest, bf16), rest_sems]
    sums = [pltpu.VMEM((groups, 8, 128), f32)] * 2
    pass_out = [((groups, 8, 128), f32)] * 2
    block4 = ((rows4, 128), f32)
    block8 = ((rows8, 128), f32)

    work = dict(flops=2 * tiles * 16 * 128 * 128, seen=tiles * 128 * 128 * 2)

    def exchange(x):
        order = [[(i + devices // 4 * 2) % devices for i in range(devices)]]
        return lax.all_to_all(
            x, "bulk", split_axis=0, concat_axis=0, tiled=True, axis_index_groups=order
        )

    ints = ((1, tiles), jnp.int32)
    lists = ((1, partner_need.shape[1]), jnp.int32)
    small = [((kb, 128), f32)] + [((qb, 128), f32)] * 3 + [ints] * 3
    step_rows = kb + qb + 8
    slots = devices * cap
    wide = 8 + slots
    assert step_rows % 8 == 0 and slots % 8 == 0 and slots <= 128
    assert devices % 2 == 0 and cap == 2
    chips = devices // 2
    same_core = [
        [(i + chips // 2) % chips * 2 + core for i in range(chips)] for core in (0, 1)
    ]

    def to_chips(x):
        return lax.all_to_all(
            x, "bulk", split_axis=0, concat_axis=0, tiled=True, axis_index_groups=same_core
        )

    def between_cores(x):
        return lax.ppermute(x, "bulk", [(i, i ^ 1) for i in range(devices)])

    f, n, energy, decay, kblock, partner, qslot, pneed, qneed, send = call(
        functools.partial(need_kernel, cap),
        "need",
        small + [lists, lists, ((chips * step_rows, 128), f32)],
        [pltpu.SemaphoreType.DMA((9,))],
        spaces={i: pltpu.HBM for i in range(9)},
    )(
        electrons,
        phonons,
        phonon_energy,
        phonon_decay,
        tile_kblock.reshape(1, tiles),
        tile_partner.reshape(1, tiles),
        tile_qslot.reshape(1, tiles),
        partner_need,
        phonon_need,
    )
    same = to_chips(send)
    c_held, c_rest, pair, gk, sk, sp, sp4, near, far_picks, mine, b0, b1 = call(
        functools.partial(prepare_kernel, cap),
        "prepare",
        [
            ((held, 128, 128), bf16),
            (rest, bf16),
            ((tiles, 2 * rows4), bf16),
            ((tiles, kb), bf16),
            ((kb, tiles), bf16),
            ((slots, tiles), bf16),
            ((rows4, tiles), bf16),
            ((rows4, chips * step_rows), bf16),
            ((rows4, chips * step_rows), bf16),
            ((rows4, 128), f32),
        ]
        + pass_out,
        [*streams, pltpu.VMEM(rest, bf16), rest_sems],
        spaces={0: pltpu.SMEM, 7: pltpu.HBM},
        out_spaces={1: pltpu.HBM},
        **work,
    )(tile_count, kblock, partner, qslot, f, pneed, qneed, coupling)
    same, c_held, b0 = lax.optimization_barrier((same, c_held, b0))
    wide_block = ((chips * wide, 128), f32)
    k_rows, q_rows = ((kb, 128), f32), ((qb, 128), f32)
    width = tiles // CHUNKS
    fetched = ((width, 128, 128), bf16)
    fetch_sem = pltpu.SemaphoreType.DMA((1,))
    short = (rest[0] - width, 128, 128)
    short_sems = pltpu.SemaphoreType.DMA((CHUNKS - HELD_CHUNKS - 1,))
    forward_scratch = [weights, pltpu.VMEM(short, bf16), short_sems] + sums
    other = between_cores(same)
    part, c_fetched = call(
        near_rows_kernel,
        "near_rows",
        [block4, fetched],
        [fetch_sem],
        spaces={2: pltpu.HBM},
        out_spaces={1: pltpu.VMEM},
    )(same, near, c_rest)
    send, e0, f1, serve, asked = call(
        functools.partial(first_kernel, cap),
        "first",
        [wide_block, k_rows, k_rows, ((rows4, 128), bf16), ((8 * devices, 128), bf16)],
        forward_scratch,
        spaces={15: pltpu.HBM},
        **work,
    )(same, other, part, far_picks, f, n, energy, decay, pair, sk, sp, b0, b1, c_held, c_fetched, c_rest)
    share, gp8, sp8, s8, st4, st8a, st8b = call(
        functools.partial(serve_kernel, cap, kb, qb),
        "serve",
        [
            ((rows4 + qb, devices * slots), bf16),
            ((tiles, rows8), bf16),
            ((rows8, 2 * tiles), bf16),
            ((rows8, 128), bf16),
            ((qb, rows4), bf16),
            ((qb, rows8), bf16),
            ((qb, rows8), bf16),
        ],
        spaces={0: pltpu.SMEM},
    )(tile_count, qslot, asked, serve, mine)
    back = call(backward_kernel, "backward", pass_out, streams, spaces={2: pltpu.HBM}, **work)

    def middle(ends, send, outs, f, e, own, n, contributions, share):
        same = to_chips(send)
        b0, b1 = back(own, gk, coupling)
        same, b0, share = lax.optimization_barrier((same, b0, share))
        other = between_cores(same)
        weight = DT / 2.0 if ends else DT
        part, total, c_fetched = call(
            functools.partial(near_half_kernel, cap, chips, weight),
            "near_half",
            [block4, q_rows, fetched],
            [fetch_sem],
            spaces={2: pltpu.HBM},
            out_spaces={2: pltpu.VMEM},
        )(same, share, c_rest)
        return call(
            functools.partial(middle_kernel, cap, ends),
            "middle",
            outs,
            forward_scratch,
            spaces={18: pltpu.HBM},
            **work,
        )(
            part, total, other, share, serve, f, e, own, n, energy, decay,
            pair, sk, contributions, b0, b1, c_held, c_fetched, c_rest,
        )

    send, base, f2 = middle(False, send, [wide_block, q_rows, k_rows], f, e0, f1, n, sp, share)
    send, n2, e2, f3 = middle(
        True, send, [block4, q_rows, k_rows, k_rows], f2, e0, f2, base, sp4, share
    )
    recv = exchange(send)
    b0, b1 = back(f3, gk, coupling)
    send, p2, n3, far = call(
        functools.partial(phonon_kernel, kb),
        "phonon",
        [block8, q_rows, q_rows, ((tiles, 128), f32)],
    )(recv, n2, energy, decay, pair, st4, sp8, s8, b0, b1)
    recv = exchange(send)
    f, n = call(
        last_kernel,
        "last",
        [k_rows, q_rows],
        forward_streams + sums,
        spaces={15: pltpu.HBM},
        **work,
    )(
        recv, far, f2, f3, e2, n2, n3, p2, energy, decay,
        gp8, sk, st8a, st8b, c_held, c_rest,
    )
    return (f, n)


def solution(mesh):
    placed = (
        P(("groups", "bulk"), None),
        P(("groups", "bulk"), None),
        P("bulk", None),
        P("bulk", None),
        P("bulk", None, None),
        P("bulk"),
        P("bulk"),
        P("bulk"),
        P("bulk"),
        P("bulk", None),
        P("bulk", None),
    )
    return jax.shard_map(
        on_device,
        mesh=mesh,
        in_specs=placed,
        out_specs=(P(("groups", "bulk"), None), P(("groups", "bulk"), None)),
        check_vma=False,
    )
```

```python
import functools

import jax
import jax.numpy as jnp
from jax import lax
from jax.experimental import pallas as pl
from jax.experimental.pallas import tpu as pltpu
from jax.sharding import PartitionSpec as P

DT = 0.05
CHUNKS = 8
HELD_CHUNKS = 2
f32 = jnp.float32
bf16 = jnp.bfloat16
VMEM_LIMIT = 48 * 1024 * 1024


def iota(shape, dim):
    return lax.broadcasted_iota(jnp.int32, shape, dim)


def dot(a, b):
    return lax.dot_general(a, b, (((1,), (0,)), ((), ())), preferred_element_type=f32)


def add_rows(onehot, x):
    hi = x.astype(bf16)
    mid = (x - hi.astype(f32)).astype(bf16)
    both = dot(onehot, jnp.concatenate([hi, mid], axis=1))
    return both[:, :128] + both[:, 128:]


def gather_pair(table, x):
    rows = x.shape[0]
    hi = x.astype(bf16)
    mid = (x - hi.astype(f32)).astype(bf16)
    blank = jnp.zeros((rows, 128), bf16)

    def both(part):
        upper = jnp.concatenate([part, blank], axis=1)
        lower = jnp.concatenate([blank, part], axis=1)
        return dot(table, jnp.concatenate([upper, lower], axis=0))

    res = both(hi) + both(mid)
    return res[:, :128], res[:, 128:]


def stacked(first, second):
    tiles = first.shape[0]
    return jnp.concatenate(
        [first.reshape(tiles // 8, 8, 128), second.reshape(tiles // 8, 8, 128)], axis=1
    ).astype(bf16)


def row_is(r):
    return iota((16, 128), 0) % 8 == r


def padded(*parts):
    rows = sum(p.shape[0] for p in parts)
    return jnp.concatenate([*parts, jnp.zeros((128 - rows, 128), f32)], axis=0)


def flat(ref):
    return ref[...].reshape(-1, 128)


def chunk_copy(src, dst, sems, i):
    size = min(src.shape[0], dst.shape[0]) // sems.shape[0]
    here = pl.ds(i * size, size)
    return pltpu.make_async_copy(src.at[here], dst.at[here], sems.at[i])


def start_chunks(src, dst, sems):
    for i in range(sems.shape[0]):
        chunk_copy(src, dst, sems, i).start()


def start(copies):
    for copy in copies:
        copy.start()


def block_diagonal(w):
    w = w.astype(f32)
    return jnp.concatenate(
        [jnp.where(row_is(r), w, 0.0).astype(bf16) for r in range(8)], axis=1
    )


def left_sides(first, second, w_ref):
    groups = w_ref.shape[0]
    w_ref[:, :, :128] = stacked(first, second)

    def spread(g, _):
        w_ref[g] = block_diagonal(w_ref[g, :, :128])
        return 0

    lax.fori_loop(0, groups, spread, 0, unroll=4)


def chunk_products(w_ref, c_ref, i, base, out0, out1):
    size = w_ref.shape[0] // CHUNKS
    for k in range(size):
        g = i * size + k
        res = dot(w_ref[base + g], c_ref[pl.ds(g * 8, 8)].reshape(1024, 128))
        out0[base + g] = res[:8]
        out1[base + g] = res[8:]


def tile_products(w_ref, parts, out0, out1):
    size = w_ref.shape[0] // CHUNKS
    for c_ref, c_hbm, sems, base in parts:
        chunks = c_ref.shape[0] // 8 // size

        def chunk(i, _):
            if c_hbm is not None:
                chunk_copy(c_hbm, c_ref, sems, i).wait()
            chunk_products(w_ref, c_ref, i, base, out0, out1)
            return 0

        lax.fori_loop(0, chunks, chunk, 0)


def backward_pass(own, c_hbm, c_ref, sems, w_ref, out0, out1):
    left_sides(1.0 - own, own, w_ref)
    tile_products(w_ref, [(c_ref, c_hbm, sems, 0)], out0, out1)


def forward_parts(w_ref, held_ref, fetched_ref, c_ref, c_hbm, sems):
    parts = [(held_ref, None, None, 0)]
    if fetched_ref is not None:
        parts.append((fetched_ref, None, None, w_ref.shape[0] - fetched_ref.shape[0] // 8))
    return parts + [(c_ref, c_hbm, sems, held_ref.shape[0] // 8)]


def electron_rate(sum_k, far, bose, f, parts, w_ref, o0, o1):
    left_sides(far * (1.0 + bose), far + bose, w_ref)
    tile_products(w_ref, parts, o0, o1)
    gain, loss = flat(o0), flat(o1)
    gain_hi, loss_hi = gain.astype(bf16), loss.astype(bf16)
    gain_lo = (gain - gain_hi.astype(f32)).astype(bf16)
    loss_lo = (loss - loss_hi.astype(f32)).astype(bf16)
    sums = dot(sum_k, jnp.concatenate([gain_hi, gain_lo, loss_hi, loss_lo], axis=1))
    return sums[:, :128] + sums[:, 128:256] - f * (sums[:, 256:384] + sums[:, 384:])


def my_core():
    return lax.rem(lax.axis_index("bulk"), 2)


def place_of(chip, chips, core):
    up = (chip + chips // 2) % chips
    down = (chips // 2 - 1 - chip + chips) % chips
    return jnp.where(core == 0, up, down)


def block_of(peer, peers):
    chips = peers // 2
    return place_of(peer // 2, chips, peer % 2) + jnp.where(peer % 2 == my_core(), 0, chips)


def to_wire(rows, send):
    half = rows.shape[0] // 4 * 2
    send[: rows.shape[0] - half] = rows[half:]
    send[rows.shape[0] - half :] = rows[:half]


def from_wire(recv):
    half = recv.shape[0] // 4 * 2
    return jnp.concatenate([recv[recv.shape[0] - half :], recv[: recv.shape[0] - half]], axis=0)


def need_kernel(cap, *refs):
    ins, outs = refs[:9], refs[9:]
    *small, pneed_ref, qneed_ref, send_ref, sems = outs
    copies = [
        pltpu.make_async_copy(src, dst, sems.at[i])
        for i, (src, dst) in enumerate(zip(ins, [*small, pneed_ref, qneed_ref]))
    ]
    start(copies)
    slots = pneed_ref.shape[1]
    step = send_ref.shape[0] // (slots // cap // 2)
    for copy in copies:
        copy.wait()
    f, n = small[0][...], small[1][...]
    own_p, own_q = pneed_ref[...].astype(f32), qneed_ref[...].astype(f32)
    row = iota((8, slots), 0)
    lists = jnp.where(row == 0, own_p, jnp.where(row == 1, own_q, 0.0))
    if slots < 128:
        lists = jnp.concatenate([lists, jnp.zeros((8, 128 - slots), f32)], axis=1)
    block = jnp.concatenate([f, n, lists], axis=0)
    for chip in range(slots // cap // 2):
        send_ref[chip * step : (chip + 1) * step] = block


def prepare_kernel(
    cap,
    count_ref,
    kblock_ref,
    partner_ref,
    qslot_ref,
    f_ref,
    pneed_ref,
    qneed_ref,
    c_hbm,
    held_ref,
    t_hbm,
    pair_ref,
    gk_ref,
    sk_ref,
    sp_ref,
    sp4_ref,
    near_ref,
    list_ref,
    mine_ref,
    b0_ref,
    b1_ref,
    w_ref,
    c_ref,
    in_sems,
    t_ref,
    out_sems,
):
    start_chunks(c_hbm, c_ref, in_sems)
    tiles = kblock_ref.shape[1]
    kb = f_ref.shape[0]
    used = iota((1, tiles), 1) < count_ref[0]
    k = kblock_ref[...]
    e = partner_ref[...]
    q = qslot_ref[...]
    rows4 = sp4_ref.shape[0]
    ind = lambda m: jnp.where(m, 1.0, 0.0)
    k_hot = ind(iota((kb, tiles), 0) == k)
    gk_ref[...] = k_hot.T.astype(bf16)
    own = add_rows(gk_ref[...], f_ref[...])
    left_sides(1.0 - own, own, w_ref)
    sk_ref[...] = jnp.where(used, k_hot, 0.0).astype(bf16)
    x = iota((rows4, tiles), 0)
    row_e = (e // cap) * (2 * cap) + e % cap
    row_p = (q // cap) * (2 * cap) + cap + q % cap
    p_hot = ind(x == row_p)
    pair_ref[...] = jnp.concatenate([ind(x == row_e), p_hot], axis=0).T.astype(bf16)
    sp4_ref[...] = jnp.where(used, p_hot, 0.0).astype(bf16)
    sp_ref[...] = jnp.where(used, ind(iota(sp_ref.shape, 0) == q), 0.0).astype(bf16)
    rows, half = list_ref.shape
    slots = pneed_ref.shape[1]
    peers = slots // cap
    x = iota((rows, slots), 0)
    y = iota((rows, slots), 1)
    peer, r = x // (2 * cap), x % (2 * cap)
    e_here = (r < cap) & (y == peer * cap + r)
    p_here = (r >= cap) & (y == peer * cap + r - cap)
    pn = jnp.broadcast_to(pneed_ref[...].astype(f32), (rows, slots))
    qn = jnp.broadcast_to(qneed_ref[...].astype(f32), (rows, slots)) + float(kb)
    col = jnp.sum(jnp.where(e_here, pn, 0.0) + jnp.where(p_here, qn, 0.0), axis=1, keepdims=True)
    mine_ref[...] = jnp.broadcast_to(col, (rows, 128))
    start_of = block_of(iota((rows, 1), 0) // (2 * cap), peers) * (2 * half // peers)
    place = col + start_of.astype(f32)
    lane = iota((rows, half), 1).astype(f32)
    near_ref[...] = ind(lane == place).astype(bf16)
    list_ref[...] = ind(lane + float(half) == place).astype(bf16)

    size = c_ref.shape[0] // CHUNKS
    held = held_ref.shape[0] // size

    rest = CHUNKS - held

    def to_held(i, _):
        chunk_copy(c_hbm, c_ref, in_sems, i).wait()
        chunk_products(w_ref, c_ref, i, 0, b0_ref, b1_ref)
        for t in range(size):
            held_ref[i * size + t] = c_ref[i * size + t].T
        return 0

    def to_rest(i, _):
        chunk_copy(c_hbm, c_ref, in_sems, held + i).wait()
        chunk_products(w_ref, c_ref, held + i, 0, b0_ref, b1_ref)
        for t in range(size):
            t_ref[i * size + t] = c_ref[(held + i) * size + t].T
        chunk_copy(t_ref, t_hbm, out_sems, i).start()
        return 0

    lax.fori_loop(0, held, to_held, 0)
    lax.fori_loop(0, rest, to_rest, 0)
    for i in range(rest):
        chunk_copy(t_ref, t_hbm, out_sems, i).wait()


def blocks(ref, count_of_blocks, first, count):
    step = ref.shape[0] // count_of_blocks
    parts = [ref[b * step + first : b * step + first + count] for b in range(count_of_blocks)]
    return jnp.concatenate(parts, axis=0)


def serve_kernel(
    cap,
    kb,
    qb,
    count_ref,
    qslot_ref,
    asked_ref,
    hot_ref,
    mine_ref,
    share_ref,
    gp8_ref,
    sp8_ref,
    s8_ref,
    st4_ref,
    st8a_ref,
    st8b_ref,
):
    hot = hot_ref[...]
    rows4, rows8 = hot.shape[0], s8_ref.shape[0]
    q = qslot_ref[...]
    tiles = q.shape[1]
    used = iota((1, tiles), 1) < count_ref[0]
    ind = lambda m: jnp.where(m, 1.0, 0.0)
    x = iota((rows8, tiles), 0)
    row_z = (q // cap) * (4 * cap) + q % cap
    gp8_ref[...] = ind(x == row_z).T.astype(bf16)
    sp8_ref[...] = jnp.concatenate(
        [
            jnp.where(used, ind(x == row_z + cap), 0.0),
            jnp.where(used, ind(x == row_z + 2 * cap), 0.0),
        ],
        axis=1,
    ).astype(bf16)
    x = iota((rows8, rows4), 0)
    y = iota((rows8, rows4), 1)
    peer, r = x // (4 * cap), x % (4 * cap)
    source = peer * (2 * cap) + cap + r % cap

    def rows_of(kind):
        here = (y == source) & (r // cap == kind)
        return dot(jnp.where(here, 1.0, 0.0).astype(bf16), hot)

    s8_ref[...] = rows_of(0).astype(bf16)
    st4_ref[...] = hot.astype(f32).T[kb : kb + qb].astype(bf16)
    st8a_ref[...] = rows_of(1).T[kb : kb + qb].astype(bf16)
    st8b_ref[...] = rows_of(2).T[kb : kb + qb].astype(bf16)

    peers = rows4 // (2 * cap)
    slots = peers * cap
    wide = peers * slots
    lists = asked_ref[...]
    pick_q = iota((peers, 8 * peers), 1) == 8 * iota((peers, 8 * peers), 0) + 1
    every_q = dot(jnp.where(pick_q, 1.0, 0.0).astype(bf16), lists).astype(bf16)
    tiled = iota((128, wide), 0) == iota((128, wide), 1) % slots
    spread = dot(every_q, jnp.where(tiled, 1.0, 0.0).astype(bf16))
    lane = iota((1, wide), 1)
    here = iota((peers, wide), 0) == lane // slots
    q = jnp.sum(jnp.where(here, spread, 0.0), axis=0, keepdims=True)
    ids = q + (lane % slots // cap * qb).astype(f32)
    row = iota((rows4, 1), 0)
    col = mine_ref[...][:, :1]
    my_ids = col - float(kb) + (row // (2 * cap) * qb).astype(f32)
    my_ids = jnp.where(row % (2 * cap) >= cap, my_ids, -1.0)
    owned = (lax.axis_index("bulk") * qb + iota((qb, 1), 0)).astype(f32)
    wanted = jnp.concatenate([my_ids, owned], axis=0)
    share_ref[...] = jnp.where(ids == wanted, 1.0, 0.0).astype(bf16)


def thermal_of(energy_ref):
    return 1.0 / (jnp.exp(energy_ref[...]) - 1.0)


def put_broadcast(send, served, contributions):
    slots = contributions.shape[0]
    chips = served.shape[0] // 8
    for chip in range(chips):
        at = pl.multiple_of(place_of(chip, chips, my_core()) * (8 + slots), 8)
        send[pl.ds(at, 8)] = served[chip * 8 : chip * 8 + 8]
        send[chip * (8 + slots) + 8 : (chip + 1) * (8 + slots)] = contributions


def phonon_terms(far, bose, b0_ref, b1_ref):
    gain = far * flat(b0_ref)
    return gain + bose * (gain - (1.0 - far) * flat(b1_ref))


def fetch_copy(c_hbm, fetched_ref, sem):
    count = fetched_ref.shape[0]
    return pltpu.make_async_copy(
        c_hbm.at[pl.ds(c_hbm.shape[0] - count, count)], fetched_ref, sem.at[0]
    )


def near_rows_kernel(same_ref, list_ref, c_hbm, part_ref, fetched_ref, sem):
    copy = fetch_copy(c_hbm, fetched_ref, sem)
    copy.start()
    part_ref[...] = add_rows(list_ref[...], same_ref[...])
    copy.wait()


def half_of_devices(cap, chips, weight, others, ref, share_ref):
    rows4 = 4 * cap * chips
    wide = share_ref.shape[1] // 2
    x = iota((rows4, 8 * chips), 0)
    peer = x // (2 * cap)
    source = 8 * place_of(peer // 2, chips, peer % 2) + 2 * cap * my_core() + x % (2 * cap)
    wanted_core = (my_core() + others) % 2
    at = (iota((rows4, 8 * chips), 1) == source) & (peer % 2 == wanted_core)
    heads = add_rows(jnp.where(at, 1.0, 0.0).astype(bf16), blocks(ref, chips, 0, 8))
    tails = blocks(ref, chips, 8, wide // chips)
    sums = add_rows(share_ref[:, others * wide : (others + 1) * wide], tails)
    return heads + weight * sums[:rows4], sums[rows4:]


def near_half_kernel(
    cap, chips, weight, same_ref, share_ref, c_hbm, part_ref, total_ref, fetched_ref, sem
):
    copy = fetch_copy(c_hbm, fetched_ref, sem)
    copy.start()
    part, total = half_of_devices(cap, chips, weight, 0, same_ref, share_ref)
    part_ref[...] = part
    total_ref[...] = total
    copy.wait()


def first_kernel(
    cap,
    same_ref,
    other_ref,
    part_ref,
    list_ref,
    f_ref,
    n_ref,
    energy_ref,
    decay_ref,
    pair_ref,
    sk_ref,
    sp_ref,
    b0_ref,
    b1_ref,
    held_ref,
    fetched_ref,
    c_hbm,
    send,
    e_ref,
    f1_ref,
    hot_ref,
    asked_ref,
    w_ref,
    c_ref,
    sems,
    o0,
    o1,
):
    start_chunks(c_hbm, c_ref, sems)
    f, n = f_ref[...], n_ref[...]
    kb, qb = f.shape[0], n.shape[0]
    rows4 = list_ref.shape[0]
    peers = rows4 // (2 * cap)
    got = part_ref[...] + add_rows(list_ref[...], other_ref[...])
    far, bose = gather_pair(pair_ref[...], got)
    contributions = add_rows(sp_ref[...], phonon_terms(far, bose, b0_ref, b1_ref))
    lists = jnp.concatenate(
        [blocks(ref, peers // 2, kb + qb, 8) for ref in (same_ref, other_ref)], axis=0
    ).astype(bf16)
    asked_ref[...] = lists
    x = iota((rows4, 8 * peers), 0)
    r = x % (2 * cap)
    kind = jnp.where(r < cap, 0, 1)
    at = iota((rows4, 8 * peers), 1) == 8 * block_of(x // (2 * cap), peers) + kind
    asked = dot(jnp.where(at, 1.0, 0.0).astype(bf16), lists)
    r = iota((rows4, 128), 0) % (2 * cap)
    lane = iota((rows4, 128), 1)
    wanted = lane == lax.axis_index("bulk") * cap + r % cap
    col = jnp.sum(jnp.where(wanted, asked, 0.0), axis=1, keepdims=True)
    col = col + jnp.where(r[:, :1] < cap, 0.0, float(kb))
    hot = jnp.where(lane.astype(f32) == col, 1.0, 0.0).astype(bf16)
    hot_ref[...] = hot
    base = n - DT * decay_ref[...] * (n - thermal_of(energy_ref))
    parts = forward_parts(w_ref, held_ref, fetched_ref, c_ref, c_hbm, sems)
    rate = electron_rate(sk_ref[...], far, bose, f, parts, w_ref, o0, o1)
    f1 = f + DT * rate
    e_ref[...] = rate
    f1_ref[...] = f1
    put_broadcast(send, add_rows(hot, padded(f1, base)), contributions)


def middle_kernel(
    cap,
    ends,
    part_ref,
    total_ref,
    other_ref,
    share_ref,
    serve_ref,
    f_ref,
    e_ref,
    own_ref,
    n_ref,
    energy_ref,
    decay_ref,
    pair_ref,
    sk_ref,
    sp_ref,
    b0_ref,
    b1_ref,
    held_ref,
    fetched_ref,
    c_hbm,
    send,
    *refs,
):
    w_ref, c_ref, sems, o0, o1 = refs[-5:]
    start_chunks(c_hbm, c_ref, sems)
    chips = serve_ref.shape[0] // (4 * cap)
    weight = DT / 2.0 if ends else DT
    part, total = half_of_devices(cap, chips, weight, 1, other_ref, share_ref)
    got = part_ref[...] + part
    total = total_ref[...] + total
    far, bose = gather_pair(pair_ref[...], got)
    terms = phonon_terms(far, bose, b0_ref, b1_ref)
    contributions = add_rows(sp_ref[...], terms)
    n = n_ref[...]
    own = own_ref[...]
    parts = forward_parts(w_ref, held_ref, fetched_ref, c_ref, c_hbm, sems)
    if ends:
        n2_ref, e2_ref, f3_ref = refs[:3]
        n2_ref[...] = n + (DT / 2.0) * total
        rate = electron_rate(sk_ref[...], far, bose, own, parts, w_ref, o0, o1)
        f3 = own + DT * rate
        e2_ref[...] = rate
        f3_ref[...] = f3
        to_wire(add_rows(serve_ref[...], padded(f3)) + contributions, send)
    else:
        base_ref, f2_ref = refs[:2]
        thermal = thermal_of(energy_ref)
        decay = decay_ref[...]
        p0 = total - decay * (n - thermal)
        n1 = n + DT * p0
        base = n + (DT / 2.0) * (p0 - decay * (n1 - thermal))
        base_ref[...] = base
        rate = electron_rate(sk_ref[...], far, bose, own, parts, w_ref, o0, o1)
        f2 = f_ref[...] + (DT / 2.0) * (e_ref[...] + rate)
        f2_ref[...] = f2
        put_broadcast(send, add_rows(serve_ref[...], padded(f2, base)), contributions)


def backward_kernel(f_ref, gk_ref, c_hbm, b0_ref, b1_ref, w_ref, c_ref, sems):
    start_chunks(c_hbm, c_ref, sems)
    own = add_rows(gk_ref[...], f_ref[...])
    backward_pass(own, c_hbm, c_ref, sems, w_ref, b0_ref, b1_ref)


def phonon_kernel(
    kb,
    recv,
    n_ref,
    energy_ref,
    decay_ref,
    pair_ref,
    st4_ref,
    sp8_ref,
    s8_ref,
    b0_ref,
    b1_ref,
    send,
    p_ref,
    n1_ref,
    far_ref,
):
    n = n_ref[...]
    got = from_wire(recv)
    thermal = thermal_of(energy_ref)
    rate = add_rows(st4_ref[...], got) - decay_ref[...] * (n - thermal)
    n1 = n + DT * rate
    p_ref[...] = rate
    n1_ref[...] = n1
    far = add_rows(pair_ref[:, : got.shape[0]], got)
    far_ref[...] = far
    gain = far * flat(b0_ref)
    both = jnp.concatenate([gain, gain - (1.0 - far) * flat(b1_ref)], axis=0)
    state = padded(jnp.zeros((kb, 128), f32), n1)
    to_wire(add_rows(s8_ref[...], state) + add_rows(sp8_ref[...], both), send)


def last_kernel(recv, *refs):
    far_ref, f_ref, f1_ref, e_ref, n_ref, n1_ref, p_ref, energy_ref, decay_ref = refs[:9]
    gp8_ref, sk_ref, st8a_ref, st8b_ref, held_ref, c_hbm = refs[9:15]
    refs = refs[15:]
    f2_ref, n2_ref, w_ref, c_ref, sems, o0, o1 = refs
    start_chunks(c_hbm, c_ref, sems)
    got = from_wire(recv)
    n, n1 = n_ref[...], n1_ref[...]
    bose = add_rows(gp8_ref[...], got)
    thermal = thermal_of(energy_ref)
    p1 = (
        add_rows(st8a_ref[...], got)
        + n1 * add_rows(st8b_ref[...], got)
        - decay_ref[...] * (n1 - thermal)
    )
    n2 = n + (DT / 2.0) * (p_ref[...] + p1)
    n2_ref[...] = n2
    parts = forward_parts(w_ref, held_ref, None, c_ref, c_hbm, sems)
    rate = electron_rate(sk_ref[...], far_ref[...], bose, f1_ref[...], parts, w_ref, o0, o1)
    f2 = f_ref[...] + (DT / 2.0) * (e_ref[...] + rate)
    f2_ref[...] = f2


def call(kernel, name, outs, scratch=(), spaces=None, out_spaces=None, flops=0, seen=0):
    def run(*args):
        places = dict(spaces or {})
        args = [
            pltpu.with_memory_space_constraint(x, pltpu.HBM)
            if places.get(i) is pltpu.HBM
            else x
            for i, x in enumerate(args)
        ]
        specs = [
            pl.BlockSpec(memory_space=places.get(i, pltpu.VMEM)) for i in range(len(args))
        ]
        return pl.pallas_call(
            kernel,
            out_shape=[
                (out_spaces or {}).get(i, jax.ShapeDtypeStruct)(*o) for i, o in enumerate(outs)
            ],
            in_specs=specs,
            out_specs=[
                pl.BlockSpec(memory_space=(out_spaces or {}).get(i, pltpu.VMEM))
                for i in range(len(outs))
            ],
            scratch_shapes=list(scratch),
            compiler_params=pltpu.CompilerParams(vmem_limit_bytes=VMEM_LIMIT),
            cost_estimate=pl.CostEstimate(
                flops=flops, bytes_accessed=seen, transcendentals=0
            ),
            name=name,
        )(*args)

    return run


def on_device(
    electrons,
    phonons,
    phonon_energy,
    phonon_decay,
    coupling,
    tile_kblock,
    tile_partner,
    tile_qslot,
    tile_count,
    partner_need,
    phonon_need,
):
    devices = lax.axis_size("bulk")
    kb = electrons.shape[0]
    qb = phonons.shape[0]
    tiles = coupling.shape[0]
    cap = partner_need.shape[1] // devices
    assert cap == phonon_need.shape[1] // devices and kb + qb <= 128
    rows4 = devices * 2 * cap
    rows8 = devices * 4 * cap
    groups = tiles // 8
    held = HELD_CHUNKS * (tiles // CHUNKS)
    weights = pltpu.VMEM((groups, 16, 1024), bf16)
    streams = [weights, pltpu.VMEM(coupling.shape, bf16), pltpu.SemaphoreType.DMA((CHUNKS,))]
    rest = (tiles - held, 128, 128)
    rest_sems = pltpu.SemaphoreType.DMA((CHUNKS - HELD_CHUNKS,))
    forward_streams = [weights, pltpu.VMEM(rest, bf16), rest_sems]
    sums = [pltpu.VMEM((groups, 8, 128), f32)] * 2
    pass_out = [((groups, 8, 128), f32)] * 2
    block4 = ((rows4, 128), f32)
    block8 = ((rows8, 128), f32)

    work = dict(flops=2 * tiles * 16 * 128 * 128, seen=tiles * 128 * 128 * 2)

    def exchange(x):
        order = [[(i + devices // 4 * 2) % devices for i in range(devices)]]
        return lax.all_to_all(
            x, "bulk", split_axis=0, concat_axis=0, tiled=True, axis_index_groups=order
        )

    ints = ((1, tiles), jnp.int32)
    lists = ((1, partner_need.shape[1]), jnp.int32)
    small = [((kb, 128), f32)] + [((qb, 128), f32)] * 3 + [ints] * 3
    step_rows = kb + qb + 8
    slots = devices * cap
    wide = 8 + slots
    assert step_rows % 8 == 0 and slots % 8 == 0 and slots <= 128
    assert devices % 2 == 0 and cap == 2
    chips = devices // 2
    same_core = [
        [(i + chips // 2) % chips * 2 for i in range(chips)],
        [(chips // 2 - 1 - i) % chips * 2 + 1 for i in range(chips)],
    ]

    def to_chips(x):
        return lax.all_to_all(
            x, "bulk", split_axis=0, concat_axis=0, tiled=True, axis_index_groups=same_core
        )

    def between_cores(x):
        return lax.ppermute(x, "bulk", [(i, i ^ 1) for i in range(devices)])

    f, n, energy, decay, kblock, partner, qslot, pneed, qneed, send = call(
        functools.partial(need_kernel, cap),
        "need",
        small + [lists, lists, ((chips * step_rows, 128), f32)],
        [pltpu.SemaphoreType.DMA((9,))],
        spaces={i: pltpu.HBM for i in range(9)},
    )(
        electrons,
        phonons,
        phonon_energy,
        phonon_decay,
        tile_kblock.reshape(1, tiles),
        tile_partner.reshape(1, tiles),
        tile_qslot.reshape(1, tiles),
        partner_need,
        phonon_need,
    )
    same = to_chips(send)
    c_held, c_rest, pair, gk, sk, sp, sp4, near, far_picks, mine, b0, b1 = call(
        functools.partial(prepare_kernel, cap),
        "prepare",
        [
            ((held, 128, 128), bf16),
            (rest, bf16),
            ((tiles, 2 * rows4), bf16),
            ((tiles, kb), bf16),
            ((kb, tiles), bf16),
            ((slots, tiles), bf16),
            ((rows4, tiles), bf16),
            ((rows4, chips * step_rows), bf16),
            ((rows4, chips * step_rows), bf16),
            ((rows4, 128), f32),
        ]
        + pass_out,
        [*streams, pltpu.VMEM(rest, bf16), rest_sems],
        spaces={0: pltpu.SMEM, 7: pltpu.HBM},
        out_spaces={1: pltpu.HBM},
        **work,
    )(tile_count, kblock, partner, qslot, f, pneed, qneed, coupling)
    same, c_held, b0 = lax.optimization_barrier((same, c_held, b0))
    wide_block = ((chips * wide, 128), f32)
    k_rows, q_rows = ((kb, 128), f32), ((qb, 128), f32)
    width = tiles // CHUNKS
    fetched = ((width, 128, 128), bf16)
    fetch_sem = pltpu.SemaphoreType.DMA((1,))
    short = (rest[0] - width, 128, 128)
    short_sems = pltpu.SemaphoreType.DMA((CHUNKS - HELD_CHUNKS - 1,))
    forward_scratch = [weights, pltpu.VMEM(short, bf16), short_sems] + sums
    other = between_cores(same)
    part, c_fetched = call(
        near_rows_kernel,
        "near_rows",
        [block4, fetched],
        [fetch_sem],
        spaces={2: pltpu.HBM},
        out_spaces={1: pltpu.VMEM},
    )(same, near, c_rest)
    send, e0, f1, serve, asked = call(
        functools.partial(first_kernel, cap),
        "first",
        [wide_block, k_rows, k_rows, ((rows4, 128), bf16), ((8 * devices, 128), bf16)],
        forward_scratch,
        spaces={15: pltpu.HBM},
        **work,
    )(same, other, part, far_picks, f, n, energy, decay, pair, sk, sp, b0, b1, c_held, c_fetched, c_rest)
    share, gp8, sp8, s8, st4, st8a, st8b = call(
        functools.partial(serve_kernel, cap, kb, qb),
        "serve",
        [
            ((rows4 + qb, devices * slots), bf16),
            ((tiles, rows8), bf16),
            ((rows8, 2 * tiles), bf16),
            ((rows8, 128), bf16),
            ((qb, rows4), bf16),
            ((qb, rows8), bf16),
            ((qb, rows8), bf16),
        ],
        spaces={0: pltpu.SMEM},
    )(tile_count, qslot, asked, serve, mine)
    back = call(backward_kernel, "backward", pass_out, streams, spaces={2: pltpu.HBM}, **work)

    def middle(ends, send, outs, f, e, own, n, contributions, share):
        same = to_chips(send)
        b0, b1 = back(own, gk, coupling)
        same, b0, share = lax.optimization_barrier((same, b0, share))
        other = between_cores(same)
        weight = DT / 2.0 if ends else DT
        part, total, c_fetched = call(
            functools.partial(near_half_kernel, cap, chips, weight),
            "near_half",
            [block4, q_rows, fetched],
            [fetch_sem],
            spaces={2: pltpu.HBM},
            out_spaces={2: pltpu.VMEM},
        )(same, share, c_rest)
        return call(
            functools.partial(middle_kernel, cap, ends),
            "middle",
            outs,
            forward_scratch,
            spaces={18: pltpu.HBM},
            **work,
        )(
            part, total, other, share, serve, f, e, own, n, energy, decay,
            pair, sk, contributions, b0, b1, c_held, c_fetched, c_rest,
        )

    send, base, f2 = middle(False, send, [wide_block, q_rows, k_rows], f, e0, f1, n, sp, share)
    send, n2, e2, f3 = middle(
        True, send, [block4, q_rows, k_rows, k_rows], f2, e0, f2, base, sp4, share
    )
    recv = exchange(send)
    b0, b1 = back(f3, gk, coupling)
    send, p2, n3, far = call(
        functools.partial(phonon_kernel, kb),
        "phonon",
        [block8, q_rows, q_rows, ((tiles, 128), f32)],
    )(recv, n2, energy, decay, pair, st4, sp8, s8, b0, b1)
    recv = exchange(send)
    f, n = call(
        last_kernel,
        "last",
        [k_rows, q_rows],
        forward_streams + sums,
        spaces={15: pltpu.HBM},
        **work,
    )(
        recv, far, f2, f3, e2, n2, n3, p2, energy, decay,
        gp8, sk, st8a, st8b, c_held, c_rest,
    )
    return (f, n)


def solution(mesh):
    placed = (
        P(("groups", "bulk"), None),
        P(("groups", "bulk"), None),
        P("bulk", None),
        P("bulk", None),
        P("bulk", None, None),
        P("bulk"),
        P("bulk"),
        P("bulk"),
        P("bulk"),
        P("bulk", None),
        P("bulk", None),
    )
    return jax.shard_map(
        on_device,
        mesh=mesh,
        in_specs=placed,
        out_specs=(P(("groups", "bulk"), None), P(("groups", "bulk"), None)),
        check_vma=False,
    )
```

```python
import functools

import jax
import jax.numpy as jnp
from jax import lax
from jax.experimental import pallas as pl
from jax.experimental.pallas import tpu as pltpu
from jax.sharding import PartitionSpec as P

DT = 0.05
CHUNKS = 8
HELD_CHUNKS = 2
f32 = jnp.float32
bf16 = jnp.bfloat16
VMEM_LIMIT = 48 * 1024 * 1024


def iota(shape, dim):
    return lax.broadcasted_iota(jnp.int32, shape, dim)


def dot(a, b):
    return lax.dot_general(a, b, (((1,), (0,)), ((), ())), preferred_element_type=f32)


def add_rows(onehot, x):
    hi = x.astype(bf16)
    mid = (x - hi.astype(f32)).astype(bf16)
    both = dot(onehot, jnp.concatenate([hi, mid], axis=1))
    return both[:, :128] + both[:, 128:]


def gather_pair(table, x):
    rows = x.shape[0]
    hi = x.astype(bf16)
    mid = (x - hi.astype(f32)).astype(bf16)
    blank = jnp.zeros((rows, 128), bf16)

    def both(part):
        upper = jnp.concatenate([part, blank], axis=1)
        lower = jnp.concatenate([blank, part], axis=1)
        return dot(table, jnp.concatenate([upper, lower], axis=0))

    res = both(hi) + both(mid)
    return res[:, :128], res[:, 128:]


def stacked(first, second):
    tiles = first.shape[0]
    return jnp.concatenate(
        [first.reshape(tiles // 8, 8, 128), second.reshape(tiles // 8, 8, 128)], axis=1
    ).astype(bf16)


def row_is(r):
    return iota((32, 128), 0) % 8 == r


def padded(*parts):
    rows = sum(p.shape[0] for p in parts)
    return jnp.concatenate([*parts, jnp.zeros((128 - rows, 128), f32)], axis=0)


def flat(ref):
    return ref[...].reshape(-1, 128)


def chunk_copy(src, dst, sems, i):
    size = min(src.shape[0], dst.shape[0]) // sems.shape[0]
    here = pl.ds(i * size, size)
    return pltpu.make_async_copy(src.at[here], dst.at[here], sems.at[i])


def start_chunks(src, dst, sems):
    for i in range(sems.shape[0]):
        chunk_copy(src, dst, sems, i).start()


def start(copies):
    for copy in copies:
        copy.start()


def block_diagonal(w):
    w = w.astype(f32)
    return jnp.concatenate(
        [jnp.where(row_is(r), w, 0.0).astype(bf16) for r in range(8)], axis=1
    )


def left_sides(first, second, w_ref):
    pairs = w_ref.shape[0]
    w_ref[:, :, :128] = stacked(first, second).reshape(pairs, 32, 128)

    def spread(g, _):
        w_ref[g] = block_diagonal(w_ref[g, :, :128])
        return 0

    lax.fori_loop(0, pairs, spread, 0, unroll=2)


def chunk_products(w_ref, c_ref, i, base, out0, out1):
    size = out0.shape[0] // CHUNKS
    for k in range(0, size, 2):
        g = i * size + k
        tiles = [c_ref[pl.ds((g + j) * 8, 8)].reshape(1024, 128) for j in (0, 1)]
        res = dot(w_ref[(base + g) // 2], jnp.concatenate(tiles, axis=1))
        for j in (0, 1):
            own = res[16 * j : 16 * (j + 1), 128 * j : 128 * (j + 1)]
            out0[base + g + j] = own[:8]
            out1[base + g + j] = own[8:]


def tile_products(w_ref, parts, out0, out1):
    size = out0.shape[0] // CHUNKS
    for c_ref, c_hbm, sems, base in parts:
        chunks = c_ref.shape[0] // 8 // size

        def chunk(i, _):
            if c_hbm is not None:
                chunk_copy(c_hbm, c_ref, sems, i).wait()
            chunk_products(w_ref, c_ref, i, base, out0, out1)
            return 0

        lax.fori_loop(0, chunks, chunk, 0)


def backward_pass(own, c_hbm, c_ref, sems, w_ref, out0, out1):
    left_sides(1.0 - own, own, w_ref)
    tile_products(w_ref, [(c_ref, c_hbm, sems, 0)], out0, out1)


def forward_parts(w_ref, held_ref, fetched_ref, c_ref, c_hbm, sems):
    parts = [(held_ref, None, None, 0)]
    if fetched_ref is not None:
        parts.append((fetched_ref, None, None, 2 * w_ref.shape[0] - fetched_ref.shape[0] // 8))
    return parts + [(c_ref, c_hbm, sems, held_ref.shape[0] // 8)]


def electron_rate(sum_k, far, bose, f, parts, w_ref, o0, o1):
    left_sides(far * (1.0 + bose), far + bose, w_ref)
    tile_products(w_ref, parts, o0, o1)
    gain, loss = flat(o0), flat(o1)
    gain_hi, loss_hi = gain.astype(bf16), loss.astype(bf16)
    gain_lo = (gain - gain_hi.astype(f32)).astype(bf16)
    loss_lo = (loss - loss_hi.astype(f32)).astype(bf16)
    sums = dot(sum_k, jnp.concatenate([gain_hi, gain_lo, loss_hi, loss_lo], axis=1))
    return sums[:, :128] + sums[:, 128:256] - f * (sums[:, 256:384] + sums[:, 384:])


def my_core():
    return lax.rem(lax.axis_index("bulk"), 2)


def place_of(chip, chips):
    return (chip + chips - chips // 2) % chips


def block_of(peer, peers):
    chips = peers // 2
    return place_of(peer // 2, chips) + jnp.where(peer % 2 == my_core(), 0, chips)


def to_wire(rows, send):
    half = rows.shape[0] // 4 * 2
    send[: rows.shape[0] - half] = rows[half:]
    send[rows.shape[0] - half :] = rows[:half]


def from_wire(recv):
    half = recv.shape[0] // 4 * 2
    return jnp.concatenate([recv[recv.shape[0] - half :], recv[: recv.shape[0] - half]], axis=0)


def need_kernel(cap, *refs):
    ins, outs = refs[:9], refs[9:]
    *small, pneed_ref, qneed_ref, send_ref, sems = outs
    copies = [
        pltpu.make_async_copy(src, dst, sems.at[i])
        for i, (src, dst) in enumerate(zip(ins, [*small, pneed_ref, qneed_ref]))
    ]
    start(copies)
    slots = pneed_ref.shape[1]
    step = send_ref.shape[0] // (slots // cap // 2)
    for copy in copies:
        copy.wait()
    f, n = small[0][...], small[1][...]
    own_p, own_q = pneed_ref[...].astype(f32), qneed_ref[...].astype(f32)
    row = iota((8, slots), 0)
    lists = jnp.where(row == 0, own_p, jnp.where(row == 1, own_q, 0.0))
    if slots < 128:
        lists = jnp.concatenate([lists, jnp.zeros((8, 128 - slots), f32)], axis=1)
    block = jnp.concatenate([f, n, lists], axis=0)
    for chip in range(slots // cap // 2):
        send_ref[chip * step : (chip + 1) * step] = block


def prepare_kernel(
    cap,
    count_ref,
    kblock_ref,
    partner_ref,
    qslot_ref,
    f_ref,
    pneed_ref,
    qneed_ref,
    c_hbm,
    held_ref,
    t_hbm,
    pair_ref,
    gk_ref,
    sk_ref,
    sp_ref,
    sp4_ref,
    near_ref,
    list_ref,
    mine_ref,
    b0_ref,
    b1_ref,
    w_ref,
    c_ref,
    in_sems,
    t_ref,
    out_sems,
):
    start_chunks(c_hbm, c_ref, in_sems)
    tiles = kblock_ref.shape[1]
    kb = f_ref.shape[0]
    used = iota((1, tiles), 1) < count_ref[0]
    k = kblock_ref[...]
    e = partner_ref[...]
    q = qslot_ref[...]
    rows4 = sp4_ref.shape[0]
    ind = lambda m: jnp.where(m, 1.0, 0.0)
    k_hot = ind(iota((kb, tiles), 0) == k)
    gk_ref[...] = k_hot.T.astype(bf16)
    own = add_rows(gk_ref[...], f_ref[...])
    left_sides(1.0 - own, own, w_ref)
    sk_ref[...] = jnp.where(used, k_hot, 0.0).astype(bf16)
    x = iota((rows4, tiles), 0)
    row_e = (e // cap) * (2 * cap) + e % cap
    row_p = (q // cap) * (2 * cap) + cap + q % cap
    p_hot = ind(x == row_p)
    pair_ref[...] = jnp.concatenate([ind(x == row_e), p_hot], axis=0).T.astype(bf16)
    sp4_ref[...] = jnp.where(used, p_hot, 0.0).astype(bf16)
    sp_ref[...] = jnp.where(used, ind(iota(sp_ref.shape, 0) == q), 0.0).astype(bf16)
    rows, half = list_ref.shape
    slots = pneed_ref.shape[1]
    peers = slots // cap
    x = iota((rows, slots), 0)
    y = iota((rows, slots), 1)
    peer, r = x // (2 * cap), x % (2 * cap)
    e_here = (r < cap) & (y == peer * cap + r)
    p_here = (r >= cap) & (y == peer * cap + r - cap)
    pn = jnp.broadcast_to(pneed_ref[...].astype(f32), (rows, slots))
    qn = jnp.broadcast_to(qneed_ref[...].astype(f32), (rows, slots)) + float(kb)
    col = jnp.sum(jnp.where(e_here, pn, 0.0) + jnp.where(p_here, qn, 0.0), axis=1, keepdims=True)
    mine_ref[...] = jnp.broadcast_to(col, (rows, 128))
    start_of = block_of(iota((rows, 1), 0) // (2 * cap), peers) * (2 * half // peers)
    place = col + start_of.astype(f32)
    lane = iota((rows, half), 1).astype(f32)
    near_ref[...] = ind(lane == place).astype(bf16)
    list_ref[...] = ind(lane + float(half) == place).astype(bf16)

    size = c_ref.shape[0] // CHUNKS
    held = held_ref.shape[0] // size

    rest = CHUNKS - held

    def to_held(i, _):
        chunk_copy(c_hbm, c_ref, in_sems, i).wait()
        chunk_products(w_ref, c_ref, i, 0, b0_ref, b1_ref)
        for t in range(size):
            held_ref[i * size + t] = c_ref[i * size + t].T
        return 0

    def to_rest(i, _):
        chunk_copy(c_hbm, c_ref, in_sems, held + i).wait()
        chunk_products(w_ref, c_ref, held + i, 0, b0_ref, b1_ref)
        for t in range(size):
            t_ref[i * size + t] = c_ref[(held + i) * size + t].T
        chunk_copy(t_ref, t_hbm, out_sems, i).start()
        return 0

    lax.fori_loop(0, held, to_held, 0)
    lax.fori_loop(0, rest, to_rest, 0)
    for i in range(rest):
        chunk_copy(t_ref, t_hbm, out_sems, i).wait()


def blocks(ref, count_of_blocks, first, count):
    step = ref.shape[0] // count_of_blocks
    parts = [ref[b * step + first : b * step + first + count] for b in range(count_of_blocks)]
    return jnp.concatenate(parts, axis=0)


def serve_kernel(
    cap,
    kb,
    qb,
    count_ref,
    qslot_ref,
    asked_ref,
    hot_ref,
    mine_ref,
    share_ref,
    gp8_ref,
    sp8_ref,
    s8_ref,
    st4_ref,
    st8a_ref,
    st8b_ref,
):
    hot = hot_ref[...]
    rows4, rows8 = hot.shape[0], s8_ref.shape[0]
    q = qslot_ref[...]
    tiles = q.shape[1]
    used = iota((1, tiles), 1) < count_ref[0]
    ind = lambda m: jnp.where(m, 1.0, 0.0)
    x = iota((rows8, tiles), 0)
    row_z = (q // cap) * (4 * cap) + q % cap
    gp8_ref[...] = ind(x == row_z).T.astype(bf16)
    sp8_ref[...] = jnp.concatenate(
        [
            jnp.where(used, ind(x == row_z + cap), 0.0),
            jnp.where(used, ind(x == row_z + 2 * cap), 0.0),
        ],
        axis=1,
    ).astype(bf16)
    x = iota((rows8, rows4), 0)
    y = iota((rows8, rows4), 1)
    peer, r = x // (4 * cap), x % (4 * cap)
    source = peer * (2 * cap) + cap + r % cap

    def rows_of(kind):
        here = (y == source) & (r // cap == kind)
        return dot(jnp.where(here, 1.0, 0.0).astype(bf16), hot)

    s8_ref[...] = rows_of(0).astype(bf16)
    st4_ref[...] = hot.astype(f32).T[kb : kb + qb].astype(bf16)
    st8a_ref[...] = rows_of(1).T[kb : kb + qb].astype(bf16)
    st8b_ref[...] = rows_of(2).T[kb : kb + qb].astype(bf16)

    peers = rows4 // (2 * cap)
    slots = peers * cap
    wide = peers * slots
    lists = asked_ref[...]
    pick_q = iota((peers, 8 * peers), 1) == 8 * iota((peers, 8 * peers), 0) + 1
    every_q = dot(jnp.where(pick_q, 1.0, 0.0).astype(bf16), lists).astype(bf16)
    tiled = iota((128, wide), 0) == iota((128, wide), 1) % slots
    spread = dot(every_q, jnp.where(tiled, 1.0, 0.0).astype(bf16))
    lane = iota((1, wide), 1)
    here = iota((peers, wide), 0) == lane // slots
    q = jnp.sum(jnp.where(here, spread, 0.0), axis=0, keepdims=True)
    ids = q + (lane % slots // cap * qb).astype(f32)
    row = iota((rows4, 1), 0)
    col = mine_ref[...][:, :1]
    my_ids = col - float(kb) + (row // (2 * cap) * qb).astype(f32)
    my_ids = jnp.where(row % (2 * cap) >= cap, my_ids, -1.0)
    owned = (lax.axis_index("bulk") * qb + iota((qb, 1), 0)).astype(f32)
    wanted = jnp.concatenate([my_ids, owned], axis=0)
    share_ref[...] = jnp.where(ids == wanted, 1.0, 0.0).astype(bf16)


def thermal_of(energy_ref):
    return 1.0 / (jnp.exp(energy_ref[...]) - 1.0)


def put_broadcast(send, served, contributions):
    slots = contributions.shape[0]
    chips = served.shape[0] // 8
    for chip in range(chips):
        at = place_of(chip, chips) * (8 + slots)
        send[at : at + 8] = served[chip * 8 : chip * 8 + 8]
        send[at + 8 : at + 8 + slots] = contributions


def phonon_terms(far, bose, b0_ref, b1_ref):
    gain = far * flat(b0_ref)
    return gain + bose * (gain - (1.0 - far) * flat(b1_ref))


def fetch_copy(c_hbm, fetched_ref, sem):
    count = fetched_ref.shape[0]
    return pltpu.make_async_copy(
        c_hbm.at[pl.ds(c_hbm.shape[0] - count, count)], fetched_ref, sem.at[0]
    )


def near_rows_kernel(same_ref, list_ref, c_hbm, part_ref, fetched_ref, sem):
    copy = fetch_copy(c_hbm, fetched_ref, sem)
    copy.start()
    part_ref[...] = add_rows(list_ref[...], same_ref[...])
    copy.wait()


def half_of_devices(cap, chips, weight, others, ref, share_ref):
    rows4 = 4 * cap * chips
    wide = share_ref.shape[1] // 2
    x = iota((rows4, 8 * chips), 0)
    peer = x // (2 * cap)
    source = 8 * place_of(peer // 2, chips) + 2 * cap * my_core() + x % (2 * cap)
    wanted_core = (my_core() + others) % 2
    at = (iota((rows4, 8 * chips), 1) == source) & (peer % 2 == wanted_core)
    heads = add_rows(jnp.where(at, 1.0, 0.0).astype(bf16), blocks(ref, chips, 0, 8))
    tails = blocks(ref, chips, 8, wide // chips)
    sums = add_rows(share_ref[:, others * wide : (others + 1) * wide], tails)
    return heads + weight * sums[:rows4], sums[rows4:]


def near_half_kernel(
    cap, chips, weight, same_ref, share_ref, c_hbm, part_ref, total_ref, fetched_ref, sem
):
    copy = fetch_copy(c_hbm, fetched_ref, sem)
    copy.start()
    part, total = half_of_devices(cap, chips, weight, 0, same_ref, share_ref)
    part_ref[...] = part
    total_ref[...] = total
    copy.wait()


def first_kernel(
    cap,
    same_ref,
    other_ref,
    part_ref,
    list_ref,
    f_ref,
    n_ref,
    energy_ref,
    decay_ref,
    pair_ref,
    sk_ref,
    sp_ref,
    b0_ref,
    b1_ref,
    held_ref,
    fetched_ref,
    c_hbm,
    send,
    e_ref,
    f1_ref,
    hot_ref,
    asked_ref,
    w_ref,
    c_ref,
    sems,
    o0,
    o1,
):
    start_chunks(c_hbm, c_ref, sems)
    f, n = f_ref[...], n_ref[...]
    kb, qb = f.shape[0], n.shape[0]
    rows4 = list_ref.shape[0]
    peers = rows4 // (2 * cap)
    got = part_ref[...] + add_rows(list_ref[...], other_ref[...])
    far, bose = gather_pair(pair_ref[...], got)
    contributions = add_rows(sp_ref[...], phonon_terms(far, bose, b0_ref, b1_ref))
    lists = jnp.concatenate(
        [blocks(ref, peers // 2, kb + qb, 8) for ref in (same_ref, other_ref)], axis=0
    ).astype(bf16)
    asked_ref[...] = lists
    x = iota((rows4, 8 * peers), 0)
    r = x % (2 * cap)
    kind = jnp.where(r < cap, 0, 1)
    at = iota((rows4, 8 * peers), 1) == 8 * block_of(x // (2 * cap), peers) + kind
    asked = dot(jnp.where(at, 1.0, 0.0).astype(bf16), lists)
    r = iota((rows4, 128), 0) % (2 * cap)
    lane = iota((rows4, 128), 1)
    wanted = lane == lax.axis_index("bulk") * cap + r % cap
    col = jnp.sum(jnp.where(wanted, asked, 0.0), axis=1, keepdims=True)
    col = col + jnp.where(r[:, :1] < cap, 0.0, float(kb))
    hot = jnp.where(lane.astype(f32) == col, 1.0, 0.0).astype(bf16)
    hot_ref[...] = hot
    base = n - DT * decay_ref[...] * (n - thermal_of(energy_ref))
    parts = forward_parts(w_ref, held_ref, fetched_ref, c_ref, c_hbm, sems)
    rate = electron_rate(sk_ref[...], far, bose, f, parts, w_ref, o0, o1)
    f1 = f + DT * rate
    e_ref[...] = rate
    f1_ref[...] = f1
    put_broadcast(send, add_rows(hot, padded(f1, base)), contributions)


def middle_kernel(
    cap,
    ends,
    part_ref,
    total_ref,
    other_ref,
    share_ref,
    serve_ref,
    f_ref,
    e_ref,
    own_ref,
    n_ref,
    energy_ref,
    decay_ref,
    pair_ref,
    sk_ref,
    sp_ref,
    b0_ref,
    b1_ref,
    held_ref,
    fetched_ref,
    c_hbm,
    send,
    *refs,
):
    w_ref, c_ref, sems, o0, o1 = refs[-5:]
    start_chunks(c_hbm, c_ref, sems)
    chips = serve_ref.shape[0] // (4 * cap)
    weight = DT / 2.0 if ends else DT
    part, total = half_of_devices(cap, chips, weight, 1, other_ref, share_ref)
    got = part_ref[...] + part
    total = total_ref[...] + total
    far, bose = gather_pair(pair_ref[...], got)
    terms = phonon_terms(far, bose, b0_ref, b1_ref)
    contributions = add_rows(sp_ref[...], terms)
    n = n_ref[...]
    own = own_ref[...]
    parts = forward_parts(w_ref, held_ref, fetched_ref, c_ref, c_hbm, sems)
    if ends:
        n2_ref, e2_ref, f3_ref = refs[:3]
        n2_ref[...] = n + (DT / 2.0) * total
        rate = electron_rate(sk_ref[...], far, bose, own, parts, w_ref, o0, o1)
        f3 = own + DT * rate
        e2_ref[...] = rate
        f3_ref[...] = f3
        to_wire(add_rows(serve_ref[...], padded(f3)) + contributions, send)
    else:
        base_ref, f2_ref = refs[:2]
        thermal = thermal_of(energy_ref)
        decay = decay_ref[...]
        p0 = total - decay * (n - thermal)
        n1 = n + DT * p0
        base = n + (DT / 2.0) * (p0 - decay * (n1 - thermal))
        base_ref[...] = base
        rate = electron_rate(sk_ref[...], far, bose, own, parts, w_ref, o0, o1)
        f2 = f_ref[...] + (DT / 2.0) * (e_ref[...] + rate)
        f2_ref[...] = f2
        put_broadcast(send, add_rows(serve_ref[...], padded(f2, base)), contributions)


def backward_kernel(f_ref, gk_ref, c_hbm, b0_ref, b1_ref, w_ref, c_ref, sems):
    start_chunks(c_hbm, c_ref, sems)
    own = add_rows(gk_ref[...], f_ref[...])
    backward_pass(own, c_hbm, c_ref, sems, w_ref, b0_ref, b1_ref)


def phonon_kernel(
    kb,
    recv,
    n_ref,
    energy_ref,
    decay_ref,
    pair_ref,
    st4_ref,
    sp8_ref,
    s8_ref,
    b0_ref,
    b1_ref,
    send,
    p_ref,
    n1_ref,
    far_ref,
):
    n = n_ref[...]
    got = from_wire(recv)
    thermal = thermal_of(energy_ref)
    rate = add_rows(st4_ref[...], got) - decay_ref[...] * (n - thermal)
    n1 = n + DT * rate
    p_ref[...] = rate
    n1_ref[...] = n1
    far = add_rows(pair_ref[:, : got.shape[0]], got)
    far_ref[...] = far
    gain = far * flat(b0_ref)
    both = jnp.concatenate([gain, gain - (1.0 - far) * flat(b1_ref)], axis=0)
    state = padded(jnp.zeros((kb, 128), f32), n1)
    to_wire(add_rows(s8_ref[...], state) + add_rows(sp8_ref[...], both), send)


def last_kernel(recv, *refs):
    far_ref, f_ref, f1_ref, e_ref, n_ref, n1_ref, p_ref, energy_ref, decay_ref = refs[:9]
    gp8_ref, sk_ref, st8a_ref, st8b_ref, held_ref, c_hbm = refs[9:15]
    refs = refs[15:]
    f2_ref, n2_ref, w_ref, c_ref, sems, o0, o1 = refs
    start_chunks(c_hbm, c_ref, sems)
    got = from_wire(recv)
    n, n1 = n_ref[...], n1_ref[...]
    bose = add_rows(gp8_ref[...], got)
    thermal = thermal_of(energy_ref)
    p1 = (
        add_rows(st8a_ref[...], got)
        + n1 * add_rows(st8b_ref[...], got)
        - decay_ref[...] * (n1 - thermal)
    )
    n2 = n + (DT / 2.0) * (p_ref[...] + p1)
    n2_ref[...] = n2
    parts = forward_parts(w_ref, held_ref, None, c_ref, c_hbm, sems)
    rate = electron_rate(sk_ref[...], far_ref[...], bose, f1_ref[...], parts, w_ref, o0, o1)
    f2 = f_ref[...] + (DT / 2.0) * (e_ref[...] + rate)
    f2_ref[...] = f2


def call(kernel, name, outs, scratch=(), spaces=None, out_spaces=None, flops=0, seen=0):
    def run(*args):
        places = dict(spaces or {})
        args = [
            pltpu.with_memory_space_constraint(x, pltpu.HBM)
            if places.get(i) is pltpu.HBM
            else x
            for i, x in enumerate(args)
        ]
        specs = [
            pl.BlockSpec(memory_space=places.get(i, pltpu.VMEM)) for i in range(len(args))
        ]
        return pl.pallas_call(
            kernel,
            out_shape=[
                (out_spaces or {}).get(i, jax.ShapeDtypeStruct)(*o) for i, o in enumerate(outs)
            ],
            in_specs=specs,
            out_specs=[
                pl.BlockSpec(memory_space=(out_spaces or {}).get(i, pltpu.VMEM))
                for i in range(len(outs))
            ],
            scratch_shapes=list(scratch),
            compiler_params=pltpu.CompilerParams(vmem_limit_bytes=VMEM_LIMIT),
            cost_estimate=pl.CostEstimate(
                flops=flops, bytes_accessed=seen, transcendentals=0
            ),
            name=name,
        )(*args)

    return run


def on_device(
    electrons,
    phonons,
    phonon_energy,
    phonon_decay,
    coupling,
    tile_kblock,
    tile_partner,
    tile_qslot,
    tile_count,
    partner_need,
    phonon_need,
):
    devices = lax.axis_size("bulk")
    kb = electrons.shape[0]
    qb = phonons.shape[0]
    tiles = coupling.shape[0]
    cap = partner_need.shape[1] // devices
    assert cap == phonon_need.shape[1] // devices and kb + qb <= 128
    rows4 = devices * 2 * cap
    rows8 = devices * 4 * cap
    groups = tiles // 8
    held = HELD_CHUNKS * (tiles // CHUNKS)
    weights = pltpu.VMEM((groups // 2, 32, 1024), bf16)
    streams = [weights, pltpu.VMEM(coupling.shape, bf16), pltpu.SemaphoreType.DMA((CHUNKS,))]
    rest = (tiles - held, 128, 128)
    rest_sems = pltpu.SemaphoreType.DMA((CHUNKS - HELD_CHUNKS,))
    forward_streams = [weights, pltpu.VMEM(rest, bf16), rest_sems]
    sums = [pltpu.VMEM((groups, 8, 128), f32)] * 2
    pass_out = [((groups, 8, 128), f32)] * 2
    block4 = ((rows4, 128), f32)
    block8 = ((rows8, 128), f32)

    work = dict(flops=2 * tiles * 16 * 128 * 128, seen=tiles * 128 * 128 * 2)

    def exchange(x):
        order = [[(i + devices // 4 * 2) % devices for i in range(devices)]]
        return lax.all_to_all(
            x, "bulk", split_axis=0, concat_axis=0, tiled=True, axis_index_groups=order
        )

    ints = ((1, tiles), jnp.int32)
    lists = ((1, partner_need.shape[1]), jnp.int32)
    small = [((kb, 128), f32)] + [((qb, 128), f32)] * 3 + [ints] * 3
    step_rows = kb + qb + 8
    slots = devices * cap
    wide = 8 + slots
    assert step_rows % 8 == 0 and slots % 8 == 0 and slots <= 128
    assert devices % 2 == 0 and cap == 2
    chips = devices // 2
    same_core = [
        [(i + chips // 2) % chips * 2 + core for i in range(chips)] for core in (0, 1)
    ]

    def to_chips(x):
        return lax.all_to_all(
            x, "bulk", split_axis=0, concat_axis=0, tiled=True, axis_index_groups=same_core
        )

    def between_cores(x):
        return lax.ppermute(x, "bulk", [(i, i ^ 1) for i in range(devices)])

    f, n, energy, decay, kblock, partner, qslot, pneed, qneed, send = call(
        functools.partial(need_kernel, cap),
        "need",
        small + [lists, lists, ((chips * step_rows, 128), f32)],
        [pltpu.SemaphoreType.DMA((9,))],
        spaces={i: pltpu.HBM for i in range(9)},
    )(
        electrons,
        phonons,
        phonon_energy,
        phonon_decay,
        tile_kblock.reshape(1, tiles),
        tile_partner.reshape(1, tiles),
        tile_qslot.reshape(1, tiles),
        partner_need,
        phonon_need,
    )
    same = to_chips(send)
    c_held, c_rest, pair, gk, sk, sp, sp4, near, far_picks, mine, b0, b1 = call(
        functools.partial(prepare_kernel, cap),
        "prepare",
        [
            ((held, 128, 128), bf16),
            (rest, bf16),
            ((tiles, 2 * rows4), bf16),
            ((tiles, kb), bf16),
            ((kb, tiles), bf16),
            ((slots, tiles), bf16),
            ((rows4, tiles), bf16),
            ((rows4, chips * step_rows), bf16),
            ((rows4, chips * step_rows), bf16),
            ((rows4, 128), f32),
        ]
        + pass_out,
        [*streams, pltpu.VMEM(rest, bf16), rest_sems],
        spaces={0: pltpu.SMEM, 7: pltpu.HBM},
        out_spaces={1: pltpu.HBM},
        **work,
    )(tile_count, kblock, partner, qslot, f, pneed, qneed, coupling)
    same, c_held, b0 = lax.optimization_barrier((same, c_held, b0))
    wide_block = ((chips * wide, 128), f32)
    k_rows, q_rows = ((kb, 128), f32), ((qb, 128), f32)
    width = tiles // CHUNKS
    fetched = ((width, 128, 128), bf16)
    fetch_sem = pltpu.SemaphoreType.DMA((1,))
    short = (rest[0] - width, 128, 128)
    short_sems = pltpu.SemaphoreType.DMA((CHUNKS - HELD_CHUNKS - 1,))
    forward_scratch = [weights, pltpu.VMEM(short, bf16), short_sems] + sums
    other = between_cores(same)
    part, c_fetched = call(
        near_rows_kernel,
        "near_rows",
        [block4, fetched],
        [fetch_sem],
        spaces={2: pltpu.HBM},
        out_spaces={1: pltpu.VMEM},
    )(same, near, c_rest)
    send, e0, f1, serve, asked = call(
        functools.partial(first_kernel, cap),
        "first",
        [wide_block, k_rows, k_rows, ((rows4, 128), bf16), ((8 * devices, 128), bf16)],
        forward_scratch,
        spaces={15: pltpu.HBM},
        **work,
    )(same, other, part, far_picks, f, n, energy, decay, pair, sk, sp, b0, b1, c_held, c_fetched, c_rest)
    share, gp8, sp8, s8, st4, st8a, st8b = call(
        functools.partial(serve_kernel, cap, kb, qb),
        "serve",
        [
            ((rows4 + qb, devices * slots), bf16),
            ((tiles, rows8), bf16),
            ((rows8, 2 * tiles), bf16),
            ((rows8, 128), bf16),
            ((qb, rows4), bf16),
            ((qb, rows8), bf16),
            ((qb, rows8), bf16),
        ],
        spaces={0: pltpu.SMEM},
    )(tile_count, qslot, asked, serve, mine)
    back = call(backward_kernel, "backward", pass_out, streams, spaces={2: pltpu.HBM}, **work)

    def middle(ends, send, outs, f, e, own, n, contributions, share):
        same = to_chips(send)
        b0, b1 = back(own, gk, coupling)
        same, b0, share = lax.optimization_barrier((same, b0, share))
        other = between_cores(same)
        weight = DT / 2.0 if ends else DT
        part, total, c_fetched = call(
            functools.partial(near_half_kernel, cap, chips, weight),
            "near_half",
            [block4, q_rows, fetched],
            [fetch_sem],
            spaces={2: pltpu.HBM},
            out_spaces={2: pltpu.VMEM},
        )(same, share, c_rest)
        return call(
            functools.partial(middle_kernel, cap, ends),
            "middle",
            outs,
            forward_scratch,
            spaces={18: pltpu.HBM},
            **work,
        )(
            part, total, other, share, serve, f, e, own, n, energy, decay,
            pair, sk, contributions, b0, b1, c_held, c_fetched, c_rest,
        )

    send, base, f2 = middle(False, send, [wide_block, q_rows, k_rows], f, e0, f1, n, sp, share)
    send, n2, e2, f3 = middle(
        True, send, [block4, q_rows, k_rows, k_rows], f2, e0, f2, base, sp4, share
    )
    recv = exchange(send)
    b0, b1 = back(f3, gk, coupling)
    send, p2, n3, far = call(
        functools.partial(phonon_kernel, kb),
        "phonon",
        [block8, q_rows, q_rows, ((tiles, 128), f32)],
    )(recv, n2, energy, decay, pair, st4, sp8, s8, b0, b1)
    recv = exchange(send)
    f, n = call(
        last_kernel,
        "last",
        [k_rows, q_rows],
        forward_streams + sums,
        spaces={15: pltpu.HBM},
        **work,
    )(
        recv, far, f2, f3, e2, n2, n3, p2, energy, decay,
        gp8, sk, st8a, st8b, c_held, c_rest,
    )
    return (f, n)


def solution(mesh):
    placed = (
        P(("groups", "bulk"), None),
        P(("groups", "bulk"), None),
        P("bulk", None),
        P("bulk", None),
        P("bulk", None, None),
        P("bulk"),
        P("bulk"),
        P("bulk"),
        P("bulk"),
        P("bulk", None),
        P("bulk", None),
    )
    return jax.shard_map(
        on_device,
        mesh=mesh,
        in_specs=placed,
        out_specs=(P(("groups", "bulk"), None), P(("groups", "bulk"), None)),
        check_vma=False,
    )
```

```python
import functools

import jax
import jax.numpy as jnp
from jax import lax
from jax.experimental import pallas as pl
from jax.experimental.pallas import tpu as pltpu
from jax.sharding import PartitionSpec as P

DT = 0.05
CHUNKS = 8
HELD_CHUNKS = 2
f32 = jnp.float32
bf16 = jnp.bfloat16
VMEM_LIMIT = 48 * 1024 * 1024


def iota(shape, dim):
    return lax.broadcasted_iota(jnp.int32, shape, dim)


def dot(a, b):
    return lax.dot_general(a, b, (((1,), (0,)), ((), ())), preferred_element_type=f32)


def add_rows(onehot, x):
    hi = x.astype(bf16)
    mid = (x - hi.astype(f32)).astype(bf16)
    both = dot(onehot, jnp.concatenate([hi, mid], axis=1))
    return both[:, :128] + both[:, 128:]


def gather_pair(table, x):
    rows = x.shape[0]
    hi = x.astype(bf16)
    mid = (x - hi.astype(f32)).astype(bf16)
    blank = jnp.zeros((rows, 128), bf16)

    def both(part):
        upper = jnp.concatenate([part, blank], axis=1)
        lower = jnp.concatenate([blank, part], axis=1)
        return dot(table, jnp.concatenate([upper, lower], axis=0))

    res = both(hi) + both(mid)
    return res[:, :128], res[:, 128:]


def stacked(first, second):
    tiles = first.shape[0]
    return jnp.concatenate(
        [first.reshape(tiles // 8, 8, 128), second.reshape(tiles // 8, 8, 128)], axis=1
    ).astype(bf16)


def row_is(r):
    return iota((16, 128), 0) % 8 == r


def padded(*parts):
    rows = sum(p.shape[0] for p in parts)
    return jnp.concatenate([*parts, jnp.zeros((128 - rows, 128), f32)], axis=0)


def flat(ref):
    return ref[...].reshape(-1, 128)


def chunk_copy(src, dst, sems, i):
    size = min(src.shape[0], dst.shape[0]) // sems.shape[0]
    here = pl.ds(i * size, size)
    return pltpu.make_async_copy(src.at[here], dst.at[here], sems.at[i])


def start_chunks(src, dst, sems):
    for i in range(sems.shape[0]):
        chunk_copy(src, dst, sems, i).start()


def start(copies):
    for copy in copies:
        copy.start()


def block_diagonal(w):
    w = w.astype(f32)
    return jnp.concatenate(
        [jnp.where(row_is(r), w, 0.0).astype(bf16) for r in range(8)], axis=1
    )


def left_sides(first, second, w_ref):
    groups = w_ref.shape[0]
    w_ref[:, :, :128] = stacked(first, second)

    def spread(g, _):
        w_ref[g] = block_diagonal(w_ref[g, :, :128])
        return 0

    lax.fori_loop(0, groups, spread, 0, unroll=2)


def chunk_products(w_ref, c_ref, i, base, out0, out1):
    size = w_ref.shape[0] // CHUNKS

    def group(k, _):
        g = i * size + k
        res = dot(w_ref[base + g], c_ref[pl.ds(g * 8, 8)].reshape(1024, 128))
        out0[base + g] = res[:8]
        out1[base + g] = res[8:]
        return 0

    lax.fori_loop(0, size, group, 0, unroll=2)


def tile_products(w_ref, parts, out0, out1):
    size = w_ref.shape[0] // CHUNKS
    for c_ref, c_hbm, sems, base in parts:
        chunks = c_ref.shape[0] // 8 // size

        def chunk(i, _):
            if c_hbm is not None:
                chunk_copy(c_hbm, c_ref, sems, i).wait()
            chunk_products(w_ref, c_ref, i, base, out0, out1)
            return 0

        lax.fori_loop(0, chunks, chunk, 0)


def backward_pass(own, c_hbm, c_ref, sems, w_ref, out0, out1):
    left_sides(1.0 - own, own, w_ref)
    tile_products(w_ref, [(c_ref, c_hbm, sems, 0)], out0, out1)


def forward_parts(w_ref, held_ref, fetched_ref, c_ref, c_hbm, sems):
    parts = [(held_ref, None, None, 0)]
    if fetched_ref is not None:
        parts.append((fetched_ref, None, None, w_ref.shape[0] - fetched_ref.shape[0] // 8))
    return parts + [(c_ref, c_hbm, sems, held_ref.shape[0] // 8)]


def electron_rate(sum_k, far, bose, f, parts, w_ref, o0, o1):
    left_sides(far * (1.0 + bose), far + bose, w_ref)
    tile_products(w_ref, parts, o0, o1)
    gain, loss = flat(o0), flat(o1)
    gain_hi, loss_hi = gain.astype(bf16), loss.astype(bf16)
    gain_lo = (gain - gain_hi.astype(f32)).astype(bf16)
    loss_lo = (loss - loss_hi.astype(f32)).astype(bf16)
    sums = dot(sum_k, jnp.concatenate([gain_hi, gain_lo, loss_hi, loss_lo], axis=1))
    return sums[:, :128] + sums[:, 128:256] - f * (sums[:, 256:384] + sums[:, 384:])


def my_core():
    return lax.rem(lax.axis_index("bulk"), 2)


def place_of(chip, chips):
    return (chip + chips - chips // 2) % chips


def block_of(peer, peers):
    chips = peers // 2
    return place_of(peer // 2, chips) + jnp.where(peer % 2 == my_core(), 0, chips)


def to_wire(rows, send):
    half = rows.shape[0] // 4 * 2
    send[: rows.shape[0] - half] = rows[half:]
    send[rows.shape[0] - half :] = rows[:half]


def from_wire(recv):
    half = recv.shape[0] // 4 * 2
    return jnp.concatenate([recv[recv.shape[0] - half :], recv[: recv.shape[0] - half]], axis=0)


def need_kernel(cap, *refs):
    ins, outs = refs[:9], refs[9:]
    *small, pneed_ref, qneed_ref, send_ref, sems = outs
    copies = [
        pltpu.make_async_copy(src, dst, sems.at[i])
        for i, (src, dst) in enumerate(zip(ins, [*small, pneed_ref, qneed_ref]))
    ]
    start(copies)
    slots = pneed_ref.shape[1]
    step = send_ref.shape[0] // (slots // cap // 2)
    for copy in copies:
        copy.wait()
    f, n = small[0][...], small[1][...]
    own_p, own_q = pneed_ref[...].astype(f32), qneed_ref[...].astype(f32)
    row = iota((8, slots), 0)
    lists = jnp.where(row == 0, own_p, jnp.where(row == 1, own_q, 0.0))
    if slots < 128:
        lists = jnp.concatenate([lists, jnp.zeros((8, 128 - slots), f32)], axis=1)
    block = jnp.concatenate([f, n, lists], axis=0)
    for chip in range(slots // cap // 2):
        send_ref[chip * step : (chip + 1) * step] = block


def prepare_kernel(
    cap,
    count_ref,
    kblock_ref,
    partner_ref,
    qslot_ref,
    f_ref,
    pneed_ref,
    qneed_ref,
    c_hbm,
    held_ref,
    t_hbm,
    pair_ref,
    gk_ref,
    sk_ref,
    sp_ref,
    sp4_ref,
    near_ref,
    list_ref,
    mine_ref,
    b0_ref,
    b1_ref,
    w_ref,
    c_ref,
    in_sems,
    t_ref,
    out_sems,
):
    start_chunks(c_hbm, c_ref, in_sems)
    tiles = kblock_ref.shape[1]
    kb = f_ref.shape[0]
    used = iota((1, tiles), 1) < count_ref[0]
    k = kblock_ref[...]
    e = partner_ref[...]
    q = qslot_ref[...]
    rows4 = sp4_ref.shape[0]
    ind = lambda m: jnp.where(m, 1.0, 0.0)
    k_hot = ind(iota((kb, tiles), 0) == k)
    gk_ref[...] = k_hot.T.astype(bf16)
    own = add_rows(gk_ref[...], f_ref[...])
    left_sides(1.0 - own, own, w_ref)
    sk_ref[...] = jnp.where(used, k_hot, 0.0).astype(bf16)
    x = iota((rows4, tiles), 0)
    row_e = (e // cap) * (2 * cap) + e % cap
    row_p = (q // cap) * (2 * cap) + cap + q % cap
    p_hot = ind(x == row_p)
    pair_ref[...] = jnp.concatenate([ind(x == row_e), p_hot], axis=0).T.astype(bf16)
    sp4_ref[...] = jnp.where(used, p_hot, 0.0).astype(bf16)
    sp_ref[...] = jnp.where(used, ind(iota(sp_ref.shape, 0) == q), 0.0).astype(bf16)
    rows, half = list_ref.shape
    slots = pneed_ref.shape[1]
    peers = slots // cap
    x = iota((rows, slots), 0)
    y = iota((rows, slots), 1)
    peer, r = x // (2 * cap), x % (2 * cap)
    e_here = (r < cap) & (y == peer * cap + r)
    p_here = (r >= cap) & (y == peer * cap + r - cap)
    pn = jnp.broadcast_to(pneed_ref[...].astype(f32), (rows, slots))
    qn = jnp.broadcast_to(qneed_ref[...].astype(f32), (rows, slots)) + float(kb)
    col = jnp.sum(jnp.where(e_here, pn, 0.0) + jnp.where(p_here, qn, 0.0), axis=1, keepdims=True)
    mine_ref[...] = jnp.broadcast_to(col, (rows, 128))
    start_of = block_of(iota((rows, 1), 0) // (2 * cap), peers) * (2 * half // peers)
    place = col + start_of.astype(f32)
    lane = iota((rows, half), 1).astype(f32)
    near_ref[...] = ind(lane == place).astype(bf16)
    list_ref[...] = ind(lane + float(half) == place).astype(bf16)

    size = c_ref.shape[0] // CHUNKS
    held = held_ref.shape[0] // size

    rest = CHUNKS - held

    def to_held(i, _):
        chunk_copy(c_hbm, c_ref, in_sems, i).wait()
        chunk_products(w_ref, c_ref, i, 0, b0_ref, b1_ref)
        for t in range(size):
            held_ref[i * size + t] = c_ref[i * size + t].T
        return 0

    def to_rest(i, _):
        chunk_copy(c_hbm, c_ref, in_sems, held + i).wait()
        chunk_products(w_ref, c_ref, held + i, 0, b0_ref, b1_ref)
        for t in range(size):
            t_ref[i * size + t] = c_ref[(held + i) * size + t].T
        chunk_copy(t_ref, t_hbm, out_sems, i).start()
        return 0

    lax.fori_loop(0, held, to_held, 0)
    lax.fori_loop(0, rest, to_rest, 0)
    for i in range(rest):
        chunk_copy(t_ref, t_hbm, out_sems, i).wait()


def blocks(ref, count_of_blocks, first, count):
    step = ref.shape[0] // count_of_blocks
    parts = [ref[b * step + first : b * step + first + count] for b in range(count_of_blocks)]
    return jnp.concatenate(parts, axis=0)


def serve_kernel(
    cap,
    kb,
    qb,
    count_ref,
    qslot_ref,
    asked_ref,
    hot_ref,
    mine_ref,
    share_ref,
    gp8_ref,
    sp8_ref,
    s8_ref,
    st4_ref,
    st8a_ref,
    st8b_ref,
):
    hot = hot_ref[...]
    rows4, rows8 = hot.shape[0], s8_ref.shape[0]
    q = qslot_ref[...]
    tiles = q.shape[1]
    used = iota((1, tiles), 1) < count_ref[0]
    ind = lambda m: jnp.where(m, 1.0, 0.0)
    x = iota((rows8, tiles), 0)
    row_z = (q // cap) * (4 * cap) + q % cap
    gp8_ref[...] = ind(x == row_z).T.astype(bf16)
    sp8_ref[...] = jnp.concatenate(
        [
            jnp.where(used, ind(x == row_z + cap), 0.0),
            jnp.where(used, ind(x == row_z + 2 * cap), 0.0),
        ],
        axis=1,
    ).astype(bf16)
    x = iota((rows8, rows4), 0)
    y = iota((rows8, rows4), 1)
    peer, r = x // (4 * cap), x % (4 * cap)
    source = peer * (2 * cap) + cap + r % cap

    def rows_of(kind):
        here = (y == source) & (r // cap == kind)
        return dot(jnp.where(here, 1.0, 0.0).astype(bf16), hot)

    s8_ref[...] = rows_of(0).astype(bf16)
    st4_ref[...] = hot.astype(f32).T[kb : kb + qb].astype(bf16)
    st8a_ref[...] = rows_of(1).T[kb : kb + qb].astype(bf16)
    st8b_ref[...] = rows_of(2).T[kb : kb + qb].astype(bf16)

    peers = rows4 // (2 * cap)
    slots = peers * cap
    wide = peers * slots
    lists = asked_ref[...]
    pick_q = iota((peers, 8 * peers), 1) == 8 * iota((peers, 8 * peers), 0) + 1
    every_q = dot(jnp.where(pick_q, 1.0, 0.0).astype(bf16), lists).astype(bf16)
    tiled = iota((128, wide), 0) == iota((128, wide), 1) % slots
    spread = dot(every_q, jnp.where(tiled, 1.0, 0.0).astype(bf16))
    lane = iota((1, wide), 1)
    here = iota((peers, wide), 0) == lane // slots
    q = jnp.sum(jnp.where(here, spread, 0.0), axis=0, keepdims=True)
    ids = q + (lane % slots // cap * qb).astype(f32)
    row = iota((rows4, 1), 0)
    col = mine_ref[...][:, :1]
    my_ids = col - float(kb) + (row // (2 * cap) * qb).astype(f32)
    my_ids = jnp.where(row % (2 * cap) >= cap, my_ids, -1.0)
    owned = (lax.axis_index("bulk") * qb + iota((qb, 1), 0)).astype(f32)
    wanted = jnp.concatenate([my_ids, owned], axis=0)
    share_ref[...] = jnp.where(ids == wanted, 1.0, 0.0).astype(bf16)


def thermal_of(energy_ref):
    return 1.0 / (jnp.exp(energy_ref[...]) - 1.0)


def put_broadcast(send, served, contributions):
    slots = contributions.shape[0]
    chips = served.shape[0] // 8
    for chip in range(chips):
        at = place_of(chip, chips) * (8 + slots)
        send[at : at + 8] = served[chip * 8 : chip * 8 + 8]
        send[at + 8 : at + 8 + slots] = contributions


def phonon_terms(far, bose, b0_ref, b1_ref):
    gain = far * flat(b0_ref)
    return gain + bose * (gain - (1.0 - far) * flat(b1_ref))


def fetch_copy(c_hbm, fetched_ref, sem):
    count = fetched_ref.shape[0]
    return pltpu.make_async_copy(
        c_hbm.at[pl.ds(c_hbm.shape[0] - count, count)], fetched_ref, sem.at[0]
    )


def near_rows_kernel(same_ref, list_ref, c_hbm, part_ref, fetched_ref, sem):
    copy = fetch_copy(c_hbm, fetched_ref, sem)
    copy.start()
    part_ref[...] = add_rows(list_ref[...], same_ref[...])
    copy.wait()


def half_of_devices(cap, chips, weight, others, ref, share_ref):
    rows4 = 4 * cap * chips
    wide = share_ref.shape[1] // 2
    x = iota((rows4, 8 * chips), 0)
    peer = x // (2 * cap)
    source = 8 * place_of(peer // 2, chips) + 2 * cap * my_core() + x % (2 * cap)
    wanted_core = (my_core() + others) % 2
    at = (iota((rows4, 8 * chips), 1) == source) & (peer % 2 == wanted_core)
    heads = add_rows(jnp.where(at, 1.0, 0.0).astype(bf16), blocks(ref, chips, 0, 8))
    tails = blocks(ref, chips, 8, wide // chips)
    sums = add_rows(share_ref[:, others * wide : (others + 1) * wide], tails)
    return heads + weight * sums[:rows4], sums[rows4:]


def near_half_kernel(
    cap, chips, weight, same_ref, share_ref, c_hbm, part_ref, total_ref, fetched_ref, sem
):
    copy = fetch_copy(c_hbm, fetched_ref, sem)
    copy.start()
    part, total = half_of_devices(cap, chips, weight, 0, same_ref, share_ref)
    part_ref[...] = part
    total_ref[...] = total
    copy.wait()


def first_kernel(
    cap,
    same_ref,
    other_ref,
    part_ref,
    list_ref,
    f_ref,
    n_ref,
    energy_ref,
    decay_ref,
    pair_ref,
    sk_ref,
    sp_ref,
    b0_ref,
    b1_ref,
    held_ref,
    fetched_ref,
    c_hbm,
    send,
    e_ref,
    f1_ref,
    hot_ref,
    asked_ref,
    w_ref,
    c_ref,
    sems,
    o0,
    o1,
):
    start_chunks(c_hbm, c_ref, sems)
    f, n = f_ref[...], n_ref[...]
    kb, qb = f.shape[0], n.shape[0]
    rows4 = list_ref.shape[0]
    peers = rows4 // (2 * cap)
    got = part_ref[...] + add_rows(list_ref[...], other_ref[...])
    far, bose = gather_pair(pair_ref[...], got)
    contributions = add_rows(sp_ref[...], phonon_terms(far, bose, b0_ref, b1_ref))
    lists = jnp.concatenate(
        [blocks(ref, peers // 2, kb + qb, 8) for ref in (same_ref, other_ref)], axis=0
    ).astype(bf16)
    asked_ref[...] = lists
    x = iota((rows4, 8 * peers), 0)
    r = x % (2 * cap)
    kind = jnp.where(r < cap, 0, 1)
    at = iota((rows4, 8 * peers), 1) == 8 * block_of(x // (2 * cap), peers) + kind
    asked = dot(jnp.where(at, 1.0, 0.0).astype(bf16), lists)
    r = iota((rows4, 128), 0) % (2 * cap)
    lane = iota((rows4, 128), 1)
    wanted = lane == lax.axis_index("bulk") * cap + r % cap
    col = jnp.sum(jnp.where(wanted, asked, 0.0), axis=1, keepdims=True)
    col = col + jnp.where(r[:, :1] < cap, 0.0, float(kb))
    hot = jnp.where(lane.astype(f32) == col, 1.0, 0.0).astype(bf16)
    hot_ref[...] = hot
    base = n - DT * decay_ref[...] * (n - thermal_of(energy_ref))
    parts = forward_parts(w_ref, held_ref, fetched_ref, c_ref, c_hbm, sems)
    rate = electron_rate(sk_ref[...], far, bose, f, parts, w_ref, o0, o1)
    f1 = f + DT * rate
    e_ref[...] = rate
    f1_ref[...] = f1
    put_broadcast(send, add_rows(hot, padded(f1, base)), contributions)


def middle_kernel(
    cap,
    ends,
    part_ref,
    total_ref,
    other_ref,
    share_ref,
    serve_ref,
    f_ref,
    e_ref,
    own_ref,
    n_ref,
    energy_ref,
    decay_ref,
    pair_ref,
    sk_ref,
    sp_ref,
    b0_ref,
    b1_ref,
    held_ref,
    fetched_ref,
    c_hbm,
    send,
    *refs,
):
    w_ref, c_ref, sems, o0, o1 = refs[-5:]
    start_chunks(c_hbm, c_ref, sems)
    chips = serve_ref.shape[0] // (4 * cap)
    weight = DT / 2.0 if ends else DT
    part, total = half_of_devices(cap, chips, weight, 1, other_ref, share_ref)
    got = part_ref[...] + part
    total = total_ref[...] + total
    far, bose = gather_pair(pair_ref[...], got)
    terms = phonon_terms(far, bose, b0_ref, b1_ref)
    contributions = add_rows(sp_ref[...], terms)
    n = n_ref[...]
    own = own_ref[...]
    parts = forward_parts(w_ref, held_ref, fetched_ref, c_ref, c_hbm, sems)
    if ends:
        n2_ref, e2_ref, f3_ref = refs[:3]
        n2_ref[...] = n + (DT / 2.0) * total
        rate = electron_rate(sk_ref[...], far, bose, own, parts, w_ref, o0, o1)
        f3 = own + DT * rate
        e2_ref[...] = rate
        f3_ref[...] = f3
        to_wire(add_rows(serve_ref[...], padded(f3)) + contributions, send)
    else:
        base_ref, f2_ref = refs[:2]
        thermal = thermal_of(energy_ref)
        decay = decay_ref[...]
        p0 = total - decay * (n - thermal)
        n1 = n + DT * p0
        base = n + (DT / 2.0) * (p0 - decay * (n1 - thermal))
        base_ref[...] = base
        rate = electron_rate(sk_ref[...], far, bose, own, parts, w_ref, o0, o1)
        f2 = f_ref[...] + (DT / 2.0) * (e_ref[...] + rate)
        f2_ref[...] = f2
        put_broadcast(send, add_rows(serve_ref[...], padded(f2, base)), contributions)


def backward_kernel(f_ref, gk_ref, c_hbm, b0_ref, b1_ref, w_ref, c_ref, sems):
    start_chunks(c_hbm, c_ref, sems)
    own = add_rows(gk_ref[...], f_ref[...])
    backward_pass(own, c_hbm, c_ref, sems, w_ref, b0_ref, b1_ref)


def phonon_kernel(
    kb,
    recv,
    n_ref,
    energy_ref,
    decay_ref,
    pair_ref,
    st4_ref,
    sp8_ref,
    s8_ref,
    b0_ref,
    b1_ref,
    send,
    p_ref,
    n1_ref,
    far_ref,
):
    n = n_ref[...]
    got = from_wire(recv)
    thermal = thermal_of(energy_ref)
    rate = add_rows(st4_ref[...], got) - decay_ref[...] * (n - thermal)
    n1 = n + DT * rate
    p_ref[...] = rate
    n1_ref[...] = n1
    far = add_rows(pair_ref[:, : got.shape[0]], got)
    far_ref[...] = far
    gain = far * flat(b0_ref)
    both = jnp.concatenate([gain, gain - (1.0 - far) * flat(b1_ref)], axis=0)
    state = padded(jnp.zeros((kb, 128), f32), n1)
    to_wire(add_rows(s8_ref[...], state) + add_rows(sp8_ref[...], both), send)


def last_kernel(recv, *refs):
    far_ref, f_ref, f1_ref, e_ref, n_ref, n1_ref, p_ref, energy_ref, decay_ref = refs[:9]
    gp8_ref, sk_ref, st8a_ref, st8b_ref, held_ref, c_hbm = refs[9:15]
    refs = refs[15:]
    f2_ref, n2_ref, w_ref, c_ref, sems, o0, o1 = refs
    start_chunks(c_hbm, c_ref, sems)
    got = from_wire(recv)
    n, n1 = n_ref[...], n1_ref[...]
    bose = add_rows(gp8_ref[...], got)
    thermal = thermal_of(energy_ref)
    p1 = (
        add_rows(st8a_ref[...], got)
        + n1 * add_rows(st8b_ref[...], got)
        - decay_ref[...] * (n1 - thermal)
    )
    n2 = n + (DT / 2.0) * (p_ref[...] + p1)
    n2_ref[...] = n2
    parts = forward_parts(w_ref, held_ref, None, c_ref, c_hbm, sems)
    rate = electron_rate(sk_ref[...], far_ref[...], bose, f1_ref[...], parts, w_ref, o0, o1)
    f2 = f_ref[...] + (DT / 2.0) * (e_ref[...] + rate)
    f2_ref[...] = f2


def call(kernel, name, outs, scratch=(), spaces=None, out_spaces=None, flops=0, seen=0):
    def run(*args):
        places = dict(spaces or {})
        args = [
            pltpu.with_memory_space_constraint(x, pltpu.HBM)
            if places.get(i) is pltpu.HBM
            else x
            for i, x in enumerate(args)
        ]
        specs = [
            pl.BlockSpec(memory_space=places.get(i, pltpu.VMEM)) for i in range(len(args))
        ]
        return pl.pallas_call(
            kernel,
            out_shape=[
                (out_spaces or {}).get(i, jax.ShapeDtypeStruct)(*o) for i, o in enumerate(outs)
            ],
            in_specs=specs,
            out_specs=[
                pl.BlockSpec(memory_space=(out_spaces or {}).get(i, pltpu.VMEM))
                for i in range(len(outs))
            ],
            scratch_shapes=list(scratch),
            compiler_params=pltpu.CompilerParams(vmem_limit_bytes=VMEM_LIMIT),
            cost_estimate=pl.CostEstimate(
                flops=flops, bytes_accessed=seen, transcendentals=0
            ),
            name=name,
        )(*args)

    return run


def on_device(
    electrons,
    phonons,
    phonon_energy,
    phonon_decay,
    coupling,
    tile_kblock,
    tile_partner,
    tile_qslot,
    tile_count,
    partner_need,
    phonon_need,
):
    devices = lax.axis_size("bulk")
    kb = electrons.shape[0]
    qb = phonons.shape[0]
    tiles = coupling.shape[0]
    cap = partner_need.shape[1] // devices
    assert cap == phonon_need.shape[1] // devices and kb + qb <= 128
    rows4 = devices * 2 * cap
    rows8 = devices * 4 * cap
    groups = tiles // 8
    held = HELD_CHUNKS * (tiles // CHUNKS)
    weights = pltpu.VMEM((groups, 16, 1024), bf16)
    streams = [weights, pltpu.VMEM(coupling.shape, bf16), pltpu.SemaphoreType.DMA((CHUNKS,))]
    rest = (tiles - held, 128, 128)
    rest_sems = pltpu.SemaphoreType.DMA((CHUNKS - HELD_CHUNKS,))
    forward_streams = [weights, pltpu.VMEM(rest, bf16), rest_sems]
    sums = [pltpu.VMEM((groups, 8, 128), f32)] * 2
    pass_out = [((groups, 8, 128), f32)] * 2
    block4 = ((rows4, 128), f32)
    block8 = ((rows8, 128), f32)

    work = dict(flops=2 * tiles * 16 * 128 * 128, seen=tiles * 128 * 128 * 2)

    def exchange(x):
        order = [[(i + devices // 4 * 2) % devices for i in range(devices)]]
        return lax.all_to_all(
            x, "bulk", split_axis=0, concat_axis=0, tiled=True, axis_index_groups=order
        )

    ints = ((1, tiles), jnp.int32)
    lists = ((1, partner_need.shape[1]), jnp.int32)
    small = [((kb, 128), f32)] + [((qb, 128), f32)] * 3 + [ints] * 3
    step_rows = kb + qb + 8
    slots = devices * cap
    wide = 8 + slots
    assert step_rows % 8 == 0 and slots % 8 == 0 and slots <= 128
    assert devices % 2 == 0 and cap == 2
    chips = devices // 2
    same_core = [
        [(i + chips // 2) % chips * 2 + core for i in range(chips)] for core in (0, 1)
    ]

    def to_chips(x):
        return lax.all_to_all(
            x, "bulk", split_axis=0, concat_axis=0, tiled=True, axis_index_groups=same_core
        )

    def between_cores(x):
        return lax.ppermute(x, "bulk", [(i, i ^ 1) for i in range(devices)])

    f, n, energy, decay, kblock, partner, qslot, pneed, qneed, send = call(
        functools.partial(need_kernel, cap),
        "need",
        small + [lists, lists, ((chips * step_rows, 128), f32)],
        [pltpu.SemaphoreType.DMA((9,))],
        spaces={i: pltpu.HBM for i in range(9)},
    )(
        electrons,
        phonons,
        phonon_energy,
        phonon_decay,
        tile_kblock.reshape(1, tiles),
        tile_partner.reshape(1, tiles),
        tile_qslot.reshape(1, tiles),
        partner_need,
        phonon_need,
    )
    same = to_chips(send)
    c_held, c_rest, pair, gk, sk, sp, sp4, near, far_picks, mine, b0, b1 = call(
        functools.partial(prepare_kernel, cap),
        "prepare",
        [
            ((held, 128, 128), bf16),
            (rest, bf16),
            ((tiles, 2 * rows4), bf16),
            ((tiles, kb), bf16),
            ((kb, tiles), bf16),
            ((slots, tiles), bf16),
            ((rows4, tiles), bf16),
            ((rows4, chips * step_rows), bf16),
            ((rows4, chips * step_rows), bf16),
            ((rows4, 128), f32),
        ]
        + pass_out,
        [*streams, pltpu.VMEM(rest, bf16), rest_sems],
        spaces={0: pltpu.SMEM, 7: pltpu.HBM},
        out_spaces={1: pltpu.HBM},
        **work,
    )(tile_count, kblock, partner, qslot, f, pneed, qneed, coupling)
    same, c_held, b0 = lax.optimization_barrier((same, c_held, b0))
    wide_block = ((chips * wide, 128), f32)
    k_rows, q_rows = ((kb, 128), f32), ((qb, 128), f32)
    width = tiles // CHUNKS
    fetched = ((width, 128, 128), bf16)
    fetch_sem = pltpu.SemaphoreType.DMA((1,))
    short = (rest[0] - width, 128, 128)
    short_sems = pltpu.SemaphoreType.DMA((CHUNKS - HELD_CHUNKS - 1,))
    forward_scratch = [weights, pltpu.VMEM(short, bf16), short_sems] + sums
    other = between_cores(same)
    part, c_fetched = call(
        near_rows_kernel,
        "near_rows",
        [block4, fetched],
        [fetch_sem],
        spaces={2: pltpu.HBM},
        out_spaces={1: pltpu.VMEM},
    )(same, near, c_rest)
    send, e0, f1, serve, asked = call(
        functools.partial(first_kernel, cap),
        "first",
        [wide_block, k_rows, k_rows, ((rows4, 128), bf16), ((8 * devices, 128), bf16)],
        forward_scratch,
        spaces={15: pltpu.HBM},
        **work,
    )(same, other, part, far_picks, f, n, energy, decay, pair, sk, sp, b0, b1, c_held, c_fetched, c_rest)
    share, gp8, sp8, s8, st4, st8a, st8b = call(
        functools.partial(serve_kernel, cap, kb, qb),
        "serve",
        [
            ((rows4 + qb, devices * slots), bf16),
            ((tiles, rows8), bf16),
            ((rows8, 2 * tiles), bf16),
            ((rows8, 128), bf16),
            ((qb, rows4), bf16),
            ((qb, rows8), bf16),
            ((qb, rows8), bf16),
        ],
        spaces={0: pltpu.SMEM},
    )(tile_count, qslot, asked, serve, mine)
    back = call(backward_kernel, "backward", pass_out, streams, spaces={2: pltpu.HBM}, **work)

    def middle(ends, send, outs, f, e, own, n, contributions, share):
        same = to_chips(send)
        b0, b1 = back(own, gk, coupling)
        same, b0, share = lax.optimization_barrier((same, b0, share))
        other = between_cores(same)
        weight = DT / 2.0 if ends else DT
        part, total, c_fetched = call(
            functools.partial(near_half_kernel, cap, chips, weight),
            "near_half",
            [block4, q_rows, fetched],
            [fetch_sem],
            spaces={2: pltpu.HBM},
            out_spaces={2: pltpu.VMEM},
        )(same, share, c_rest)
        return call(
            functools.partial(middle_kernel, cap, ends),
            "middle",
            outs,
            forward_scratch,
            spaces={18: pltpu.HBM},
            **work,
        )(
            part, total, other, share, serve, f, e, own, n, energy, decay,
            pair, sk, contributions, b0, b1, c_held, c_fetched, c_rest,
        )

    send, base, f2 = middle(False, send, [wide_block, q_rows, k_rows], f, e0, f1, n, sp, share)
    send, n2, e2, f3 = middle(
        True, send, [block4, q_rows, k_rows, k_rows], f2, e0, f2, base, sp4, share
    )
    recv = exchange(send)
    b0, b1 = back(f3, gk, coupling)
    send, p2, n3, far = call(
        functools.partial(phonon_kernel, kb),
        "phonon",
        [block8, q_rows, q_rows, ((tiles, 128), f32)],
    )(recv, n2, energy, decay, pair, st4, sp8, s8, b0, b1)
    recv = exchange(send)
    f, n = call(
        last_kernel,
        "last",
        [k_rows, q_rows],
        forward_streams + sums,
        spaces={15: pltpu.HBM},
        **work,
    )(
        recv, far, f2, f3, e2, n2, n3, p2, energy, decay,
        gp8, sk, st8a, st8b, c_held, c_rest,
    )
    return (f, n)


def solution(mesh):
    placed = (
        P(("groups", "bulk"), None),
        P(("groups", "bulk"), None),
        P("bulk", None),
        P("bulk", None),
        P("bulk", None, None),
        P("bulk"),
        P("bulk"),
        P("bulk"),
        P("bulk"),
        P("bulk", None),
        P("bulk", None),
    )
    return jax.shard_map(
        on_device,
        mesh=mesh,
        in_specs=placed,
        out_specs=(P(("groups", "bulk"), None), P(("groups", "bulk"), None)),
        check_vma=False,
    )
```

```python
import functools

import jax
import jax.numpy as jnp
from jax import lax
from jax.experimental import pallas as pl
from jax.experimental.pallas import tpu as pltpu
from jax.sharding import PartitionSpec as P

DT = 0.05
CHUNKS = 8
HELD_CHUNKS = 2
SHORT_CHUNKS = 4
f32 = jnp.float32
bf16 = jnp.bfloat16
VMEM_LIMIT = 48 * 1024 * 1024


def iota(shape, dim):
    return lax.broadcasted_iota(jnp.int32, shape, dim)


def dot(a, b):
    return lax.dot_general(a, b, (((1,), (0,)), ((), ())), preferred_element_type=f32)


def add_rows(onehot, x):
    hi = x.astype(bf16)
    mid = (x - hi.astype(f32)).astype(bf16)
    both = dot(onehot, jnp.concatenate([hi, mid], axis=1))
    return both[:, :128] + both[:, 128:]


def gather_pair(table, x):
    rows = x.shape[0]
    hi = x.astype(bf16)
    mid = (x - hi.astype(f32)).astype(bf16)
    blank = jnp.zeros((rows, 128), bf16)

    def both(part):
        upper = jnp.concatenate([part, blank], axis=1)
        lower = jnp.concatenate([blank, part], axis=1)
        return dot(table, jnp.concatenate([upper, lower], axis=0))

    res = both(hi) + both(mid)
    return res[:, :128], res[:, 128:]


def stacked(first, second):
    tiles = first.shape[0]
    return jnp.concatenate(
        [first.reshape(tiles // 8, 8, 128), second.reshape(tiles // 8, 8, 128)], axis=1
    ).astype(bf16)


def row_is(r):
    return iota((16, 128), 0) % 8 == r


def padded(*parts):
    rows = sum(p.shape[0] for p in parts)
    return jnp.concatenate([*parts, jnp.zeros((128 - rows, 128), f32)], axis=0)


def flat(ref):
    return ref[...].reshape(-1, 128)


def chunk_copy(src, dst, sems, i):
    size = min(src.shape[0], dst.shape[0]) // sems.shape[0]
    here = pl.ds(i * size, size)
    return pltpu.make_async_copy(src.at[here], dst.at[here], sems.at[i])


def start_chunks(src, dst, sems):
    for i in range(sems.shape[0]):
        chunk_copy(src, dst, sems, i).start()


def start(copies):
    for copy in copies:
        copy.start()


def block_diagonal(w):
    w = w.astype(f32)
    return jnp.concatenate(
        [jnp.where(row_is(r), w, 0.0).astype(bf16) for r in range(8)], axis=1
    )


def left_sides(first, second, w_ref):
    groups = w_ref.shape[0]
    w_ref[:, :, :128] = stacked(first, second)

    def spread(g, _):
        w_ref[g] = block_diagonal(w_ref[g, :, :128])
        return 0

    lax.fori_loop(0, groups, spread, 0, unroll=4)


def chunk_products(w_ref, c_ref, i, base, out0, out1, size):
    for k in range(size):
        g = i * size + k
        res = dot(w_ref[base + g], c_ref[pl.ds(g * 8, 8)].reshape(1024, 128))
        out0[base + g] = res[:8]
        out1[base + g] = res[8:]


def tile_products(w_ref, parts, out0, out1):
    for c_ref, c_hbm, sems, base in parts:
        groups = c_ref.shape[0] // 8
        if c_hbm is None:
            chunk_products(w_ref, c_ref, 0, base, out0, out1, groups)
            continue
        size = groups // sems.shape[0]

        def chunk(i, _):
            chunk_copy(c_hbm, c_ref, sems, i).wait()
            chunk_products(w_ref, c_ref, i, base, out0, out1, size)
            return 0

        lax.fori_loop(0, sems.shape[0], chunk, 0)


def backward_pass(own, c_hbm, c_ref, sems, w_ref, out0, out1):
    left_sides(1.0 - own, own, w_ref)
    tile_products(w_ref, [(c_ref, c_hbm, sems, 0)], out0, out1)


def forward_parts(w_ref, held_ref, fetched_ref, c_ref, c_hbm, sems):
    parts = [(held_ref, None, None, 0)]
    if fetched_ref is not None:
        parts.append((fetched_ref, None, None, w_ref.shape[0] - fetched_ref.shape[0] // 8))
    return parts + [(c_ref, c_hbm, sems, held_ref.shape[0] // 8)]


def electron_rate(sum_k, far, bose, f, parts, w_ref, o0, o1):
    left_sides(far * (1.0 + bose), far + bose, w_ref)
    tile_products(w_ref, parts, o0, o1)
    gain, loss = flat(o0), flat(o1)
    gain_hi, loss_hi = gain.astype(bf16), loss.astype(bf16)
    gain_lo = (gain - gain_hi.astype(f32)).astype(bf16)
    loss_lo = (loss - loss_hi.astype(f32)).astype(bf16)
    sums = dot(sum_k, jnp.concatenate([gain_hi, gain_lo, loss_hi, loss_lo], axis=1))
    return sums[:, :128] + sums[:, 128:256] - f * (sums[:, 256:384] + sums[:, 384:])


def my_core():
    return lax.rem(lax.axis_index("bulk"), 2)


def place_of(chip, chips):
    return (chip + chips - chips // 2) % chips


def block_of(peer, peers):
    chips = peers // 2
    return place_of(peer // 2, chips) + jnp.where(peer % 2 == my_core(), 0, chips)


def to_wire(rows, send):
    half = rows.shape[0] // 4 * 2
    send[: rows.shape[0] - half] = rows[half:]
    send[rows.shape[0] - half :] = rows[:half]


def from_wire(recv):
    half = recv.shape[0] // 4 * 2
    return jnp.concatenate([recv[recv.shape[0] - half :], recv[: recv.shape[0] - half]], axis=0)


def need_kernel(cap, *refs):
    ins, outs = refs[:9], refs[9:]
    *small, pneed_ref, qneed_ref, send_ref, sems = outs
    copies = [
        pltpu.make_async_copy(src, dst, sems.at[i])
        for i, (src, dst) in enumerate(zip(ins, [*small, pneed_ref, qneed_ref]))
    ]
    start(copies)
    slots = pneed_ref.shape[1]
    step = send_ref.shape[0] // (slots // cap // 2)
    for copy in copies:
        copy.wait()
    f, n = small[0][...], small[1][...]
    own_p, own_q = pneed_ref[...].astype(f32), qneed_ref[...].astype(f32)
    row = iota((8, slots), 0)
    lists = jnp.where(row == 0, own_p, jnp.where(row == 1, own_q, 0.0))
    if slots < 128:
        lists = jnp.concatenate([lists, jnp.zeros((8, 128 - slots), f32)], axis=1)
    block = jnp.concatenate([f, n, lists], axis=0)
    for chip in range(slots // cap // 2):
        send_ref[chip * step : (chip + 1) * step] = block


def prepare_kernel(
    cap,
    count_ref,
    kblock_ref,
    partner_ref,
    qslot_ref,
    f_ref,
    pneed_ref,
    qneed_ref,
    c_hbm,
    held_ref,
    t_hbm,
    pair_ref,
    gk_ref,
    sk_ref,
    sp_ref,
    sp4_ref,
    near_ref,
    list_ref,
    mine_ref,
    b0_ref,
    b1_ref,
    w_ref,
    c_ref,
    in_sems,
    t_ref,
    out_sems,
):
    start_chunks(c_hbm, c_ref, in_sems)
    tiles = kblock_ref.shape[1]
    kb = f_ref.shape[0]
    used = iota((1, tiles), 1) < count_ref[0]
    k = kblock_ref[...]
    e = partner_ref[...]
    q = qslot_ref[...]
    rows4 = sp4_ref.shape[0]
    ind = lambda m: jnp.where(m, 1.0, 0.0)
    k_hot = ind(iota((kb, tiles), 0) == k)
    gk_ref[...] = k_hot.T.astype(bf16)
    own = add_rows(gk_ref[...], f_ref[...])
    left_sides(1.0 - own, own, w_ref)
    sk_ref[...] = jnp.where(used, k_hot, 0.0).astype(bf16)
    x = iota((rows4, tiles), 0)
    row_e = (e // cap) * (2 * cap) + e % cap
    row_p = (q // cap) * (2 * cap) + cap + q % cap
    p_hot = ind(x == row_p)
    pair_ref[...] = jnp.concatenate([ind(x == row_e), p_hot], axis=0).T.astype(bf16)
    sp4_ref[...] = jnp.where(used, p_hot, 0.0).astype(bf16)
    sp_ref[...] = jnp.where(used, ind(iota(sp_ref.shape, 0) == q), 0.0).astype(bf16)
    rows, half = list_ref.shape
    slots = pneed_ref.shape[1]
    peers = slots // cap
    x = iota((rows, slots), 0)
    y = iota((rows, slots), 1)
    peer, r = x // (2 * cap), x % (2 * cap)
    e_here = (r < cap) & (y == peer * cap + r)
    p_here = (r >= cap) & (y == peer * cap + r - cap)
    pn = jnp.broadcast_to(pneed_ref[...].astype(f32), (rows, slots))
    qn = jnp.broadcast_to(qneed_ref[...].astype(f32), (rows, slots)) + float(kb)
    col = jnp.sum(jnp.where(e_here, pn, 0.0) + jnp.where(p_here, qn, 0.0), axis=1, keepdims=True)
    mine_ref[...] = jnp.broadcast_to(col, (rows, 128))
    start_of = block_of(iota((rows, 1), 0) // (2 * cap), peers) * (2 * half // peers)
    place = col + start_of.astype(f32)
    lane = iota((rows, half), 1).astype(f32)
    near_ref[...] = ind(lane == place).astype(bf16)
    list_ref[...] = ind(lane + float(half) == place).astype(bf16)

    size = c_ref.shape[0] // CHUNKS
    held = held_ref.shape[0] // size

    rest = CHUNKS - held

    def to_held(i, _):
        chunk_copy(c_hbm, c_ref, in_sems, i).wait()
        chunk_products(w_ref, c_ref, i, 0, b0_ref, b1_ref, size // 8)
        for t in range(size):
            held_ref[i * size + t] = c_ref[i * size + t].T
        return 0

    def to_rest(i, _):
        chunk_copy(c_hbm, c_ref, in_sems, held + i).wait()
        chunk_products(w_ref, c_ref, held + i, 0, b0_ref, b1_ref, size // 8)
        for t in range(size):
            t_ref[i * size + t] = c_ref[(held + i) * size + t].T
        chunk_copy(t_ref, t_hbm, out_sems, i).start()
        return 0

    lax.fori_loop(0, held, to_held, 0)
    lax.fori_loop(0, rest, to_rest, 0)
    for i in range(rest):
        chunk_copy(t_ref, t_hbm, out_sems, i).wait()


def blocks(ref, count_of_blocks, first, count):
    step = ref.shape[0] // count_of_blocks
    parts = [ref[b * step + first : b * step + first + count] for b in range(count_of_blocks)]
    return jnp.concatenate(parts, axis=0)


def serve_kernel(
    cap,
    kb,
    qb,
    count_ref,
    qslot_ref,
    asked_ref,
    hot_ref,
    mine_ref,
    share_ref,
    gp8_ref,
    sp8_ref,
    s8_ref,
    st4_ref,
    st8a_ref,
    st8b_ref,
):
    hot = hot_ref[...]
    rows4, rows8 = hot.shape[0], s8_ref.shape[0]
    q = qslot_ref[...]
    tiles = q.shape[1]
    used = iota((1, tiles), 1) < count_ref[0]
    ind = lambda m: jnp.where(m, 1.0, 0.0)
    x = iota((rows8, tiles), 0)
    row_z = (q // cap) * (4 * cap) + q % cap
    gp8_ref[...] = ind(x == row_z).T.astype(bf16)
    sp8_ref[...] = jnp.concatenate(
        [
            jnp.where(used, ind(x == row_z + cap), 0.0),
            jnp.where(used, ind(x == row_z + 2 * cap), 0.0),
        ],
        axis=1,
    ).astype(bf16)
    x = iota((rows8, rows4), 0)
    y = iota((rows8, rows4), 1)
    peer, r = x // (4 * cap), x % (4 * cap)
    source = peer * (2 * cap) + cap + r % cap

    def rows_of(kind):
        here = (y == source) & (r // cap == kind)
        return dot(jnp.where(here, 1.0, 0.0).astype(bf16), hot)

    s8_ref[...] = rows_of(0).astype(bf16)
    st4_ref[...] = hot.astype(f32).T[kb : kb + qb].astype(bf16)
    st8a_ref[...] = rows_of(1).T[kb : kb + qb].astype(bf16)
    st8b_ref[...] = rows_of(2).T[kb : kb + qb].astype(bf16)

    peers = rows4 // (2 * cap)
    slots = peers * cap
    wide = peers * slots
    lists = asked_ref[...]
    pick_q = iota((peers, 8 * peers), 1) == 8 * iota((peers, 8 * peers), 0) + 1
    every_q = dot(jnp.where(pick_q, 1.0, 0.0).astype(bf16), lists).astype(bf16)
    tiled = iota((128, wide), 0) == iota((128, wide), 1) % slots
    spread = dot(every_q, jnp.where(tiled, 1.0, 0.0).astype(bf16))
    lane = iota((1, wide), 1)
    here = iota((peers, wide), 0) == lane // slots
    q = jnp.sum(jnp.where(here, spread, 0.0), axis=0, keepdims=True)
    ids = q + (lane % slots // cap * qb).astype(f32)
    row = iota((rows4, 1), 0)
    col = mine_ref[...][:, :1]
    my_ids = col - float(kb) + (row // (2 * cap) * qb).astype(f32)
    my_ids = jnp.where(row % (2 * cap) >= cap, my_ids, -1.0)
    owned = (lax.axis_index("bulk") * qb + iota((qb, 1), 0)).astype(f32)
    wanted = jnp.concatenate([my_ids, owned], axis=0)
    share_ref[...] = jnp.where(ids == wanted, 1.0, 0.0).astype(bf16)


def thermal_of(energy_ref):
    return 1.0 / (jnp.exp(energy_ref[...]) - 1.0)


def put_broadcast(send, served, contributions):
    slots = contributions.shape[0]
    chips = served.shape[0] // 8
    for chip in range(chips):
        at = place_of(chip, chips) * (8 + slots)
        send[at : at + 8] = served[chip * 8 : chip * 8 + 8]
        send[at + 8 : at + 8 + slots] = contributions


def phonon_terms(far, bose, b0_ref, b1_ref):
    gain = far * flat(b0_ref)
    return gain + bose * (gain - (1.0 - far) * flat(b1_ref))


def fetch_copy(c_hbm, fetched_ref, sem):
    count = fetched_ref.shape[0]
    return pltpu.make_async_copy(
        c_hbm.at[pl.ds(c_hbm.shape[0] - count, count)], fetched_ref, sem.at[0]
    )


def near_rows_kernel(same_ref, list_ref, c_hbm, part_ref, fetched_ref, sem):
    copy = fetch_copy(c_hbm, fetched_ref, sem)
    copy.start()
    part_ref[...] = add_rows(list_ref[...], same_ref[...])
    copy.wait()


def half_of_devices(cap, chips, weight, others, ref, share_ref):
    rows4 = 4 * cap * chips
    wide = share_ref.shape[1] // 2
    x = iota((rows4, 8 * chips), 0)
    peer = x // (2 * cap)
    source = 8 * place_of(peer // 2, chips) + 2 * cap * my_core() + x % (2 * cap)
    wanted_core = (my_core() + others) % 2
    at = (iota((rows4, 8 * chips), 1) == source) & (peer % 2 == wanted_core)
    heads = add_rows(jnp.where(at, 1.0, 0.0).astype(bf16), blocks(ref, chips, 0, 8))
    tails = blocks(ref, chips, 8, wide // chips)
    sums = add_rows(share_ref[:, others * wide : (others + 1) * wide], tails)
    return heads + weight * sums[:rows4], sums[rows4:]


def near_half_kernel(
    cap, chips, weight, same_ref, share_ref, c_hbm, part_ref, total_ref, fetched_ref, sem
):
    copy = fetch_copy(c_hbm, fetched_ref, sem)
    copy.start()
    part, total = half_of_devices(cap, chips, weight, 0, same_ref, share_ref)
    part_ref[...] = part
    total_ref[...] = total
    copy.wait()


def first_kernel(
    cap,
    same_ref,
    other_ref,
    part_ref,
    list_ref,
    f_ref,
    n_ref,
    energy_ref,
    decay_ref,
    pair_ref,
    sk_ref,
    sp_ref,
    b0_ref,
    b1_ref,
    held_ref,
    fetched_ref,
    c_hbm,
    send,
    e_ref,
    f1_ref,
    hot_ref,
    asked_ref,
    w_ref,
    c_ref,
    sems,
    o0,
    o1,
):
    start_chunks(c_hbm, c_ref, sems)
    f, n = f_ref[...], n_ref[...]
    kb, qb = f.shape[0], n.shape[0]
    rows4 = list_ref.shape[0]
    peers = rows4 // (2 * cap)
    got = part_ref[...] + add_rows(list_ref[...], other_ref[...])
    far, bose = gather_pair(pair_ref[...], got)
    contributions = add_rows(sp_ref[...], phonon_terms(far, bose, b0_ref, b1_ref))
    lists = jnp.concatenate(
        [blocks(ref, peers // 2, kb + qb, 8) for ref in (same_ref, other_ref)], axis=0
    ).astype(bf16)
    asked_ref[...] = lists
    x = iota((rows4, 8 * peers), 0)
    r = x % (2 * cap)
    kind = jnp.where(r < cap, 0, 1)
    at = iota((rows4, 8 * peers), 1) == 8 * block_of(x // (2 * cap), peers) + kind
    asked = dot(jnp.where(at, 1.0, 0.0).astype(bf16), lists)
    r = iota((rows4, 128), 0) % (2 * cap)
    lane = iota((rows4, 128), 1)
    wanted = lane == lax.axis_index("bulk") * cap + r % cap
    col = jnp.sum(jnp.where(wanted, asked, 0.0), axis=1, keepdims=True)
    col = col + jnp.where(r[:, :1] < cap, 0.0, float(kb))
    hot = jnp.where(lane.astype(f32) == col, 1.0, 0.0).astype(bf16)
    hot_ref[...] = hot
    base = n - DT * decay_ref[...] * (n - thermal_of(energy_ref))
    parts = forward_parts(w_ref, held_ref, fetched_ref, c_ref, c_hbm, sems)
    rate = electron_rate(sk_ref[...], far, bose, f, parts, w_ref, o0, o1)
    f1 = f + DT * rate
    e_ref[...] = rate
    f1_ref[...] = f1
    put_broadcast(send, add_rows(hot, padded(f1, base)), contributions)


def middle_kernel(
    cap,
    ends,
    part_ref,
    total_ref,
    other_ref,
    share_ref,
    serve_ref,
    f_ref,
    e_ref,
    own_ref,
    n_ref,
    energy_ref,
    decay_ref,
    pair_ref,
    sk_ref,
    sp_ref,
    b0_ref,
    b1_ref,
    held_ref,
    fetched_ref,
    c_hbm,
    send,
    *refs,
):
    w_ref, c_ref, sems, o0, o1 = refs[-5:]
    start_chunks(c_hbm, c_ref, sems)
    chips = serve_ref.shape[0] // (4 * cap)
    weight = DT / 2.0 if ends else DT
    part, total = half_of_devices(cap, chips, weight, 1, other_ref, share_ref)
    got = part_ref[...] + part
    total = total_ref[...] + total
    far, bose = gather_pair(pair_ref[...], got)
    terms = phonon_terms(far, bose, b0_ref, b1_ref)
    contributions = add_rows(sp_ref[...], terms)
    n = n_ref[...]
    own = own_ref[...]
    parts = forward_parts(w_ref, held_ref, fetched_ref, c_ref, c_hbm, sems)
    if ends:
        n2_ref, e2_ref, f3_ref = refs[:3]
        n2_ref[...] = n + (DT / 2.0) * total
        rate = electron_rate(sk_ref[...], far, bose, own, parts, w_ref, o0, o1)
        f3 = own + DT * rate
        e2_ref[...] = rate
        f3_ref[...] = f3
        to_wire(add_rows(serve_ref[...], padded(f3)) + contributions, send)
    else:
        base_ref, f2_ref = refs[:2]
        thermal = thermal_of(energy_ref)
        decay = decay_ref[...]
        p0 = total - decay * (n - thermal)
        n1 = n + DT * p0
        base = n + (DT / 2.0) * (p0 - decay * (n1 - thermal))
        base_ref[...] = base
        rate = electron_rate(sk_ref[...], far, bose, own, parts, w_ref, o0, o1)
        f2 = f_ref[...] + (DT / 2.0) * (e_ref[...] + rate)
        f2_ref[...] = f2
        put_broadcast(send, add_rows(serve_ref[...], padded(f2, base)), contributions)


def backward_kernel(f_ref, gk_ref, c_hbm, b0_ref, b1_ref, w_ref, c_ref, sems):
    start_chunks(c_hbm, c_ref, sems)
    own = add_rows(gk_ref[...], f_ref[...])
    backward_pass(own, c_hbm, c_ref, sems, w_ref, b0_ref, b1_ref)


def phonon_kernel(
    kb,
    recv,
    n_ref,
    energy_ref,
    decay_ref,
    pair_ref,
    st4_ref,
    sp8_ref,
    s8_ref,
    b0_ref,
    b1_ref,
    send,
    p_ref,
    n1_ref,
    far_ref,
):
    n = n_ref[...]
    got = from_wire(recv)
    thermal = thermal_of(energy_ref)
    rate = add_rows(st4_ref[...], got) - decay_ref[...] * (n - thermal)
    n1 = n + DT * rate
    p_ref[...] = rate
    n1_ref[...] = n1
    far = add_rows(pair_ref[:, : got.shape[0]], got)
    far_ref[...] = far
    gain = far * flat(b0_ref)
    both = jnp.concatenate([gain, gain - (1.0 - far) * flat(b1_ref)], axis=0)
    state = padded(jnp.zeros((kb, 128), f32), n1)
    to_wire(add_rows(s8_ref[...], state) + add_rows(sp8_ref[...], both), send)


def last_kernel(recv, *refs):
    far_ref, f_ref, f1_ref, e_ref, n_ref, n1_ref, p_ref, energy_ref, decay_ref = refs[:9]
    gp8_ref, sk_ref, st8a_ref, st8b_ref, held_ref, c_hbm = refs[9:15]
    refs = refs[15:]
    f2_ref, n2_ref, w_ref, c_ref, sems, o0, o1 = refs
    start_chunks(c_hbm, c_ref, sems)
    got = from_wire(recv)
    n, n1 = n_ref[...], n1_ref[...]
    bose = add_rows(gp8_ref[...], got)
    thermal = thermal_of(energy_ref)
    p1 = (
        add_rows(st8a_ref[...], got)
        + n1 * add_rows(st8b_ref[...], got)
        - decay_ref[...] * (n1 - thermal)
    )
    n2 = n + (DT / 2.0) * (p_ref[...] + p1)
    n2_ref[...] = n2
    parts = forward_parts(w_ref, held_ref, None, c_ref, c_hbm, sems)
    rate = electron_rate(sk_ref[...], far_ref[...], bose, f1_ref[...], parts, w_ref, o0, o1)
    f2 = f_ref[...] + (DT / 2.0) * (e_ref[...] + rate)
    f2_ref[...] = f2


def call(kernel, name, outs, scratch=(), spaces=None, out_spaces=None, flops=0, seen=0):
    def run(*args):
        places = dict(spaces or {})
        args = [
            pltpu.with_memory_space_constraint(x, pltpu.HBM)
            if places.get(i) is pltpu.HBM
            else x
            for i, x in enumerate(args)
        ]
        specs = [
            pl.BlockSpec(memory_space=places.get(i, pltpu.VMEM)) for i in range(len(args))
        ]
        return pl.pallas_call(
            kernel,
            out_shape=[
                (out_spaces or {}).get(i, jax.ShapeDtypeStruct)(*o) for i, o in enumerate(outs)
            ],
            in_specs=specs,
            out_specs=[
                pl.BlockSpec(memory_space=(out_spaces or {}).get(i, pltpu.VMEM))
                for i in range(len(outs))
            ],
            scratch_shapes=list(scratch),
            compiler_params=pltpu.CompilerParams(vmem_limit_bytes=VMEM_LIMIT),
            cost_estimate=pl.CostEstimate(
                flops=flops, bytes_accessed=seen, transcendentals=0
            ),
            name=name,
        )(*args)

    return run


def on_device(
    electrons,
    phonons,
    phonon_energy,
    phonon_decay,
    coupling,
    tile_kblock,
    tile_partner,
    tile_qslot,
    tile_count,
    partner_need,
    phonon_need,
):
    devices = lax.axis_size("bulk")
    kb = electrons.shape[0]
    qb = phonons.shape[0]
    tiles = coupling.shape[0]
    cap = partner_need.shape[1] // devices
    assert cap == phonon_need.shape[1] // devices and kb + qb <= 128
    rows4 = devices * 2 * cap
    rows8 = devices * 4 * cap
    groups = tiles // 8
    held = HELD_CHUNKS * (tiles // CHUNKS)
    weights = pltpu.VMEM((groups, 16, 1024), bf16)
    streams = [weights, pltpu.VMEM(coupling.shape, bf16), pltpu.SemaphoreType.DMA((CHUNKS,))]
    rest = (tiles - held, 128, 128)
    rest_sems = pltpu.SemaphoreType.DMA((CHUNKS - HELD_CHUNKS,))
    forward_streams = [weights, pltpu.VMEM(rest, bf16), rest_sems]
    sums = [pltpu.VMEM((groups, 8, 128), f32)] * 2
    pass_out = [((groups, 8, 128), f32)] * 2
    block4 = ((rows4, 128), f32)
    block8 = ((rows8, 128), f32)

    work = dict(flops=2 * tiles * 16 * 128 * 128, seen=tiles * 128 * 128 * 2)

    def exchange(x):
        order = [[(i + devices // 4 * 2) % devices for i in range(devices)]]
        return lax.all_to_all(
            x, "bulk", split_axis=0, concat_axis=0, tiled=True, axis_index_groups=order
        )

    ints = ((1, tiles), jnp.int32)
    lists = ((1, partner_need.shape[1]), jnp.int32)
    small = [((kb, 128), f32)] + [((qb, 128), f32)] * 3 + [ints] * 3
    step_rows = kb + qb + 8
    slots = devices * cap
    wide = 8 + slots
    assert step_rows % 8 == 0 and slots % 8 == 0 and slots <= 128
    assert devices % 2 == 0 and cap == 2
    chips = devices // 2
    same_core = [
        [(i + chips // 2) % chips * 2 + core for i in range(chips)] for core in (0, 1)
    ]

    def to_chips(x):
        return lax.all_to_all(
            x, "bulk", split_axis=0, concat_axis=0, tiled=True, axis_index_groups=same_core
        )

    def between_cores(x):
        return lax.ppermute(x, "bulk", [(i, i ^ 1) for i in range(devices)])

    f, n, energy, decay, kblock, partner, qslot, pneed, qneed, send = call(
        functools.partial(need_kernel, cap),
        "need",
        small + [lists, lists, ((chips * step_rows, 128), f32)],
        [pltpu.SemaphoreType.DMA((9,))],
        spaces={i: pltpu.HBM for i in range(9)},
    )(
        electrons,
        phonons,
        phonon_energy,
        phonon_decay,
        tile_kblock.reshape(1, tiles),
        tile_partner.reshape(1, tiles),
        tile_qslot.reshape(1, tiles),
        partner_need,
        phonon_need,
    )
    same = to_chips(send)
    c_held, c_rest, pair, gk, sk, sp, sp4, near, far_picks, mine, b0, b1 = call(
        functools.partial(prepare_kernel, cap),
        "prepare",
        [
            ((held, 128, 128), bf16),
            (rest, bf16),
            ((tiles, 2 * rows4), bf16),
            ((tiles, kb), bf16),
            ((kb, tiles), bf16),
            ((slots, tiles), bf16),
            ((rows4, tiles), bf16),
            ((rows4, chips * step_rows), bf16),
            ((rows4, chips * step_rows), bf16),
            ((rows4, 128), f32),
        ]
        + pass_out,
        [*streams, pltpu.VMEM(rest, bf16), rest_sems],
        spaces={0: pltpu.SMEM, 7: pltpu.HBM},
        out_spaces={1: pltpu.HBM},
        **work,
    )(tile_count, kblock, partner, qslot, f, pneed, qneed, coupling)
    same, c_held, b0 = lax.optimization_barrier((same, c_held, b0))
    wide_block = ((chips * wide, 128), f32)
    k_rows, q_rows = ((kb, 128), f32), ((qb, 128), f32)
    width = tiles // CHUNKS
    fetched = ((width, 128, 128), bf16)
    fetch_sem = pltpu.SemaphoreType.DMA((1,))
    short = (rest[0] - width, 128, 128)
    short_sems = pltpu.SemaphoreType.DMA((SHORT_CHUNKS,))
    forward_scratch = [weights, pltpu.VMEM(short, bf16), short_sems] + sums
    other = between_cores(same)
    part, c_fetched = call(
        near_rows_kernel,
        "near_rows",
        [block4, fetched],
        [fetch_sem],
        spaces={2: pltpu.HBM},
        out_spaces={1: pltpu.VMEM},
    )(same, near, c_rest)
    send, e0, f1, serve, asked = call(
        functools.partial(first_kernel, cap),
        "first",
        [wide_block, k_rows, k_rows, ((rows4, 128), bf16), ((8 * devices, 128), bf16)],
        forward_scratch,
        spaces={15: pltpu.HBM},
        **work,
    )(same, other, part, far_picks, f, n, energy, decay, pair, sk, sp, b0, b1, c_held, c_fetched, c_rest)
    share, gp8, sp8, s8, st4, st8a, st8b = call(
        functools.partial(serve_kernel, cap, kb, qb),
        "serve",
        [
            ((rows4 + qb, devices * slots), bf16),
            ((tiles, rows8), bf16),
            ((rows8, 2 * tiles), bf16),
            ((rows8, 128), bf16),
            ((qb, rows4), bf16),
            ((qb, rows8), bf16),
            ((qb, rows8), bf16),
        ],
        spaces={0: pltpu.SMEM},
    )(tile_count, qslot, asked, serve, mine)
    back = call(backward_kernel, "backward", pass_out, streams, spaces={2: pltpu.HBM}, **work)

    def middle(ends, send, outs, f, e, own, n, contributions, share):
        same = to_chips(send)
        b0, b1 = back(own, gk, coupling)
        same, b0, share = lax.optimization_barrier((same, b0, share))
        other = between_cores(same)
        weight = DT / 2.0 if ends else DT
        part, total, c_fetched = call(
            functools.partial(near_half_kernel, cap, chips, weight),
            "near_half",
            [block4, q_rows, fetched],
            [fetch_sem],
            spaces={2: pltpu.HBM},
            out_spaces={2: pltpu.VMEM},
        )(same, share, c_rest)
        return call(
            functools.partial(middle_kernel, cap, ends),
            "middle",
            outs,
            forward_scratch,
            spaces={18: pltpu.HBM},
            **work,
        )(
            part, total, other, share, serve, f, e, own, n, energy, decay,
            pair, sk, contributions, b0, b1, c_held, c_fetched, c_rest,
        )

    send, base, f2 = middle(False, send, [wide_block, q_rows, k_rows], f, e0, f1, n, sp, share)
    send, n2, e2, f3 = middle(
        True, send, [block4, q_rows, k_rows, k_rows], f2, e0, f2, base, sp4, share
    )
    recv = exchange(send)
    b0, b1 = back(f3, gk, coupling)
    send, p2, n3, far = call(
        functools.partial(phonon_kernel, kb),
        "phonon",
        [block8, q_rows, q_rows, ((tiles, 128), f32)],
    )(recv, n2, energy, decay, pair, st4, sp8, s8, b0, b1)
    recv = exchange(send)
    f, n = call(
        last_kernel,
        "last",
        [k_rows, q_rows],
        forward_streams + sums,
        spaces={15: pltpu.HBM},
        **work,
    )(
        recv, far, f2, f3, e2, n2, n3, p2, energy, decay,
        gp8, sk, st8a, st8b, c_held, c_rest,
    )
    return (f, n)


def solution(mesh):
    placed = (
        P(("groups", "bulk"), None),
        P(("groups", "bulk"), None),
        P("bulk", None),
        P("bulk", None),
        P("bulk", None, None),
        P("bulk"),
        P("bulk"),
        P("bulk"),
        P("bulk"),
        P("bulk", None),
        P("bulk", None),
    )
    return jax.shard_map(
        on_device,
        mesh=mesh,
        in_specs=placed,
        out_specs=(P(("groups", "bulk"), None), P(("groups", "bulk"), None)),
        check_vma=False,
    )
```

```python
import functools

import jax
import jax.numpy as jnp
from jax import lax
from jax.experimental import pallas as pl
from jax.experimental.pallas import tpu as pltpu
from jax.sharding import PartitionSpec as P

DT = 0.05
CHUNKS = 8
HELD_CHUNKS = 2
SHORT_CHUNKS = 3
f32 = jnp.float32
bf16 = jnp.bfloat16
VMEM_LIMIT = 48 * 1024 * 1024


def iota(shape, dim):
    return lax.broadcasted_iota(jnp.int32, shape, dim)


def dot(a, b):
    return lax.dot_general(a, b, (((1,), (0,)), ((), ())), preferred_element_type=f32)


def add_rows(onehot, x):
    hi = x.astype(bf16)
    mid = (x - hi.astype(f32)).astype(bf16)
    both = dot(onehot, jnp.concatenate([hi, mid], axis=1))
    return both[:, :128] + both[:, 128:]


def gather_pair(table, x):
    rows = x.shape[0]
    hi = x.astype(bf16)
    mid = (x - hi.astype(f32)).astype(bf16)
    blank = jnp.zeros((rows, 128), bf16)

    def both(part):
        upper = jnp.concatenate([part, blank], axis=1)
        lower = jnp.concatenate([blank, part], axis=1)
        return dot(table, jnp.concatenate([upper, lower], axis=0))

    res = both(hi) + both(mid)
    return res[:, :128], res[:, 128:]


def stacked(first, second):
    tiles = first.shape[0]
    return jnp.concatenate(
        [first.reshape(tiles // 8, 8, 128), second.reshape(tiles // 8, 8, 128)], axis=1
    ).astype(bf16)


def row_is(r):
    return iota((16, 128), 0) % 8 == r


def padded(*parts):
    rows = sum(p.shape[0] for p in parts)
    return jnp.concatenate([*parts, jnp.zeros((128 - rows, 128), f32)], axis=0)


def flat(ref):
    return ref[...].reshape(-1, 128)


def chunk_copy(src, dst, sems, i):
    size = min(src.shape[0], dst.shape[0]) // sems.shape[0]
    here = pl.ds(i * size, size)
    return pltpu.make_async_copy(src.at[here], dst.at[here], sems.at[i])


def start_chunks(src, dst, sems):
    for i in range(sems.shape[0]):
        chunk_copy(src, dst, sems, i).start()


def start(copies):
    for copy in copies:
        copy.start()


def block_diagonal(w):
    w = w.astype(f32)
    return jnp.concatenate(
        [jnp.where(row_is(r), w, 0.0).astype(bf16) for r in range(8)], axis=1
    )


def left_sides(first, second, w_ref):
    groups = w_ref.shape[0]
    w_ref[:, :, :128] = stacked(first, second)

    def spread(g, _):
        w_ref[g] = block_diagonal(w_ref[g, :, :128])
        return 0

    lax.fori_loop(0, groups, spread, 0, unroll=4)


def chunk_products(w_ref, c_ref, i, base, out0, out1, size):
    for k in range(size):
        g = i * size + k
        res = dot(w_ref[base + g], c_ref[pl.ds(g * 8, 8)].reshape(1024, 128))
        out0[base + g] = res[:8]
        out1[base + g] = res[8:]


def tile_products(w_ref, parts, out0, out1):
    for c_ref, c_hbm, sems, base in parts:
        groups = c_ref.shape[0] // 8
        if c_hbm is None:
            chunk_products(w_ref, c_ref, 0, base, out0, out1, groups)
            continue
        size = groups // sems.shape[0]

        def chunk(i, _):
            chunk_copy(c_hbm, c_ref, sems, i).wait()
            chunk_products(w_ref, c_ref, i, base, out0, out1, size)
            return 0

        lax.fori_loop(0, sems.shape[0], chunk, 0)


def backward_pass(own, c_hbm, c_ref, sems, w_ref, out0, out1):
    left_sides(1.0 - own, own, w_ref)
    tile_products(w_ref, [(c_ref, c_hbm, sems, 0)], out0, out1)


def forward_parts(w_ref, held_ref, fetched_ref, c_ref, c_hbm, sems):
    parts = [(held_ref, None, None, 0)]
    if fetched_ref is not None:
        parts.append((fetched_ref, None, None, w_ref.shape[0] - fetched_ref.shape[0] // 8))
    return parts + [(c_ref, c_hbm, sems, held_ref.shape[0] // 8)]


def electron_rate(sum_k, far, bose, f, parts, w_ref, o0, o1):
    left_sides(far * (1.0 + bose), far + bose, w_ref)
    tile_products(w_ref, parts, o0, o1)
    gain, loss = flat(o0), flat(o1)
    gain_hi, loss_hi = gain.astype(bf16), loss.astype(bf16)
    gain_lo = (gain - gain_hi.astype(f32)).astype(bf16)
    loss_lo = (loss - loss_hi.astype(f32)).astype(bf16)
    sums = dot(sum_k, jnp.concatenate([gain_hi, gain_lo, loss_hi, loss_lo], axis=1))
    return sums[:, :128] + sums[:, 128:256] - f * (sums[:, 256:384] + sums[:, 384:])


def my_core():
    return lax.rem(lax.axis_index("bulk"), 2)


def place_of(chip, chips):
    return (chip + chips - chips // 2) % chips


def block_of(peer, peers):
    chips = peers // 2
    return place_of(peer // 2, chips) + jnp.where(peer % 2 == my_core(), 0, chips)


def to_wire(rows, send):
    half = rows.shape[0] // 4 * 2
    send[: rows.shape[0] - half] = rows[half:]
    send[rows.shape[0] - half :] = rows[:half]


def from_wire(recv):
    half = recv.shape[0] // 4 * 2
    return jnp.concatenate([recv[recv.shape[0] - half :], recv[: recv.shape[0] - half]], axis=0)


def need_kernel(cap, *refs):
    ins, outs = refs[:9], refs[9:]
    *small, pneed_ref, qneed_ref, send_ref, sems = outs
    copies = [
        pltpu.make_async_copy(src, dst, sems.at[i])
        for i, (src, dst) in enumerate(zip(ins, [*small, pneed_ref, qneed_ref]))
    ]
    start(copies)
    slots = pneed_ref.shape[1]
    step = send_ref.shape[0] // (slots // cap // 2)
    for copy in copies:
        copy.wait()
    f, n = small[0][...], small[1][...]
    own_p, own_q = pneed_ref[...].astype(f32), qneed_ref[...].astype(f32)
    row = iota((8, slots), 0)
    lists = jnp.where(row == 0, own_p, jnp.where(row == 1, own_q, 0.0))
    if slots < 128:
        lists = jnp.concatenate([lists, jnp.zeros((8, 128 - slots), f32)], axis=1)
    block = jnp.concatenate([f, n, lists], axis=0)
    for chip in range(slots // cap // 2):
        send_ref[chip * step : (chip + 1) * step] = block


def prepare_kernel(
    cap,
    count_ref,
    kblock_ref,
    partner_ref,
    qslot_ref,
    f_ref,
    pneed_ref,
    qneed_ref,
    c_hbm,
    held_ref,
    t_hbm,
    pair_ref,
    gk_ref,
    sk_ref,
    sp_ref,
    sp4_ref,
    near_ref,
    list_ref,
    mine_ref,
    b0_ref,
    b1_ref,
    w_ref,
    c_ref,
    in_sems,
    t_ref,
    out_sems,
):
    start_chunks(c_hbm, c_ref, in_sems)
    tiles = kblock_ref.shape[1]
    kb = f_ref.shape[0]
    used = iota((1, tiles), 1) < count_ref[0]
    k = kblock_ref[...]
    e = partner_ref[...]
    q = qslot_ref[...]
    rows4 = sp4_ref.shape[0]
    ind = lambda m: jnp.where(m, 1.0, 0.0)
    k_hot = ind(iota((kb, tiles), 0) == k)
    gk_ref[...] = k_hot.T.astype(bf16)
    own = add_rows(gk_ref[...], f_ref[...])
    left_sides(1.0 - own, own, w_ref)
    sk_ref[...] = jnp.where(used, k_hot, 0.0).astype(bf16)
    x = iota((rows4, tiles), 0)
    row_e = (e // cap) * (2 * cap) + e % cap
    row_p = (q // cap) * (2 * cap) + cap + q % cap
    p_hot = ind(x == row_p)
    pair_ref[...] = jnp.concatenate([ind(x == row_e), p_hot], axis=0).T.astype(bf16)
    sp4_ref[...] = jnp.where(used, p_hot, 0.0).astype(bf16)
    sp_ref[...] = jnp.where(used, ind(iota(sp_ref.shape, 0) == q), 0.0).astype(bf16)
    rows, half = list_ref.shape
    slots = pneed_ref.shape[1]
    peers = slots // cap
    x = iota((rows, slots), 0)
    y = iota((rows, slots), 1)
    peer, r = x // (2 * cap), x % (2 * cap)
    e_here = (r < cap) & (y == peer * cap + r)
    p_here = (r >= cap) & (y == peer * cap + r - cap)
    pn = jnp.broadcast_to(pneed_ref[...].astype(f32), (rows, slots))
    qn = jnp.broadcast_to(qneed_ref[...].astype(f32), (rows, slots)) + float(kb)
    col = jnp.sum(jnp.where(e_here, pn, 0.0) + jnp.where(p_here, qn, 0.0), axis=1, keepdims=True)
    mine_ref[...] = jnp.broadcast_to(col, (rows, 128))
    start_of = block_of(iota((rows, 1), 0) // (2 * cap), peers) * (2 * half // peers)
    place = col + start_of.astype(f32)
    lane = iota((rows, half), 1).astype(f32)
    near_ref[...] = ind(lane == place).astype(bf16)
    list_ref[...] = ind(lane + float(half) == place).astype(bf16)

    size = c_ref.shape[0] // CHUNKS
    held = held_ref.shape[0] // size

    rest = CHUNKS - held

    def to_held(i, _):
        chunk_copy(c_hbm, c_ref, in_sems, i).wait()
        chunk_products(w_ref, c_ref, i, 0, b0_ref, b1_ref, size // 8)
        for t in range(size):
            held_ref[i * size + t] = c_ref[i * size + t].T
        return 0

    def to_rest(i, _):
        chunk_copy(c_hbm, c_ref, in_sems, held + i).wait()
        chunk_products(w_ref, c_ref, held + i, 0, b0_ref, b1_ref, size // 8)
        for t in range(size):
            t_ref[i * size + t] = c_ref[(held + i) * size + t].T
        chunk_copy(t_ref, t_hbm, out_sems, i).start()
        return 0

    lax.fori_loop(0, held, to_held, 0)
    lax.fori_loop(0, rest, to_rest, 0)
    for i in range(rest):
        chunk_copy(t_ref, t_hbm, out_sems, i).wait()


def blocks(ref, count_of_blocks, first, count):
    step = ref.shape[0] // count_of_blocks
    parts = [ref[b * step + first : b * step + first + count] for b in range(count_of_blocks)]
    return jnp.concatenate(parts, axis=0)


def serve_kernel(
    cap,
    kb,
    qb,
    count_ref,
    qslot_ref,
    asked_ref,
    hot_ref,
    mine_ref,
    share_ref,
    gp8_ref,
    sp8_ref,
    s8_ref,
    st4_ref,
    st8a_ref,
    st8b_ref,
):
    hot = hot_ref[...]
    rows4, rows8 = hot.shape[0], s8_ref.shape[0]
    q = qslot_ref[...]
    tiles = q.shape[1]
    used = iota((1, tiles), 1) < count_ref[0]
    ind = lambda m: jnp.where(m, 1.0, 0.0)
    x = iota((rows8, tiles), 0)
    row_z = (q // cap) * (4 * cap) + q % cap
    gp8_ref[...] = ind(x == row_z).T.astype(bf16)
    sp8_ref[...] = jnp.concatenate(
        [
            jnp.where(used, ind(x == row_z + cap), 0.0),
            jnp.where(used, ind(x == row_z + 2 * cap), 0.0),
        ],
        axis=1,
    ).astype(bf16)
    x = iota((rows8, rows4), 0)
    y = iota((rows8, rows4), 1)
    peer, r = x // (4 * cap), x % (4 * cap)
    source = peer * (2 * cap) + cap + r % cap

    def rows_of(kind):
        here = (y == source) & (r // cap == kind)
        return dot(jnp.where(here, 1.0, 0.0).astype(bf16), hot)

    s8_ref[...] = rows_of(0).astype(bf16)
    st4_ref[...] = hot.astype(f32).T[kb : kb + qb].astype(bf16)
    st8a_ref[...] = rows_of(1).T[kb : kb + qb].astype(bf16)
    st8b_ref[...] = rows_of(2).T[kb : kb + qb].astype(bf16)

    peers = rows4 // (2 * cap)
    slots = peers * cap
    wide = peers * slots
    lists = asked_ref[...]
    pick_q = iota((peers, 8 * peers), 1) == 8 * iota((peers, 8 * peers), 0) + 1
    every_q = dot(jnp.where(pick_q, 1.0, 0.0).astype(bf16), lists).astype(bf16)
    tiled = iota((128, wide), 0) == iota((128, wide), 1) % slots
    spread = dot(every_q, jnp.where(tiled, 1.0, 0.0).astype(bf16))
    lane = iota((1, wide), 1)
    here = iota((peers, wide), 0) == lane // slots
    q = jnp.sum(jnp.where(here, spread, 0.0), axis=0, keepdims=True)
    ids = q + (lane % slots // cap * qb).astype(f32)
    row = iota((rows4, 1), 0)
    col = mine_ref[...][:, :1]
    my_ids = col - float(kb) + (row // (2 * cap) * qb).astype(f32)
    my_ids = jnp.where(row % (2 * cap) >= cap, my_ids, -1.0)
    owned = (lax.axis_index("bulk") * qb + iota((qb, 1), 0)).astype(f32)
    wanted = jnp.concatenate([my_ids, owned], axis=0)
    share_ref[...] = jnp.where(ids == wanted, 1.0, 0.0).astype(bf16)


def thermal_of(energy_ref):
    return 1.0 / (jnp.exp(energy_ref[...]) - 1.0)


def put_broadcast(send, served, contributions):
    slots = contributions.shape[0]
    chips = served.shape[0] // 8
    for chip in range(chips):
        at = place_of(chip, chips) * (8 + slots)
        send[at : at + 8] = served[chip * 8 : chip * 8 + 8]
        send[at + 8 : at + 8 + slots] = contributions


def phonon_terms(far, bose, b0_ref, b1_ref):
    gain = far * flat(b0_ref)
    return gain + bose * (gain - (1.0 - far) * flat(b1_ref))


def fetch_copy(c_hbm, fetched_ref, sem):
    count = fetched_ref.shape[0]
    return pltpu.make_async_copy(
        c_hbm.at[pl.ds(c_hbm.shape[0] - count, count)], fetched_ref, sem.at[0]
    )


def near_rows_kernel(same_ref, list_ref, c_hbm, part_ref, fetched_ref, sem):
    copy = fetch_copy(c_hbm, fetched_ref, sem)
    copy.start()
    part_ref[...] = add_rows(list_ref[...], same_ref[...])
    copy.wait()


def half_of_devices(cap, chips, weight, others, ref, share_ref):
    rows4 = 4 * cap * chips
    wide = share_ref.shape[1] // 2
    x = iota((rows4, 8 * chips), 0)
    peer = x // (2 * cap)
    source = 8 * place_of(peer // 2, chips) + 2 * cap * my_core() + x % (2 * cap)
    wanted_core = (my_core() + others) % 2
    at = (iota((rows4, 8 * chips), 1) == source) & (peer % 2 == wanted_core)
    heads = add_rows(jnp.where(at, 1.0, 0.0).astype(bf16), blocks(ref, chips, 0, 8))
    tails = blocks(ref, chips, 8, wide // chips)
    sums = add_rows(share_ref[:, others * wide : (others + 1) * wide], tails)
    return heads + weight * sums[:rows4], sums[rows4:]


def near_half_kernel(
    cap, chips, weight, same_ref, share_ref, c_hbm, part_ref, total_ref, fetched_ref, sem
):
    copy = fetch_copy(c_hbm, fetched_ref, sem)
    copy.start()
    part, total = half_of_devices(cap, chips, weight, 0, same_ref, share_ref)
    part_ref[...] = part
    total_ref[...] = total
    copy.wait()


def first_kernel(
    cap,
    same_ref,
    other_ref,
    part_ref,
    list_ref,
    f_ref,
    n_ref,
    energy_ref,
    decay_ref,
    pair_ref,
    sk_ref,
    sp_ref,
    b0_ref,
    b1_ref,
    held_ref,
    fetched_ref,
    c_hbm,
    send,
    e_ref,
    f1_ref,
    hot_ref,
    asked_ref,
    w_ref,
    c_ref,
    sems,
    o0,
    o1,
):
    start_chunks(c_hbm, c_ref, sems)
    f, n = f_ref[...], n_ref[...]
    kb, qb = f.shape[0], n.shape[0]
    rows4 = list_ref.shape[0]
    peers = rows4 // (2 * cap)
    got = part_ref[...] + add_rows(list_ref[...], other_ref[...])
    far, bose = gather_pair(pair_ref[...], got)
    contributions = add_rows(sp_ref[...], phonon_terms(far, bose, b0_ref, b1_ref))
    lists = jnp.concatenate(
        [blocks(ref, peers // 2, kb + qb, 8) for ref in (same_ref, other_ref)], axis=0
    ).astype(bf16)
    asked_ref[...] = lists
    x = iota((rows4, 8 * peers), 0)
    r = x % (2 * cap)
    kind = jnp.where(r < cap, 0, 1)
    at = iota((rows4, 8 * peers), 1) == 8 * block_of(x // (2 * cap), peers) + kind
    asked = dot(jnp.where(at, 1.0, 0.0).astype(bf16), lists)
    r = iota((rows4, 128), 0) % (2 * cap)
    lane = iota((rows4, 128), 1)
    wanted = lane == lax.axis_index("bulk") * cap + r % cap
    col = jnp.sum(jnp.where(wanted, asked, 0.0), axis=1, keepdims=True)
    col = col + jnp.where(r[:, :1] < cap, 0.0, float(kb))
    hot = jnp.where(lane.astype(f32) == col, 1.0, 0.0).astype(bf16)
    hot_ref[...] = hot
    base = n - DT * decay_ref[...] * (n - thermal_of(energy_ref))
    parts = forward_parts(w_ref, held_ref, fetched_ref, c_ref, c_hbm, sems)
    rate = electron_rate(sk_ref[...], far, bose, f, parts, w_ref, o0, o1)
    f1 = f + DT * rate
    e_ref[...] = rate
    f1_ref[...] = f1
    put_broadcast(send, add_rows(hot, padded(f1, base)), contributions)


def middle_kernel(
    cap,
    ends,
    part_ref,
    total_ref,
    other_ref,
    share_ref,
    serve_ref,
    f_ref,
    e_ref,
    own_ref,
    n_ref,
    energy_ref,
    decay_ref,
    pair_ref,
    sk_ref,
    sp_ref,
    b0_ref,
    b1_ref,
    held_ref,
    fetched_ref,
    c_hbm,
    send,
    *refs,
):
    w_ref, c_ref, sems, o0, o1 = refs[-5:]
    start_chunks(c_hbm, c_ref, sems)
    chips = serve_ref.shape[0] // (4 * cap)
    weight = DT / 2.0 if ends else DT
    part, total = half_of_devices(cap, chips, weight, 1, other_ref, share_ref)
    got = part_ref[...] + part
    total = total_ref[...] + total
    far, bose = gather_pair(pair_ref[...], got)
    terms = phonon_terms(far, bose, b0_ref, b1_ref)
    contributions = add_rows(sp_ref[...], terms)
    n = n_ref[...]
    own = own_ref[...]
    parts = forward_parts(w_ref, held_ref, fetched_ref, c_ref, c_hbm, sems)
    if ends:
        n2_ref, e2_ref, f3_ref = refs[:3]
        n2_ref[...] = n + (DT / 2.0) * total
        rate = electron_rate(sk_ref[...], far, bose, own, parts, w_ref, o0, o1)
        f3 = own + DT * rate
        e2_ref[...] = rate
        f3_ref[...] = f3
        to_wire(add_rows(serve_ref[...], padded(f3)) + contributions, send)
    else:
        base_ref, f2_ref = refs[:2]
        thermal = thermal_of(energy_ref)
        decay = decay_ref[...]
        p0 = total - decay * (n - thermal)
        n1 = n + DT * p0
        base = n + (DT / 2.0) * (p0 - decay * (n1 - thermal))
        base_ref[...] = base
        rate = electron_rate(sk_ref[...], far, bose, own, parts, w_ref, o0, o1)
        f2 = f_ref[...] + (DT / 2.0) * (e_ref[...] + rate)
        f2_ref[...] = f2
        put_broadcast(send, add_rows(serve_ref[...], padded(f2, base)), contributions)


def backward_kernel(f_ref, gk_ref, c_hbm, b0_ref, b1_ref, w_ref, c_ref, sems):
    start_chunks(c_hbm, c_ref, sems)
    own = add_rows(gk_ref[...], f_ref[...])
    backward_pass(own, c_hbm, c_ref, sems, w_ref, b0_ref, b1_ref)


def phonon_kernel(
    kb,
    recv,
    n_ref,
    energy_ref,
    decay_ref,
    pair_ref,
    st4_ref,
    sp8_ref,
    s8_ref,
    b0_ref,
    b1_ref,
    send,
    p_ref,
    n1_ref,
    far_ref,
):
    n = n_ref[...]
    got = from_wire(recv)
    thermal = thermal_of(energy_ref)
    rate = add_rows(st4_ref[...], got) - decay_ref[...] * (n - thermal)
    n1 = n + DT * rate
    p_ref[...] = rate
    n1_ref[...] = n1
    far = add_rows(pair_ref[:, : got.shape[0]], got)
    far_ref[...] = far
    gain = far * flat(b0_ref)
    both = jnp.concatenate([gain, gain - (1.0 - far) * flat(b1_ref)], axis=0)
    state = padded(jnp.zeros((kb, 128), f32), n1)
    to_wire(add_rows(s8_ref[...], state) + add_rows(sp8_ref[...], both), send)


def last_kernel(recv, *refs):
    far_ref, f_ref, f1_ref, e_ref, n_ref, n1_ref, p_ref, energy_ref, decay_ref = refs[:9]
    gp8_ref, sk_ref, st8a_ref, st8b_ref, held_ref, c_hbm = refs[9:15]
    refs = refs[15:]
    f2_ref, n2_ref, w_ref, c_ref, sems, o0, o1 = refs
    start_chunks(c_hbm, c_ref, sems)
    got = from_wire(recv)
    n, n1 = n_ref[...], n1_ref[...]
    bose = add_rows(gp8_ref[...], got)
    thermal = thermal_of(energy_ref)
    p1 = (
        add_rows(st8a_ref[...], got)
        + n1 * add_rows(st8b_ref[...], got)
        - decay_ref[...] * (n1 - thermal)
    )
    n2 = n + (DT / 2.0) * (p_ref[...] + p1)
    n2_ref[...] = n2
    parts = forward_parts(w_ref, held_ref, None, c_ref, c_hbm, sems)
    rate = electron_rate(sk_ref[...], far_ref[...], bose, f1_ref[...], parts, w_ref, o0, o1)
    f2 = f_ref[...] + (DT / 2.0) * (e_ref[...] + rate)
    f2_ref[...] = f2


def call(kernel, name, outs, scratch=(), spaces=None, out_spaces=None, flops=0, seen=0):
    def run(*args):
        places = dict(spaces or {})
        args = [
            pltpu.with_memory_space_constraint(x, pltpu.HBM)
            if places.get(i) is pltpu.HBM
            else x
            for i, x in enumerate(args)
        ]
        specs = [
            pl.BlockSpec(memory_space=places.get(i, pltpu.VMEM)) for i in range(len(args))
        ]
        return pl.pallas_call(
            kernel,
            out_shape=[
                (out_spaces or {}).get(i, jax.ShapeDtypeStruct)(*o) for i, o in enumerate(outs)
            ],
            in_specs=specs,
            out_specs=[
                pl.BlockSpec(memory_space=(out_spaces or {}).get(i, pltpu.VMEM))
                for i in range(len(outs))
            ],
            scratch_shapes=list(scratch),
            compiler_params=pltpu.CompilerParams(vmem_limit_bytes=VMEM_LIMIT),
            cost_estimate=pl.CostEstimate(
                flops=flops, bytes_accessed=seen, transcendentals=0
            ),
            name=name,
        )(*args)

    return run


def on_device(
    electrons,
    phonons,
    phonon_energy,
    phonon_decay,
    coupling,
    tile_kblock,
    tile_partner,
    tile_qslot,
    tile_count,
    partner_need,
    phonon_need,
):
    devices = lax.axis_size("bulk")
    kb = electrons.shape[0]
    qb = phonons.shape[0]
    tiles = coupling.shape[0]
    cap = partner_need.shape[1] // devices
    assert cap == phonon_need.shape[1] // devices and kb + qb <= 128
    rows4 = devices * 2 * cap
    rows8 = devices * 4 * cap
    groups = tiles // 8
    held = HELD_CHUNKS * (tiles // CHUNKS)
    weights = pltpu.VMEM((groups, 16, 1024), bf16)
    streams = [weights, pltpu.VMEM(coupling.shape, bf16), pltpu.SemaphoreType.DMA((CHUNKS,))]
    rest = (tiles - held, 128, 128)
    rest_sems = pltpu.SemaphoreType.DMA((CHUNKS - HELD_CHUNKS,))
    forward_streams = [weights, pltpu.VMEM(rest, bf16), rest_sems]
    sums = [pltpu.VMEM((groups, 8, 128), f32)] * 2
    pass_out = [((groups, 8, 128), f32)] * 2
    block4 = ((rows4, 128), f32)
    block8 = ((rows8, 128), f32)

    work = dict(flops=2 * tiles * 16 * 128 * 128, seen=tiles * 128 * 128 * 2)

    def exchange(x):
        order = [[(i + devices // 4 * 2) % devices for i in range(devices)]]
        return lax.all_to_all(
            x, "bulk", split_axis=0, concat_axis=0, tiled=True, axis_index_groups=order
        )

    ints = ((1, tiles), jnp.int32)
    lists = ((1, partner_need.shape[1]), jnp.int32)
    small = [((kb, 128), f32)] + [((qb, 128), f32)] * 3 + [ints] * 3
    step_rows = kb + qb + 8
    slots = devices * cap
    wide = 8 + slots
    assert step_rows % 8 == 0 and slots % 8 == 0 and slots <= 128
    assert devices % 2 == 0 and cap == 2
    chips = devices // 2
    same_core = [
        [(i + chips // 2) % chips * 2 + core for i in range(chips)] for core in (0, 1)
    ]

    def to_chips(x):
        return lax.all_to_all(
            x, "bulk", split_axis=0, concat_axis=0, tiled=True, axis_index_groups=same_core
        )

    def between_cores(x):
        return lax.ppermute(x, "bulk", [(i, i ^ 1) for i in range(devices)])

    f, n, energy, decay, kblock, partner, qslot, pneed, qneed, send = call(
        functools.partial(need_kernel, cap),
        "need",
        small + [lists, lists, ((chips * step_rows, 128), f32)],
        [pltpu.SemaphoreType.DMA((9,))],
        spaces={i: pltpu.HBM for i in range(9)},
    )(
        electrons,
        phonons,
        phonon_energy,
        phonon_decay,
        tile_kblock.reshape(1, tiles),
        tile_partner.reshape(1, tiles),
        tile_qslot.reshape(1, tiles),
        partner_need,
        phonon_need,
    )
    same = to_chips(send)
    c_held, c_rest, pair, gk, sk, sp, sp4, near, far_picks, mine, b0, b1 = call(
        functools.partial(prepare_kernel, cap),
        "prepare",
        [
            ((held, 128, 128), bf16),
            (rest, bf16),
            ((tiles, 2 * rows4), bf16),
            ((tiles, kb), bf16),
            ((kb, tiles), bf16),
            ((slots, tiles), bf16),
            ((rows4, tiles), bf16),
            ((rows4, chips * step_rows), bf16),
            ((rows4, chips * step_rows), bf16),
            ((rows4, 128), f32),
        ]
        + pass_out,
        [*streams, pltpu.VMEM(rest, bf16), rest_sems],
        spaces={0: pltpu.SMEM, 7: pltpu.HBM},
        out_spaces={1: pltpu.HBM},
        **work,
    )(tile_count, kblock, partner, qslot, f, pneed, qneed, coupling)
    same, c_held, b0 = lax.optimization_barrier((same, c_held, b0))
    wide_block = ((chips * wide, 128), f32)
    k_rows, q_rows = ((kb, 128), f32), ((qb, 128), f32)
    width = 3 * (tiles // CHUNKS) // 2
    fetched = ((width, 128, 128), bf16)
    fetch_sem = pltpu.SemaphoreType.DMA((1,))
    short = (rest[0] - width, 128, 128)
    short_sems = pltpu.SemaphoreType.DMA((SHORT_CHUNKS,))
    forward_scratch = [weights, pltpu.VMEM(short, bf16), short_sems] + sums
    other = between_cores(same)
    part, c_fetched = call(
        near_rows_kernel,
        "near_rows",
        [block4, fetched],
        [fetch_sem],
        spaces={2: pltpu.HBM},
        out_spaces={1: pltpu.VMEM},
    )(same, near, c_rest)
    send, e0, f1, serve, asked = call(
        functools.partial(first_kernel, cap),
        "first",
        [wide_block, k_rows, k_rows, ((rows4, 128), bf16), ((8 * devices, 128), bf16)],
        forward_scratch,
        spaces={15: pltpu.HBM},
        **work,
    )(same, other, part, far_picks, f, n, energy, decay, pair, sk, sp, b0, b1, c_held, c_fetched, c_rest)
    share, gp8, sp8, s8, st4, st8a, st8b = call(
        functools.partial(serve_kernel, cap, kb, qb),
        "serve",
        [
            ((rows4 + qb, devices * slots), bf16),
            ((tiles, rows8), bf16),
            ((rows8, 2 * tiles), bf16),
            ((rows8, 128), bf16),
            ((qb, rows4), bf16),
            ((qb, rows8), bf16),
            ((qb, rows8), bf16),
        ],
        spaces={0: pltpu.SMEM},
    )(tile_count, qslot, asked, serve, mine)
    back = call(backward_kernel, "backward", pass_out, streams, spaces={2: pltpu.HBM}, **work)

    def middle(ends, send, outs, f, e, own, n, contributions, share):
        same = to_chips(send)
        b0, b1 = back(own, gk, coupling)
        same, b0, share = lax.optimization_barrier((same, b0, share))
        other = between_cores(same)
        weight = DT / 2.0 if ends else DT
        part, total, c_fetched = call(
            functools.partial(near_half_kernel, cap, chips, weight),
            "near_half",
            [block4, q_rows, fetched],
            [fetch_sem],
            spaces={2: pltpu.HBM},
            out_spaces={2: pltpu.VMEM},
        )(same, share, c_rest)
        return call(
            functools.partial(middle_kernel, cap, ends),
            "middle",
            outs,
            forward_scratch,
            spaces={18: pltpu.HBM},
            **work,
        )(
            part, total, other, share, serve, f, e, own, n, energy, decay,
            pair, sk, contributions, b0, b1, c_held, c_fetched, c_rest,
        )

    send, base, f2 = middle(False, send, [wide_block, q_rows, k_rows], f, e0, f1, n, sp, share)
    send, n2, e2, f3 = middle(
        True, send, [block4, q_rows, k_rows, k_rows], f2, e0, f2, base, sp4, share
    )
    recv = exchange(send)
    b0, b1 = back(f3, gk, coupling)
    send, p2, n3, far = call(
        functools.partial(phonon_kernel, kb),
        "phonon",
        [block8, q_rows, q_rows, ((tiles, 128), f32)],
    )(recv, n2, energy, decay, pair, st4, sp8, s8, b0, b1)
    recv = exchange(send)
    f, n = call(
        last_kernel,
        "last",
        [k_rows, q_rows],
        forward_streams + sums,
        spaces={15: pltpu.HBM},
        **work,
    )(
        recv, far, f2, f3, e2, n2, n3, p2, energy, decay,
        gp8, sk, st8a, st8b, c_held, c_rest,
    )
    return (f, n)


def solution(mesh):
    placed = (
        P(("groups", "bulk"), None),
        P(("groups", "bulk"), None),
        P("bulk", None),
        P("bulk", None),
        P("bulk", None, None),
        P("bulk"),
        P("bulk"),
        P("bulk"),
        P("bulk"),
        P("bulk", None),
        P("bulk", None),
    )
    return jax.shard_map(
        on_device,
        mesh=mesh,
        in_specs=placed,
        out_specs=(P(("groups", "bulk"), None), P(("groups", "bulk"), None)),
        check_vma=False,
    )
```

```python
import functools

import jax
import jax.numpy as jnp
from jax import lax
from jax.experimental import pallas as pl
from jax.experimental.pallas import tpu as pltpu
from jax.sharding import PartitionSpec as P

DT = 0.05
CHUNKS = 8
HELD_CHUNKS = 2
f32 = jnp.float32
bf16 = jnp.bfloat16
VMEM_LIMIT = 48 * 1024 * 1024


def iota(shape, dim):
    return lax.broadcasted_iota(jnp.int32, shape, dim)


def dot(a, b):
    return lax.dot_general(a, b, (((1,), (0,)), ((), ())), preferred_element_type=f32)


def add_rows(onehot, x):
    hi = x.astype(bf16)
    mid = (x - hi.astype(f32)).astype(bf16)
    both = dot(onehot, jnp.concatenate([hi, mid], axis=1))
    return both[:, :128] + both[:, 128:]


def gather_pair(table, x):
    rows = x.shape[0]
    hi = x.astype(bf16)
    mid = (x - hi.astype(f32)).astype(bf16)
    blank = jnp.zeros((rows, 128), bf16)

    def both(part):
        upper = jnp.concatenate([part, blank], axis=1)
        lower = jnp.concatenate([blank, part], axis=1)
        return dot(table, jnp.concatenate([upper, lower], axis=0))

    res = both(hi) + both(mid)
    return res[:, :128], res[:, 128:]


def stacked(first, second):
    tiles = first.shape[0]
    return jnp.concatenate(
        [first.reshape(tiles // 8, 8, 128), second.reshape(tiles // 8, 8, 128)], axis=1
    ).astype(bf16)


def row_is(r):
    return iota((16, 128), 0) % 8 == r


def padded(*parts):
    rows = sum(p.shape[0] for p in parts)
    return jnp.concatenate([*parts, jnp.zeros((128 - rows, 128), f32)], axis=0)


def flat(ref):
    return ref[...].reshape(-1, 128)


def chunk_copy(src, dst, sems, i):
    size = min(src.shape[0], dst.shape[0]) // sems.shape[0]
    here = pl.ds(i * size, size)
    return pltpu.make_async_copy(src.at[here], dst.at[here], sems.at[i])


def start_chunks(src, dst, sems):
    for i in range(sems.shape[0]):
        chunk_copy(src, dst, sems, i).start()


def start(copies):
    for copy in copies:
        copy.start()


def block_diagonal(w):
    w = w.astype(f32)
    return jnp.concatenate(
        [jnp.where(row_is(r), w, 0.0).astype(bf16) for r in range(8)], axis=1
    )


def left_sides(first, second, w_ref):
    groups = w_ref.shape[0]
    w_ref[:, :, :128] = stacked(first, second)

    def spread(g, _):
        w_ref[g] = block_diagonal(w_ref[g, :, :128])
        return 0

    lax.fori_loop(0, groups, spread, 0, unroll=4)


def chunk_products(w_ref, c_ref, i, base, out0, out1):
    size = w_ref.shape[0] // CHUNKS
    for k in range(size):
        g = i * size + k
        res = dot(w_ref[base + g], c_ref[pl.ds(g * 8, 8)].reshape(1024, 128))
        out0[base + g] = res[:8]
        out1[base + g] = res[8:]


def tile_products(w_ref, parts, out0, out1):
    size = w_ref.shape[0] // CHUNKS
    for c_ref, c_hbm, sems, base in parts:
        chunks = c_ref.shape[0] // 8 // size

        def chunk(i, _):
            if c_hbm is not None:
                chunk_copy(c_hbm, c_ref, sems, i).wait()
            chunk_products(w_ref, c_ref, i, base, out0, out1)
            return 0

        lax.fori_loop(0, chunks, chunk, 0)


def backward_pass(own, c_hbm, c_ref, sems, w_ref, out0, out1):
    left_sides(1.0 - own, own, w_ref)
    tile_products(w_ref, [(c_ref, c_hbm, sems, 0)], out0, out1)


def forward_parts(w_ref, held_ref, fetched_ref, c_ref, c_hbm, sems):
    parts = [(held_ref, None, None, 0)]
    if fetched_ref is not None:
        parts.append((fetched_ref, None, None, w_ref.shape[0] - fetched_ref.shape[0] // 8))
    return parts + [(c_ref, c_hbm, sems, held_ref.shape[0] // 8)]


def electron_rate(sum_k, far, bose, f, parts, w_ref, o0, o1):
    left_sides(far * (1.0 + bose), far + bose, w_ref)
    tile_products(w_ref, parts, o0, o1)
    gain, loss = flat(o0), flat(o1)
    gain_hi, loss_hi = gain.astype(bf16), loss.astype(bf16)
    gain_lo = (gain - gain_hi.astype(f32)).astype(bf16)
    loss_lo = (loss - loss_hi.astype(f32)).astype(bf16)
    sums = dot(sum_k, jnp.concatenate([gain_hi, gain_lo, loss_hi, loss_lo], axis=1))
    return sums[:, :128] + sums[:, 128:256] - f * (sums[:, 256:384] + sums[:, 384:])


def my_core():
    return lax.rem(lax.axis_index("bulk"), 2)


def place_of(chip, chips):
    return (chip + chips - chips // 2) % chips


def block_of(peer, peers):
    chips = peers // 2
    return place_of(peer // 2, chips) + jnp.where(peer % 2 == my_core(), 0, chips)


def to_wire(rows, send):
    half = rows.shape[0] // 4 * 2
    send[: rows.shape[0] - half] = rows[half:]
    send[rows.shape[0] - half :] = rows[:half]


def from_wire(recv):
    half = recv.shape[0] // 4 * 2
    return jnp.concatenate([recv[recv.shape[0] - half :], recv[: recv.shape[0] - half]], axis=0)


def need_kernel(cap, *refs):
    ins, outs = refs[:9], refs[9:]
    *small, pneed_ref, qneed_ref, send_hbm, sems, block_ref, out_sems = outs
    copies = [
        pltpu.make_async_copy(src, dst, sems.at[i])
        for i, (src, dst) in enumerate(zip(ins, [*small, pneed_ref, qneed_ref]))
    ]
    start(copies)
    slots = pneed_ref.shape[1]
    chips = slots // cap // 2
    step = send_hbm.shape[0] // chips
    for copy in copies:
        copy.wait()
    f, n = small[0][...], small[1][...]
    own_p, own_q = pneed_ref[...].astype(f32), qneed_ref[...].astype(f32)
    row = iota((8, slots), 0)
    lists = jnp.where(row == 0, own_p, jnp.where(row == 1, own_q, 0.0))
    if slots < 128:
        lists = jnp.concatenate([lists, jnp.zeros((8, 128 - slots), f32)], axis=1)
    block_ref[...] = jnp.concatenate([f, n, lists], axis=0)
    copies = [
        pltpu.make_async_copy(
            block_ref, send_hbm.at[pl.ds(chip * step, step)], out_sems.at[chip]
        )
        for chip in range(chips)
    ]
    start(copies)
    for copy in copies:
        copy.wait()


def prepare_kernel(
    cap,
    count_ref,
    kblock_ref,
    partner_ref,
    qslot_ref,
    f_ref,
    pneed_ref,
    qneed_ref,
    c_hbm,
    held_ref,
    t_hbm,
    pair_ref,
    gk_ref,
    sk_ref,
    sp_ref,
    sp4_ref,
    near_ref,
    list_ref,
    mine_ref,
    b0_ref,
    b1_ref,
    w_ref,
    c_ref,
    in_sems,
    t_ref,
    out_sems,
):
    start_chunks(c_hbm, c_ref, in_sems)
    tiles = kblock_ref.shape[1]
    kb = f_ref.shape[0]
    used = iota((1, tiles), 1) < count_ref[0]
    k = kblock_ref[...]
    e = partner_ref[...]
    q = qslot_ref[...]
    rows4 = sp4_ref.shape[0]
    ind = lambda m: jnp.where(m, 1.0, 0.0)
    k_hot = ind(iota((kb, tiles), 0) == k)
    gk_ref[...] = k_hot.T.astype(bf16)
    own = add_rows(gk_ref[...], f_ref[...])
    left_sides(1.0 - own, own, w_ref)
    sk_ref[...] = jnp.where(used, k_hot, 0.0).astype(bf16)
    x = iota((rows4, tiles), 0)
    row_e = (e // cap) * (2 * cap) + e % cap
    row_p = (q // cap) * (2 * cap) + cap + q % cap
    p_hot = ind(x == row_p)
    pair_ref[...] = jnp.concatenate([ind(x == row_e), p_hot], axis=0).T.astype(bf16)
    sp4_ref[...] = jnp.where(used, p_hot, 0.0).astype(bf16)
    sp_ref[...] = jnp.where(used, ind(iota(sp_ref.shape, 0) == q), 0.0).astype(bf16)
    rows, half = list_ref.shape
    slots = pneed_ref.shape[1]
    peers = slots // cap
    x = iota((rows, slots), 0)
    y = iota((rows, slots), 1)
    peer, r = x // (2 * cap), x % (2 * cap)
    e_here = (r < cap) & (y == peer * cap + r)
    p_here = (r >= cap) & (y == peer * cap + r - cap)
    pn = jnp.broadcast_to(pneed_ref[...].astype(f32), (rows, slots))
    qn = jnp.broadcast_to(qneed_ref[...].astype(f32), (rows, slots)) + float(kb)
    col = jnp.sum(jnp.where(e_here, pn, 0.0) + jnp.where(p_here, qn, 0.0), axis=1, keepdims=True)
    mine_ref[...] = jnp.broadcast_to(col, (rows, 128))
    start_of = block_of(iota((rows, 1), 0) // (2 * cap), peers) * (2 * half // peers)
    place = col + start_of.astype(f32)
    lane = iota((rows, half), 1).astype(f32)
    near_ref[...] = ind(lane == place).astype(bf16)
    list_ref[...] = ind(lane + float(half) == place).astype(bf16)

    size = c_ref.shape[0] // CHUNKS
    held = held_ref.shape[0] // size

    rest = CHUNKS - held

    def to_held(i, _):
        chunk_copy(c_hbm, c_ref, in_sems, i).wait()
        chunk_products(w_ref, c_ref, i, 0, b0_ref, b1_ref)
        for t in range(size):
            held_ref[i * size + t] = c_ref[i * size + t].T
        return 0

    def to_rest(i, _):
        chunk_copy(c_hbm, c_ref, in_sems, held + i).wait()
        chunk_products(w_ref, c_ref, held + i, 0, b0_ref, b1_ref)
        for t in range(size):
            t_ref[i * size + t] = c_ref[(held + i) * size + t].T
        chunk_copy(t_ref, t_hbm, out_sems, i).start()
        return 0

    lax.fori_loop(0, held, to_held, 0)
    lax.fori_loop(0, rest, to_rest, 0)
    for i in range(rest):
        chunk_copy(t_ref, t_hbm, out_sems, i).wait()


def blocks(ref, count_of_blocks, first, count):
    step = ref.shape[0] // count_of_blocks
    parts = [ref[b * step + first : b * step + first + count] for b in range(count_of_blocks)]
    return jnp.concatenate(parts, axis=0)


def serve_kernel(
    cap,
    kb,
    qb,
    count_ref,
    qslot_ref,
    asked_ref,
    hot_ref,
    mine_ref,
    share_ref,
    gp8_ref,
    sp8_ref,
    s8_ref,
    st4_ref,
    st8a_ref,
    st8b_ref,
):
    hot = hot_ref[...]
    rows4, rows8 = hot.shape[0], s8_ref.shape[0]
    q = qslot_ref[...]
    tiles = q.shape[1]
    used = iota((1, tiles), 1) < count_ref[0]
    ind = lambda m: jnp.where(m, 1.0, 0.0)
    x = iota((rows8, tiles), 0)
    row_z = (q // cap) * (4 * cap) + q % cap
    gp8_ref[...] = ind(x == row_z).T.astype(bf16)
    sp8_ref[...] = jnp.concatenate(
        [
            jnp.where(used, ind(x == row_z + cap), 0.0),
            jnp.where(used, ind(x == row_z + 2 * cap), 0.0),
        ],
        axis=1,
    ).astype(bf16)
    x = iota((rows8, rows4), 0)
    y = iota((rows8, rows4), 1)
    peer, r = x // (4 * cap), x % (4 * cap)
    source = peer * (2 * cap) + cap + r % cap

    def rows_of(kind):
        here = (y == source) & (r // cap == kind)
        return dot(jnp.where(here, 1.0, 0.0).astype(bf16), hot)

    s8_ref[...] = rows_of(0).astype(bf16)
    st4_ref[...] = hot.astype(f32).T[kb : kb + qb].astype(bf16)
    st8a_ref[...] = rows_of(1).T[kb : kb + qb].astype(bf16)
    st8b_ref[...] = rows_of(2).T[kb : kb + qb].astype(bf16)

    peers = rows4 // (2 * cap)
    slots = peers * cap
    wide = peers * slots
    lists = asked_ref[...]
    pick_q = iota((peers, 8 * peers), 1) == 8 * iota((peers, 8 * peers), 0) + 1
    every_q = dot(jnp.where(pick_q, 1.0, 0.0).astype(bf16), lists).astype(bf16)
    tiled = iota((128, wide), 0) == iota((128, wide), 1) % slots
    spread = dot(every_q, jnp.where(tiled, 1.0, 0.0).astype(bf16))
    lane = iota((1, wide), 1)
    here = iota((peers, wide), 0) == lane // slots
    q = jnp.sum(jnp.where(here, spread, 0.0), axis=0, keepdims=True)
    ids = q + (lane % slots // cap * qb).astype(f32)
    row = iota((rows4, 1), 0)
    col = mine_ref[...][:, :1]
    my_ids = col - float(kb) + (row // (2 * cap) * qb).astype(f32)
    my_ids = jnp.where(row % (2 * cap) >= cap, my_ids, -1.0)
    owned = (lax.axis_index("bulk") * qb + iota((qb, 1), 0)).astype(f32)
    wanted = jnp.concatenate([my_ids, owned], axis=0)
    share_ref[...] = jnp.where(ids == wanted, 1.0, 0.0).astype(bf16)


def thermal_of(energy_ref):
    return 1.0 / (jnp.exp(energy_ref[...]) - 1.0)


def put_broadcast(send, served, contributions):
    slots = contributions.shape[0]
    chips = served.shape[0] // 8
    for chip in range(chips):
        at = place_of(chip, chips) * (8 + slots)
        send[at : at + 8] = served[chip * 8 : chip * 8 + 8]
        send[at + 8 : at + 8 + slots] = contributions


def phonon_terms(far, bose, b0_ref, b1_ref):
    gain = far * flat(b0_ref)
    return gain + bose * (gain - (1.0 - far) * flat(b1_ref))


def fetch_copy(c_hbm, fetched_ref, sem):
    count = fetched_ref.shape[0]
    return pltpu.make_async_copy(
        c_hbm.at[pl.ds(c_hbm.shape[0] - count, count)], fetched_ref, sem.at[0]
    )


def near_rows_kernel(same_ref, list_ref, c_hbm, part_ref, fetched_ref, sem):
    copy = fetch_copy(c_hbm, fetched_ref, sem)
    copy.start()
    part_ref[...] = add_rows(list_ref[...], same_ref[...])
    copy.wait()


def half_of_devices(cap, chips, weight, others, ref, share_ref):
    rows4 = 4 * cap * chips
    wide = share_ref.shape[1] // 2
    x = iota((rows4, 8 * chips), 0)
    peer = x // (2 * cap)
    source = 8 * place_of(peer // 2, chips) + 2 * cap * my_core() + x % (2 * cap)
    wanted_core = (my_core() + others) % 2
    at = (iota((rows4, 8 * chips), 1) == source) & (peer % 2 == wanted_core)
    heads = add_rows(jnp.where(at, 1.0, 0.0).astype(bf16), blocks(ref, chips, 0, 8))
    tails = blocks(ref, chips, 8, wide // chips)
    sums = add_rows(share_ref[:, others * wide : (others + 1) * wide], tails)
    return heads + weight * sums[:rows4], sums[rows4:]


def near_half_kernel(
    cap, chips, weight, same_ref, share_ref, c_hbm, part_ref, total_ref, fetched_ref, sem
):
    copy = fetch_copy(c_hbm, fetched_ref, sem)
    copy.start()
    part, total = half_of_devices(cap, chips, weight, 0, same_ref, share_ref)
    part_ref[...] = part
    total_ref[...] = total
    copy.wait()


def first_kernel(
    cap,
    same_ref,
    other_ref,
    part_ref,
    list_ref,
    f_ref,
    n_ref,
    energy_ref,
    decay_ref,
    pair_ref,
    sk_ref,
    sp_ref,
    b0_ref,
    b1_ref,
    held_ref,
    fetched_ref,
    c_hbm,
    send,
    e_ref,
    f1_ref,
    hot_ref,
    asked_ref,
    w_ref,
    c_ref,
    sems,
    o0,
    o1,
):
    start_chunks(c_hbm, c_ref, sems)
    f, n = f_ref[...], n_ref[...]
    kb, qb = f.shape[0], n.shape[0]
    rows4 = list_ref.shape[0]
    peers = rows4 // (2 * cap)
    got = part_ref[...] + add_rows(list_ref[...], other_ref[...])
    far, bose = gather_pair(pair_ref[...], got)
    contributions = add_rows(sp_ref[...], phonon_terms(far, bose, b0_ref, b1_ref))
    lists = jnp.concatenate(
        [blocks(ref, peers // 2, kb + qb, 8) for ref in (same_ref, other_ref)], axis=0
    ).astype(bf16)
    asked_ref[...] = lists
    x = iota((rows4, 8 * peers), 0)
    r = x % (2 * cap)
    kind = jnp.where(r < cap, 0, 1)
    at = iota((rows4, 8 * peers), 1) == 8 * block_of(x // (2 * cap), peers) + kind
    asked = dot(jnp.where(at, 1.0, 0.0).astype(bf16), lists)
    r = iota((rows4, 128), 0) % (2 * cap)
    lane = iota((rows4, 128), 1)
    wanted = lane == lax.axis_index("bulk") * cap + r % cap
    col = jnp.sum(jnp.where(wanted, asked, 0.0), axis=1, keepdims=True)
    col = col + jnp.where(r[:, :1] < cap, 0.0, float(kb))
    hot = jnp.where(lane.astype(f32) == col, 1.0, 0.0).astype(bf16)
    hot_ref[...] = hot
    base = n - DT * decay_ref[...] * (n - thermal_of(energy_ref))
    parts = forward_parts(w_ref, held_ref, fetched_ref, c_ref, c_hbm, sems)
    rate = electron_rate(sk_ref[...], far, bose, f, parts, w_ref, o0, o1)
    f1 = f + DT * rate
    e_ref[...] = rate
    f1_ref[...] = f1
    put_broadcast(send, add_rows(hot, padded(f1, base)), contributions)


def middle_kernel(
    cap,
    ends,
    part_ref,
    total_ref,
    other_ref,
    share_ref,
    serve_ref,
    f_ref,
    e_ref,
    own_ref,
    n_ref,
    energy_ref,
    decay_ref,
    pair_ref,
    sk_ref,
    sp_ref,
    b0_ref,
    b1_ref,
    held_ref,
    fetched_ref,
    c_hbm,
    send,
    *refs,
):
    w_ref, c_ref, sems, o0, o1 = refs[-5:]
    start_chunks(c_hbm, c_ref, sems)
    chips = serve_ref.shape[0] // (4 * cap)
    weight = DT / 2.0 if ends else DT
    part, total = half_of_devices(cap, chips, weight, 1, other_ref, share_ref)
    got = part_ref[...] + part
    total = total_ref[...] + total
    far, bose = gather_pair(pair_ref[...], got)
    terms = phonon_terms(far, bose, b0_ref, b1_ref)
    contributions = add_rows(sp_ref[...], terms)
    n = n_ref[...]
    own = own_ref[...]
    parts = forward_parts(w_ref, held_ref, fetched_ref, c_ref, c_hbm, sems)
    if ends:
        n2_ref, e2_ref, f3_ref = refs[:3]
        n2_ref[...] = n + (DT / 2.0) * total
        rate = electron_rate(sk_ref[...], far, bose, own, parts, w_ref, o0, o1)
        f3 = own + DT * rate
        e2_ref[...] = rate
        f3_ref[...] = f3
        to_wire(add_rows(serve_ref[...], padded(f3)) + contributions, send)
    else:
        base_ref, f2_ref = refs[:2]
        thermal = thermal_of(energy_ref)
        decay = decay_ref[...]
        p0 = total - decay * (n - thermal)
        n1 = n + DT * p0
        base = n + (DT / 2.0) * (p0 - decay * (n1 - thermal))
        base_ref[...] = base
        rate = electron_rate(sk_ref[...], far, bose, own, parts, w_ref, o0, o1)
        f2 = f_ref[...] + (DT / 2.0) * (e_ref[...] + rate)
        f2_ref[...] = f2
        put_broadcast(send, add_rows(serve_ref[...], padded(f2, base)), contributions)


def backward_kernel(f_ref, gk_ref, c_hbm, b0_ref, b1_ref, w_ref, c_ref, sems):
    start_chunks(c_hbm, c_ref, sems)
    own = add_rows(gk_ref[...], f_ref[...])
    backward_pass(own, c_hbm, c_ref, sems, w_ref, b0_ref, b1_ref)


def phonon_kernel(
    kb,
    recv,
    n_ref,
    energy_ref,
    decay_ref,
    pair_ref,
    st4_ref,
    sp8_ref,
    s8_ref,
    b0_ref,
    b1_ref,
    send,
    p_ref,
    n1_ref,
    far_ref,
):
    n = n_ref[...]
    got = from_wire(recv)
    thermal = thermal_of(energy_ref)
    rate = add_rows(st4_ref[...], got) - decay_ref[...] * (n - thermal)
    n1 = n + DT * rate
    p_ref[...] = rate
    n1_ref[...] = n1
    far = add_rows(pair_ref[:, : got.shape[0]], got)
    far_ref[...] = far
    gain = far * flat(b0_ref)
    both = jnp.concatenate([gain, gain - (1.0 - far) * flat(b1_ref)], axis=0)
    state = padded(jnp.zeros((kb, 128), f32), n1)
    to_wire(add_rows(s8_ref[...], state) + add_rows(sp8_ref[...], both), send)


def last_kernel(recv, *refs):
    far_ref, f_ref, f1_ref, e_ref, n_ref, n1_ref, p_ref, energy_ref, decay_ref = refs[:9]
    gp8_ref, sk_ref, st8a_ref, st8b_ref, held_ref, c_hbm = refs[9:15]
    refs = refs[15:]
    f2_ref, n2_ref, w_ref, c_ref, sems, o0, o1 = refs
    start_chunks(c_hbm, c_ref, sems)
    got = from_wire(recv)
    n, n1 = n_ref[...], n1_ref[...]
    bose = add_rows(gp8_ref[...], got)
    thermal = thermal_of(energy_ref)
    p1 = (
        add_rows(st8a_ref[...], got)
        + n1 * add_rows(st8b_ref[...], got)
        - decay_ref[...] * (n1 - thermal)
    )
    n2 = n + (DT / 2.0) * (p_ref[...] + p1)
    n2_ref[...] = n2
    parts = forward_parts(w_ref, held_ref, None, c_ref, c_hbm, sems)
    rate = electron_rate(sk_ref[...], far_ref[...], bose, f1_ref[...], parts, w_ref, o0, o1)
    f2 = f_ref[...] + (DT / 2.0) * (e_ref[...] + rate)
    f2_ref[...] = f2


def call(kernel, name, outs, scratch=(), spaces=None, out_spaces=None, flops=0, seen=0):
    def run(*args):
        places = dict(spaces or {})
        args = [
            pltpu.with_memory_space_constraint(x, pltpu.HBM)
            if places.get(i) is pltpu.HBM
            else x
            for i, x in enumerate(args)
        ]
        specs = [
            pl.BlockSpec(memory_space=places.get(i, pltpu.VMEM)) for i in range(len(args))
        ]
        return pl.pallas_call(
            kernel,
            out_shape=[
                (out_spaces or {}).get(i, jax.ShapeDtypeStruct)(*o) for i, o in enumerate(outs)
            ],
            in_specs=specs,
            out_specs=[
                pl.BlockSpec(memory_space=(out_spaces or {}).get(i, pltpu.VMEM))
                for i in range(len(outs))
            ],
            scratch_shapes=list(scratch),
            compiler_params=pltpu.CompilerParams(vmem_limit_bytes=VMEM_LIMIT),
            cost_estimate=pl.CostEstimate(
                flops=flops, bytes_accessed=seen, transcendentals=0
            ),
            name=name,
        )(*args)

    return run


def on_device(
    electrons,
    phonons,
    phonon_energy,
    phonon_decay,
    coupling,
    tile_kblock,
    tile_partner,
    tile_qslot,
    tile_count,
    partner_need,
    phonon_need,
):
    devices = lax.axis_size("bulk")
    kb = electrons.shape[0]
    qb = phonons.shape[0]
    tiles = coupling.shape[0]
    cap = partner_need.shape[1] // devices
    assert cap == phonon_need.shape[1] // devices and kb + qb <= 128
    rows4 = devices * 2 * cap
    rows8 = devices * 4 * cap
    groups = tiles // 8
    held = HELD_CHUNKS * (tiles // CHUNKS)
    weights = pltpu.VMEM((groups, 16, 1024), bf16)
    streams = [weights, pltpu.VMEM(coupling.shape, bf16), pltpu.SemaphoreType.DMA((CHUNKS,))]
    rest = (tiles - held, 128, 128)
    rest_sems = pltpu.SemaphoreType.DMA((CHUNKS - HELD_CHUNKS,))
    forward_streams = [weights, pltpu.VMEM(rest, bf16), rest_sems]
    sums = [pltpu.VMEM((groups, 8, 128), f32)] * 2
    pass_out = [((groups, 8, 128), f32)] * 2
    block4 = ((rows4, 128), f32)
    block8 = ((rows8, 128), f32)

    work = dict(flops=2 * tiles * 16 * 128 * 128, seen=tiles * 128 * 128 * 2)

    def exchange(x):
        order = [[(i + devices // 4 * 2) % devices for i in range(devices)]]
        return lax.all_to_all(
            x, "bulk", split_axis=0, concat_axis=0, tiled=True, axis_index_groups=order
        )

    ints = ((1, tiles), jnp.int32)
    lists = ((1, partner_need.shape[1]), jnp.int32)
    small = [((kb, 128), f32)] + [((qb, 128), f32)] * 3 + [ints] * 3
    step_rows = kb + qb + 8
    slots = devices * cap
    wide = 8 + slots
    assert step_rows % 8 == 0 and slots % 8 == 0 and slots <= 128
    assert devices % 2 == 0 and cap == 2
    chips = devices // 2
    same_core = [
        [(i + chips // 2) % chips * 2 + core for i in range(chips)] for core in (0, 1)
    ]

    def to_chips(x):
        return lax.all_to_all(
            x, "bulk", split_axis=0, concat_axis=0, tiled=True, axis_index_groups=same_core
        )

    def between_cores(x):
        return lax.ppermute(x, "bulk", [(i, i ^ 1) for i in range(devices)])

    f, n, energy, decay, kblock, partner, qslot, pneed, qneed, send = call(
        functools.partial(need_kernel, cap),
        "need",
        small + [lists, lists, ((chips * step_rows, 128), f32)],
        [
            pltpu.SemaphoreType.DMA((9,)),
            pltpu.VMEM((step_rows, 128), f32),
            pltpu.SemaphoreType.DMA((chips,)),
        ],
        spaces={i: pltpu.HBM for i in range(9)},
        out_spaces={9: pltpu.HBM},
    )(
        electrons,
        phonons,
        phonon_energy,
        phonon_decay,
        tile_kblock.reshape(1, tiles),
        tile_partner.reshape(1, tiles),
        tile_qslot.reshape(1, tiles),
        partner_need,
        phonon_need,
    )
    same = to_chips(send)
    c_held, c_rest, pair, gk, sk, sp, sp4, near, far_picks, mine, b0, b1 = call(
        functools.partial(prepare_kernel, cap),
        "prepare",
        [
            ((held, 128, 128), bf16),
            (rest, bf16),
            ((tiles, 2 * rows4), bf16),
            ((tiles, kb), bf16),
            ((kb, tiles), bf16),
            ((slots, tiles), bf16),
            ((rows4, tiles), bf16),
            ((rows4, chips * step_rows), bf16),
            ((rows4, chips * step_rows), bf16),
            ((rows4, 128), f32),
        ]
        + pass_out,
        [*streams, pltpu.VMEM(rest, bf16), rest_sems],
        spaces={0: pltpu.SMEM, 7: pltpu.HBM},
        out_spaces={1: pltpu.HBM},
        **work,
    )(tile_count, kblock, partner, qslot, f, pneed, qneed, coupling)
    same, c_held, b0 = lax.optimization_barrier((same, c_held, b0))
    wide_block = ((chips * wide, 128), f32)
    k_rows, q_rows = ((kb, 128), f32), ((qb, 128), f32)
    width = tiles // CHUNKS
    fetched = ((width, 128, 128), bf16)
    fetch_sem = pltpu.SemaphoreType.DMA((1,))
    short = (rest[0] - width, 128, 128)
    short_sems = pltpu.SemaphoreType.DMA((CHUNKS - HELD_CHUNKS - 1,))
    forward_scratch = [weights, pltpu.VMEM(short, bf16), short_sems] + sums
    other = between_cores(same)
    part, c_fetched = call(
        near_rows_kernel,
        "near_rows",
        [block4, fetched],
        [fetch_sem],
        spaces={2: pltpu.HBM},
        out_spaces={1: pltpu.VMEM},
    )(same, near, c_rest)
    send, e0, f1, serve, asked = call(
        functools.partial(first_kernel, cap),
        "first",
        [wide_block, k_rows, k_rows, ((rows4, 128), bf16), ((8 * devices, 128), bf16)],
        forward_scratch,
        spaces={15: pltpu.HBM},
        **work,
    )(same, other, part, far_picks, f, n, energy, decay, pair, sk, sp, b0, b1, c_held, c_fetched, c_rest)
    share, gp8, sp8, s8, st4, st8a, st8b = call(
        functools.partial(serve_kernel, cap, kb, qb),
        "serve",
        [
            ((rows4 + qb, devices * slots), bf16),
            ((tiles, rows8), bf16),
            ((rows8, 2 * tiles), bf16),
            ((rows8, 128), bf16),
            ((qb, rows4), bf16),
            ((qb, rows8), bf16),
            ((qb, rows8), bf16),
        ],
        spaces={0: pltpu.SMEM},
    )(tile_count, qslot, asked, serve, mine)
    back = call(backward_kernel, "backward", pass_out, streams, spaces={2: pltpu.HBM}, **work)

    def middle(ends, send, outs, f, e, own, n, contributions, share):
        same = to_chips(send)
        b0, b1 = back(own, gk, coupling)
        same, b0, share = lax.optimization_barrier((same, b0, share))
        other = between_cores(same)
        weight = DT / 2.0 if ends else DT
        part, total, c_fetched = call(
            functools.partial(near_half_kernel, cap, chips, weight),
            "near_half",
            [block4, q_rows, fetched],
            [fetch_sem],
            spaces={2: pltpu.HBM},
            out_spaces={2: pltpu.VMEM},
        )(same, share, c_rest)
        return call(
            functools.partial(middle_kernel, cap, ends),
            "middle",
            outs,
            forward_scratch,
            spaces={18: pltpu.HBM},
            **work,
        )(
            part, total, other, share, serve, f, e, own, n, energy, decay,
            pair, sk, contributions, b0, b1, c_held, c_fetched, c_rest,
        )

    send, base, f2 = middle(False, send, [wide_block, q_rows, k_rows], f, e0, f1, n, sp, share)
    send, n2, e2, f3 = middle(
        True, send, [block4, q_rows, k_rows, k_rows], f2, e0, f2, base, sp4, share
    )
    recv = exchange(send)
    b0, b1 = back(f3, gk, coupling)
    send, p2, n3, far = call(
        functools.partial(phonon_kernel, kb),
        "phonon",
        [block8, q_rows, q_rows, ((tiles, 128), f32)],
    )(recv, n2, energy, decay, pair, st4, sp8, s8, b0, b1)
    recv = exchange(send)
    f, n = call(
        last_kernel,
        "last",
        [k_rows, q_rows],
        forward_streams + sums,
        spaces={15: pltpu.HBM},
        **work,
    )(
        recv, far, f2, f3, e2, n2, n3, p2, energy, decay,
        gp8, sk, st8a, st8b, c_held, c_rest,
    )
    return (f, n)


def solution(mesh):
    placed = (
        P(("groups", "bulk"), None),
        P(("groups", "bulk"), None),
        P("bulk", None),
        P("bulk", None),
        P("bulk", None, None),
        P("bulk"),
        P("bulk"),
        P("bulk"),
        P("bulk"),
        P("bulk", None),
        P("bulk", None),
    )
    return jax.shard_map(
        on_device,
        mesh=mesh,
        in_specs=placed,
        out_specs=(P(("groups", "bulk"), None), P(("groups", "bulk"), None)),
        check_vma=False,
    )
```
